128 devices in a mesh: seq: 4 (over x), ctx: 16 (over z, y), fsdp: 2 (over core).
Axes of the slice: x: 4, y: 4, z: 4, core: 2. Of those that a mesh axis runs over, the one named last changes fastest.
Arguments:
- tokens: bfloat16 [8, 2560, 1024], P(('seq', 'fsdp'), 'ctx'), may hold values from -6 to 6
- pairs: int32 [8, 16], P(('seq', 'fsdp')), may hold values from 0 to 15, each once within a row
- w_query: bfloat16 [1024, 1024], P(('ctx', 'fsdp')), may hold values from -0.1875 to 0.1875
- w_key: bfloat16 [1024, 512], P(('ctx', 'fsdp')), may hold values from -0.1875 to 0.1875
- w_value: bfloat16 [1024, 512], P(('ctx', 'fsdp')), may hold values from -0.1875 to 0.1875
- w_out: bfloat16 [1024, 1024], P(('ctx', 'fsdp')), may hold values from -2.5 to 2.5
- w_gate: bfloat16 [1024, 4608], P(('ctx', 'fsdp')), may hold values from -0.1875 to 0.1875
- w_up: bfloat16 [1024, 4608], P(('ctx', 'fsdp')), may hold values from -0.1875 to 0.1875
- w_down: bfloat16 [4608, 1024], P(('ctx', 'fsdp')), may hold values from -0.09375 to 0.09375
- g_attn: float32 [1024], replicated, may hold values from 0.1 to 1.9
- g_query: float32 [64], replicated, may hold values from 0.1 to 1.9
- g_key: float32 [64], replicated, may hold values from 0.1 to 1.9
- g_ffn: float32 [1024], replicated, may hold values from 0.1 to 1.9
- cotangent: bfloat16 [8, 2560, 1024], P(('seq', 'fsdp'), 'ctx'), may hold values from -6 to 6
Outputs:
- output: bfloat16 [8, 2560, 1024], P(('seq', 'fsdp'), 'ctx')
- grad_tokens: bfloat16 [8, 2560, 1024], P(('seq', 'fsdp'), 'ctx')
- grad_w_query: float32 [1024, 1024], P(('ctx', 'fsdp'))
- grad_w_key: float32 [1024, 512], P(('ctx', 'fsdp'))
- grad_w_value: float32 [1024, 512], P(('ctx', 'fsdp'))
- grad_w_out: float32 [1024, 1024], P(('ctx', 'fsdp'))
- grad_w_gate: float32 [1024, 4608], P(('ctx', 'fsdp'))
- grad_w_up: float32 [1024, 4608], P(('ctx', 'fsdp'))
- grad_w_down: float32 [4608, 1024], P(('ctx', 'fsdp'))
- grad_g_attn: float32 [1024], replicated
- grad_g_query: float32 [64], replicated
- grad_g_key: float32 [64], replicated
- grad_g_ffn: float32 [1024], replicated
The draws below stay inside these ranges and needn't reach their ends.
Inputs may be any that keep to these rules, and one draw needn't show every extreme that they name: Each row of pairs holds every number of 0 to 15 once: device c of the context axis holds blocks pairs[s, c] and 31 - pairs[s, c] of sequence s, in this order, each of 80 tokens.
All inputs are finite; a program needn't handle non-finite values.
Results may differ from the reference program's by a relative error of at most 0.025.
Values may be sent and summed in bfloat16 or wider, within the bound.
A program may use at most 192 MiB of HBM per device.

```python
import math
import jax
import jax.numpy as jnp
from jax import lax

D = 1024
H = 16
KV = 8
HD = 64
FF = 4608
LEN = 2560
BLK = 80
SEQS = 8
HQ = 1024
KVD = 512
N_CTX = 16


def block_levels(own_key, dims, cuts, low, largest):
    factor_of = 1.0
    for dim, parts in cuts:
        steps = jax.random.uniform(jax.random.fold_in(jax.random.fold_in(own_key, 6), dim), (parts,), jnp.float32, low / len(cuts), largest / len(cuts))
        factor_of = factor_of * jnp.repeat(jnp.exp(steps), dims[dim] // parts).reshape((-1,) + (1,) * (len(dims) - 1 - dim))
    return factor_of


def gaussian(own_key, dims, spread, reach, pieces=(), kind=jnp.bfloat16):
    values = spread * jax.random.normal(own_key, dims, jnp.float32)
    if pieces:
        values = values * block_levels(own_key, dims, pieces, -0.22, 0.18)
    return jnp.clip(values, -reach, reach).astype(kind)


def setup_inputs(seed: int = 0) -> dict:
    arg_keys = jax.random.split(jax.random.key(seed), 15)
    return {
        "tokens": gaussian(arg_keys[0], (SEQS, LEN, D), 1.0, 6.0, ((0, 8), (1, 16))),
        "pairs": jax.vmap(lambda own: jax.random.permutation(own, N_CTX))(jax.random.split(arg_keys[1], SEQS)).reshape((SEQS, N_CTX)).astype(jnp.int32),
        "w_query": gaussian(arg_keys[2], (D, HQ), D ** -0.5, 0.1875, ((0, 32),)),
        "w_key": gaussian(arg_keys[3], (D, KVD), D ** -0.5, 0.1875, ((0, 32),)),
        "w_value": gaussian(arg_keys[4], (D, KVD), D ** -0.5, 0.1875, ((0, 32),)),
        "w_out": gaussian(arg_keys[5], (HQ, D), (max(4, H * HD * 16 // LEN)) ** -0.5, 2.5, ((0, 32),)),
        "w_gate": gaussian(arg_keys[6], (D, FF), D ** -0.5, 0.1875, ((0, 32),)),
        "w_up": gaussian(arg_keys[7], (D, FF), D ** -0.5, 0.1875, ((0, 32),)),
        "w_down": gaussian(arg_keys[8], (FF, D), FF ** -0.5, 0.09375, ((0, 32),)),
        "g_attn": jnp.clip(1.0 + 0.18 * jax.random.normal(arg_keys[9], (D,), jnp.float32), 0.1, 1.9),
        "g_query": jnp.clip(1.0 + 0.18 * jax.random.normal(arg_keys[10], (HD,), jnp.float32), 0.1, 1.9),
        "g_key": jnp.clip(1.0 + 0.18 * jax.random.normal(arg_keys[11], (HD,), jnp.float32), 0.1, 1.9),
        "g_ffn": jnp.clip(1.0 + 0.18 * jax.random.normal(arg_keys[12], (D,), jnp.float32), 0.1, 1.9),
        "cotangent": gaussian(arg_keys[13], (SEQS, LEN, D), 1.0, 6.0, ((0, 8), (1, 16))),
    }


EPSILON = 1e-05
ROPE_BASE = 1000000.0
PRECISE = lax.Precision.HIGHEST
NEG_LARGE = -1e+30

@jax.custom_vjp
def low(v):
    return lax.optimization_barrier(v.astype(jnp.bfloat16)).astype(jnp.float32)

@jax.custom_vjp
def low_back(v):
    return v

def low_keep(v):
    return (low(v), None)

def low_pass(kept, grad):
    return (grad,)

def back_keep(v):
    return (v, None)

def back_low(kept, grad):
    return (low(grad),)
low.defvjp(low_keep, low_pass)
low_back.defvjp(back_keep, back_low)

def rms_norm(values_in, gain):
    inv_rms = lax.rsqrt(lax.optimization_barrier(jnp.mean(values_in * values_in, axis=-1, keepdims=True)) + EPSILON)
    return values_in * inv_rms * gain

def positions_of(pair_row):
    blocks_of = jnp.stack([pair_row, 2 * N_CTX - 1 - pair_row], axis=1).reshape(-1)
    offsets = jnp.arange(BLK, dtype=jnp.int32)
    return (blocks_of[:, None] * BLK + offsets[None, :]).reshape(-1)

def angle_tables(positions):
    frequencies = ROPE_BASE ** (-jnp.arange(0, HD // 2, dtype=jnp.float32) * 2.0 / HD)
    phases = positions.astype(jnp.float32)[:, None] * frequencies[None, :]
    phases = jnp.concatenate([phases, phases], axis=-1)
    return (jnp.cos(phases), jnp.sin(phases))

def rotate(values_in, cos_table, sin_table):
    half_dim = HD // 2
    turned = jnp.concatenate([-values_in[..., half_dim:], values_in[..., :half_dim]], axis=-1)
    return values_in * cos_table[:, None, :] + turned * sin_table[:, None, :]

def attention(queries, keys, values, positions):
    q_block_size = math.gcd(LEN, 512)
    block_count = LEN // q_block_size
    q_blocks = queries.reshape(block_count, q_block_size, KV, H // KV, HD)
    pos_blocks = positions.reshape(block_count, q_block_size)

    def one_block(q_block, q_pos, key_heads, value_heads):
        raw_scores = jnp.einsum('qkgd,nkd->kgqn', q_block, key_heads, precision=PRECISE) * HD ** (-0.5)
        raw_scores = low_back(raw_scores)
        allowed = positions[None, :] <= q_pos[:, None]
        masked = jnp.where(allowed, raw_scores, NEG_LARGE)
        row_top = lax.optimization_barrier(jnp.max(masked, axis=-1, keepdims=True))
        weights_exp = jnp.exp(masked - row_top)
        row_total = lax.optimization_barrier(jnp.sum(weights_exp, axis=-1))
        summed = jnp.einsum('kgqn,nkd->kgqd', low(weights_exp), value_heads, precision=PRECISE)
        result_block = summed / row_total[..., None]
        return result_block.transpose(2, 0, 1, 3).reshape(q_block_size, HQ)
    checked = jax.checkpoint(one_block)
    results = lax.map(lambda pair_in: checked(pair_in[0], pair_in[1], keys, values), (q_blocks, pos_blocks))
    return results.reshape(LEN, HQ)

def block_layer(inputs, w_query, w_key, w_value, w_out, w_gate, w_up, w_down, g_attn, g_query, g_key, g_ffn, positions):
    h_attn = low(rms_norm(inputs, g_attn))
    q_proj = low_back(jnp.dot(h_attn, w_query, precision=PRECISE))
    k_proj = low_back(jnp.dot(h_attn, w_key, precision=PRECISE))
    v_proj = low_back(jnp.dot(h_attn, w_value, precision=PRECISE))
    cos_table, sin_table = angle_tables(positions)
    queries = low(rotate(rms_norm(q_proj.reshape(LEN, H, HD), g_query), cos_table, sin_table))
    keys = low(rotate(rms_norm(k_proj.reshape(LEN, KV, HD), g_key), cos_table, sin_table))
    values = low(v_proj).reshape(LEN, KV, HD)
    attended = attention(queries, keys, values, positions)
    mixed = low(low_back(attended))
    branch = low_back(jnp.dot(mixed, w_out, precision=PRECISE))
    middle = inputs + branch
    h_ffn = low(rms_norm(middle, g_ffn))
    gate_act = low_back(jnp.dot(h_ffn, w_gate, precision=PRECISE))
    up_act = low_back(jnp.dot(h_ffn, w_up, precision=PRECISE))
    hidden = low(jax.nn.silu(gate_act) * up_act)
    result = low_back(jnp.dot(hidden, w_down, precision=PRECISE))
    return middle + result

def reference(tokens, pairs, w_query, w_key, w_value, w_out, w_gate, w_up, w_down, g_attn, g_query, g_key, g_ffn, cotangent):
    params = (w_query.astype(jnp.float32), w_key.astype(jnp.float32), w_value.astype(jnp.float32), w_out.astype(jnp.float32), w_gate.astype(jnp.float32), w_up.astype(jnp.float32), w_down.astype(jnp.float32), g_attn, g_query, g_key, g_ffn)

    def one_sequence(sums_in, seq_item):
        seq_tokens, pair_row, seq_cot = seq_item
        positions = positions_of(pair_row)

        def layer_forward(inputs, *weights_in):
            return block_layer(inputs, *weights_in, positions)
        layer_out, pullback = jax.vjp(layer_forward, seq_tokens.astype(jnp.float32), *params)
        grads = pullback(seq_cot.astype(jnp.float32))
        new_sums = tuple((acc + part for acc, part in zip(sums_in, grads[1:])))
        return (new_sums, (layer_out.astype(jnp.bfloat16), grads[0].astype(jnp.bfloat16)))
    zeros_init = tuple((jnp.zeros(p.shape, jnp.float32) for p in params))
    sums_out, (output, grad_tokens) = lax.scan(one_sequence, zeros_init, (tokens, pairs, cotangent))
    return (output, grad_tokens, sums_out[0], sums_out[1], sums_out[2], sums_out[3], sums_out[4], sums_out[5], sums_out[6], sums_out[7], sums_out[8], sums_out[9], sums_out[10])
```

```python
import functools

import jax
import jax.numpy as jnp
import numpy as np
from jax import lax
from jax.experimental import pallas as pl
from jax.experimental.pallas import tpu as pltpu
from jax.sharding import Mesh
from jax.sharding import PartitionSpec as P

D = 1024
H = 16
KV = 8
HD = 64
FF = 4608
LEN = 2560
BLK = 80
ROWS = 2 * BLK
NX = 4
FX = FF // NX
QX = H * HD // NX
KX = KV * HD // NX
TILE = 512
N_TILES = LEN // TILE
CTX = ("ctx_0", "ctx_1")
CTX_FSDP = ("ctx_0", "ctx_1", "fsdp")
SEQ_CTX_FSDP = ("seq", "ctx_0", "ctx_1", "fsdp")
EPSILON = 1e-05
ROPE_BASE = 1000000.0
MESH = pl.DeviceIdType.MESH
BF16 = jnp.bfloat16
F32 = jnp.float32
VMEM_BYTES = 56 * 1024 * 1024


SIZE = {"x": 4, "c": 16, "p": 32, "t": 16, "r": 16, "d": 4}


def coords():
    return tuple(lax.axis_index(a) for a in SEQ_CTX_FSDP)


def target(group, t):
    s, z, y, c = coords()
    if group == "x":
        return (t, z, y, c), s
    if group == "c":
        return (s, t // 4, lax.rem(t, 4), c), z * 4 + y
    if group == "p":
        return (s, t // 8, lax.rem(t // 2, 4), lax.rem(t, 2)), (z * 4 + y) * 2 + c
    if group == "t":
        return (z, t // 4, lax.rem(t, 4), c), s * 4 + y
    if group == "d":
        return (t, s, y, c), z
    return (t // 4, s, lax.rem(t, 4), c), z * 4 + y


def source(group, t):
    s, z, y, c = coords()
    if group == "t":
        return (t // 4, s, lax.rem(t, 4), c)
    if group == "r":
        return (z, t // 4, lax.rem(t, 4), c)
    if group == "d":
        return (z, t, y, c)
    return target(group, t)[0]


def own(group):
    s, z, y, c = coords()
    if group == "t":
        return s == z, z * 4 + y, s * 4 + y
    if group == "r":
        return s == z, s * 4 + y, z * 4 + y
    if group == "d":
        return s == z, s, z
    me = target(group, 0)[1]
    return None, me, me


def exchange_kernel(items, *refs):
    n = len(items)
    srcs, outs, sems = refs[:n], refs[n : 2 * n], refs[2 * n :]
    barrier = pltpu.get_barrier_semaphore()
    expected = 0
    starts = []
    for i, (g, _) in enumerate(items):
        has_own, sent, _ = own(g)
        size = SIZE[g]
        if has_own is None:
            starts.append((jnp.int32(1), sent))
            expected = expected + size - 1
        else:
            starts.append((has_own.astype(jnp.int32), sent))
            expected = expected + size - has_own.astype(jnp.int32)
        place = own(g)[2]
        first = starts[i][0]

        def greet(k, carry, g=g, size=size, place=place):
            dev = source(g, lax.rem(place + k, size))
            pl.semaphore_signal(barrier, inc=1, device_id=dev, device_id_type=MESH)
            return carry

        lax.fori_loop(first, size, greet, 0)

    def own_copy(i):
        g, mode = items[i]
        _, sent, place = own(g)
        src = srcs[i] if mode == "ag" else srcs[i].at[sent]
        return pltpu.make_async_copy(src, outs[i].at[place], sems[3 * i + 2])

    for i, (g, _) in enumerate(items):
        if own(g)[0] is None:
            own_copy(i).start()
        else:
            pl.when(own(g)[0])(lambda i=i: own_copy(i).start())
    pl.semaphore_wait(barrier, expected)

    def remote(i, t, place):
        g, mode = items[i]
        dev, there = target(g, t)
        src = srcs[i] if mode == "ag" else srcs[i].at[t]
        return pltpu.make_async_remote_copy(
            src_ref=src,
            dst_ref=outs[i].at[there if place is None else place],
            send_sem=sems[3 * i].at[t],
            recv_sem=sems[3 * i + 1].at[there if place is None else place],
            device_id=dev,
            device_id_type=MESH,
        )

    for i, (g, _) in enumerate(items):
        first, sent = starts[i]

        def send(k, carry, i=i, g=g, sent=sent):
            remote(i, lax.rem(sent + k, SIZE[g]), None).start()
            return carry

        lax.fori_loop(first, SIZE[g], send, 0)
    for i, (g, _) in enumerate(items):
        first, sent = starts[i]
        place = own(g)[2]

        def drain(k, carry, i=i, g=g, sent=sent, place=place):
            remote(i, lax.rem(sent + k, SIZE[g]), None).wait_send()
            remote(i, lax.rem(sent + k, SIZE[g]), lax.rem(place + k, SIZE[g])).wait_recv()
            return carry

        lax.fori_loop(first, SIZE[g], drain, 0)
        if own(g)[0] is None:
            own_copy(i).wait()
        else:
            pl.when(own(g)[0])(lambda i=i: own_copy(i).wait())


def exchange(number, name, *parts):
    items = tuple((g, m) for g, m, _ in parts)
    arrays = [a for _, _, a in parts]
    outs = [
        jax.ShapeDtypeStruct((SIZE[g],) + (a.shape if m == "ag" else a.shape[1:]), a.dtype)
        for g, m, a in parts
    ]
    scratch = []
    for g, _ in items:
        scratch += [
            pltpu.SemaphoreType.DMA((SIZE[g],)),
            pltpu.SemaphoreType.DMA((SIZE[g],)),
            pltpu.SemaphoreType.DMA,
        ]
    return pl.pallas_call(
        functools.partial(exchange_kernel, items),
        out_shape=outs,
        in_specs=[pl.BlockSpec(memory_space=pl.ANY)] * len(arrays),
        out_specs=[pl.BlockSpec(memory_space=pl.ANY)] * len(arrays),
        scratch_shapes=scratch,
        compiler_params=pltpu.CompilerParams(collective_id=number, has_side_effects=True),
        name=name,
    )(*arrays)


def lanes(shape):
    return lax.broadcasted_iota(jnp.int32, shape, len(shape) - 1)


def low_half(shape):
    return lanes(shape) < HD


def swap(v):
    return pltpu.roll(v, HD, 1)


def swap_halves(v):
    first = lax.rem(lanes(v.shape), HD) < HD // 2
    return jnp.where(first, pltpu.roll(v, 2 * HD - HD // 2, 1), pltpu.roll(v, HD // 2, 1))


def head_mean(v):
    m = low_half(v.shape)
    a = jnp.sum(jnp.where(m, v, 0.0), axis=-1, keepdims=True)
    b = jnp.sum(jnp.where(m, 0.0, v), axis=-1, keepdims=True)
    return jnp.where(m, a, b) * (1.0 / HD)


def nt(a, b):
    return lax.dot_general(a, b, (((1,), (1,)), ((), ())), preferred_element_type=F32)


def nn(a, b):
    return lax.dot_general(a, b, (((1,), (0,)), ((), ())), preferred_element_type=F32)


def tn(a, b):
    return lax.dot_general(a, b, (((0,), (0,)), ((), ())), preferred_element_type=F32)


def rows_of(block):
    return pl.ds(pl.multiple_of(block * BLK, 16), BLK)


def rope_rows(blocks, table, s):
    return jnp.concatenate([table[rows_of(blocks[2 * s]), :], table[rows_of(blocks[2 * s + 1]), :]], 0)


def project_kernel(blocks, h, w, cos_t, sin_t, g_q, g_k, send, raw, acc):
    acc[...] = nn(h[...], w[...])
    m = low_half((ROWS, 2 * HD))
    mh = low_half((BLK, 2 * HD))
    for s in range(NX):
        at = slice(s * ROWS, (s + 1) * ROWS)
        cos_r, sin_r = rope_rows(blocks, cos_t, s), rope_rows(blocks, sin_t, s)
        raw[at, :] = acc[at, : QX + KX]
        turned = []
        for p in range(3):
            v = acc[at, p * 128 : (p + 1) * 128]
            gain = g_q[...] if p < 2 else g_k[...]
            normed = v * lax.rsqrt(head_mean(v * v) + EPSILON) * gain
            turned.append(normed * cos_r + swap_halves(normed) * sin_r)
        keys = turned[2]
        swapped_keys = swap(keys)
        values = acc[at, 3 * 128 :]
        top, bottom = values[:BLK], values[BLK:]
        packed = (jnp.where(mh, top, swap(bottom)), jnp.where(mh, swap(top), bottom))
        for hh in range(4):
            q = turned[hh // 2]
            q = q if hh % 2 == 0 else swap(q)
            k = swapped_keys if hh < 2 else keys
            send[s * 4 + hh, :ROWS, :] = jnp.where(m, q, k).astype(BF16)
            send[s * 4 + hh, ROWS:, :] = packed[hh // 2].astype(BF16)


def project(blocks, h, w, cos_t, sin_t, g_q, g_k):
    return pl.pallas_call(
        project_kernel,
        grid_spec=pltpu.PrefetchScalarGridSpec(
            num_scalar_prefetch=1,
            in_specs=[pl.BlockSpec(memory_space=pltpu.VMEM)] * 6,
            out_specs=[pl.BlockSpec(memory_space=pltpu.VMEM)] * 2,
            scratch_shapes=[pltpu.VMEM((NX * ROWS, QX + 2 * KX), F32)],
        ),
        out_shape=[
            jax.ShapeDtypeStruct((16, ROWS + BLK, 2 * HD), BF16),
            jax.ShapeDtypeStruct((NX * ROWS, QX + KX), F32),
        ],
        compiler_params=pltpu.CompilerParams(vmem_limit_bytes=VMEM_BYTES),
        name="project",
    )(blocks, h, w, cos_t, sin_t, g_q, g_k)


def attend_kernel(pair, recv, out, q_s, k_s, v_s, o_t, inv, o_s, v_t):
    m = low_half((BLK, 2 * HD))
    for j in range(16):
        packed = recv[j, ROWS:, :].astype(F32)
        for half in range(2):
            block = pair[j] if half == 0 else 31 - pair[j]
            both = recv[j, half * BLK : (half + 1) * BLK, :].astype(F32)
            vals = packed if half == 0 else swap(packed)
            q_s[rows_of(block), :] = jnp.where(m, both * HD**-0.5, 0.0).astype(BF16)
            k_s[rows_of(block), :] = jnp.where(m, swap(both), 0.0).astype(BF16)
            v_s[rows_of(block), :] = jnp.where(m, vals, 0.0).astype(BF16)
    for t in range(N_TILES):
        at = slice(t * TILE, (t + 1) * TILE)
        v_t[:, at] = v_s[at, :].T[:HD]
    causal = lax.broadcasted_iota(jnp.int32, (TILE, TILE), 0) <= lanes((TILE, TILE))
    for i in range(N_TILES):
        at = slice(i * TILE, (i + 1) * TILE)
        q = q_s[at, :]

        e = jnp.where(causal, jnp.exp(nt(k_s[at, :], q)), 0.0)
        first = (jnp.sum(e, axis=0, keepdims=True), nn(v_t[:, at], e.astype(BF16)))

        def step(t, carry, q=q):
            total, acc = carry
            there = pl.ds(pl.multiple_of(t * TILE, TILE), TILE)
            e = jnp.exp(nt(k_s[there, :], q))
            total = total + jnp.sum(e, axis=0, keepdims=True)
            return total, acc + nn(v_t[:, there], e.astype(BF16))

        total, acc = lax.fori_loop(0, i, step, first) if i else first
        over = 1.0 / total
        attended = acc * over
        o_t[:, at] = attended
        inv[:, at] = jnp.broadcast_to(over, (8, TILE))
        o_s[at, :] = jnp.concatenate([attended, jnp.zeros_like(attended)], 0).T
    for j in range(16):
        low_rows = o_s[rows_of(pair[j]), :]
        high_rows = o_s[rows_of(31 - pair[j]), :]
        out[j, :, :] = (low_rows + swap(high_rows)).astype(BF16)


def attend(pair, recv):
    wide = jax.ShapeDtypeStruct((LEN, 2 * HD), BF16)
    return pl.pallas_call(
        attend_kernel,
        grid_spec=pltpu.PrefetchScalarGridSpec(
            num_scalar_prefetch=1,
            in_specs=[pl.BlockSpec(memory_space=pltpu.VMEM)],
            out_specs=[pl.BlockSpec(memory_space=pltpu.VMEM)] * 6,
            scratch_shapes=[pltpu.VMEM((LEN, 2 * HD), F32), pltpu.VMEM((HD, LEN), BF16)],
        ),
        out_shape=[
            jax.ShapeDtypeStruct((16, BLK, 2 * HD), BF16),
            wide,
            wide,
            wide,
            jax.ShapeDtypeStruct((HD, LEN), F32),
            jax.ShapeDtypeStruct((8, LEN), F32),
        ],
        compiler_params=pltpu.CompilerParams(vmem_limit_bytes=VMEM_BYTES),
        name="attend",
    )(pair, recv)


def attend_back_kernel(pair, recv, q_s, k_s, v_s, o_t, inv, out, g_s, k_t, delta, dq_t, dk_s, dv_s):
    m = low_half((BLK, 2 * HD))
    for j in range(16):
        packed = recv[j, :, :].astype(F32)
        g_s[rows_of(pair[j]), :] = jnp.where(m, packed, 0.0).astype(BF16)
        g_s[rows_of(31 - pair[j]), :] = jnp.where(m, swap(packed), 0.0).astype(BF16)
    for t in range(N_TILES):
        at = slice(t * TILE, (t + 1) * TILE)
        k_t[:, at] = k_s[at, :].T[:HD]
        g_t = g_s[at, :].astype(F32).T[:HD]
        row = jnp.sum(g_t * o_t[:, at], axis=0, keepdims=True)
        delta[:, at] = jnp.broadcast_to(row, (8, TILE))
    dq_t[...] = jnp.zeros_like(dq_t)
    causal = lax.broadcasted_iota(jnp.int32, (TILE, TILE), 0) <= lanes((TILE, TILE))
    for i in range(N_TILES):
        at = slice(i * TILE, (i + 1) * TILE)
        k, v, kt = k_s[at, :], v_s[at, :], k_t[:, at]

        def pair_of_tiles(there, masked, k=k, v=v, kt=kt):
            q, g = q_s[there, :], g_s[there, :]
            e = jnp.exp(nt(k, q))
            if masked:
                e = jnp.where(causal, e, 0.0)
            probs = e * inv[0:1, there]
            ds = (probs * (nt(v, g) - delta[0:1, there])).astype(BF16)
            dq_t[:, there] = dq_t[:, there] + nn(kt, ds)
            return nn(ds, q), nn(probs.astype(BF16), g)

        first = pair_of_tiles(at, True)

        def step(t, carry, pair_of_tiles=pair_of_tiles):
            dk, dv = pair_of_tiles(pl.ds(pl.multiple_of(t * TILE, TILE), TILE), False)
            return carry[0] + dk, carry[1] + dv

        dk, dv = lax.fori_loop(i + 1, N_TILES, step, first) if i + 1 < N_TILES else first
        dk_s[at, :] = dk
        dv_s[at, :] = dv
    for i in range(N_TILES):
        at = slice(i * TILE, (i + 1) * TILE)
        dq = dq_t[:, at] * HD**-0.5
        dk_s[at, :] = jnp.concatenate([dq, jnp.zeros_like(dq)], 0).T + swap(dk_s[at, :])
    for j in range(16):
        for half in range(2):
            block = pair[j] if half == 0 else 31 - pair[j]
            out[j, half * BLK : (half + 1) * BLK, :] = dk_s[rows_of(block), :].astype(BF16)
        out[j, ROWS:, :] = (dv_s[rows_of(pair[j]), :] + swap(dv_s[rows_of(31 - pair[j]), :])).astype(BF16)


def attend_back(pair, recv, q_s, k_s, v_s, o_t, inv):
    return pl.pallas_call(
        attend_back_kernel,
        grid_spec=pltpu.PrefetchScalarGridSpec(
            num_scalar_prefetch=1,
            in_specs=[pl.BlockSpec(memory_space=pltpu.VMEM)] * 6,
            out_specs=pl.BlockSpec(memory_space=pltpu.VMEM),
            scratch_shapes=[
                pltpu.VMEM((LEN, 2 * HD), BF16),
                pltpu.VMEM((HD, LEN), BF16),
                pltpu.VMEM((8, LEN), F32),
                pltpu.VMEM((HD, LEN), F32),
                pltpu.VMEM((LEN, 2 * HD), F32),
                pltpu.VMEM((LEN, 2 * HD), F32),
            ],
        ),
        out_shape=jax.ShapeDtypeStruct((16, ROWS + BLK, 2 * HD), BF16),
        compiler_params=pltpu.CompilerParams(vmem_limit_bytes=VMEM_BYTES),
        name="attend_back",
    )(pair, recv, q_s, k_s, v_s, o_t, inv)


def project_back_kernel(blocks, recv, raw, h, w, cos_t, sin_t, g_q, g_k, gh, dw, gains, low):
    m = low_half((ROWS, 2 * HD))
    mh = low_half((BLK, 2 * HD))
    gq_sum = jnp.zeros((1, 2 * HD), F32)
    gk_sum = jnp.zeros((1, 2 * HD), F32)
    for s in range(NX):
        at = slice(s * ROWS, (s + 1) * ROWS)
        cos_r, sin_r = rope_rows(blocks, cos_t, s), rope_rows(blocks, sin_t, s)
        part = [recv[s * 4 + hh, :ROWS, :].astype(F32) for hh in range(4)]
        vals = [recv[s * 4 + hh, ROWS:, :].astype(F32) for hh in range(4)]
        grads = [
            jnp.where(m, part[0], swap(part[1])),
            jnp.where(m, part[2], swap(part[3])),
            jnp.where(m, swap(part[0] + part[1]), part[2] + part[3]),
        ]
        for p in range(3):
            turned = grads[p] * cos_r + swap_halves(grads[p] * sin_r)
            v = raw[at, p * 128 : (p + 1) * 128]
            gain = g_q[...] if p < 2 else g_k[...]
            r = lax.rsqrt(head_mean(v * v) + EPSILON)
            weighted = turned * gain
            grad = r * weighted - v * (r * r * r) * head_mean(weighted * v)
            low[at, p * 128 : (p + 1) * 128] = grad.astype(BF16)
            term = jnp.sum(turned * v * r, axis=0, keepdims=True)
            if p < 2:
                gq_sum = gq_sum + term
            else:
                gk_sum = gk_sum + term
        a, b = vals[0] + vals[1], vals[2] + vals[3]
        grad_v = jnp.concatenate([jnp.where(mh, a, swap(b)), jnp.where(mh, swap(a), b)], 0)
        low[at, 3 * 128 :] = grad_v.astype(BF16)
    gains[...] = jnp.concatenate([gq_sum, gk_sum, jnp.zeros((6, 2 * HD), F32)], 0)
    gh[...] = nt(low[...], w[...]).astype(BF16)
    dw[...] = tn(h[...], low[...]).astype(BF16)


def project_back(blocks, recv, raw, h, w, cos_t, sin_t, g_q, g_k):
    return pl.pallas_call(
        project_back_kernel,
        grid_spec=pltpu.PrefetchScalarGridSpec(
            num_scalar_prefetch=1,
            in_specs=[pl.BlockSpec(memory_space=pltpu.VMEM)] * 8,
            out_specs=[pl.BlockSpec(memory_space=pltpu.VMEM)] * 3,
            scratch_shapes=[pltpu.VMEM((NX * ROWS, QX + 2 * KX), BF16)],
        ),
        out_shape=[
            jax.ShapeDtypeStruct((NX * ROWS, D), BF16),
            jax.ShapeDtypeStruct((D, QX + 2 * KX), BF16),
            jax.ShapeDtypeStruct((8, 2 * HD), F32),
        ],
        compiler_params=pltpu.CompilerParams(vmem_limit_bytes=VMEM_BYTES),
        name="project_back",
    )(blocks, recv, raw, h, w, cos_t, sin_t, g_q, g_k)


def angle_constants():
    frequencies = ROPE_BASE ** (-np.arange(0, HD // 2, dtype=np.float64) * 2.0 / HD)
    phases = np.arange(LEN, dtype=np.float64)[:, None] * frequencies[None, :]
    cos, sin = np.cos(phases).astype(np.float32), np.sin(phases).astype(np.float32)
    return np.concatenate([cos] * 4, 1), np.concatenate([-sin, sin, -sin, sin], 1)


def rms_rows(values_in, gain):
    inv_rms = lax.rsqrt(jnp.mean(values_in * values_in, axis=-1, keepdims=True) + EPSILON)
    return (values_in * inv_rms * gain, inv_rms)


def rms_rows_back(values_in, gain, inv_rms, grad_in):
    weighted = grad_in * gain
    inner = jnp.mean(weighted * values_in, axis=-1, keepdims=True)
    grad_values = inv_rms * weighted - values_in * (inv_rms * inv_rms * inv_rms) * inner
    gain_terms = grad_in * values_in * inv_rms
    return (grad_values, gain_terms)


def columns_of(w, x, width):
    return lax.dynamic_slice_in_dim(w, x * width, width, axis=1)


def body(
    tokens,
    pairs,
    w_query,
    w_key,
    w_value,
    w_out,
    w_gate,
    w_up,
    w_down,
    g_attn,
    g_query,
    g_key,
    g_ffn,
    cotangent,
):
    x, z, y, c = coords()
    ctx = z * 4 + y
    cos_np, sin_np = angle_constants()
    cos_t, sin_t = jnp.asarray(cos_np), jnp.asarray(sin_np)
    gq2 = jnp.concatenate([g_query, g_query])[None]
    gk2 = jnp.concatenate([g_key, g_key])[None]

    mine = jnp.concatenate([columns_of(w_gate, x, FX), columns_of(w_up, x, FX), w_out], axis=1)
    wide = lax.all_gather(mine, CTX_FSDP, axis=0, tiled=True)
    w_gu, full_out = wide[:, : 2 * FX], wide[:, 2 * FX :]
    swap_xz = [(a * 4 + b, b * 4 + a) for a in range(4) for b in range(4)]
    down_part = lax.ppermute(columns_of(w_down, x, D // 4), ("seq", "ctx_0"), swap_xz)
    w_dn = lax.all_gather(down_part, CTX_FSDP, axis=0, tiled=True).reshape(4, FX, D // 4)

    inputs = tokens[0].astype(F32)
    normed_attn, inv_attn = rms_rows(inputs, g_attn)
    h_attn = normed_attn.astype(BF16)
    w_x = jnp.concatenate(
        [columns_of(w_query, x, QX), columns_of(w_key, x, KX), columns_of(w_value, x, KX)], axis=1
    )
    pairs_pad = jnp.pad(pairs, ((0, 7), (0, 112)))
    h_all, w_qkv, pairs_all = exchange(
        1, "gather_in", ("x", "ag", h_attn), ("p", "ag", w_x), ("x", "ag", pairs_pad)
    )
    h_all = h_all.reshape(NX * ROWS, D)
    w_qkv = w_qkv.reshape(D, QX + 2 * KX)
    pairs_all = pairs_all[:, 0, :16]
    first = lax.dynamic_slice_in_dim(pairs_all, ctx, 1, axis=1)[:, 0]
    blocks = jnp.stack([first, 31 - first], axis=1).reshape(8)
    pair = lax.dynamic_slice_in_dim(pairs_all, z, 1, axis=0)[0]

    send, raw = project(blocks, h_all, w_qkv, cos_t, sin_t, gq2, gk2)
    recv, cot_all = exchange(2, "to_heads", ("c", "a2a", send), ("x", "ag", cotangent[0]))
    heads_out, q_s, k_s, v_s, o_t, inv = attend(pair, recv)
    (mixed_parts,) = exchange(3, "to_tokens", ("t", "a2a", heads_out))
    mixed = mixed_parts.reshape(16, BLK, 2, HD).transpose(2, 1, 0, 3).reshape(ROWS, D)
    branch = jnp.dot(mixed, full_out, preferred_element_type=F32)
    middle = inputs + branch
    normed_ffn, inv_ffn = rms_rows(middle, g_ffn)
    (h4,) = exchange(4, "gather_ffn", ("x", "ag", normed_ffn.astype(BF16)))
    h4 = h4.reshape(NX * ROWS, D)
    cot4 = cot_all.reshape(NX * ROWS, D)

    gate_up = jnp.dot(h4, w_gu, preferred_element_type=F32)
    gate_act, up_act = gate_up[:, :FX], gate_up[:, FX:]
    sigmoid_gate = jax.nn.sigmoid(gate_act)
    silu_gate = gate_act * sigmoid_gate
    hidden = (silu_gate * up_act).astype(BF16)
    grad_hidden = sum(
        jnp.einsum(
            "rd,fd->rf", cot4[:, q * 256 : (q + 1) * 256], w_dn[q], preferred_element_type=F32
        )
        for q in range(4)
    )
    grad_gate = (
        grad_hidden * up_act * (sigmoid_gate * (1.0 + gate_act * (1.0 - sigmoid_gate)))
    ).astype(BF16)
    grad_up = (grad_hidden * silu_gate).astype(BF16)
    grad_gu = jnp.concatenate([grad_gate, grad_up], axis=1)
    grad_h4 = jnp.einsum("rf,df->rd", grad_gu, w_gu, preferred_element_type=F32).astype(BF16)
    (grad_h_parts,) = exchange(5, "sum_ffn", ("x", "a2a", grad_h4.reshape(NX, ROWS, D)))
    result4 = jnp.concatenate(
        [jnp.dot(hidden, w_dn[q], preferred_element_type=F32) for q in range(4)], axis=1
    ).astype(BF16)

    grad_h_ffn = jnp.sum(grad_h_parts.astype(F32), axis=0)
    grad_out = cotangent[0].astype(F32)
    grad_middle_norm, ffn_gain_terms = rms_rows_back(middle, g_ffn, inv_ffn, grad_h_ffn)
    grad_middle = grad_out + grad_middle_norm
    grad_branch = grad_middle.astype(BF16)
    grad_mixed = jnp.einsum("rd,hd->rh", grad_branch, full_out, preferred_element_type=F32).astype(BF16)
    back_parts = grad_mixed.reshape(2, BLK, 16, HD).transpose(2, 1, 0, 3).reshape(16, BLK, 2 * HD)
    recv_g, result_parts = exchange(
        6, "to_heads_back", ("r", "a2a", back_parts), ("x", "a2a", result4.reshape(NX, ROWS, D))
    )
    output = (middle + jnp.sum(result_parts.astype(F32), axis=0)).astype(BF16)[None]

    grad_w_gu = jnp.einsum("rd,rf->df", h4, grad_gu, preferred_element_type=F32).astype(BF16)
    grad_w_o = jnp.einsum("rh,rd->hd", mixed, grad_branch, preferred_element_type=F32).astype(BF16)
    grad_w_d = jnp.stack(
        [
            jnp.einsum(
                "rf,rd->fd", hidden, cot4[:, q * 256 : (q + 1) * 256], preferred_element_type=F32
            )
            for q in range(4)
        ]
    ).astype(BF16)
    sum_go = lax.psum_scatter(
        jnp.concatenate([grad_w_gu, grad_w_o], axis=1), CTX_FSDP, scatter_dimension=0, tiled=True
    )
    sum_d = lax.psum_scatter(
        grad_w_d.reshape(4 * FX, D // 4), CTX_FSDP, scatter_dimension=0, tiled=True
    )

    sends_back = attend_back(pair, recv_g, q_s, k_s, v_s, o_t, inv)
    (recv_back,) = exchange(7, "to_tokens_back", ("c", "a2a", sends_back))
    grad_h_qkv, grad_w_qkv, gains_qk = project_back(
        blocks, recv_back, raw, h_all, w_qkv, cos_t, sin_t, gq2, gk2
    )
    grad_h_parts, grad_w_parts = exchange(
        8,
        "sum_qkv",
        ("x", "a2a", grad_h_qkv.reshape(NX, ROWS, D)),
        ("p", "a2a", grad_w_qkv.reshape(32, 32, QX + 2 * KX)),
    )
    grad_h_attn = jnp.sum(grad_h_parts.astype(F32), axis=0)
    grad_inputs_norm, attn_gain_terms = rms_rows_back(inputs, g_attn, inv_attn, grad_h_attn)
    grad_tokens = (grad_middle + grad_inputs_norm).astype(BF16)[None]
    sum_qkv = jnp.sum(grad_w_parts.astype(F32), axis=0).astype(BF16)
    gains = jnp.concatenate(
        [
            jnp.sum(attn_gain_terms, axis=0).reshape(8, 128),
            jnp.sum(ffn_gain_terms, axis=0).reshape(8, 128),
            gains_qk,
        ]
    )
    last, gains_x, down_x = exchange(
        9,
        "gather_out",
        ("x", "ag", jnp.concatenate([sum_qkv, sum_go], axis=1)),
        ("x", "ag", gains),
        ("d", "ag", sum_d),
    )
    (gains_p,) = exchange(10, "gather_gains", ("p", "ag", jnp.sum(gains_x, axis=0)))
    gains = jnp.sum(gains_p, axis=0)
    last = last.astype(F32)
    grad_w_query = last[:, :, :QX].transpose(1, 0, 2).reshape(32, H * HD)
    grad_w_key = last[:, :, QX : QX + KX].transpose(1, 0, 2).reshape(32, KV * HD)
    grad_w_value = last[:, :, QX + KX : QX + 2 * KX].transpose(1, 0, 2).reshape(32, KV * HD)
    rest = last[:, :, QX + 2 * KX :]
    grad_w_gate = rest[:, :, :FX].transpose(1, 0, 2).reshape(32, FF)
    grad_w_up = rest[:, :, FX : 2 * FX].transpose(1, 0, 2).reshape(32, FF)
    grad_w_out = jnp.sum(rest[:, :, 2 * FX :], axis=0)
    grad_w_down = down_x.astype(F32).transpose(1, 0, 2).reshape(FF // 32, D)
    g_q = gains[16, :HD] + gains[16, HD:]
    g_k = gains[17, :HD] + gains[17, HD:]
    return (
        output,
        grad_tokens,
        grad_w_query,
        grad_w_key,
        grad_w_value,
        grad_w_out,
        grad_w_gate,
        grad_w_up,
        grad_w_down,
        gains[:8].reshape(D),
        g_q,
        g_k,
        gains[8:16].reshape(D),
    )


def solution(mesh):
    finer = Mesh(
        mesh.devices.reshape(mesh.shape["seq"], 4, 4, mesh.shape["fsdp"]),
        ("seq", "ctx_0", "ctx_1", "fsdp"),
    )
    tokens_spec = P(("seq", "fsdp"), CTX, None)
    rows_spec = P(CTX_FSDP, None)
    return jax.shard_map(
        body,
        mesh=finer,
        in_specs=(tokens_spec, P(("seq", "fsdp"), None))
        + (rows_spec,) * 7
        + (P(),) * 4
        + (tokens_spec,),
        out_specs=(tokens_spec, tokens_spec) + (rows_spec,) * 7 + (P(),) * 4,
        check_vma=False,
    )
```

```python
import functools

import jax
import jax.numpy as jnp
import numpy as np
from jax import lax
from jax.experimental import pallas as pl
from jax.experimental.pallas import tpu as pltpu
from jax.sharding import Mesh
from jax.sharding import PartitionSpec as P

D = 1024
H = 16
KV = 8
HD = 64
FF = 4608
LEN = 2560
BLK = 80
ROWS = 2 * BLK
NX = 4
FX = FF // NX
QX = H * HD // NX
KX = KV * HD // NX
TILE = 512
N_TILES = LEN // TILE
CTX = ("ctx_0", "ctx_1")
CTX_FSDP = ("ctx_0", "ctx_1", "fsdp")
SEQ_CTX_FSDP = ("seq", "ctx_0", "ctx_1", "fsdp")
EPSILON = 1e-05
ROPE_BASE = 1000000.0
MESH = pl.DeviceIdType.MESH
BF16 = jnp.bfloat16
F32 = jnp.float32
VMEM_BYTES = 56 * 1024 * 1024


SIZE = {"x": 4, "c": 16, "p": 32, "t": 16, "r": 16, "d": 4}


def coords():
    return tuple(lax.axis_index(a) for a in SEQ_CTX_FSDP)


def twisted(x, v):
    return lax.rem(v + 2 * (1 - lax.rem(x, 2)) * (1 - lax.rem(v, 2)), 4)


def sequence_at(x, z):
    return lax.rem(x + twisted(x, z), 4)


def place_of(x, s):
    return twisted(x, lax.rem(s - x + 4, 4))


def target(group, t):
    s, z, y, c = coords()
    if group == "x":
        return (t, z, y, c), s
    if group == "c":
        return (s, t // 4, lax.rem(t, 4), c), z * 4 + y
    if group == "p":
        return (s, t // 8, lax.rem(t // 2, 4), lax.rem(t, 2)), (z * 4 + y) * 2 + c
    if group == "t":
        return (sequence_at(s, z), t // 4, lax.rem(t, 4), c), s * 4 + y
    if group == "d":
        return (t, s, y, c), z
    return (t // 4, place_of(t // 4, s), lax.rem(t, 4), c), z * 4 + y


def source(group, t):
    s, z, y, c = coords()
    if group == "t":
        return (t // 4, place_of(t // 4, s), lax.rem(t, 4), c)
    if group == "r":
        return (sequence_at(s, z), t // 4, lax.rem(t, 4), c)
    if group == "d":
        return (z, t, y, c)
    return target(group, t)[0]


def own(group):
    s, z, y, c = coords()
    if group == "t":
        return sequence_at(s, z) == s, z * 4 + y, s * 4 + y
    if group == "r":
        return sequence_at(s, z) == s, s * 4 + y, z * 4 + y
    if group == "d":
        return s == z, s, z
    me = target(group, 0)[1]
    return None, me, me


def exchange_kernel(items, *refs):
    n = len(items)
    srcs, outs, sems = refs[:n], refs[n : 2 * n], refs[2 * n :]
    barrier = pltpu.get_barrier_semaphore()
    expected = 0
    starts = []
    for i, (g, _) in enumerate(items):
        has_own, sent, _ = own(g)
        size = SIZE[g]
        if has_own is None:
            starts.append((jnp.int32(1), sent))
            expected = expected + size - 1
        else:
            starts.append((has_own.astype(jnp.int32), sent))
            expected = expected + size - has_own.astype(jnp.int32)
        place = own(g)[2]
        first = starts[i][0]

        def greet(k, carry, g=g, size=size, place=place):
            dev = source(g, lax.rem(place + k, size))
            pl.semaphore_signal(barrier, inc=1, device_id=dev, device_id_type=MESH)
            return carry

        lax.fori_loop(first, size, greet, 0)

    def own_copy(i):
        g, mode = items[i]
        _, sent, place = own(g)
        src = srcs[i] if mode == "ag" else srcs[i].at[sent]
        return pltpu.make_async_copy(src, outs[i].at[place], sems[3 * i + 2])

    for i, (g, _) in enumerate(items):
        if own(g)[0] is None:
            own_copy(i).start()
        else:
            pl.when(own(g)[0])(lambda i=i: own_copy(i).start())
    pl.semaphore_wait(barrier, expected)

    def remote(i, t, place):
        g, mode = items[i]
        dev, there = target(g, t)
        src = srcs[i] if mode == "ag" else srcs[i].at[t]
        return pltpu.make_async_remote_copy(
            src_ref=src,
            dst_ref=outs[i].at[there if place is None else place],
            send_sem=sems[3 * i].at[t],
            recv_sem=sems[3 * i + 1].at[there if place is None else place],
            device_id=dev,
            device_id_type=MESH,
        )

    for i, (g, _) in enumerate(items):
        first, sent = starts[i]

        def send(k, carry, i=i, g=g, sent=sent):
            remote(i, lax.rem(sent + k, SIZE[g]), None).start()
            return carry

        lax.fori_loop(first, SIZE[g], send, 0)
    for i, (g, _) in enumerate(items):
        first, sent = starts[i]
        place = own(g)[2]

        def drain(k, carry, i=i, g=g, sent=sent, place=place):
            remote(i, lax.rem(sent + k, SIZE[g]), None).wait_send()
            remote(i, lax.rem(sent + k, SIZE[g]), lax.rem(place + k, SIZE[g])).wait_recv()
            return carry

        lax.fori_loop(first, SIZE[g], drain, 0)
        if own(g)[0] is None:
            own_copy(i).wait()
        else:
            pl.when(own(g)[0])(lambda i=i: own_copy(i).wait())


def exchange(number, name, *parts):
    items = tuple((g, m) for g, m, _ in parts)
    arrays = [a for _, _, a in parts]
    outs = [
        jax.ShapeDtypeStruct((SIZE[g],) + (a.shape if m == "ag" else a.shape[1:]), a.dtype)
        for g, m, a in parts
    ]
    scratch = []
    for g, _ in items:
        scratch += [
            pltpu.SemaphoreType.DMA((SIZE[g],)),
            pltpu.SemaphoreType.DMA((SIZE[g],)),
            pltpu.SemaphoreType.DMA,
        ]
    return pl.pallas_call(
        functools.partial(exchange_kernel, items),
        out_shape=outs,
        in_specs=[pl.BlockSpec(memory_space=pl.ANY)] * len(arrays),
        out_specs=[pl.BlockSpec(memory_space=pl.ANY)] * len(arrays),
        scratch_shapes=scratch,
        compiler_params=pltpu.CompilerParams(collective_id=number, has_side_effects=True),
        name=name,
    )(*arrays)


def lanes(shape):
    return lax.broadcasted_iota(jnp.int32, shape, len(shape) - 1)


def low_half(shape):
    return lanes(shape) < HD


def swap(v):
    return pltpu.roll(v, HD, 1)


def swap_halves(v):
    first = lax.rem(lanes(v.shape), HD) < HD // 2
    return jnp.where(first, pltpu.roll(v, 2 * HD - HD // 2, 1), pltpu.roll(v, HD // 2, 1))


def head_mean(v):
    m = low_half(v.shape)
    a = jnp.sum(jnp.where(m, v, 0.0), axis=-1, keepdims=True)
    b = jnp.sum(jnp.where(m, 0.0, v), axis=-1, keepdims=True)
    return jnp.where(m, a, b) * (1.0 / HD)


def nt(a, b):
    return lax.dot_general(a, b, (((1,), (1,)), ((), ())), preferred_element_type=F32)


def nn(a, b):
    return lax.dot_general(a, b, (((1,), (0,)), ((), ())), preferred_element_type=F32)


def tn(a, b):
    return lax.dot_general(a, b, (((0,), (0,)), ((), ())), preferred_element_type=F32)


def rows_of(block):
    return pl.ds(pl.multiple_of(block * BLK, 16), BLK)


def rope_rows(blocks, table, s):
    return jnp.concatenate([table[rows_of(blocks[2 * s]), :], table[rows_of(blocks[2 * s + 1]), :]], 0)


def project_kernel(blocks, h, w, cos_t, sin_t, g_q, g_k, send, raw, acc):
    acc[...] = nn(h[...], w[...])
    m = low_half((ROWS, 2 * HD))
    mh = low_half((BLK, 2 * HD))
    for s in range(NX):
        at = slice(s * ROWS, (s + 1) * ROWS)
        cos_r, sin_r = rope_rows(blocks, cos_t, s), rope_rows(blocks, sin_t, s)
        raw[at, :] = acc[at, : QX + KX]
        turned = []
        for p in range(3):
            v = acc[at, p * 128 : (p + 1) * 128]
            gain = g_q[...] if p < 2 else g_k[...]
            normed = v * lax.rsqrt(head_mean(v * v) + EPSILON) * gain
            turned.append(normed * cos_r + swap_halves(normed) * sin_r)
        keys = turned[2]
        swapped_keys = swap(keys)
        values = acc[at, 3 * 128 :]
        top, bottom = values[:BLK], values[BLK:]
        packed = (jnp.where(mh, top, swap(bottom)), jnp.where(mh, swap(top), bottom))
        for hh in range(4):
            q = turned[hh // 2]
            q = q if hh % 2 == 0 else swap(q)
            k = swapped_keys if hh < 2 else keys
            send[blocks[8 + s] * 4 + hh, :ROWS, :] = jnp.where(m, q, k).astype(BF16)
            send[blocks[8 + s] * 4 + hh, ROWS:, :] = packed[hh // 2].astype(BF16)


def project(blocks, h, w, cos_t, sin_t, g_q, g_k):
    return pl.pallas_call(
        project_kernel,
        grid_spec=pltpu.PrefetchScalarGridSpec(
            num_scalar_prefetch=1,
            in_specs=[pl.BlockSpec(memory_space=pltpu.VMEM)] * 6,
            out_specs=[pl.BlockSpec(memory_space=pltpu.VMEM)] * 2,
            scratch_shapes=[pltpu.VMEM((NX * ROWS, QX + 2 * KX), F32)],
        ),
        out_shape=[
            jax.ShapeDtypeStruct((16, ROWS + BLK, 2 * HD), BF16),
            jax.ShapeDtypeStruct((NX * ROWS, QX + KX), F32),
        ],
        compiler_params=pltpu.CompilerParams(vmem_limit_bytes=VMEM_BYTES),
        name="project",
    )(blocks, h, w, cos_t, sin_t, g_q, g_k)


def attend_kernel(pair, recv, out, q_s, k_s, v_s, o_t, inv, o_s, v_t):
    m = low_half((BLK, 2 * HD))
    for j in range(16):
        packed = recv[j, ROWS:, :].astype(F32)
        for half in range(2):
            block = pair[j] if half == 0 else 31 - pair[j]
            both = recv[j, half * BLK : (half + 1) * BLK, :].astype(F32)
            vals = packed if half == 0 else swap(packed)
            q_s[rows_of(block), :] = jnp.where(m, both * HD**-0.5, 0.0).astype(BF16)
            k_s[rows_of(block), :] = jnp.where(m, swap(both), 0.0).astype(BF16)
            v_s[rows_of(block), :] = jnp.where(m, vals, 0.0).astype(BF16)
    for t in range(N_TILES):
        at = slice(t * TILE, (t + 1) * TILE)
        v_t[:, at] = v_s[at, :].T[:HD]
    causal = lax.broadcasted_iota(jnp.int32, (TILE, TILE), 0) <= lanes((TILE, TILE))
    for i in range(N_TILES):
        at = slice(i * TILE, (i + 1) * TILE)
        q = q_s[at, :]

        e = jnp.where(causal, jnp.exp(nt(k_s[at, :], q)), 0.0)
        first = (jnp.sum(e, axis=0, keepdims=True), nn(v_t[:, at], e.astype(BF16)))

        def step(t, carry, q=q):
            total, acc = carry
            there = pl.ds(pl.multiple_of(t * TILE, TILE), TILE)
            e = jnp.exp(nt(k_s[there, :], q))
            total = total + jnp.sum(e, axis=0, keepdims=True)
            return total, acc + nn(v_t[:, there], e.astype(BF16))

        total, acc = lax.fori_loop(0, i, step, first) if i else first
        over = 1.0 / total
        attended = acc * over
        o_t[:, at] = attended
        inv[:, at] = jnp.broadcast_to(over, (8, TILE))
        o_s[at, :] = jnp.concatenate([attended, jnp.zeros_like(attended)], 0).T
    for j in range(16):
        low_rows = o_s[rows_of(pair[j]), :]
        high_rows = o_s[rows_of(31 - pair[j]), :]
        out[j, :, :] = (low_rows + swap(high_rows)).astype(BF16)


def attend(pair, recv):
    wide = jax.ShapeDtypeStruct((LEN, 2 * HD), BF16)
    return pl.pallas_call(
        attend_kernel,
        grid_spec=pltpu.PrefetchScalarGridSpec(
            num_scalar_prefetch=1,
            in_specs=[pl.BlockSpec(memory_space=pltpu.VMEM)],
            out_specs=[pl.BlockSpec(memory_space=pltpu.VMEM)] * 6,
            scratch_shapes=[pltpu.VMEM((LEN, 2 * HD), F32), pltpu.VMEM((HD, LEN), BF16)],
        ),
        out_shape=[
            jax.ShapeDtypeStruct((16, BLK, 2 * HD), BF16),
            wide,
            wide,
            wide,
            jax.ShapeDtypeStruct((HD, LEN), F32),
            jax.ShapeDtypeStruct((8, LEN), F32),
        ],
        compiler_params=pltpu.CompilerParams(vmem_limit_bytes=VMEM_BYTES),
        name="attend",
    )(pair, recv)


def attend_back_kernel(pair, recv, q_s, k_s, v_s, o_t, inv, out, g_s, k_t, delta, dq_t, dk_s, dv_s):
    m = low_half((BLK, 2 * HD))
    for j in range(16):
        packed = recv[j, :, :].astype(F32)
        g_s[rows_of(pair[j]), :] = jnp.where(m, packed, 0.0).astype(BF16)
        g_s[rows_of(31 - pair[j]), :] = jnp.where(m, swap(packed), 0.0).astype(BF16)
    for t in range(N_TILES):
        at = slice(t * TILE, (t + 1) * TILE)
        k_t[:, at] = k_s[at, :].T[:HD]
        g_t = g_s[at, :].astype(F32).T[:HD]
        row = jnp.sum(g_t * o_t[:, at], axis=0, keepdims=True)
        delta[:, at] = jnp.broadcast_to(row, (8, TILE))
    dq_t[...] = jnp.zeros_like(dq_t)
    causal = lax.broadcasted_iota(jnp.int32, (TILE, TILE), 0) <= lanes((TILE, TILE))
    for i in range(N_TILES):
        at = slice(i * TILE, (i + 1) * TILE)
        k, v, kt = k_s[at, :], v_s[at, :], k_t[:, at]

        def pair_of_tiles(there, masked, k=k, v=v, kt=kt):
            q, g = q_s[there, :], g_s[there, :]
            e = jnp.exp(nt(k, q))
            if masked:
                e = jnp.where(causal, e, 0.0)
            probs = e * inv[0:1, there]
            ds = (probs * (nt(v, g) - delta[0:1, there])).astype(BF16)
            dq_t[:, there] = dq_t[:, there] + nn(kt, ds)
            return nn(ds, q), nn(probs.astype(BF16), g)

        first = pair_of_tiles(at, True)

        def step(t, carry, pair_of_tiles=pair_of_tiles):
            dk, dv = pair_of_tiles(pl.ds(pl.multiple_of(t * TILE, TILE), TILE), False)
            return carry[0] + dk, carry[1] + dv

        dk, dv = lax.fori_loop(i + 1, N_TILES, step, first) if i + 1 < N_TILES else first
        dk_s[at, :] = dk
        dv_s[at, :] = dv
    for i in range(N_TILES):
        at = slice(i * TILE, (i + 1) * TILE)
        dq = dq_t[:, at] * HD**-0.5
        dk_s[at, :] = jnp.concatenate([dq, jnp.zeros_like(dq)], 0).T + swap(dk_s[at, :])
    for j in range(16):
        for half in range(2):
            block = pair[j] if half == 0 else 31 - pair[j]
            out[j, half * BLK : (half + 1) * BLK, :] = dk_s[rows_of(block), :].astype(BF16)
        out[j, ROWS:, :] = (dv_s[rows_of(pair[j]), :] + swap(dv_s[rows_of(31 - pair[j]), :])).astype(BF16)


def attend_back(pair, recv, q_s, k_s, v_s, o_t, inv):
    return pl.pallas_call(
        attend_back_kernel,
        grid_spec=pltpu.PrefetchScalarGridSpec(
            num_scalar_prefetch=1,
            in_specs=[pl.BlockSpec(memory_space=pltpu.VMEM)] * 6,
            out_specs=pl.BlockSpec(memory_space=pltpu.VMEM),
            scratch_shapes=[
                pltpu.VMEM((LEN, 2 * HD), BF16),
                pltpu.VMEM((HD, LEN), BF16),
                pltpu.VMEM((8, LEN), F32),
                pltpu.VMEM((HD, LEN), F32),
                pltpu.VMEM((LEN, 2 * HD), F32),
                pltpu.VMEM((LEN, 2 * HD), F32),
            ],
        ),
        out_shape=jax.ShapeDtypeStruct((16, ROWS + BLK, 2 * HD), BF16),
        compiler_params=pltpu.CompilerParams(vmem_limit_bytes=VMEM_BYTES),
        name="attend_back",
    )(pair, recv, q_s, k_s, v_s, o_t, inv)


def project_back_kernel(blocks, recv, raw, h, w, cos_t, sin_t, g_q, g_k, gh, dw, gains, attn, low):
    m = low_half((ROWS, 2 * HD))
    mh = low_half((BLK, 2 * HD))
    gq_sum = jnp.zeros((1, 2 * HD), F32)
    gk_sum = jnp.zeros((1, 2 * HD), F32)
    for s in range(NX):
        at = slice(s * ROWS, (s + 1) * ROWS)
        cos_r, sin_r = rope_rows(blocks, cos_t, s), rope_rows(blocks, sin_t, s)
        part = [recv[blocks[8 + s] * 4 + hh, :ROWS, :].astype(F32) for hh in range(4)]
        vals = [recv[blocks[8 + s] * 4 + hh, ROWS:, :].astype(F32) for hh in range(4)]
        grads = [
            jnp.where(m, part[0], swap(part[1])),
            jnp.where(m, part[2], swap(part[3])),
            jnp.where(m, swap(part[0] + part[1]), part[2] + part[3]),
        ]
        for p in range(3):
            turned = grads[p] * cos_r + swap_halves(grads[p] * sin_r)
            v = raw[at, p * 128 : (p + 1) * 128]
            gain = g_q[...] if p < 2 else g_k[...]
            r = lax.rsqrt(head_mean(v * v) + EPSILON)
            weighted = turned * gain
            grad = r * weighted - v * (r * r * r) * head_mean(weighted * v)
            low[at, p * 128 : (p + 1) * 128] = grad.astype(BF16)
            term = jnp.sum(turned * v * r, axis=0, keepdims=True)
            if p < 2:
                gq_sum = gq_sum + term
            else:
                gk_sum = gk_sum + term
        a, b = vals[0] + vals[1], vals[2] + vals[3]
        grad_v = jnp.concatenate([jnp.where(mh, a, swap(b)), jnp.where(mh, swap(a), b)], 0)
        low[at, 3 * 128 :] = grad_v.astype(BF16)
    gains[...] = jnp.concatenate([gq_sum, gk_sum, jnp.zeros((6, 2 * HD), F32)], 0)
    for s in range(NX):
        at = slice(s * ROWS, (s + 1) * ROWS)
        grad_h = nt(low[at, :], w[...])
        gh[at, :] = grad_h.astype(BF16)
        term = jnp.sum(grad_h * h[at, :].astype(F32), axis=0, keepdims=True)
        attn[...] = term if s == 0 else attn[...] + term
    dw[...] = tn(h[...], low[...]).astype(BF16)


def project_back(blocks, recv, raw, h, w, cos_t, sin_t, g_q, g_k):
    return pl.pallas_call(
        project_back_kernel,
        grid_spec=pltpu.PrefetchScalarGridSpec(
            num_scalar_prefetch=1,
            in_specs=[pl.BlockSpec(memory_space=pltpu.VMEM)] * 8,
            out_specs=[pl.BlockSpec(memory_space=pltpu.VMEM)] * 4,
            scratch_shapes=[pltpu.VMEM((NX * ROWS, QX + 2 * KX), BF16)],
        ),
        out_shape=[
            jax.ShapeDtypeStruct((NX * ROWS, D), BF16),
            jax.ShapeDtypeStruct((D, QX + 2 * KX), BF16),
            jax.ShapeDtypeStruct((8, 2 * HD), F32),
            jax.ShapeDtypeStruct((1, D), F32),
        ],
        compiler_params=pltpu.CompilerParams(vmem_limit_bytes=VMEM_BYTES),
        name="project_back",
    )(blocks, recv, raw, h, w, cos_t, sin_t, g_q, g_k)


def angle_constants():
    frequencies = ROPE_BASE ** (-np.arange(0, HD // 2, dtype=np.float64) * 2.0 / HD)
    phases = np.arange(LEN, dtype=np.float64)[:, None] * frequencies[None, :]
    cos, sin = np.cos(phases).astype(np.float32), np.sin(phases).astype(np.float32)
    return np.concatenate([cos] * 4, 1), np.concatenate([-sin, sin, -sin, sin], 1)


def rms_rows(values_in, gain):
    inv_rms = lax.rsqrt(jnp.mean(values_in * values_in, axis=-1, keepdims=True) + EPSILON)
    return (values_in * inv_rms * gain, inv_rms)


def rms_rows_back(values_in, gain, inv_rms, grad_in):
    weighted = grad_in * gain
    inner = jnp.mean(weighted * values_in, axis=-1, keepdims=True)
    grad_values = inv_rms * weighted - values_in * (inv_rms * inv_rms * inv_rms) * inner
    gain_terms = grad_in * values_in * inv_rms
    return (grad_values, gain_terms)


def columns_of(w, x, width):
    return lax.dynamic_slice_in_dim(w, x * width, width, axis=1)


def by_tiles(blocks):
    return blocks.reshape(-1, 9, 16, 2, 128).transpose(0, 3, 2, 1, 4).reshape(-1, 32, FX)


def from_tiles(blocks):
    return blocks.reshape(-1, 2, 16, 9, 128).transpose(0, 3, 2, 1, 4).reshape(-1, FF // 32, D // 4)


def body(
    tokens,
    pairs,
    w_query,
    w_key,
    w_value,
    w_out,
    w_gate,
    w_up,
    w_down,
    g_attn,
    g_query,
    g_key,
    g_ffn,
    cotangent,
):
    x, z, y, c = coords()
    ctx = z * 4 + y
    cos_np, sin_np = angle_constants()
    cos_t, sin_t = jnp.asarray(cos_np), jnp.asarray(sin_np)
    gq2 = jnp.concatenate([g_query, g_query])[None]
    gk2 = jnp.concatenate([g_key, g_key])[None]

    swap_xz = [(a * 4 + b, b * 4 + a) for a in range(4) for b in range(4)]
    down_part = lax.ppermute(columns_of(w_down, x, D // 4), ("seq", "ctx_0"), swap_xz)
    mine = jnp.concatenate(
        [columns_of(w_gate, x, FX), columns_of(w_up, x, FX), w_out, by_tiles(down_part[None])[0]],
        axis=1,
    )

    inputs = tokens[0].astype(F32)
    normed_attn, inv_attn = rms_rows(inputs, g_attn)
    h_attn = normed_attn.astype(BF16)
    w_x = jnp.concatenate(
        [columns_of(w_query, x, QX), columns_of(w_key, x, KX), columns_of(w_value, x, KX)], axis=1
    )
    pairs_pad = jnp.pad(pairs, ((0, 7), (0, 112)))
    h_all, w_qkv, pairs_all = exchange(
        1, "gather_in", ("x", "ag", h_attn), ("p", "ag", w_x), ("x", "ag", pairs_pad)
    )
    h_all, mine = lax.optimization_barrier((h_all, mine))
    wide = lax.all_gather(mine, CTX_FSDP, axis=0, tiled=True)
    w_gu, full_out = wide[:, : 2 * FX], wide[:, 2 * FX : 2 * FX + D]
    w_dn = from_tiles(wide[:, 2 * FX + D :].reshape(32, 32, FX)).reshape(4, FX, D // 4)
    h_all = h_all.reshape(NX * ROWS, D)
    w_qkv = w_qkv.reshape(D, QX + 2 * KX)
    pairs_all = pairs_all[:, 0, :16]
    first = lax.dynamic_slice_in_dim(pairs_all, ctx, 1, axis=1)[:, 0]
    places = jnp.stack([place_of(x, s) for s in range(4)])
    blocks = jnp.concatenate([jnp.stack([first, 31 - first], axis=1).reshape(8), places])
    pair = lax.dynamic_slice_in_dim(pairs_all, sequence_at(x, z), 1, axis=0)[0]

    send, raw = project(blocks, h_all, w_qkv, cos_t, sin_t, gq2, gk2)
    recv, cot_all = exchange(2, "to_heads", ("c", "a2a", send), ("x", "ag", cotangent[0]))
    heads_out, q_s, k_s, v_s, o_t, inv = attend(pair, recv)
    (mixed_parts,) = exchange(3, "to_tokens", ("t", "a2a", heads_out))
    mixed = mixed_parts.reshape(16, BLK, 2, HD).transpose(2, 1, 0, 3).reshape(ROWS, D)
    branch = jnp.dot(mixed, full_out, preferred_element_type=F32)
    middle = inputs + branch
    normed_ffn, inv_ffn = rms_rows(middle, g_ffn)
    (h4,) = exchange(4, "gather_ffn", ("x", "ag", normed_ffn.astype(BF16)))
    h4 = h4.reshape(NX * ROWS, D)
    cot4 = cot_all.reshape(NX * ROWS, D)

    gate_up = jnp.dot(h4, w_gu, preferred_element_type=F32)
    gate_act, up_act = gate_up[:, :FX], gate_up[:, FX:]
    sigmoid_gate = jax.nn.sigmoid(gate_act)
    silu_gate = gate_act * sigmoid_gate
    hidden = (silu_gate * up_act).astype(BF16)
    grad_hidden = sum(
        jnp.einsum(
            "rd,fd->rf", cot4[:, q * 256 : (q + 1) * 256], w_dn[q], preferred_element_type=F32
        )
        for q in range(4)
    )
    grad_gate = (
        grad_hidden * up_act * (sigmoid_gate * (1.0 + gate_act * (1.0 - sigmoid_gate)))
    ).astype(BF16)
    grad_up = (grad_hidden * silu_gate).astype(BF16)
    grad_gu = jnp.concatenate([grad_gate, grad_up], axis=1)
    grad_h4 = jnp.einsum("rf,df->rd", grad_gu, w_gu, preferred_element_type=F32).astype(BF16)
    grad_w_gu = jnp.einsum("rd,rf->df", h4, grad_gu, preferred_element_type=F32).astype(BF16)
    grad_w_d = jnp.stack(
        [
            jnp.einsum(
                "rf,rd->fd", hidden, cot4[:, q * 256 : (q + 1) * 256], preferred_element_type=F32
            )
            for q in range(4)
        ]
    ).astype(BF16)
    grad_w_d = by_tiles(grad_w_d.reshape(32, FF // 32, D // 4)).reshape(D, FX)
    sums = lax.psum_scatter(
        jnp.concatenate([grad_w_gu, grad_w_d], axis=1), CTX_FSDP, scatter_dimension=0, tiled=True
    )
    sum_gu, sum_d = sums[:, : 2 * FX], from_tiles(sums[:, 2 * FX :][None])[0]
    (grad_h_parts,) = exchange(5, "sum_ffn", ("x", "a2a", grad_h4.reshape(NX, ROWS, D)))
    result4 = jnp.concatenate(
        [jnp.dot(hidden, w_dn[q], preferred_element_type=F32) for q in range(4)], axis=1
    ).astype(BF16)

    grad_h_ffn = jnp.sum(grad_h_parts.astype(F32), axis=0)
    grad_out = cotangent[0].astype(F32)
    grad_middle_norm, ffn_gain_terms = rms_rows_back(middle, g_ffn, inv_ffn, grad_h_ffn)
    grad_middle = grad_out + grad_middle_norm
    grad_branch = grad_middle.astype(BF16)
    grad_mixed = jnp.einsum("rd,hd->rh", grad_branch, full_out, preferred_element_type=F32).astype(BF16)
    back_parts = grad_mixed.reshape(2, BLK, 16, HD).transpose(2, 1, 0, 3).reshape(16, BLK, 2 * HD)
    recv_g, result_parts = exchange(
        6, "to_heads_back", ("r", "a2a", back_parts), ("x", "a2a", result4.reshape(NX, ROWS, D))
    )
    output = (middle + jnp.sum(result_parts.astype(F32), axis=0)).astype(BF16)[None]

    sends_back = attend_back(pair, recv_g, q_s, k_s, v_s, o_t, inv)
    recv_back, branch_x, mixed_x, gains_ffn = exchange(
        7,
        "to_tokens_back",
        ("c", "a2a", sends_back),
        ("x", "ag", grad_branch),
        ("x", "a2a", mixed.reshape(ROWS, NX, QX).transpose(1, 0, 2)),
        ("p", "ag", jnp.sum(ffn_gain_terms, axis=0).reshape(8, 128)),
    )
    grad_h_qkv, grad_w_qkv, gains_qk, gains_attn = project_back(
        blocks, recv_back, raw, h_all, w_qkv, cos_t, sin_t, gq2, gk2
    )
    gains = jnp.concatenate([(gains_attn / g_attn).reshape(8, 128), gains_qk])
    grad_w_o = jnp.einsum(
        "rh,rd->hd",
        mixed_x.reshape(NX * ROWS, QX),
        branch_x.reshape(NX * ROWS, D),
        preferred_element_type=F32,
    ).astype(BF16)
    grad_w_o = grad_w_o.reshape(8, 32, 4, D // 4).transpose(2, 0, 1, 3).reshape(32, 32, D // 4)
    grad_h_parts, grad_w_parts, grad_o_parts, gains_p = exchange(
        8,
        "sum_qkv",
        ("x", "a2a", grad_h_qkv.reshape(NX, ROWS, D)),
        ("p", "a2a", grad_w_qkv.reshape(32, 32, QX + 2 * KX)),
        ("p", "a2a", grad_w_o),
        ("p", "ag", gains),
    )
    grad_h_attn = jnp.sum(grad_h_parts.astype(F32), axis=0)
    grad_inputs_norm, _ = rms_rows_back(inputs, g_attn, inv_attn, grad_h_attn)
    grad_tokens = (grad_middle + grad_inputs_norm).astype(BF16)[None]
    sum_qkv = jnp.sum(grad_w_parts.astype(F32), axis=0).astype(BF16)
    sum_o = jnp.sum(grad_o_parts.astype(F32), axis=0).astype(BF16)
    gains = jnp.concatenate([jnp.sum(gains_p, axis=0), jnp.sum(gains_ffn, axis=0)])
    last, gains_x, quarters = exchange(
        9,
        "gather_out",
        ("x", "ag", jnp.concatenate([sum_qkv, sum_gu], axis=1)),
        ("x", "ag", gains),
        ("d", "ag", jnp.concatenate([sum_o, sum_d], axis=0)),
    )
    gains = jnp.sum(gains_x, axis=0)
    last = last.astype(F32)
    grad_w_query = last[:, :, :QX].transpose(1, 0, 2).reshape(32, H * HD)
    grad_w_key = last[:, :, QX : QX + KX].transpose(1, 0, 2).reshape(32, KV * HD)
    grad_w_value = last[:, :, QX + KX : QX + 2 * KX].transpose(1, 0, 2).reshape(32, KV * HD)
    rest = last[:, :, QX + 2 * KX :]
    grad_w_gate = rest[:, :, :FX].transpose(1, 0, 2).reshape(32, FF)
    grad_w_up = rest[:, :, FX : 2 * FX].transpose(1, 0, 2).reshape(32, FF)
    quarters = quarters.astype(F32)
    grad_w_out = quarters[:, :32].transpose(1, 0, 2).reshape(32, D)
    grad_w_down = quarters[:, 32:].transpose(1, 0, 2).reshape(FF // 32, D)
    g_q = gains[8, :HD] + gains[8, HD:]
    g_k = gains[9, :HD] + gains[9, HD:]
    return (
        output,
        grad_tokens,
        grad_w_query,
        grad_w_key,
        grad_w_value,
        grad_w_out,
        grad_w_gate,
        grad_w_up,
        grad_w_down,
        gains[:8].reshape(D),
        g_q,
        g_k,
        gains[16:].reshape(D),
    )


def solution(mesh):
    finer = Mesh(
        mesh.devices.reshape(mesh.shape["seq"], 4, 4, mesh.shape["fsdp"]),
        ("seq", "ctx_0", "ctx_1", "fsdp"),
    )
    tokens_spec = P(("seq", "fsdp"), CTX, None)
    rows_spec = P(CTX_FSDP, None)
    return jax.shard_map(
        body,
        mesh=finer,
        in_specs=(tokens_spec, P(("seq", "fsdp"), None))
        + (rows_spec,) * 7
        + (P(),) * 4
        + (tokens_spec,),
        out_specs=(tokens_spec, tokens_spec) + (rows_spec,) * 7 + (P(),) * 4,
        check_vma=False,
    )
```

```python
import functools

import jax
import jax.numpy as jnp
import numpy as np
from jax import lax
from jax.experimental import pallas as pl
from jax.experimental.pallas import tpu as pltpu
from jax.sharding import Mesh
from jax.sharding import PartitionSpec as P

D = 1024
H = 16
KV = 8
HD = 64
FF = 4608
LEN = 2560
BLK = 80
ROWS = 2 * BLK
NX = 4
FX = FF // NX
QX = H * HD // NX
KX = KV * HD // NX
TILE = 512
N_TILES = LEN // TILE
CTX = ("ctx_0", "ctx_1")
CTX_FSDP = ("ctx_0", "ctx_1", "fsdp")
SEQ_CTX_FSDP = ("seq", "ctx_0", "ctx_1", "fsdp")
EPSILON = 1e-05
ROPE_BASE = 1000000.0
MESH = pl.DeviceIdType.MESH
BF16 = jnp.bfloat16
F32 = jnp.float32
VMEM_BYTES = 56 * 1024 * 1024


SIZE = {"x": 4, "c": 16, "p": 32, "t": 16, "r": 16, "d": 4}


def coords():
    return tuple(lax.axis_index(a) for a in SEQ_CTX_FSDP)


def twisted(x, v):
    return lax.rem(v + 2 * (1 - lax.rem(x, 2)) * (1 - lax.rem(v, 2)), 4)


def sequence_at(x, z):
    return lax.rem(x + twisted(x, z), 4)


def place_of(x, s):
    return twisted(x, lax.rem(s - x + 4, 4))


def target(group, t):
    s, z, y, c = coords()
    if group == "x":
        return (t, z, y, c), s
    if group == "c":
        return (s, t // 4, lax.rem(t, 4), c), z * 4 + y
    if group == "p":
        return (s, t // 8, lax.rem(t // 2, 4), lax.rem(t, 2)), (z * 4 + y) * 2 + c
    if group == "t":
        return (sequence_at(s, z), t // 4, lax.rem(t, 4), c), s * 4 + y
    if group == "d":
        return (t, s, y, c), z
    return (t // 4, place_of(t // 4, s), lax.rem(t, 4), c), z * 4 + y


def source(group, t):
    s, z, y, c = coords()
    if group == "t":
        return (t // 4, place_of(t // 4, s), lax.rem(t, 4), c)
    if group == "r":
        return (sequence_at(s, z), t // 4, lax.rem(t, 4), c)
    if group == "d":
        return (z, t, y, c)
    return target(group, t)[0]


def own(group):
    s, z, y, c = coords()
    if group == "t":
        return sequence_at(s, z) == s, z * 4 + y, s * 4 + y
    if group == "r":
        return sequence_at(s, z) == s, s * 4 + y, z * 4 + y
    if group == "d":
        return s == z, s, z
    me = target(group, 0)[1]
    return None, me, me


def exchange_kernel(items, *refs):
    n = len(items)
    srcs, outs, sems = refs[:n], refs[n : 2 * n], refs[2 * n :]
    barrier = pltpu.get_barrier_semaphore()
    expected = 0
    starts = []
    for i, (g, _) in enumerate(items):
        has_own, sent, _ = own(g)
        size = SIZE[g]
        if has_own is None:
            starts.append((jnp.int32(1), sent))
            expected = expected + size - 1
        else:
            starts.append((has_own.astype(jnp.int32), sent))
            expected = expected + size - has_own.astype(jnp.int32)
        place = own(g)[2]
        first = starts[i][0]

        def greet(k, carry, g=g, size=size, place=place):
            dev = source(g, lax.rem(place + k, size))
            pl.semaphore_signal(barrier, inc=1, device_id=dev, device_id_type=MESH)
            return carry

        lax.fori_loop(first, size, greet, 0)

    def own_copy(i):
        g, mode = items[i]
        _, sent, place = own(g)
        src = srcs[i] if mode == "ag" else srcs[i].at[sent]
        return pltpu.make_async_copy(src, outs[i].at[place], sems[3 * i + 2])

    for i, (g, _) in enumerate(items):
        if own(g)[0] is None:
            own_copy(i).start()
        else:
            pl.when(own(g)[0])(lambda i=i: own_copy(i).start())
    pl.semaphore_wait(barrier, expected)

    def remote(i, t, place):
        g, mode = items[i]
        dev, there = target(g, t)
        src = srcs[i] if mode == "ag" else srcs[i].at[t]
        return pltpu.make_async_remote_copy(
            src_ref=src,
            dst_ref=outs[i].at[there if place is None else place],
            send_sem=sems[3 * i].at[t],
            recv_sem=sems[3 * i + 1].at[there if place is None else place],
            device_id=dev,
            device_id_type=MESH,
        )

    for i, (g, _) in enumerate(items):
        first, sent = starts[i]

        def send(k, carry, i=i, g=g, sent=sent):
            remote(i, lax.rem(sent + k, SIZE[g]), None).start()
            return carry

        lax.fori_loop(first, SIZE[g], send, 0)
    for i, (g, _) in enumerate(items):
        first, sent = starts[i]
        place = own(g)[2]

        def drain(k, carry, i=i, g=g, sent=sent, place=place):
            remote(i, lax.rem(sent + k, SIZE[g]), None).wait_send()
            remote(i, lax.rem(sent + k, SIZE[g]), lax.rem(place + k, SIZE[g])).wait_recv()
            return carry

        lax.fori_loop(first, SIZE[g], drain, 0)
        if own(g)[0] is None:
            own_copy(i).wait()
        else:
            pl.when(own(g)[0])(lambda i=i: own_copy(i).wait())


def exchange(number, name, *parts):
    items = tuple((g, m) for g, m, _ in parts)
    arrays = [a for _, _, a in parts]
    outs = [
        jax.ShapeDtypeStruct((SIZE[g],) + (a.shape if m == "ag" else a.shape[1:]), a.dtype)
        for g, m, a in parts
    ]
    scratch = []
    for g, _ in items:
        scratch += [
            pltpu.SemaphoreType.DMA((SIZE[g],)),
            pltpu.SemaphoreType.DMA((SIZE[g],)),
            pltpu.SemaphoreType.DMA,
        ]
    return pl.pallas_call(
        functools.partial(exchange_kernel, items),
        out_shape=outs,
        in_specs=[pl.BlockSpec(memory_space=pl.ANY)] * len(arrays),
        out_specs=[pl.BlockSpec(memory_space=pl.ANY)] * len(arrays),
        scratch_shapes=scratch,
        compiler_params=pltpu.CompilerParams(collective_id=number, has_side_effects=True),
        name=name,
    )(*arrays)


def lanes(shape):
    return lax.broadcasted_iota(jnp.int32, shape, len(shape) - 1)


def low_half(shape):
    return lanes(shape) < HD


def swap(v):
    return pltpu.roll(v, HD, 1)


def swap_halves(v):
    first = lax.rem(lanes(v.shape), HD) < HD // 2
    return jnp.where(first, pltpu.roll(v, 2 * HD - HD // 2, 1), pltpu.roll(v, HD // 2, 1))


def head_mean(v):
    m = low_half(v.shape)
    a = jnp.sum(jnp.where(m, v, 0.0), axis=-1, keepdims=True)
    b = jnp.sum(jnp.where(m, 0.0, v), axis=-1, keepdims=True)
    return jnp.where(m, a, b) * (1.0 / HD)


def nt(a, b):
    return lax.dot_general(a, b, (((1,), (1,)), ((), ())), preferred_element_type=F32)


def nn(a, b):
    return lax.dot_general(a, b, (((1,), (0,)), ((), ())), preferred_element_type=F32)


def tn(a, b):
    return lax.dot_general(a, b, (((0,), (0,)), ((), ())), preferred_element_type=F32)


def rows_of(block):
    return pl.ds(pl.multiple_of(block * BLK, 16), BLK)


def rope_rows(blocks, table, s):
    return jnp.concatenate([table[rows_of(blocks[2 * s]), :], table[rows_of(blocks[2 * s + 1]), :]], 0)


def project_kernel(blocks, h, w, cos_t, sin_t, g_q, g_k, send, raw, acc):
    acc[...] = nn(h[...], w[...])
    m = low_half((ROWS, 2 * HD))
    mh = low_half((BLK, 2 * HD))
    for s in range(NX):
        at = slice(s * ROWS, (s + 1) * ROWS)
        cos_r, sin_r = rope_rows(blocks, cos_t, s), rope_rows(blocks, sin_t, s)
        raw[at, :] = acc[at, : QX + KX]
        turned = []
        for p in range(3):
            v = acc[at, p * 128 : (p + 1) * 128]
            gain = g_q[...] if p < 2 else g_k[...]
            normed = v * lax.rsqrt(head_mean(v * v) + EPSILON) * gain
            turned.append(normed * cos_r + swap_halves(normed) * sin_r)
        keys = turned[2]
        swapped_keys = swap(keys)
        values = acc[at, 3 * 128 :]
        top, bottom = values[:BLK], values[BLK:]
        packed = (jnp.where(mh, top, swap(bottom)), jnp.where(mh, swap(top), bottom))
        for hh in range(4):
            q = turned[hh // 2]
            q = q if hh % 2 == 0 else swap(q)
            k = swapped_keys if hh < 2 else keys
            send[blocks[8 + s] * 4 + hh, :ROWS, :] = jnp.where(m, q, k).astype(BF16)
            send[blocks[8 + s] * 4 + hh, ROWS:, :] = packed[hh // 2].astype(BF16)


def project(blocks, h, w, cos_t, sin_t, g_q, g_k):
    return pl.pallas_call(
        project_kernel,
        grid_spec=pltpu.PrefetchScalarGridSpec(
            num_scalar_prefetch=1,
            in_specs=[pl.BlockSpec(memory_space=pltpu.VMEM)] * 6,
            out_specs=[pl.BlockSpec(memory_space=pltpu.VMEM)] * 2,
            scratch_shapes=[pltpu.VMEM((NX * ROWS, QX + 2 * KX), F32)],
        ),
        out_shape=[
            jax.ShapeDtypeStruct((16, ROWS + BLK, 2 * HD), BF16),
            jax.ShapeDtypeStruct((NX * ROWS, QX + KX), F32),
        ],
        compiler_params=pltpu.CompilerParams(vmem_limit_bytes=VMEM_BYTES),
        name="project",
    )(blocks, h, w, cos_t, sin_t, g_q, g_k)


def attend_kernel(pair, recv, out, q_s, k_s, v_s, o_t, inv, o_s, v_t):
    m = low_half((BLK, 2 * HD))
    for j in range(16):
        packed = recv[j, ROWS:, :].astype(F32)
        for half in range(2):
            block = pair[j] if half == 0 else 31 - pair[j]
            both = recv[j, half * BLK : (half + 1) * BLK, :].astype(F32)
            vals = packed if half == 0 else swap(packed)
            q_s[rows_of(block), :] = jnp.where(m, both * HD**-0.5, 0.0).astype(BF16)
            k_s[rows_of(block), :] = jnp.where(m, swap(both), 0.0).astype(BF16)
            v_s[rows_of(block), :] = jnp.where(m, vals, 0.0).astype(BF16)
    for t in range(N_TILES):
        at = slice(t * TILE, (t + 1) * TILE)
        v_t[:, at] = v_s[at, :].T[:HD]
    causal = lax.broadcasted_iota(jnp.int32, (TILE, TILE), 0) <= lanes((TILE, TILE))
    for i in range(N_TILES):
        at = slice(i * TILE, (i + 1) * TILE)
        q = q_s[at, :]

        e = jnp.where(causal, jnp.exp(nt(k_s[at, :], q)), 0.0)
        first = (jnp.sum(e, axis=0, keepdims=True), nn(v_t[:, at], e.astype(BF16)))

        def step(t, carry, q=q):
            total, acc = carry
            there = pl.ds(pl.multiple_of(t * TILE, TILE), TILE)
            e = jnp.exp(nt(k_s[there, :], q))
            total = total + jnp.sum(e, axis=0, keepdims=True)
            return total, acc + nn(v_t[:, there], e.astype(BF16))

        total, acc = lax.fori_loop(0, i, step, first) if i else first
        over = 1.0 / total
        attended = acc * over
        o_t[:, at] = attended
        inv[:, at] = jnp.broadcast_to(over, (8, TILE))
        o_s[at, :] = jnp.concatenate([attended, jnp.zeros_like(attended)], 0).T
    for j in range(16):
        low_rows = o_s[rows_of(pair[j]), :]
        high_rows = o_s[rows_of(31 - pair[j]), :]
        out[j, :, :] = (low_rows + swap(high_rows)).astype(BF16)


def attend(pair, recv):
    wide = jax.ShapeDtypeStruct((LEN, 2 * HD), BF16)
    return pl.pallas_call(
        attend_kernel,
        grid_spec=pltpu.PrefetchScalarGridSpec(
            num_scalar_prefetch=1,
            in_specs=[pl.BlockSpec(memory_space=pltpu.VMEM)],
            out_specs=[pl.BlockSpec(memory_space=pltpu.VMEM)] * 6,
            scratch_shapes=[pltpu.VMEM((LEN, 2 * HD), F32), pltpu.VMEM((HD, LEN), BF16)],
        ),
        out_shape=[
            jax.ShapeDtypeStruct((16, BLK, 2 * HD), BF16),
            wide,
            wide,
            wide,
            jax.ShapeDtypeStruct((HD, LEN), F32),
            jax.ShapeDtypeStruct((8, LEN), F32),
        ],
        compiler_params=pltpu.CompilerParams(vmem_limit_bytes=VMEM_BYTES),
        name="attend",
    )(pair, recv)


def attend_back_kernel(pair, recv, q_s, k_s, v_s, o_t, inv, out, g_s, k_t, delta, dq_t, dk_s, dv_s):
    m = low_half((BLK, 2 * HD))
    for j in range(16):
        packed = recv[j, :, :].astype(F32)
        g_s[rows_of(pair[j]), :] = jnp.where(m, packed, 0.0).astype(BF16)
        g_s[rows_of(31 - pair[j]), :] = jnp.where(m, swap(packed), 0.0).astype(BF16)
    for t in range(N_TILES):
        at = slice(t * TILE, (t + 1) * TILE)
        k_t[:, at] = k_s[at, :].T[:HD]
        g_t = g_s[at, :].astype(F32).T[:HD]
        row = jnp.sum(g_t * o_t[:, at], axis=0, keepdims=True)
        delta[:, at] = jnp.broadcast_to(row, (8, TILE))
    dq_t[...] = jnp.zeros_like(dq_t)
    causal = lax.broadcasted_iota(jnp.int32, (TILE, TILE), 0) <= lanes((TILE, TILE))
    for i in range(N_TILES):
        at = slice(i * TILE, (i + 1) * TILE)
        k, v, kt = k_s[at, :], v_s[at, :], k_t[:, at]

        def pair_of_tiles(there, masked, k=k, v=v, kt=kt):
            q, g = q_s[there, :], g_s[there, :]
            e = jnp.exp(nt(k, q))
            if masked:
                e = jnp.where(causal, e, 0.0)
            probs = e * inv[0:1, there]
            ds = (probs * (nt(v, g) - delta[0:1, there])).astype(BF16)
            dq_t[:, there] = dq_t[:, there] + nn(kt, ds)
            return nn(ds, q), nn(probs.astype(BF16), g)

        first = pair_of_tiles(at, True)

        def step(t, carry, pair_of_tiles=pair_of_tiles):
            dk, dv = pair_of_tiles(pl.ds(pl.multiple_of(t * TILE, TILE), TILE), False)
            return carry[0] + dk, carry[1] + dv

        dk, dv = lax.fori_loop(i + 1, N_TILES, step, first) if i + 1 < N_TILES else first
        dk_s[at, :] = dk
        dv_s[at, :] = dv
    for i in range(N_TILES):
        at = slice(i * TILE, (i + 1) * TILE)
        dq = dq_t[:, at] * HD**-0.5
        dk_s[at, :] = jnp.concatenate([dq, jnp.zeros_like(dq)], 0).T + swap(dk_s[at, :])
    for j in range(16):
        for half in range(2):
            block = pair[j] if half == 0 else 31 - pair[j]
            out[j, half * BLK : (half + 1) * BLK, :] = dk_s[rows_of(block), :].astype(BF16)
        out[j, ROWS:, :] = (dv_s[rows_of(pair[j]), :] + swap(dv_s[rows_of(31 - pair[j]), :])).astype(BF16)


def attend_back(pair, recv, q_s, k_s, v_s, o_t, inv):
    return pl.pallas_call(
        attend_back_kernel,
        grid_spec=pltpu.PrefetchScalarGridSpec(
            num_scalar_prefetch=1,
            in_specs=[pl.BlockSpec(memory_space=pltpu.VMEM)] * 6,
            out_specs=pl.BlockSpec(memory_space=pltpu.VMEM),
            scratch_shapes=[
                pltpu.VMEM((LEN, 2 * HD), BF16),
                pltpu.VMEM((HD, LEN), BF16),
                pltpu.VMEM((8, LEN), F32),
                pltpu.VMEM((HD, LEN), F32),
                pltpu.VMEM((LEN, 2 * HD), F32),
                pltpu.VMEM((LEN, 2 * HD), F32),
            ],
        ),
        out_shape=jax.ShapeDtypeStruct((16, ROWS + BLK, 2 * HD), BF16),
        compiler_params=pltpu.CompilerParams(vmem_limit_bytes=VMEM_BYTES),
        name="attend_back",
    )(pair, recv, q_s, k_s, v_s, o_t, inv)


def middle_kernel(
    parts,
    tokens,
    cot,
    g_ffn,
    wide,
    mid_o,
    result_o,
    dw_o,
    gmid_o,
    branch_o,
    mixed_o,
    back_o,
    gain_o,
    w_o,
    w_gu,
    dnp,
    w_dn,
    h_all,
    part,
    gparts,
    gu_s,
    dh_s,
    ggu,
    hid,
    h_t,
    hid_t,
    wsem,
    ss1,
    rs1,
    ss2,
    rs2,
):
    me, z, y, c = coords()
    barrier = pltpu.get_barrier_semaphore()
    for k in range(1, NX):
        pl.semaphore_signal(
            barrier, inc=1, device_id=(lax.rem(me + k, NX), z, y, c), device_id_type=MESH
        )
    loads = [
        pltpu.make_async_copy(wide.at[:, pl.ds(at, width)], there, wsem.at[i])
        for i, (at, width, there) in enumerate(
            ((0, D, w_o), (D, 2 * FX, w_gu), (D + 2 * FX, FX, dnp))
        )
    ]
    for load in loads:
        load.start()
    m = low_half((BLK, 2 * HD))
    for p in range(8):
        a, b = parts[2 * p, :, :].astype(F32), parts[2 * p + 1, :, :].astype(F32)
        at = slice((p % 2) * 128, (p % 2) * 128 + 128)
        mixed_o[p // 2, :BLK, at] = jnp.where(m, a, swap(b)).astype(BF16)
        mixed_o[p // 2, BLK:, at] = jnp.where(m, swap(a), b).astype(BF16)
    loads[0].wait()
    middle = tokens[...].astype(F32)
    for q in range(NX):
        middle = middle + nn(mixed_o[q, :, :], w_o[q * QX : (q + 1) * QX, :])
    mid_o[...] = middle
    r = lax.rsqrt(jnp.mean(middle * middle, axis=-1, keepdims=True) + EPSILON)
    h_all[me] = (middle * r * g_ffn[...]).astype(BF16)
    pl.semaphore_wait(barrier, NX - 1)

    def send_h(t, place):
        return pltpu.make_async_remote_copy(
            src_ref=h_all.at[me],
            dst_ref=h_all.at[place],
            send_sem=ss1.at[t],
            recv_sem=rs1.at[place],
            device_id=(t, z, y, c),
            device_id_type=MESH,
        )

    def send_grad(t, place):
        return pltpu.make_async_remote_copy(
            src_ref=part.at[t],
            dst_ref=gparts.at[place],
            send_sem=ss2.at[t],
            recv_sem=rs2.at[place],
            device_id=(t, z, y, c),
            device_id_type=MESH,
        )

    for k in (1, 3, 2):
        send_h(lax.rem(me + k, NX), me).start()
    loads[1].wait()
    loads[2].wait()
    for o in range(32):
        for rg in range(9):
            for l in range(2):
                row = (o % 8) * 144 + rg * 16
                w_dn[o // 8, row : row + 16, l * 128 : l * 128 + 128] = dnp[
                    o * 32 + l * 16 : o * 32 + l * 16 + 16, rg * 128 : rg * 128 + 128
                ]

    def block(k, carry):
        t = lax.rem(me + k + k // 2 - 2 * (k // 2) * lax.rem(k, 2), NX)

        @pl.when(k > 0)
        def _():
            send_h(t, t).wait_recv()

        rows = pl.ds(pl.multiple_of(t * ROWS, ROWS), ROWS)
        gu_s[...] = nn(h_all[t], w_gu[...])
        cot_t = cot[t]
        grad_hidden = nt(cot_t[:, :256], w_dn[0])
        for q in range(1, NX):
            grad_hidden = grad_hidden + nt(cot_t[:, q * 256 : (q + 1) * 256], w_dn[q])
        dh_s[...] = grad_hidden
        for j in range(FX // 128):
            at, above = slice(j * 128, j * 128 + 128), slice(FX + j * 128, FX + j * 128 + 128)
            gate, up, dh = gu_s[:, at], gu_s[:, above], dh_s[:, at]
            sig = jax.nn.sigmoid(gate)
            silu = gate * sig
            hid[rows, at] = (silu * up).astype(BF16)
            ggu[rows, at] = (dh * up * (sig * (1.0 + gate * (1.0 - sig)))).astype(BF16)
            ggu[rows, above] = (dh * silu).astype(BF16)
        part[t] = nt(ggu[rows, :], w_gu[...]).astype(BF16)

        @pl.when(k > 0)
        def _():
            send_grad(t, me).start()

        hidden = hid[rows, :]
        for q in range(NX):
            result_o[t, :, q * 256 : (q + 1) * 256] = nn(hidden, w_dn[q]).astype(BF16)
        return carry

    lax.fori_loop(0, NX, block, 0)

    h_t[...] = h_all[...].reshape(NX * ROWS, D).T

    def columns(j, carry):
        at = pl.ds(pl.multiple_of(j * 256, 256), 256)
        dw_o[:, at] = nn(h_t[...], ggu[:, at]).astype(BF16)
        return carry

    lax.fori_loop(0, 2 * FX // 256, columns, 0)
    hid_t[...] = hid[...].T
    for q in range(NX):
        cot_q = cot[:, :, q * 256 : (q + 1) * 256].reshape(NX * ROWS, 256)
        grad = nn(hid_t[...], cot_q).astype(BF16)
        for o in range(8):
            for rg in range(9):
                for l in range(2):
                    row, there = o * 144 + rg * 16, (q * 8 + o) * 32 + l * 16
                    dw_o[there : there + 16, 2 * FX + rg * 128 : 2 * FX + rg * 128 + 128] = grad[
                        row : row + 16, l * 128 : l * 128 + 128
                    ]

    grad_h = part[me].astype(F32)
    for k in (1, 3, 2):
        t = lax.rem(me + k, NX)
        send_grad(t, t).wait_recv()
        grad_h = grad_h + gparts[t].astype(F32)
    for k in (1, 3, 2):
        t = lax.rem(me + k, NX)
        send_h(t, me).wait_send()
        send_grad(t, me).wait_send()
    middle = mid_o[...]
    r = lax.rsqrt(jnp.mean(middle * middle, axis=-1, keepdims=True) + EPSILON)
    weighted = grad_h * g_ffn[...]
    inner = jnp.mean(weighted * middle, axis=-1, keepdims=True)
    gain_o[...] = jnp.sum(grad_h * middle * r, axis=0, keepdims=True)
    grad_middle = cot[me].astype(F32) + r * weighted - middle * (r * r * r) * inner
    gmid_o[...] = grad_middle
    branch_o[...] = grad_middle.astype(BF16)
    for q in range(NX):
        grad = nt(branch_o[...], w_o[q * QX : (q + 1) * QX, :]).astype(BF16).astype(F32)
        for p in range(2):
            top, bottom = grad[:BLK, p * 128 : p * 128 + 128], grad[BLK:, p * 128 : p * 128 + 128]
            back_o[4 * q + 2 * p, :, :] = jnp.where(m, top, swap(bottom)).astype(BF16)
            back_o[4 * q + 2 * p + 1, :, :] = jnp.where(m, swap(top), bottom).astype(BF16)


def middle_part(number, parts, tokens, cot, g_ffn, wide):
    vmem = pl.BlockSpec(memory_space=pltpu.VMEM)
    blocks = (NX, ROWS, D)
    return pl.pallas_call(
        middle_kernel,
        in_specs=[vmem] * 4 + [pl.BlockSpec(memory_space=pl.ANY)],
        out_specs=[vmem] * 8,
        out_shape=[
            jax.ShapeDtypeStruct((ROWS, D), F32),
            jax.ShapeDtypeStruct(blocks, BF16),
            jax.ShapeDtypeStruct((D, 3 * FX), BF16),
            jax.ShapeDtypeStruct((ROWS, D), F32),
            jax.ShapeDtypeStruct((ROWS, D), BF16),
            jax.ShapeDtypeStruct((NX, ROWS, QX), BF16),
            jax.ShapeDtypeStruct((16, BLK, 2 * HD), BF16),
            jax.ShapeDtypeStruct((1, D), F32),
        ],
        scratch_shapes=[
            pltpu.VMEM((D, D), BF16),
            pltpu.VMEM((D, 2 * FX), BF16),
            pltpu.VMEM((D, FX), BF16),
            pltpu.VMEM((4, FX, D // 4), BF16),
            pltpu.VMEM(blocks, BF16),
            pltpu.VMEM(blocks, BF16),
            pltpu.VMEM(blocks, BF16),
            pltpu.VMEM((ROWS, 2 * FX), F32),
            pltpu.VMEM((ROWS, FX), F32),
            pltpu.VMEM((NX * ROWS, 2 * FX), BF16),
            pltpu.VMEM((NX * ROWS, FX), BF16),
            pltpu.VMEM((D, NX * ROWS), BF16),
            pltpu.VMEM((FX, NX * ROWS), BF16),
            pltpu.SemaphoreType.DMA((3,)),
            pltpu.SemaphoreType.DMA((NX,)),
            pltpu.SemaphoreType.DMA((NX,)),
            pltpu.SemaphoreType.DMA((NX,)),
            pltpu.SemaphoreType.DMA((NX,)),
        ],
        compiler_params=pltpu.CompilerParams(
            collective_id=number, has_side_effects=True, vmem_limit_bytes=VMEM_BYTES
        ),
        name="middle_part",
    )(parts, tokens, cot, g_ffn, wide)


def project_back_kernel(blocks, recv, raw, h, w, cos_t, sin_t, g_q, g_k, gh, dw, gains, attn, low):
    m = low_half((ROWS, 2 * HD))
    mh = low_half((BLK, 2 * HD))
    gq_sum = jnp.zeros((1, 2 * HD), F32)
    gk_sum = jnp.zeros((1, 2 * HD), F32)
    for s in range(NX):
        at = slice(s * ROWS, (s + 1) * ROWS)
        cos_r, sin_r = rope_rows(blocks, cos_t, s), rope_rows(blocks, sin_t, s)
        part = [recv[blocks[8 + s] * 4 + hh, :ROWS, :].astype(F32) for hh in range(4)]
        vals = [recv[blocks[8 + s] * 4 + hh, ROWS:, :].astype(F32) for hh in range(4)]
        grads = [
            jnp.where(m, part[0], swap(part[1])),
            jnp.where(m, part[2], swap(part[3])),
            jnp.where(m, swap(part[0] + part[1]), part[2] + part[3]),
        ]
        for p in range(3):
            turned = grads[p] * cos_r + swap_halves(grads[p] * sin_r)
            v = raw[at, p * 128 : (p + 1) * 128]
            gain = g_q[...] if p < 2 else g_k[...]
            r = lax.rsqrt(head_mean(v * v) + EPSILON)
            weighted = turned * gain
            grad = r * weighted - v * (r * r * r) * head_mean(weighted * v)
            low[at, p * 128 : (p + 1) * 128] = grad.astype(BF16)
            term = jnp.sum(turned * v * r, axis=0, keepdims=True)
            if p < 2:
                gq_sum = gq_sum + term
            else:
                gk_sum = gk_sum + term
        a, b = vals[0] + vals[1], vals[2] + vals[3]
        grad_v = jnp.concatenate([jnp.where(mh, a, swap(b)), jnp.where(mh, swap(a), b)], 0)
        low[at, 3 * 128 :] = grad_v.astype(BF16)
    gains[...] = jnp.concatenate([gq_sum, gk_sum, jnp.zeros((6, 2 * HD), F32)], 0)
    for s in range(NX):
        at = slice(s * ROWS, (s + 1) * ROWS)
        grad_h = nt(low[at, :], w[...])
        gh[at, :] = grad_h.astype(BF16)
        term = jnp.sum(grad_h * h[at, :].astype(F32), axis=0, keepdims=True)
        attn[...] = term if s == 0 else attn[...] + term
    dw[...] = tn(h[...], low[...]).astype(BF16)


def project_back(blocks, recv, raw, h, w, cos_t, sin_t, g_q, g_k):
    return pl.pallas_call(
        project_back_kernel,
        grid_spec=pltpu.PrefetchScalarGridSpec(
            num_scalar_prefetch=1,
            in_specs=[pl.BlockSpec(memory_space=pltpu.VMEM)] * 8,
            out_specs=[pl.BlockSpec(memory_space=pltpu.VMEM)] * 4,
            scratch_shapes=[pltpu.VMEM((NX * ROWS, QX + 2 * KX), BF16)],
        ),
        out_shape=[
            jax.ShapeDtypeStruct((NX * ROWS, D), BF16),
            jax.ShapeDtypeStruct((D, QX + 2 * KX), BF16),
            jax.ShapeDtypeStruct((8, 2 * HD), F32),
            jax.ShapeDtypeStruct((1, D), F32),
        ],
        compiler_params=pltpu.CompilerParams(vmem_limit_bytes=VMEM_BYTES),
        name="project_back",
    )(blocks, recv, raw, h, w, cos_t, sin_t, g_q, g_k)


def angle_constants():
    frequencies = ROPE_BASE ** (-np.arange(0, HD // 2, dtype=np.float64) * 2.0 / HD)
    phases = np.arange(LEN, dtype=np.float64)[:, None] * frequencies[None, :]
    cos, sin = np.cos(phases).astype(np.float32), np.sin(phases).astype(np.float32)
    return np.concatenate([cos] * 4, 1), np.concatenate([-sin, sin, -sin, sin], 1)


def rms_rows(values_in, gain):
    inv_rms = lax.rsqrt(jnp.mean(values_in * values_in, axis=-1, keepdims=True) + EPSILON)
    return (values_in * inv_rms * gain, inv_rms)


def rms_rows_back(values_in, gain, inv_rms, grad_in):
    weighted = grad_in * gain
    inner = jnp.mean(weighted * values_in, axis=-1, keepdims=True)
    grad_values = inv_rms * weighted - values_in * (inv_rms * inv_rms * inv_rms) * inner
    gain_terms = grad_in * values_in * inv_rms
    return (grad_values, gain_terms)


def columns_of(w, x, width):
    return lax.dynamic_slice_in_dim(w, x * width, width, axis=1)


def by_tiles(blocks):
    return blocks.reshape(-1, 9, 16, 2, 128).transpose(0, 3, 2, 1, 4).reshape(-1, 32, FX)


def from_tiles(blocks):
    return blocks.reshape(-1, 2, 16, 9, 128).transpose(0, 3, 2, 1, 4).reshape(-1, FF // 32, D // 4)


def body(
    tokens,
    pairs,
    w_query,
    w_key,
    w_value,
    w_out,
    w_gate,
    w_up,
    w_down,
    g_attn,
    g_query,
    g_key,
    g_ffn,
    cotangent,
):
    x, z, y, c = coords()
    ctx = z * 4 + y
    cos_np, sin_np = angle_constants()
    cos_t, sin_t = jnp.asarray(cos_np), jnp.asarray(sin_np)
    gq2 = jnp.concatenate([g_query, g_query])[None]
    gk2 = jnp.concatenate([g_key, g_key])[None]

    swap_xz = [(a * 4 + b, b * 4 + a) for a in range(4) for b in range(4)]
    down_part = lax.ppermute(columns_of(w_down, x, D // 4), ("seq", "ctx_0"), swap_xz)
    mine = jnp.concatenate(
        [w_out, columns_of(w_gate, x, FX), columns_of(w_up, x, FX), by_tiles(down_part[None])[0]],
        axis=1,
    )

    inputs = tokens[0].astype(F32)
    normed_attn, inv_attn = rms_rows(inputs, g_attn)
    h_attn = normed_attn.astype(BF16)
    w_x = jnp.concatenate(
        [columns_of(w_query, x, QX), columns_of(w_key, x, KX), columns_of(w_value, x, KX)], axis=1
    )
    pairs_pad = jnp.pad(pairs, ((0, 7), (0, 112)))
    h_all, w_qkv, pairs_all = exchange(
        1, "gather_in", ("x", "ag", h_attn), ("p", "ag", w_x), ("x", "ag", pairs_pad)
    )
    h_all, mine = lax.optimization_barrier((h_all, mine))
    wide = lax.all_gather(mine, CTX_FSDP, axis=0, tiled=True)
    h_all = h_all.reshape(NX * ROWS, D)
    w_qkv = w_qkv.reshape(D, QX + 2 * KX)
    pairs_all = pairs_all[:, 0, :16]
    first = lax.dynamic_slice_in_dim(pairs_all, ctx, 1, axis=1)[:, 0]
    places = jnp.stack([place_of(x, s) for s in range(4)])
    blocks = jnp.concatenate([jnp.stack([first, 31 - first], axis=1).reshape(8), places])
    pair = lax.dynamic_slice_in_dim(pairs_all, sequence_at(x, z), 1, axis=0)[0]

    send, raw = project(blocks, h_all, w_qkv, cos_t, sin_t, gq2, gk2)
    recv, cot_all = exchange(2, "to_heads", ("c", "a2a", send), ("x", "ag", cotangent[0]))
    heads_out, q_s, k_s, v_s, o_t, inv = attend(pair, recv)
    (mixed_parts,) = exchange(3, "to_tokens", ("t", "a2a", heads_out))
    middle, result4, grad_w_ffn, grad_middle, grad_branch, mixed, back_parts, gain_ffn = middle_part(
        4, mixed_parts, tokens[0], cot_all, g_ffn[None], wide
    )
    sums = lax.psum_scatter(grad_w_ffn, CTX_FSDP, scatter_dimension=0, tiled=True)
    sum_gu, sum_d = sums[:, : 2 * FX], from_tiles(sums[:, 2 * FX :][None])[0]
    recv_g, result_parts = exchange(
        6, "to_heads_back", ("r", "a2a", back_parts), ("x", "a2a", result4)
    )
    output = (middle + jnp.sum(result_parts.astype(F32), axis=0)).astype(BF16)[None]

    sends_back = attend_back(pair, recv_g, q_s, k_s, v_s, o_t, inv)
    recv_back, branch_x, mixed_x, gains_ffn = exchange(
        7,
        "to_tokens_back",
        ("c", "a2a", sends_back),
        ("x", "ag", grad_branch),
        ("x", "a2a", mixed),
        ("p", "ag", gain_ffn.reshape(8, 128)),
    )
    grad_h_qkv, grad_w_qkv, gains_qk, gains_attn = project_back(
        blocks, recv_back, raw, h_all, w_qkv, cos_t, sin_t, gq2, gk2
    )
    gains = jnp.concatenate([(gains_attn / g_attn).reshape(8, 128), gains_qk])
    grad_w_o = jnp.einsum(
        "rh,rd->hd",
        mixed_x.reshape(NX * ROWS, QX),
        branch_x.reshape(NX * ROWS, D),
        preferred_element_type=F32,
    ).astype(BF16)
    grad_w_o = grad_w_o.reshape(8, 32, 4, D // 4).transpose(2, 0, 1, 3).reshape(32, 32, D // 4)
    grad_h_parts, grad_w_parts, grad_o_parts, gains_p = exchange(
        8,
        "sum_qkv",
        ("x", "a2a", grad_h_qkv.reshape(NX, ROWS, D)),
        ("p", "a2a", grad_w_qkv.reshape(32, 32, QX + 2 * KX)),
        ("p", "a2a", grad_w_o),
        ("p", "ag", gains),
    )
    grad_h_attn = jnp.sum(grad_h_parts.astype(F32), axis=0)
    grad_inputs_norm, _ = rms_rows_back(inputs, g_attn, inv_attn, grad_h_attn)
    grad_tokens = (grad_middle + grad_inputs_norm).astype(BF16)[None]
    sum_qkv = jnp.sum(grad_w_parts.astype(F32), axis=0).astype(BF16)
    sum_o = jnp.sum(grad_o_parts.astype(F32), axis=0).astype(BF16)
    gains = jnp.concatenate([jnp.sum(gains_p, axis=0), jnp.sum(gains_ffn, axis=0)])
    last, gains_x, quarters = exchange(
        9,
        "gather_out",
        ("x", "ag", jnp.concatenate([sum_qkv, sum_gu], axis=1)),
        ("x", "ag", gains),
        ("d", "ag", jnp.concatenate([sum_o, sum_d], axis=0)),
    )
    gains = jnp.sum(gains_x, axis=0)
    last = last.astype(F32)
    grad_w_query = last[:, :, :QX].transpose(1, 0, 2).reshape(32, H * HD)
    grad_w_key = last[:, :, QX : QX + KX].transpose(1, 0, 2).reshape(32, KV * HD)
    grad_w_value = last[:, :, QX + KX : QX + 2 * KX].transpose(1, 0, 2).reshape(32, KV * HD)
    rest = last[:, :, QX + 2 * KX :]
    grad_w_gate = rest[:, :, :FX].transpose(1, 0, 2).reshape(32, FF)
    grad_w_up = rest[:, :, FX : 2 * FX].transpose(1, 0, 2).reshape(32, FF)
    quarters = quarters.astype(F32)
    grad_w_out = quarters[:, :32].transpose(1, 0, 2).reshape(32, D)
    grad_w_down = quarters[:, 32:].transpose(1, 0, 2).reshape(FF // 32, D)
    g_q = gains[8, :HD] + gains[8, HD:]
    g_k = gains[9, :HD] + gains[9, HD:]
    return (
        output,
        grad_tokens,
        grad_w_query,
        grad_w_key,
        grad_w_value,
        grad_w_out,
        grad_w_gate,
        grad_w_up,
        grad_w_down,
        gains[:8].reshape(D),
        g_q,
        g_k,
        gains[16:].reshape(D),
    )


def solution(mesh):
    finer = Mesh(
        mesh.devices.reshape(mesh.shape["seq"], 4, 4, mesh.shape["fsdp"]),
        ("seq", "ctx_0", "ctx_1", "fsdp"),
    )
    tokens_spec = P(("seq", "fsdp"), CTX, None)
    rows_spec = P(CTX_FSDP, None)
    return jax.shard_map(
        body,
        mesh=finer,
        in_specs=(tokens_spec, P(("seq", "fsdp"), None))
        + (rows_spec,) * 7
        + (P(),) * 4
        + (tokens_spec,),
        out_specs=(tokens_spec, tokens_spec) + (rows_spec,) * 7 + (P(),) * 4,
        check_vma=False,
    )
```

```python
import functools

import jax
import jax.numpy as jnp
import numpy as np
from jax import lax
from jax.experimental import pallas as pl
from jax.experimental.pallas import tpu as pltpu
from jax.sharding import Mesh
from jax.sharding import PartitionSpec as P

D = 1024
H = 16
KV = 8
HD = 64
FF = 4608
LEN = 2560
BLK = 80
ROWS = 2 * BLK
NX = 4
FX = FF // NX
QX = H * HD // NX
KX = KV * HD // NX
TILE = 512
N_TILES = LEN // TILE
CTX = ("ctx_0", "ctx_1")
CTX_FSDP = ("ctx_0", "ctx_1", "fsdp")
SEQ_CTX_FSDP = ("seq", "ctx_0", "ctx_1", "fsdp")
EPSILON = 1e-05
ROPE_BASE = 1000000.0
MESH = pl.DeviceIdType.MESH
BF16 = jnp.bfloat16
F32 = jnp.float32
VMEM_BYTES = 56 * 1024 * 1024


SIZE = {"x": 4, "c": 16, "p": 32, "t": 16, "r": 16, "d": 4}


def coords():
    return tuple(lax.axis_index(a) for a in SEQ_CTX_FSDP)


def twisted(x, v):
    return lax.rem(v + 2 * (1 - lax.rem(x, 2)) * (1 - lax.rem(v, 2)), 4)


def sequence_at(x, z):
    return lax.rem(x + twisted(x, z), 4)


def place_of(x, s):
    return twisted(x, lax.rem(s - x + 4, 4))


def target(group, t):
    s, z, y, c = coords()
    if group == "x":
        return (t, z, y, c), s
    if group == "c":
        return (s, t // 4, lax.rem(t, 4), c), z * 4 + y
    if group == "p":
        return (s, t // 8, lax.rem(t // 2, 4), lax.rem(t, 2)), (z * 4 + y) * 2 + c
    if group == "t":
        return (sequence_at(s, z), t // 4, lax.rem(t, 4), c), s * 4 + y
    if group == "d":
        return (t, s, y, c), z
    return (t // 4, place_of(t // 4, s), lax.rem(t, 4), c), z * 4 + y


def source(group, t):
    s, z, y, c = coords()
    if group == "t":
        return (t // 4, place_of(t // 4, s), lax.rem(t, 4), c)
    if group == "r":
        return (sequence_at(s, z), t // 4, lax.rem(t, 4), c)
    if group == "d":
        return (z, t, y, c)
    return target(group, t)[0]


def own(group):
    s, z, y, c = coords()
    if group == "t":
        return sequence_at(s, z) == s, z * 4 + y, s * 4 + y
    if group == "r":
        return sequence_at(s, z) == s, s * 4 + y, z * 4 + y
    if group == "d":
        return s == z, s, z
    me = target(group, 0)[1]
    return None, me, me


def exchange_kernel(items, *refs):
    n = len(items)
    srcs, outs, sems = refs[:n], refs[n : 2 * n], refs[2 * n :]
    barrier = pltpu.get_barrier_semaphore()
    expected = 0
    starts = []
    for i, (g, _, _) in enumerate(items):
        has_own, sent, _ = own(g)
        size = SIZE[g]
        if has_own is None:
            starts.append((jnp.int32(1), sent))
            expected = expected + size - 1
        else:
            starts.append((has_own.astype(jnp.int32), sent))
            expected = expected + size - has_own.astype(jnp.int32)
        place = own(g)[2]
        first = starts[i][0]

        def greet(k, carry, g=g, size=size, place=place):
            dev = source(g, lax.rem(place + k, size))
            pl.semaphore_signal(barrier, inc=1, device_id=dev, device_id_type=MESH)
            return carry

        lax.fori_loop(first, size, greet, 0)

    def block_of(i, t):
        _, mode, cols = items[i]
        if cols is not None:
            return srcs[i].at[:, pl.ds(*cols)]
        return srcs[i] if mode == "ag" else srcs[i].at[t]

    def own_copy(i):
        g = items[i][0]
        _, sent, place = own(g)
        src = block_of(i, sent)
        return pltpu.make_async_copy(src, outs[i].at[place], sems[3 * i + 2])

    for i, (g, _, _) in enumerate(items):
        if own(g)[0] is None:
            own_copy(i).start()
        else:
            pl.when(own(g)[0])(lambda i=i: own_copy(i).start())
    pl.semaphore_wait(barrier, expected)

    def remote(i, t, place):
        g = items[i][0]
        dev, there = target(g, t)
        src = block_of(i, t)
        return pltpu.make_async_remote_copy(
            src_ref=src,
            dst_ref=outs[i].at[there if place is None else place],
            send_sem=sems[3 * i].at[t],
            recv_sem=sems[3 * i + 1].at[there if place is None else place],
            device_id=dev,
            device_id_type=MESH,
        )

    for i, (g, _, _) in enumerate(items):
        first, sent = starts[i]

        def send(k, carry, i=i, g=g, sent=sent):
            remote(i, lax.rem(sent + k, SIZE[g]), None).start()
            return carry

        lax.fori_loop(first, SIZE[g], send, 0)
    for i, (g, _, _) in enumerate(items):
        first, sent = starts[i]
        place = own(g)[2]

        def drain(k, carry, i=i, g=g, sent=sent, place=place):
            remote(i, lax.rem(sent + k, SIZE[g]), None).wait_send()
            remote(i, lax.rem(sent + k, SIZE[g]), lax.rem(place + k, SIZE[g])).wait_recv()
            return carry

        lax.fori_loop(first, SIZE[g], drain, 0)
        if own(g)[0] is None:
            own_copy(i).wait()
        else:
            pl.when(own(g)[0])(lambda i=i: own_copy(i).wait())


def exchange(number, name, *parts):
    items = tuple((part[0], part[1], part[3] if len(part) > 3 else None) for part in parts)
    arrays = [part[2] for part in parts]
    outs = []
    for (g, m, cols), a in zip(items, arrays):
        shape = a.shape if m == "ag" else a.shape[1:]
        shape = shape if cols is None else shape[:-1] + (cols[1],)
        outs.append(jax.ShapeDtypeStruct((SIZE[g],) + shape, a.dtype))
    scratch = []
    for g, _, _ in items:
        scratch += [
            pltpu.SemaphoreType.DMA((SIZE[g],)),
            pltpu.SemaphoreType.DMA((SIZE[g],)),
            pltpu.SemaphoreType.DMA,
        ]
    return pl.pallas_call(
        functools.partial(exchange_kernel, items),
        out_shape=outs,
        in_specs=[pl.BlockSpec(memory_space=pl.ANY)] * len(arrays),
        out_specs=[pl.BlockSpec(memory_space=pl.ANY)] * len(arrays),
        scratch_shapes=scratch,
        compiler_params=pltpu.CompilerParams(collective_id=number, has_side_effects=True),
        name=name,
    )(*arrays)


def lanes(shape):
    return lax.broadcasted_iota(jnp.int32, shape, len(shape) - 1)


def low_half(shape):
    return lanes(shape) < HD


def swap(v):
    return pltpu.roll(v, HD, 1)


def swap_halves(v):
    first = lax.rem(lanes(v.shape), HD) < HD // 2
    return jnp.where(first, pltpu.roll(v, 2 * HD - HD // 2, 1), pltpu.roll(v, HD // 2, 1))


def head_mean(v):
    m = low_half(v.shape)
    a = jnp.sum(jnp.where(m, v, 0.0), axis=-1, keepdims=True)
    b = jnp.sum(jnp.where(m, 0.0, v), axis=-1, keepdims=True)
    return jnp.where(m, a, b) * (1.0 / HD)


def nt(a, b):
    return lax.dot_general(a, b, (((1,), (1,)), ((), ())), preferred_element_type=F32)


def nn(a, b):
    return lax.dot_general(a, b, (((1,), (0,)), ((), ())), preferred_element_type=F32)


def tn(a, b):
    return lax.dot_general(a, b, (((0,), (0,)), ((), ())), preferred_element_type=F32)


def rows_of(block):
    return pl.ds(pl.multiple_of(block * BLK, 16), BLK)


def rope_rows(blocks, table, s):
    return jnp.concatenate([table[rows_of(blocks[2 * s]), :], table[rows_of(blocks[2 * s + 1]), :]], 0)


def project_kernel(blocks, h, w, cos_t, sin_t, g_q, g_k, send, raw, cos_o, sin_o, acc):
    acc[...] = nn(h[...], w[...])
    m = low_half((ROWS, 2 * HD))
    mh = low_half((BLK, 2 * HD))
    for s in range(NX):
        at = slice(s * ROWS, (s + 1) * ROWS)
        cos_r, sin_r = rope_rows(blocks, cos_t, s), rope_rows(blocks, sin_t, s)
        cos_o[at, :], sin_o[at, :] = cos_r, sin_r
        raw[at, :] = acc[at, : QX + KX]
        turned = []
        for p in range(3):
            v = acc[at, p * 128 : (p + 1) * 128]
            gain = g_q[...] if p < 2 else g_k[...]
            normed = v * lax.rsqrt(head_mean(v * v) + EPSILON) * gain
            turned.append(normed * cos_r + swap_halves(normed) * sin_r)
        keys = turned[2]
        swapped_keys = swap(keys)
        values = acc[at, 3 * 128 :]
        top, bottom = values[:BLK], values[BLK:]
        packed = (jnp.where(mh, top, swap(bottom)), jnp.where(mh, swap(top), bottom))
        for hh in range(4):
            q = turned[hh // 2]
            q = q if hh % 2 == 0 else swap(q)
            k = swapped_keys if hh < 2 else keys
            send[blocks[8 + s] * 4 + hh, :ROWS, :] = jnp.where(m, q, k).astype(BF16)
            send[blocks[8 + s] * 4 + hh, ROWS:, :] = packed[hh // 2].astype(BF16)


def project(blocks, h, w, cos_t, sin_t, g_q, g_k):
    return pl.pallas_call(
        project_kernel,
        grid_spec=pltpu.PrefetchScalarGridSpec(
            num_scalar_prefetch=1,
            in_specs=[pl.BlockSpec(memory_space=pltpu.VMEM)] * 6,
            out_specs=[pl.BlockSpec(memory_space=pltpu.VMEM)] * 4,
            scratch_shapes=[pltpu.VMEM((NX * ROWS, QX + 2 * KX), F32)],
        ),
        out_shape=[
            jax.ShapeDtypeStruct((16, ROWS + BLK, 2 * HD), BF16),
            jax.ShapeDtypeStruct((NX * ROWS, QX + KX), F32),
            jax.ShapeDtypeStruct((NX * ROWS, 2 * HD), F32),
            jax.ShapeDtypeStruct((NX * ROWS, 2 * HD), F32),
        ],
        compiler_params=pltpu.CompilerParams(vmem_limit_bytes=VMEM_BYTES),
        name="project",
    )(blocks, h, w, cos_t, sin_t, g_q, g_k)


def attend_kernel(pair, recv, out, q_s, k_s, v_s, o_t, inv, o_s, v_t):
    m = low_half((BLK, 2 * HD))
    for j in range(16):
        packed = recv[j, ROWS:, :].astype(F32)
        for half in range(2):
            block = pair[j] if half == 0 else 31 - pair[j]
            both = recv[j, half * BLK : (half + 1) * BLK, :].astype(F32)
            vals = packed if half == 0 else swap(packed)
            q_s[rows_of(block), :] = jnp.where(m, both * HD**-0.5, 0.0).astype(BF16)
            k_s[rows_of(block), :] = jnp.where(m, swap(both), 0.0).astype(BF16)
            v_s[rows_of(block), :] = jnp.where(m, vals, 0.0).astype(BF16)
    for t in range(N_TILES):
        at = slice(t * TILE, (t + 1) * TILE)
        v_t[:, at] = v_s[at, :].T[:HD]
    causal = lax.broadcasted_iota(jnp.int32, (TILE, TILE), 0) <= lanes((TILE, TILE))
    for i in range(N_TILES):
        at = slice(i * TILE, (i + 1) * TILE)
        q = q_s[at, :]

        e = jnp.where(causal, jnp.exp(nt(k_s[at, :], q)), 0.0)
        first = (jnp.sum(e, axis=0, keepdims=True), nn(v_t[:, at], e.astype(BF16)))

        def step(t, carry, q=q):
            total, acc = carry
            there = pl.ds(pl.multiple_of(t * TILE, TILE), TILE)
            e = jnp.exp(nt(k_s[there, :], q))
            total = total + jnp.sum(e, axis=0, keepdims=True)
            return total, acc + nn(v_t[:, there], e.astype(BF16))

        total, acc = lax.fori_loop(0, i, step, first) if i else first
        over = 1.0 / total
        attended = acc * over
        o_t[:, at] = attended
        inv[:, at] = jnp.broadcast_to(over, (8, TILE))
        o_s[at, :] = jnp.concatenate([attended, jnp.zeros_like(attended)], 0).T
    for j in range(16):
        low_rows = o_s[rows_of(pair[j]), :]
        high_rows = o_s[rows_of(31 - pair[j]), :]
        out[j, :, :] = (low_rows + swap(high_rows)).astype(BF16)


def attend(pair, recv):
    wide = jax.ShapeDtypeStruct((LEN, 2 * HD), BF16)
    return pl.pallas_call(
        attend_kernel,
        grid_spec=pltpu.PrefetchScalarGridSpec(
            num_scalar_prefetch=1,
            in_specs=[pl.BlockSpec(memory_space=pltpu.VMEM)],
            out_specs=[pl.BlockSpec(memory_space=pltpu.VMEM)] * 6,
            scratch_shapes=[pltpu.VMEM((LEN, 2 * HD), F32), pltpu.VMEM((HD, LEN), BF16)],
        ),
        out_shape=[
            jax.ShapeDtypeStruct((16, BLK, 2 * HD), BF16),
            wide,
            wide,
            wide,
            jax.ShapeDtypeStruct((HD, LEN), F32),
            jax.ShapeDtypeStruct((8, LEN), F32),
        ],
        compiler_params=pltpu.CompilerParams(vmem_limit_bytes=VMEM_BYTES),
        name="attend",
    )(pair, recv)


def attend_back_kernel(pair, recv, q_s, k_s, v_s, o_t, inv, out, g_s, k_t, delta, dq_t, dk_s, dv_s):
    m = low_half((BLK, 2 * HD))
    for j in range(16):
        packed = recv[j, :, :].astype(F32)
        g_s[rows_of(pair[j]), :] = jnp.where(m, packed, 0.0).astype(BF16)
        g_s[rows_of(31 - pair[j]), :] = jnp.where(m, swap(packed), 0.0).astype(BF16)
    for t in range(N_TILES):
        at = slice(t * TILE, (t + 1) * TILE)
        k_t[:, at] = k_s[at, :].T[:HD]
        g_t = g_s[at, :].astype(F32).T[:HD]
        row = jnp.sum(g_t * o_t[:, at], axis=0, keepdims=True)
        delta[:, at] = jnp.broadcast_to(row, (8, TILE))
    dq_t[...] = jnp.zeros_like(dq_t)
    causal = lax.broadcasted_iota(jnp.int32, (TILE, TILE), 0) <= lanes((TILE, TILE))
    for i in range(N_TILES):
        at = slice(i * TILE, (i + 1) * TILE)
        k, v, kt = k_s[at, :], v_s[at, :], k_t[:, at]

        def pair_of_tiles(there, masked, k=k, v=v, kt=kt):
            q, g = q_s[there, :], g_s[there, :]
            e = jnp.exp(nt(k, q))
            if masked:
                e = jnp.where(causal, e, 0.0)
            probs = e * inv[0:1, there]
            ds = (probs * (nt(v, g) - delta[0:1, there])).astype(BF16)
            dq_t[:, there] = dq_t[:, there] + nn(kt, ds)
            return nn(ds, q), nn(probs.astype(BF16), g)

        first = pair_of_tiles(at, True)

        def step(t, carry, pair_of_tiles=pair_of_tiles):
            dk, dv = pair_of_tiles(pl.ds(pl.multiple_of(t * TILE, TILE), TILE), False)
            return carry[0] + dk, carry[1] + dv

        dk, dv = lax.fori_loop(i + 1, N_TILES, step, first) if i + 1 < N_TILES else first
        dk_s[at, :] = dk
        dv_s[at, :] = dv
    for i in range(N_TILES):
        at = slice(i * TILE, (i + 1) * TILE)
        dq = dq_t[:, at] * HD**-0.5
        dk_s[at, :] = jnp.concatenate([dq, jnp.zeros_like(dq)], 0).T + swap(dk_s[at, :])
    for j in range(16):
        for half in range(2):
            block = pair[j] if half == 0 else 31 - pair[j]
            out[j, half * BLK : (half + 1) * BLK, :] = dk_s[rows_of(block), :].astype(BF16)
        out[j, ROWS:, :] = (dv_s[rows_of(pair[j]), :] + swap(dv_s[rows_of(31 - pair[j]), :])).astype(BF16)


def attend_back(pair, recv, q_s, k_s, v_s, o_t, inv):
    return pl.pallas_call(
        attend_back_kernel,
        grid_spec=pltpu.PrefetchScalarGridSpec(
            num_scalar_prefetch=1,
            in_specs=[pl.BlockSpec(memory_space=pltpu.VMEM)] * 6,
            out_specs=pl.BlockSpec(memory_space=pltpu.VMEM),
            scratch_shapes=[
                pltpu.VMEM((LEN, 2 * HD), BF16),
                pltpu.VMEM((HD, LEN), BF16),
                pltpu.VMEM((8, LEN), F32),
                pltpu.VMEM((HD, LEN), F32),
                pltpu.VMEM((LEN, 2 * HD), F32),
                pltpu.VMEM((LEN, 2 * HD), F32),
            ],
        ),
        out_shape=jax.ShapeDtypeStruct((16, ROWS + BLK, 2 * HD), BF16),
        compiler_params=pltpu.CompilerParams(vmem_limit_bytes=VMEM_BYTES),
        name="attend_back",
    )(pair, recv, q_s, k_s, v_s, o_t, inv)


def middle_kernel(
    parts,
    tokens,
    cot,
    g_ffn,
    wide,
    mid_o,
    result_o,
    dw_o,
    gmid_o,
    branch_o,
    mixed_o,
    back_o,
    gain_o,
    w_o,
    w_gu,
    dnp,
    w_dn,
    h_all,
    part,
    gparts,
    gu_s,
    dh_s,
    ggu,
    hid,
    h_t,
    hid_t,
    wsem,
    ss1,
    rs1,
    ss2,
    rs2,
):
    me, z, y, c = coords()
    barrier = pltpu.get_barrier_semaphore()
    for k in range(1, NX):
        pl.semaphore_signal(
            barrier, inc=1, device_id=(lax.rem(me + k, NX), z, y, c), device_id_type=MESH
        )
    loads = [
        pltpu.make_async_copy(wide.at[:, pl.ds(at, width)], there, wsem.at[i])
        for i, (at, width, there) in enumerate(
            ((0, D, w_o), (D, 2 * FX, w_gu), (D + 2 * FX, FX, dnp))
        )
    ]
    for load in loads:
        load.start()
    m = low_half((BLK, 2 * HD))
    for p in range(8):
        a, b = parts[2 * p, :, :].astype(F32), parts[2 * p + 1, :, :].astype(F32)
        at = slice((p % 2) * 128, (p % 2) * 128 + 128)
        mixed_o[p // 2, :BLK, at] = jnp.where(m, a, swap(b)).astype(BF16)
        mixed_o[p // 2, BLK:, at] = jnp.where(m, swap(a), b).astype(BF16)
    loads[0].wait()
    middle = tokens[...].astype(F32)
    for q in range(NX):
        middle = middle + nn(mixed_o[q, :, :], w_o[q * QX : (q + 1) * QX, :])
    mid_o[...] = middle
    r = lax.rsqrt(jnp.mean(middle * middle, axis=-1, keepdims=True) + EPSILON)
    h_all[me] = (middle * r * g_ffn[...]).astype(BF16)
    pl.semaphore_wait(barrier, NX - 1)

    def send_h(t, place):
        return pltpu.make_async_remote_copy(
            src_ref=h_all.at[me],
            dst_ref=h_all.at[place],
            send_sem=ss1.at[t],
            recv_sem=rs1.at[place],
            device_id=(t, z, y, c),
            device_id_type=MESH,
        )

    def send_grad(t, place):
        return pltpu.make_async_remote_copy(
            src_ref=part.at[t],
            dst_ref=gparts.at[place],
            send_sem=ss2.at[t],
            recv_sem=rs2.at[place],
            device_id=(t, z, y, c),
            device_id_type=MESH,
        )

    for k in (1, 3, 2):
        send_h(lax.rem(me + k, NX), me).start()
    loads[1].wait()
    loads[2].wait()
    for o in range(32):
        for rg in range(9):
            for l in range(2):
                row = (o % 8) * 144 + rg * 16
                w_dn[o // 8, row : row + 16, l * 128 : l * 128 + 128] = dnp[
                    o * 32 + l * 16 : o * 32 + l * 16 + 16, rg * 128 : rg * 128 + 128
                ]

    def block(k, carry):
        t = lax.rem(me + k + k // 2 - 2 * (k // 2) * lax.rem(k, 2), NX)

        @pl.when(k > 0)
        def _():
            send_h(t, t).wait_recv()

        rows = pl.ds(pl.multiple_of(t * ROWS, ROWS), ROWS)
        gu_s[...] = nn(h_all[t], w_gu[...])
        cot_t = cot[t]
        grad_hidden = nt(cot_t[:, :256], w_dn[0])
        for q in range(1, NX):
            grad_hidden = grad_hidden + nt(cot_t[:, q * 256 : (q + 1) * 256], w_dn[q])
        dh_s[...] = grad_hidden
        for j in range(FX // 128):
            at, above = slice(j * 128, j * 128 + 128), slice(FX + j * 128, FX + j * 128 + 128)
            gate, up, dh = gu_s[:, at], gu_s[:, above], dh_s[:, at]
            sig = jax.nn.sigmoid(gate)
            silu = gate * sig
            hid[rows, at] = (silu * up).astype(BF16)
            ggu[rows, at] = (dh * up * (sig * (1.0 + gate * (1.0 - sig)))).astype(BF16)
            ggu[rows, above] = (dh * silu).astype(BF16)
        part[t] = nt(ggu[rows, :], w_gu[...]).astype(BF16)

        @pl.when(k > 0)
        def _():
            send_grad(t, me).start()

        hidden = hid[rows, :]
        for q in range(NX):
            result_o[t, :, q * 256 : (q + 1) * 256] = nn(hidden, w_dn[q]).astype(BF16)
        return carry

    lax.fori_loop(0, NX, block, 0)

    h_t[...] = h_all[...].reshape(NX * ROWS, D).T

    def columns(j, carry):
        at = pl.ds(pl.multiple_of(j * 256, 256), 256)
        dw_o[:, at] = nn(h_t[...], ggu[:, at]).astype(BF16)
        return carry

    lax.fori_loop(0, 2 * FX // 256, columns, 0)
    hid_t[...] = hid[...].T
    for q in range(NX):
        cot_q = cot[:, :, q * 256 : (q + 1) * 256].reshape(NX * ROWS, 256)
        grad = nn(hid_t[...], cot_q).astype(BF16)
        for o in range(8):
            for rg in range(9):
                for l in range(2):
                    row, there = o * 144 + rg * 16, (q * 8 + o) * 32 + l * 16
                    dw_o[there : there + 16, 2 * FX + rg * 128 : 2 * FX + rg * 128 + 128] = grad[
                        row : row + 16, l * 128 : l * 128 + 128
                    ]

    grad_h = part[me].astype(F32)
    for k in (1, 3, 2):
        t = lax.rem(me + k, NX)
        send_grad(t, t).wait_recv()
        grad_h = grad_h + gparts[t].astype(F32)
    for k in (1, 3, 2):
        t = lax.rem(me + k, NX)
        send_h(t, me).wait_send()
        send_grad(t, me).wait_send()
    middle = mid_o[...]
    r = lax.rsqrt(jnp.mean(middle * middle, axis=-1, keepdims=True) + EPSILON)
    weighted = grad_h * g_ffn[...]
    inner = jnp.mean(weighted * middle, axis=-1, keepdims=True)
    gain_o[...] = jnp.sum(grad_h * middle * r, axis=0, keepdims=True)
    grad_middle = cot[me].astype(F32) + r * weighted - middle * (r * r * r) * inner
    gmid_o[...] = grad_middle
    branch_o[...] = grad_middle.astype(BF16)
    for q in range(NX):
        grad = nt(branch_o[...], w_o[q * QX : (q + 1) * QX, :]).astype(BF16).astype(F32)
        for p in range(2):
            top, bottom = grad[:BLK, p * 128 : p * 128 + 128], grad[BLK:, p * 128 : p * 128 + 128]
            back_o[4 * q + 2 * p, :, :] = jnp.where(m, top, swap(bottom)).astype(BF16)
            back_o[4 * q + 2 * p + 1, :, :] = jnp.where(m, swap(top), bottom).astype(BF16)


def middle_part(number, parts, tokens, cot, g_ffn, wide):
    vmem = pl.BlockSpec(memory_space=pltpu.VMEM)
    blocks = (NX, ROWS, D)
    return pl.pallas_call(
        middle_kernel,
        in_specs=[vmem] * 4 + [pl.BlockSpec(memory_space=pl.ANY)],
        out_specs=[vmem] * 8,
        out_shape=[
            jax.ShapeDtypeStruct((ROWS, D), F32),
            jax.ShapeDtypeStruct(blocks, BF16),
            jax.ShapeDtypeStruct((D, 3 * FX), BF16),
            jax.ShapeDtypeStruct((ROWS, D), F32),
            jax.ShapeDtypeStruct((ROWS, D), BF16),
            jax.ShapeDtypeStruct((NX, ROWS, QX), BF16),
            jax.ShapeDtypeStruct((16, BLK, 2 * HD), BF16),
            jax.ShapeDtypeStruct((1, D), F32),
        ],
        scratch_shapes=[
            pltpu.VMEM((D, D), BF16),
            pltpu.VMEM((D, 2 * FX), BF16),
            pltpu.VMEM((D, FX), BF16),
            pltpu.VMEM((4, FX, D // 4), BF16),
            pltpu.VMEM(blocks, BF16),
            pltpu.VMEM(blocks, BF16),
            pltpu.VMEM(blocks, BF16),
            pltpu.VMEM((ROWS, 2 * FX), F32),
            pltpu.VMEM((ROWS, FX), F32),
            pltpu.VMEM((NX * ROWS, 2 * FX), BF16),
            pltpu.VMEM((NX * ROWS, FX), BF16),
            pltpu.VMEM((D, NX * ROWS), BF16),
            pltpu.VMEM((FX, NX * ROWS), BF16),
            pltpu.SemaphoreType.DMA((3,)),
            pltpu.SemaphoreType.DMA((NX,)),
            pltpu.SemaphoreType.DMA((NX,)),
            pltpu.SemaphoreType.DMA((NX,)),
            pltpu.SemaphoreType.DMA((NX,)),
        ],
        compiler_params=pltpu.CompilerParams(
            collective_id=number, has_side_effects=True, vmem_limit_bytes=VMEM_BYTES
        ),
        name="middle_part",
    )(parts, tokens, cot, g_ffn, wide)


def project_back_kernel(
    recv,
    raw,
    h,
    w,
    cos_r,
    sin_r,
    g_q,
    g_k,
    g_attn,
    mixed_x,
    branch_x,
    result,
    gain_ffn,
    tokens,
    grad_middle,
    middle,
    out_o,
    tokens_o,
    qkv_o,
    wo_o,
    gains_o,
    low,
    attn,
    gh,
    gh_parts,
    result_parts,
    dw,
    sibling_dw,
    reduced,
    dw_parts,
    gains,
    sibling_gains,
    gains_all,
    ss_r,
    rs_r,
    ss_h,
    rs_h,
    ss_s,
    rs_s,
    ss_w,
    rs_w,
    ss_g,
    rs_g,
):
    x, z, y, c = coords()
    ctx = z * 4 + y
    barrier = pltpu.get_barrier_semaphore()
    for k in range(1, NX):
        pl.semaphore_signal(
            barrier, inc=1, device_id=(lax.rem(x + k, NX), z, y, c), device_id_type=MESH
        )
    pl.semaphore_signal(barrier, inc=1, device_id=(x, z, y, 1 - c), device_id_type=MESH)

    def greet(k, carry):
        t = lax.rem(ctx + k, 16)
        dev = (x, t // 4, lax.rem(t, 4), c)
        pl.semaphore_signal(barrier, inc=1, device_id=dev, device_id_type=MESH)
        return carry

    lax.fori_loop(1, 16, greet, 0)
    pl.semaphore_wait(barrier, NX + 15)

    def along_x(src, dst, ss, rs, t, place):
        return pltpu.make_async_remote_copy(
            src_ref=src.at[t],
            dst_ref=dst.at[place],
            send_sem=ss.at[t],
            recv_sem=rs.at[place],
            device_id=(t, z, y, c),
            device_id_type=MESH,
        )

    def to_sibling(i):
        src, dst = ((dw.at[1 - c], sibling_dw), (gains, sibling_gains))[i]
        return pltpu.make_async_remote_copy(
            src_ref=src,
            dst_ref=dst,
            send_sem=ss_s.at[i],
            recv_sem=rs_s.at[i],
            device_id=(x, z, y, 1 - c),
            device_id_type=MESH,
        )

    def over_ctx(i, t, place):
        src, dst, ss, rs = (
            (reduced.at[t], dw_parts, ss_w, rs_w),
            (gains, gains_all, ss_g, rs_g),
        )[i]
        return pltpu.make_async_remote_copy(
            src_ref=src,
            dst_ref=dst.at[place],
            send_sem=ss.at[t],
            recv_sem=rs.at[place],
            device_id=(x, t // 4, lax.rem(t, 4), c),
            device_id_type=MESH,
        )

    m = low_half((ROWS, 2 * HD))
    mh = low_half((BLK, 2 * HD))
    gq_sum = jnp.zeros((1, 2 * HD), F32)
    gk_sum = jnp.zeros((1, 2 * HD), F32)
    for n, k in enumerate((1, 3, 2, 0)):
        s = lax.rem(x + k, NX)
        at = pl.ds(pl.multiple_of(s * ROWS, ROWS), ROWS)
        place = place_of(x, s) * 4
        cos_s, sin_s = cos_r[at, :], sin_r[at, :]
        part = [recv[place + hh, :ROWS, :].astype(F32) for hh in range(4)]
        vals = [recv[place + hh, ROWS:, :].astype(F32) for hh in range(4)]
        grads = [
            jnp.where(m, part[0], swap(part[1])),
            jnp.where(m, part[2], swap(part[3])),
            jnp.where(m, swap(part[0] + part[1]), part[2] + part[3]),
        ]
        for p in range(3):
            turned = grads[p] * cos_s + swap_halves(grads[p] * sin_s)
            v = raw[at, p * 128 : (p + 1) * 128]
            gain = g_q[...] if p < 2 else g_k[...]
            r = lax.rsqrt(head_mean(v * v) + EPSILON)
            weighted = turned * gain
            grad = r * weighted - v * (r * r * r) * head_mean(weighted * v)
            low[at, p * 128 : (p + 1) * 128] = grad.astype(BF16)
            term = jnp.sum(turned * v * r, axis=0, keepdims=True)
            if p < 2:
                gq_sum = gq_sum + term
            else:
                gk_sum = gk_sum + term
        a, b = vals[0] + vals[1], vals[2] + vals[3]
        grad_v = jnp.concatenate([jnp.where(mh, a, swap(b)), jnp.where(mh, swap(a), b)], 0)
        low[at, 3 * 128 :] = grad_v.astype(BF16)
        grad_h = nt(low[at, :], w[...])
        gh[s] = grad_h.astype(BF16)
        if k:
            along_x(gh, gh_parts, ss_h, rs_h, s, x).start()
        term = jnp.sum(grad_h * h[at, :].astype(F32), axis=0, keepdims=True)
        attn[...] = term if n == 0 else attn[...] + term
    for i in range(8):
        cols = slice(i * 128, i * 128 + 128)
        gains[i : i + 1, :] = attn[:, cols] / g_attn[:, cols]
        gains[8 + i : 9 + i, :] = gain_ffn[:, cols]
    gains[16:, :] = jnp.concatenate([gq_sum, gk_sum, jnp.zeros((6, 2 * HD), F32)], 0)
    grad_w = tn(h[...], low[...]).astype(BF16)
    for i in range(32):
        dw[i % 2, i // 2, :, : QX + 2 * KX] = grad_w[i * 32 : (i + 1) * 32, :]
    grad_w = tn(
        mixed_x[...].reshape(NX * ROWS, QX), branch_x[...].reshape(NX * ROWS, D)
    ).astype(BF16)
    for q in range(4):
        for i in range(8):
            dw[i % 2, q * 4 + i // 2, :, QX + 2 * KX :] = grad_w[
                i * 32 : (i + 1) * 32, q * 256 : (q + 1) * 256
            ]
    to_sibling(0).start()
    to_sibling(1).start()
    for k in (1, 3, 2):
        along_x(result, result_parts, ss_r, rs_r, lax.rem(x + k, NX), x).start()
    to_sibling(1).wait()
    gains[...] = gains[...] + sibling_gains[...]
    to_sibling(0).wait()

    def send(k, carry):
        t = lax.rem(ctx + k, 16)
        reduced[t] = (dw[c, t].astype(F32) + sibling_dw[t].astype(F32)).astype(BF16)
        over_ctx(0, t, ctx).start()
        over_ctx(1, t, ctx).start()
        return carry

    lax.fori_loop(1, 16, send, 0)
    total = dw[c, ctx].astype(F32) + sibling_dw[ctx].astype(F32)
    all_gains = gains[...]

    grad_h = gh[x].astype(F32)
    for k in (1, 3, 2):
        t = lax.rem(x + k, NX)
        along_x(gh, gh_parts, ss_h, rs_h, t, t).wait_recv()
        grad_h = grad_h + gh_parts[t].astype(F32)
    inputs = tokens[...].astype(F32)
    r = lax.rsqrt(jnp.mean(inputs * inputs, axis=-1, keepdims=True) + EPSILON)
    weighted = grad_h * g_attn[...]
    inner = jnp.mean(weighted * inputs, axis=-1, keepdims=True)
    tokens_o[...] = (
        grad_middle[...] + r * weighted - inputs * (r * r * r) * inner
    ).astype(BF16)
    out = middle[...] + result[x].astype(F32)
    for k in (1, 3, 2):
        t = lax.rem(x + k, NX)
        along_x(result, result_parts, ss_r, rs_r, t, t).wait_recv()
        out = out + result_parts[t].astype(F32)
    out_o[...] = out.astype(BF16)

    def collect(k, carry):
        t = lax.rem(ctx + k, 16)
        over_ctx(0, t, t).wait_recv()
        over_ctx(1, t, t).wait_recv()
        return carry[0] + dw_parts[t].astype(F32), carry[1] + gains_all[t]

    total, all_gains = lax.fori_loop(1, 16, collect, (total, all_gains))
    qkv_o[...] = total[:, : QX + 2 * KX].astype(BF16)
    wo_o[...] = total[:, QX + 2 * KX :].astype(BF16)
    gains_o[...] = all_gains

    def drain(k, carry):
        t = lax.rem(ctx + k, 16)
        over_ctx(0, t, ctx).wait_send()
        over_ctx(1, t, ctx).wait_send()
        return carry

    lax.fori_loop(1, 16, drain, 0)
    for k in (1, 3, 2):
        t = lax.rem(x + k, NX)
        along_x(gh, gh_parts, ss_h, rs_h, t, x).wait_send()
        along_x(result, result_parts, ss_r, rs_r, t, x).wait_send()


def project_back(number, *operands):
    vmem = pl.BlockSpec(memory_space=pltpu.VMEM)
    tokens = (NX, ROWS, D)
    wide = QX + 2 * KX + QX
    return pl.pallas_call(
        project_back_kernel,
        in_specs=[vmem] * 16,
        out_specs=[vmem] * 5,
        out_shape=[
            jax.ShapeDtypeStruct((ROWS, D), BF16),
            jax.ShapeDtypeStruct((ROWS, D), BF16),
            jax.ShapeDtypeStruct((32, QX + 2 * KX), BF16),
            jax.ShapeDtypeStruct((32, QX), BF16),
            jax.ShapeDtypeStruct((24, 2 * HD), F32),
        ],
        scratch_shapes=[
            pltpu.VMEM((NX * ROWS, QX + 2 * KX), BF16),
            pltpu.VMEM((1, D), F32),
            pltpu.VMEM(tokens, BF16),
            pltpu.VMEM(tokens, BF16),
            pltpu.VMEM(tokens, BF16),
            pltpu.VMEM((2, 16, 32, wide), BF16),
            pltpu.VMEM((16, 32, wide), BF16),
            pltpu.VMEM((16, 32, wide), BF16),
            pltpu.VMEM((16, 32, wide), BF16),
            pltpu.VMEM((24, 2 * HD), F32),
            pltpu.VMEM((24, 2 * HD), F32),
            pltpu.VMEM((16, 24, 2 * HD), F32),
        ]
        + [pltpu.SemaphoreType.DMA((n,)) for n in (NX, NX, NX, NX, 2, 2, 16, 16, 16, 16)],
        compiler_params=pltpu.CompilerParams(
            collective_id=number, has_side_effects=True, vmem_limit_bytes=VMEM_BYTES
        ),
        name="project_back",
    )(*operands)


def hand_out_kernel(qkv, gu, wo, wd, gains, q_o, k_o, v_o, o_o, g_o, u_o, d_o, ga_o, gf_o, gh_o):
    for s in range(NX):
        q_o[:, s * QX : (s + 1) * QX] = qkv[s, :, :QX].astype(F32)
        k_o[:, s * KX : (s + 1) * KX] = qkv[s, :, QX : QX + KX].astype(F32)
        v_o[:, s * KX : (s + 1) * KX] = qkv[s, :, QX + KX :].astype(F32)
        g_o[:, s * FX : (s + 1) * FX] = gu[s, :, :FX].astype(F32)
        u_o[:, s * FX : (s + 1) * FX] = gu[s, :, FX:].astype(F32)
        o_o[:, s * 256 : (s + 1) * 256] = wo[s, :, :].astype(F32)
        for rg in range(9):
            for l in range(2):
                at = slice(s * 256 + l * 128, s * 256 + l * 128 + 128)
                d_o[rg * 16 : rg * 16 + 16, at] = wd[
                    s, l * 16 : l * 16 + 16, rg * 128 : rg * 128 + 128
                ].astype(F32)
    total = gains[0] + gains[1] + gains[2] + gains[3]
    for i in range(8):
        ga_o[:, i * 128 : i * 128 + 128] = total[i : i + 1, :]
        gf_o[:, i * 128 : i * 128 + 128] = total[8 + i : 9 + i, :]
    gh_o[...] = total[16:, :] + swap(total[16:, :])


def hand_out(*operands):
    vmem = pl.BlockSpec(memory_space=pltpu.VMEM)
    shapes = [(32, D), (32, KV * HD), (32, KV * HD), (32, D), (32, FF), (32, FF), (FF // 32, D)]
    shapes += [(1, D), (1, D), (8, 2 * HD)]
    return pl.pallas_call(
        hand_out_kernel,
        in_specs=[vmem] * 5,
        out_specs=[vmem] * 10,
        out_shape=[jax.ShapeDtypeStruct(s, F32) for s in shapes],
        compiler_params=pltpu.CompilerParams(vmem_limit_bytes=VMEM_BYTES),
        name="hand_out",
    )(*operands)


def angle_constants():
    frequencies = ROPE_BASE ** (-np.arange(0, HD // 2, dtype=np.float64) * 2.0 / HD)
    phases = np.arange(LEN, dtype=np.float64)[:, None] * frequencies[None, :]
    cos, sin = np.cos(phases).astype(np.float32), np.sin(phases).astype(np.float32)
    return np.concatenate([cos] * 4, 1), np.concatenate([-sin, sin, -sin, sin], 1)


def rms_rows(values_in, gain):
    inv_rms = lax.rsqrt(jnp.mean(values_in * values_in, axis=-1, keepdims=True) + EPSILON)
    return (values_in * inv_rms * gain, inv_rms)


def columns_of(w, x, width):
    return lax.dynamic_slice_in_dim(w, x * width, width, axis=1)


def by_tiles(blocks):
    return blocks.reshape(-1, 9, 16, 2, 128).transpose(0, 3, 2, 1, 4).reshape(-1, 32, FX)


def from_tiles(blocks):
    return blocks.reshape(-1, 2, 16, 9, 128).transpose(0, 3, 2, 1, 4).reshape(-1, FF // 32, D // 4)


def body(
    tokens,
    pairs,
    w_query,
    w_key,
    w_value,
    w_out,
    w_gate,
    w_up,
    w_down,
    g_attn,
    g_query,
    g_key,
    g_ffn,
    cotangent,
):
    x, z, y, c = coords()
    ctx = z * 4 + y
    cos_np, sin_np = angle_constants()
    cos_t, sin_t = jnp.asarray(cos_np), jnp.asarray(sin_np)
    gq2 = jnp.concatenate([g_query, g_query])[None]
    gk2 = jnp.concatenate([g_key, g_key])[None]

    swap_xz = [(a * 4 + b, b * 4 + a) for a in range(4) for b in range(4)]
    down_part = lax.ppermute(columns_of(w_down, x, D // 4), ("seq", "ctx_0"), swap_xz)
    mine = jnp.concatenate(
        [w_out, columns_of(w_gate, x, FX), columns_of(w_up, x, FX), by_tiles(down_part[None])[0]],
        axis=1,
    )

    inputs = tokens[0].astype(F32)
    normed_attn, _ = rms_rows(inputs, g_attn)
    h_attn = normed_attn.astype(BF16)
    w_x = jnp.concatenate(
        [columns_of(w_query, x, QX), columns_of(w_key, x, KX), columns_of(w_value, x, KX)], axis=1
    )
    pairs_pad = jnp.pad(pairs, ((0, 7), (0, 112)))
    h_all, w_qkv, pairs_all = exchange(
        1, "gather_in", ("x", "ag", h_attn), ("p", "ag", w_x), ("x", "ag", pairs_pad)
    )
    h_all, mine = lax.optimization_barrier((h_all, mine))
    wide = lax.all_gather(mine, CTX_FSDP, axis=0, tiled=True)
    h_all = h_all.reshape(NX * ROWS, D)
    w_qkv = w_qkv.reshape(D, QX + 2 * KX)
    pairs_all = pairs_all[:, 0, :16]
    first = lax.dynamic_slice_in_dim(pairs_all, ctx, 1, axis=1)[:, 0]
    places = jnp.stack([place_of(x, s) for s in range(4)])
    blocks = jnp.concatenate([jnp.stack([first, 31 - first], axis=1).reshape(8), places])
    pair = lax.dynamic_slice_in_dim(pairs_all, sequence_at(x, z), 1, axis=0)[0]

    send, raw, cos_r, sin_r = project(blocks, h_all, w_qkv, cos_t, sin_t, gq2, gk2)
    recv, cot_all = exchange(2, "to_heads", ("c", "a2a", send), ("x", "ag", cotangent[0]))
    heads_out, q_s, k_s, v_s, o_t, inv = attend(pair, recv)
    (mixed_parts,) = exchange(3, "to_tokens", ("t", "a2a", heads_out))
    middle, result4, grad_w_ffn, grad_middle, grad_branch, mixed, back_parts, gain_ffn = middle_part(
        4, mixed_parts, tokens[0], cot_all, g_ffn[None], wide
    )
    sums = lax.psum_scatter(grad_w_ffn, CTX_FSDP, scatter_dimension=0, tiled=True)
    (recv_g,) = exchange(6, "to_heads_back", ("r", "a2a", back_parts))
    sends_back = attend_back(pair, recv_g, q_s, k_s, v_s, o_t, inv)
    recv_back, branch_x, mixed_x = exchange(
        7,
        "to_tokens_back",
        ("c", "a2a", sends_back),
        ("x", "ag", grad_branch),
        ("x", "a2a", mixed),
    )
    output, grad_tokens, sum_qkv, sum_o, gains = project_back(
        8,
        recv_back,
        raw,
        h_all,
        w_qkv,
        cos_r,
        sin_r,
        gq2,
        gk2,
        g_attn[None],
        mixed_x,
        branch_x,
        result4,
        gain_ffn,
        tokens[0],
        grad_middle,
        middle,
    )
    qkv, gate_up, out_rows, down_rows, gains = exchange(
        9,
        "gather_out",
        ("x", "ag", sum_qkv),
        ("x", "ag", sums, (0, 2 * FX)),
        ("d", "ag", sum_o),
        ("d", "ag", sums, (2 * FX, FX)),
        ("x", "ag", gains),
    )
    *weights, gain_a, gain_f, gain_h = hand_out(qkv, gate_up, out_rows, down_rows, gains)
    return (
        output[None],
        grad_tokens[None],
        *weights,
        gain_a[0],
        gain_h[0, :HD],
        gain_h[1, :HD],
        gain_f[0],
    )


def solution(mesh):
    finer = Mesh(
        mesh.devices.reshape(mesh.shape["seq"], 4, 4, mesh.shape["fsdp"]),
        ("seq", "ctx_0", "ctx_1", "fsdp"),
    )
    tokens_spec = P(("seq", "fsdp"), CTX, None)
    rows_spec = P(CTX_FSDP, None)
    return jax.shard_map(
        body,
        mesh=finer,
        in_specs=(tokens_spec, P(("seq", "fsdp"), None))
        + (rows_spec,) * 7
        + (P(),) * 4
        + (tokens_spec,),
        out_specs=(tokens_spec, tokens_spec) + (rows_spec,) * 7 + (P(),) * 4,
        check_vma=False,
    )
```

```python
import functools

import jax
import jax.numpy as jnp
import numpy as np
from jax import lax
from jax.experimental import pallas as pl
from jax.experimental.pallas import tpu as pltpu
from jax.sharding import Mesh
from jax.sharding import PartitionSpec as P

D = 1024
H = 16
KV = 8
HD = 64
FF = 4608
LEN = 2560
BLK = 80
ROWS = 2 * BLK
NX = 4
FX = FF // NX
QX = H * HD // NX
KX = KV * HD // NX
TILE = 512
N_TILES = LEN // TILE
CTX = ("ctx_0", "ctx_1")
CTX_FSDP = ("ctx_0", "ctx_1", "fsdp")
SEQ_CTX_FSDP = ("seq", "ctx_0", "ctx_1", "fsdp")
EPSILON = 1e-05
ROPE_BASE = 1000000.0
MESH = pl.DeviceIdType.MESH
BF16 = jnp.bfloat16
F32 = jnp.float32
VMEM_BYTES = 56 * 1024 * 1024


SIZE = {"x": 4, "c": 16, "p": 32, "t": 16, "r": 16, "d": 4}


def coords():
    return tuple(lax.axis_index(a) for a in SEQ_CTX_FSDP)


def twisted(x, v):
    return lax.rem(v + 2 * (1 - lax.rem(x, 2)) * (1 - lax.rem(v, 2)), 4)


def sequence_at(x, z):
    return lax.rem(x + twisted(x, z), 4)


def place_of(x, s):
    return twisted(x, lax.rem(s - x + 4, 4))


def target(group, t):
    s, z, y, c = coords()
    if group == "x":
        return (t, z, y, c), s
    if group == "c":
        return (s, t // 4, lax.rem(t, 4), c), z * 4 + y
    if group == "p":
        return (s, t // 8, lax.rem(t // 2, 4), lax.rem(t, 2)), (z * 4 + y) * 2 + c
    if group == "t":
        return (sequence_at(s, z), t // 4, lax.rem(t, 4), c), s * 4 + y
    if group == "d":
        return (t, s, y, c), z
    return (t // 4, place_of(t // 4, s), lax.rem(t, 4), c), z * 4 + y


def source(group, t):
    s, z, y, c = coords()
    if group == "t":
        return (t // 4, place_of(t // 4, s), lax.rem(t, 4), c)
    if group == "r":
        return (sequence_at(s, z), t // 4, lax.rem(t, 4), c)
    if group == "d":
        return (z, t, y, c)
    return target(group, t)[0]


def own(group):
    s, z, y, c = coords()
    if group == "t":
        return sequence_at(s, z) == s, z * 4 + y, s * 4 + y
    if group == "r":
        return sequence_at(s, z) == s, s * 4 + y, z * 4 + y
    if group == "d":
        return s == z, s, z
    me = target(group, 0)[1]
    return None, me, me


def exchange_kernel(items, *refs):
    n = len(items)
    srcs, outs, sems = refs[:n], refs[n : 2 * n], refs[2 * n :]
    barrier = pltpu.get_barrier_semaphore()
    expected = 0
    starts = []
    for i, (g, _, _) in enumerate(items):
        has_own, sent, _ = own(g)
        size = SIZE[g]
        if has_own is None:
            starts.append((jnp.int32(1), sent))
            expected = expected + size - 1
        else:
            starts.append((has_own.astype(jnp.int32), sent))
            expected = expected + size - has_own.astype(jnp.int32)
        place = own(g)[2]
        first = starts[i][0]

        def greet(k, carry, g=g, size=size, place=place):
            dev = source(g, lax.rem(place + k, size))
            pl.semaphore_signal(barrier, inc=1, device_id=dev, device_id_type=MESH)
            return carry

        lax.fori_loop(first, size, greet, 0)

    def block_of(i, t):
        _, mode, cols = items[i]
        if cols is not None:
            return srcs[i].at[:, pl.ds(*cols)]
        return srcs[i] if mode == "ag" else srcs[i].at[t]

    def own_copy(i):
        g = items[i][0]
        _, sent, place = own(g)
        src = block_of(i, sent)
        return pltpu.make_async_copy(src, outs[i].at[place], sems[3 * i + 2])

    for i, (g, _, _) in enumerate(items):
        if own(g)[0] is None:
            own_copy(i).start()
        else:
            pl.when(own(g)[0])(lambda i=i: own_copy(i).start())
    pl.semaphore_wait(barrier, expected)

    def remote(i, t, place):
        g = items[i][0]
        dev, there = target(g, t)
        src = block_of(i, t)
        return pltpu.make_async_remote_copy(
            src_ref=src,
            dst_ref=outs[i].at[there if place is None else place],
            send_sem=sems[3 * i].at[t],
            recv_sem=sems[3 * i + 1].at[there if place is None else place],
            device_id=dev,
            device_id_type=MESH,
        )

    for i, (g, _, _) in enumerate(items):
        first, sent = starts[i]

        def send(k, carry, i=i, g=g, sent=sent):
            remote(i, lax.rem(sent + k, SIZE[g]), None).start()
            return carry

        lax.fori_loop(first, SIZE[g], send, 0)
    for i, (g, _, _) in enumerate(items):
        first, sent = starts[i]
        place = own(g)[2]

        def drain(k, carry, i=i, g=g, sent=sent, place=place):
            remote(i, lax.rem(sent + k, SIZE[g]), None).wait_send()
            remote(i, lax.rem(sent + k, SIZE[g]), lax.rem(place + k, SIZE[g])).wait_recv()
            return carry

        lax.fori_loop(first, SIZE[g], drain, 0)
        if own(g)[0] is None:
            own_copy(i).wait()
        else:
            pl.when(own(g)[0])(lambda i=i: own_copy(i).wait())


def exchange(number, name, *parts):
    items = tuple((part[0], part[1], part[3] if len(part) > 3 else None) for part in parts)
    arrays = [part[2] for part in parts]
    outs = []
    for (g, m, cols), a in zip(items, arrays):
        shape = a.shape if m == "ag" else a.shape[1:]
        shape = shape if cols is None else shape[:-1] + (cols[1],)
        outs.append(jax.ShapeDtypeStruct((SIZE[g],) + shape, a.dtype))
    scratch = []
    for g, _, _ in items:
        scratch += [
            pltpu.SemaphoreType.DMA((SIZE[g],)),
            pltpu.SemaphoreType.DMA((SIZE[g],)),
            pltpu.SemaphoreType.DMA,
        ]
    return pl.pallas_call(
        functools.partial(exchange_kernel, items),
        out_shape=outs,
        in_specs=[pl.BlockSpec(memory_space=pl.ANY)] * len(arrays),
        out_specs=[pl.BlockSpec(memory_space=pl.ANY)] * len(arrays),
        scratch_shapes=scratch,
        compiler_params=pltpu.CompilerParams(collective_id=number, has_side_effects=True),
        name=name,
    )(*arrays)


def lanes(shape):
    return lax.broadcasted_iota(jnp.int32, shape, len(shape) - 1)


def low_half(shape):
    return lanes(shape) < HD


def swap(v):
    return pltpu.roll(v, HD, 1)


def swap_halves(v):
    first = lax.rem(lanes(v.shape), HD) < HD // 2
    return jnp.where(first, pltpu.roll(v, 2 * HD - HD // 2, 1), pltpu.roll(v, HD // 2, 1))


def head_mean(v):
    m = low_half(v.shape)
    a = jnp.sum(jnp.where(m, v, 0.0), axis=-1, keepdims=True)
    b = jnp.sum(jnp.where(m, 0.0, v), axis=-1, keepdims=True)
    return jnp.where(m, a, b) * (1.0 / HD)


def nt(a, b):
    return lax.dot_general(a, b, (((1,), (1,)), ((), ())), preferred_element_type=F32)


def nn(a, b):
    return lax.dot_general(a, b, (((1,), (0,)), ((), ())), preferred_element_type=F32)


def tn(a, b):
    return lax.dot_general(a, b, (((0,), (0,)), ((), ())), preferred_element_type=F32)


def my_pairs(pairs):
    x, z, _, _ = coords()
    line = sequence_at(x, z) * 8
    return [pairs[line, j] for j in range(16)]


def rows_of(block):
    return pl.ds(pl.multiple_of(block * BLK, 16), BLK)


def rope_rows(block, table):
    return jnp.concatenate([table[rows_of(block), :], table[rows_of(31 - block), :]], 0)


def gather_in_kernel(
    tokens,
    g_attn,
    w_q,
    w_k,
    w_v,
    pairs,
    h_o,
    w_o,
    pairs_o,
    h,
    w,
    row,
    ss_h,
    rs_h,
    ss_p,
    rs_p,
    ss_w,
    rs_w,
    ss_f,
    rs_f,
    own_sem,
):
    x, z, y, c = coords()
    ctx = z * 4 + y
    barrier = pltpu.get_barrier_semaphore()
    for k in range(1, NX):
        pl.semaphore_signal(
            barrier, inc=1, device_id=(lax.rem(x + k, NX), z, y, c), device_id_type=MESH
        )
    pl.semaphore_signal(barrier, inc=1, device_id=(x, z, y, 1 - c), device_id_type=MESH)

    def greet(k, carry):
        t = lax.rem(ctx + k, 16)
        dev = (x, t // 4, lax.rem(t, 4), c)
        pl.semaphore_signal(barrier, inc=1, device_id=dev, device_id_type=MESH)
        return carry

    lax.fori_loop(1, 16, greet, 0)
    w[:, :QX] = w_q[:, pl.ds(pl.multiple_of(x * QX, QX), QX)]
    w[:, QX : QX + KX] = w_k[:, pl.ds(pl.multiple_of(x * KX, KX), KX)]
    w[:, QX + KX :] = w_v[:, pl.ds(pl.multiple_of(x * KX, KX), KX)]
    row[...] = jnp.zeros_like(row)
    row[0:1, :16] = pairs[...]
    inputs = tokens[...].astype(F32)
    inv_rms = lax.rsqrt(jnp.mean(inputs * inputs, axis=-1, keepdims=True) + EPSILON)
    h[...] = (inputs * inv_rms * g_attn[...]).astype(BF16)

    def along_x(src, dst, ss, rs, t, place):
        return pltpu.make_async_remote_copy(
            src_ref=src,
            dst_ref=dst.at[place],
            send_sem=ss.at[t],
            recv_sem=rs.at[place],
            device_id=(t, z, y, c),
            device_id_type=MESH,
        )

    def over_ctx(t, place):
        return pltpu.make_async_remote_copy(
            src_ref=w,
            dst_ref=w_o.at[place * 2 + c],
            send_sem=ss_w.at[t],
            recv_sem=rs_w.at[place],
            device_id=(x, t // 4, lax.rem(t, 4), c),
            device_id_type=MESH,
        )

    def to_sibling(t, core, src):
        return pltpu.make_async_remote_copy(
            src_ref=src,
            dst_ref=w_o.at[t * 2 + core],
            send_sem=ss_f.at[t],
            recv_sem=rs_f.at[t],
            device_id=(x, z, y, 1 - c),
            device_id_type=MESH,
        )

    mine = [
        pltpu.make_async_copy(h, h_o.at[x], own_sem.at[0]),
        pltpu.make_async_copy(row, pairs_o.at[x], own_sem.at[1]),
        pltpu.make_async_copy(w, w_o.at[ctx * 2 + c], own_sem.at[2]),
    ]
    for copy in mine:
        copy.start()
    pl.semaphore_wait(barrier, NX + 15)
    for k in (1, 3, 2):
        t = lax.rem(x + k, NX)
        along_x(h, h_o, ss_h, rs_h, t, x).start()
        along_x(row, pairs_o, ss_p, rs_p, t, x).start()

    def send(k, carry):
        over_ctx(lax.rem(ctx + k, 16), ctx).start()
        return carry

    lax.fori_loop(1, 16, send, 0)
    to_sibling(ctx, c, w).start()

    def forward(k, carry):
        t = lax.rem(ctx + k, 16)
        over_ctx(t, t).wait_recv()
        to_sibling(t, c, w_o.at[t * 2 + c]).start()
        return carry

    lax.fori_loop(1, 16, forward, 0)

    def drain(k, carry):
        t = lax.rem(ctx + k, 16)
        to_sibling(t, 1 - c, w).wait_recv()
        to_sibling(t, c, w).wait_send()
        return carry

    lax.fori_loop(0, 16, drain, 0)

    def drain_ctx(k, carry):
        over_ctx(lax.rem(ctx + k, 16), ctx).wait_send()
        return carry

    lax.fori_loop(1, 16, drain_ctx, 0)
    for k in (1, 3, 2):
        t = lax.rem(x + k, NX)
        along_x(h, h_o, ss_h, rs_h, t, x).wait_send()
        along_x(row, pairs_o, ss_p, rs_p, t, x).wait_send()
        along_x(h, h_o, ss_h, rs_h, t, t).wait_recv()
        along_x(row, pairs_o, ss_p, rs_p, t, t).wait_recv()
    for copy in mine:
        copy.wait()


def gather_in(number, *operands):
    wide = QX + 2 * KX
    return pl.pallas_call(
        gather_in_kernel,
        in_specs=[pl.BlockSpec(memory_space=pltpu.VMEM)] * 6,
        out_specs=[pl.BlockSpec(memory_space=pl.ANY)] * 3,
        out_shape=[
            jax.ShapeDtypeStruct((NX, ROWS, D), BF16),
            jax.ShapeDtypeStruct((32, 32, wide), BF16),
            jax.ShapeDtypeStruct((NX, 8, 128), jnp.int32),
        ],
        scratch_shapes=[
            pltpu.VMEM((ROWS, D), BF16),
            pltpu.VMEM((32, wide), BF16),
            pltpu.VMEM((8, 128), jnp.int32),
        ]
        + [pltpu.SemaphoreType.DMA((n,)) for n in (NX, NX, NX, NX, 16, 16, 16, 16, 3)],
        compiler_params=pltpu.CompilerParams(collective_id=number, has_side_effects=True),
        name="gather_in",
    )(*operands)


def project_kernel(pairs, h, w, cos_t, sin_t, g_q, g_k, send, raw, cos_o, sin_o, acc):
    x, z, y, _ = coords()
    acc[...] = nn(h[...], w[...])
    m = low_half((ROWS, 2 * HD))
    mh = low_half((BLK, 2 * HD))
    for s in range(NX):
        at = slice(s * ROWS, (s + 1) * ROWS)
        cos_r, sin_r = (rope_rows(pairs[s * 8, z * 4 + y], table) for table in (cos_t, sin_t))
        cos_o[at, :], sin_o[at, :] = cos_r, sin_r
        raw[at, :] = acc[at, : QX + KX]
        turned = []
        for p in range(3):
            v = acc[at, p * 128 : (p + 1) * 128]
            gain = g_q[...] if p < 2 else g_k[...]
            normed = v * lax.rsqrt(head_mean(v * v) + EPSILON) * gain
            turned.append(normed * cos_r + swap_halves(normed) * sin_r)
        keys = turned[2]
        swapped_keys = swap(keys)
        values = acc[at, 3 * 128 :]
        top, bottom = values[:BLK], values[BLK:]
        packed = (jnp.where(mh, top, swap(bottom)), jnp.where(mh, swap(top), bottom))
        for hh in range(4):
            q = turned[hh // 2]
            q = q if hh % 2 == 0 else swap(q)
            k = swapped_keys if hh < 2 else keys
            send[place_of(x, s) * 4 + hh, :ROWS, :] = jnp.where(m, q, k).astype(BF16)
            send[place_of(x, s) * 4 + hh, ROWS:, :] = packed[hh // 2].astype(BF16)


def project(pairs, h, w, cos_t, sin_t, g_q, g_k):
    return pl.pallas_call(
        project_kernel,
        grid_spec=pltpu.PrefetchScalarGridSpec(
            num_scalar_prefetch=1,
            in_specs=[pl.BlockSpec(memory_space=pltpu.VMEM)] * 6,
            out_specs=[pl.BlockSpec(memory_space=pltpu.VMEM)] * 4,
            scratch_shapes=[pltpu.VMEM((NX * ROWS, QX + 2 * KX), F32)],
        ),
        out_shape=[
            jax.ShapeDtypeStruct((16, ROWS + BLK, 2 * HD), BF16),
            jax.ShapeDtypeStruct((NX * ROWS, QX + KX), F32),
            jax.ShapeDtypeStruct((NX * ROWS, 2 * HD), F32),
            jax.ShapeDtypeStruct((NX * ROWS, 2 * HD), F32),
        ],
        compiler_params=pltpu.CompilerParams(vmem_limit_bytes=VMEM_BYTES),
        name="project",
    )(pairs, h, w, cos_t, sin_t, g_q, g_k)


def attend_kernel(pairs, recv, out, q_s, k_s, v_s, o_t, inv, o_s, v_t):
    m = low_half((BLK, 2 * HD))
    pair = my_pairs(pairs)
    for j in range(16):
        packed = recv[j, ROWS:, :].astype(F32)
        for half in range(2):
            block = pair[j] if half == 0 else 31 - pair[j]
            both = recv[j, half * BLK : (half + 1) * BLK, :].astype(F32)
            vals = packed if half == 0 else swap(packed)
            q_s[rows_of(block), :] = jnp.where(m, both * HD**-0.5, 0.0).astype(BF16)
            k_s[rows_of(block), :] = jnp.where(m, swap(both), 0.0).astype(BF16)
            v_s[rows_of(block), :] = jnp.where(m, vals, 0.0).astype(BF16)
    for t in range(N_TILES):
        at = slice(t * TILE, (t + 1) * TILE)
        v_t[:, at] = v_s[at, :].T[:HD]
    causal = lax.broadcasted_iota(jnp.int32, (TILE, TILE), 0) <= lanes((TILE, TILE))
    for i in range(N_TILES):
        at = slice(i * TILE, (i + 1) * TILE)
        q = q_s[at, :]

        e = jnp.where(causal, jnp.exp(nt(k_s[at, :], q)), 0.0)
        first = (jnp.sum(e, axis=0, keepdims=True), nn(v_t[:, at], e.astype(BF16)))

        def step(t, carry, q=q):
            total, acc = carry
            there = pl.ds(pl.multiple_of(t * TILE, TILE), TILE)
            e = jnp.exp(nt(k_s[there, :], q))
            total = total + jnp.sum(e, axis=0, keepdims=True)
            return total, acc + nn(v_t[:, there], e.astype(BF16))

        total, acc = lax.fori_loop(0, i, step, first) if i else first
        over = 1.0 / total
        attended = acc * over
        o_t[:, at] = attended
        inv[:, at] = jnp.broadcast_to(over, (8, TILE))
        o_s[at, :] = jnp.concatenate([attended, jnp.zeros_like(attended)], 0).T
    for j in range(16):
        low_rows = o_s[rows_of(pair[j]), :]
        high_rows = o_s[rows_of(31 - pair[j]), :]
        out[j, :, :] = (low_rows + swap(high_rows)).astype(BF16)


def attend(pairs, recv):
    wide = jax.ShapeDtypeStruct((LEN, 2 * HD), BF16)
    return pl.pallas_call(
        attend_kernel,
        grid_spec=pltpu.PrefetchScalarGridSpec(
            num_scalar_prefetch=1,
            in_specs=[pl.BlockSpec(memory_space=pltpu.VMEM)],
            out_specs=[pl.BlockSpec(memory_space=pltpu.VMEM)] * 6,
            scratch_shapes=[pltpu.VMEM((LEN, 2 * HD), F32), pltpu.VMEM((HD, LEN), BF16)],
        ),
        out_shape=[
            jax.ShapeDtypeStruct((16, BLK, 2 * HD), BF16),
            wide,
            wide,
            wide,
            jax.ShapeDtypeStruct((HD, LEN), F32),
            jax.ShapeDtypeStruct((8, LEN), F32),
        ],
        compiler_params=pltpu.CompilerParams(vmem_limit_bytes=VMEM_BYTES),
        name="attend",
    )(pairs, recv)


def attend_back_kernel(pairs, recv, q_s, k_s, v_s, o_t, inv, out, g_s, k_t, delta, dq_t, dk_s, dv_s):
    m = low_half((BLK, 2 * HD))
    pair = my_pairs(pairs)
    for j in range(16):
        packed = recv[j, :, :].astype(F32)
        g_s[rows_of(pair[j]), :] = jnp.where(m, packed, 0.0).astype(BF16)
        g_s[rows_of(31 - pair[j]), :] = jnp.where(m, swap(packed), 0.0).astype(BF16)
    for t in range(N_TILES):
        at = slice(t * TILE, (t + 1) * TILE)
        k_t[:, at] = k_s[at, :].T[:HD]
        g_t = g_s[at, :].astype(F32).T[:HD]
        row = jnp.sum(g_t * o_t[:, at], axis=0, keepdims=True)
        delta[:, at] = jnp.broadcast_to(row, (8, TILE))
    dq_t[...] = jnp.zeros_like(dq_t)
    causal = lax.broadcasted_iota(jnp.int32, (TILE, TILE), 0) <= lanes((TILE, TILE))
    for i in range(N_TILES):
        at = slice(i * TILE, (i + 1) * TILE)
        k, v, kt = k_s[at, :], v_s[at, :], k_t[:, at]

        def pair_of_tiles(there, masked, k=k, v=v, kt=kt):
            q, g = q_s[there, :], g_s[there, :]
            e = jnp.exp(nt(k, q))
            if masked:
                e = jnp.where(causal, e, 0.0)
            probs = e * inv[0:1, there]
            ds = (probs * (nt(v, g) - delta[0:1, there])).astype(BF16)
            dq_t[:, there] = dq_t[:, there] + nn(kt, ds)
            return nn(ds, q), nn(probs.astype(BF16), g)

        first = pair_of_tiles(at, True)

        def step(t, carry, pair_of_tiles=pair_of_tiles):
            dk, dv = pair_of_tiles(pl.ds(pl.multiple_of(t * TILE, TILE), TILE), False)
            return carry[0] + dk, carry[1] + dv

        dk, dv = lax.fori_loop(i + 1, N_TILES, step, first) if i + 1 < N_TILES else first
        dk_s[at, :] = dk
        dv_s[at, :] = dv
    for i in range(N_TILES):
        at = slice(i * TILE, (i + 1) * TILE)
        dq = dq_t[:, at] * HD**-0.5
        dk_s[at, :] = jnp.concatenate([dq, jnp.zeros_like(dq)], 0).T + swap(dk_s[at, :])
    for j in range(16):
        for half in range(2):
            block = pair[j] if half == 0 else 31 - pair[j]
            out[j, half * BLK : (half + 1) * BLK, :] = dk_s[rows_of(block), :].astype(BF16)
        out[j, ROWS:, :] = (dv_s[rows_of(pair[j]), :] + swap(dv_s[rows_of(31 - pair[j]), :])).astype(BF16)


def attend_back(pairs, recv, q_s, k_s, v_s, o_t, inv):
    return pl.pallas_call(
        attend_back_kernel,
        grid_spec=pltpu.PrefetchScalarGridSpec(
            num_scalar_prefetch=1,
            in_specs=[pl.BlockSpec(memory_space=pltpu.VMEM)] * 6,
            out_specs=pl.BlockSpec(memory_space=pltpu.VMEM),
            scratch_shapes=[
                pltpu.VMEM((LEN, 2 * HD), BF16),
                pltpu.VMEM((HD, LEN), BF16),
                pltpu.VMEM((8, LEN), F32),
                pltpu.VMEM((HD, LEN), F32),
                pltpu.VMEM((LEN, 2 * HD), F32),
                pltpu.VMEM((LEN, 2 * HD), F32),
            ],
        ),
        out_shape=jax.ShapeDtypeStruct((16, ROWS + BLK, 2 * HD), BF16),
        compiler_params=pltpu.CompilerParams(vmem_limit_bytes=VMEM_BYTES),
        name="attend_back",
    )(pairs, recv, q_s, k_s, v_s, o_t, inv)


def middle_kernel(
    parts,
    tokens,
    cot,
    g_ffn,
    wide,
    mid_o,
    result_o,
    dw_o,
    gmid_o,
    branch_o,
    mixed_o,
    back_o,
    gain_o,
    w_o,
    w_gu,
    dnp,
    w_dn,
    h_all,
    part,
    gparts,
    gu_s,
    dh_s,
    ggu,
    hid,
    h_t,
    hid_t,
    wsem,
    ss1,
    rs1,
    ss2,
    rs2,
):
    me, z, y, c = coords()
    barrier = pltpu.get_barrier_semaphore()
    for k in range(1, NX):
        pl.semaphore_signal(
            barrier, inc=1, device_id=(lax.rem(me + k, NX), z, y, c), device_id_type=MESH
        )
    loads = [
        pltpu.make_async_copy(wide.at[:, pl.ds(at, width)], there, wsem.at[i])
        for i, (at, width, there) in enumerate(
            ((0, D, w_o), (D, 2 * FX, w_gu), (D + 2 * FX, FX, dnp))
        )
    ]
    for load in loads:
        load.start()
    m = low_half((BLK, 2 * HD))
    for p in range(8):
        a, b = parts[2 * p, :, :].astype(F32), parts[2 * p + 1, :, :].astype(F32)
        at = slice((p % 2) * 128, (p % 2) * 128 + 128)
        mixed_o[p // 2, :BLK, at] = jnp.where(m, a, swap(b)).astype(BF16)
        mixed_o[p // 2, BLK:, at] = jnp.where(m, swap(a), b).astype(BF16)
    loads[0].wait()
    middle = tokens[...].astype(F32)
    for q in range(NX):
        middle = middle + nn(mixed_o[q, :, :], w_o[q * QX : (q + 1) * QX, :])
    mid_o[...] = middle
    r = lax.rsqrt(jnp.mean(middle * middle, axis=-1, keepdims=True) + EPSILON)
    h_all[me] = (middle * r * g_ffn[...]).astype(BF16)
    pl.semaphore_wait(barrier, NX - 1)

    def send_h(t, place):
        return pltpu.make_async_remote_copy(
            src_ref=h_all.at[me],
            dst_ref=h_all.at[place],
            send_sem=ss1.at[t],
            recv_sem=rs1.at[place],
            device_id=(t, z, y, c),
            device_id_type=MESH,
        )

    def send_grad(t, place):
        return pltpu.make_async_remote_copy(
            src_ref=part.at[t],
            dst_ref=gparts.at[place],
            send_sem=ss2.at[t],
            recv_sem=rs2.at[place],
            device_id=(t, z, y, c),
            device_id_type=MESH,
        )

    for k in (1, 3, 2):
        send_h(lax.rem(me + k, NX), me).start()
    loads[1].wait()
    loads[2].wait()
    for o in range(32):
        for rg in range(9):
            for l in range(2):
                row = (o % 8) * 144 + rg * 16
                w_dn[o // 8, row : row + 16, l * 128 : l * 128 + 128] = dnp[
                    o * 32 + l * 16 : o * 32 + l * 16 + 16, rg * 128 : rg * 128 + 128
                ]

    def block(k, carry):
        t = lax.rem(me + k + k // 2 - 2 * (k // 2) * lax.rem(k, 2), NX)

        @pl.when(k > 0)
        def _():
            send_h(t, t).wait_recv()

        rows = pl.ds(pl.multiple_of(t * ROWS, ROWS), ROWS)
        gu_s[...] = nn(h_all[t], w_gu[...])
        cot_t = cot[t]
        grad_hidden = nt(cot_t[:, :256], w_dn[0])
        for q in range(1, NX):
            grad_hidden = grad_hidden + nt(cot_t[:, q * 256 : (q + 1) * 256], w_dn[q])
        dh_s[...] = grad_hidden
        for j in range(FX // 128):
            at, above = slice(j * 128, j * 128 + 128), slice(FX + j * 128, FX + j * 128 + 128)
            gate, up, dh = gu_s[:, at], gu_s[:, above], dh_s[:, at]
            sig = jax.nn.sigmoid(gate)
            silu = gate * sig
            hid[rows, at] = (silu * up).astype(BF16)
            ggu[rows, at] = (dh * up * (sig * (1.0 + gate * (1.0 - sig)))).astype(BF16)
            ggu[rows, above] = (dh * silu).astype(BF16)
        part[t] = nt(ggu[rows, :], w_gu[...]).astype(BF16)

        @pl.when(k > 0)
        def _():
            send_grad(t, me).start()

        hidden = hid[rows, :]
        for q in range(NX):
            result_o[t, :, q * 256 : (q + 1) * 256] = nn(hidden, w_dn[q]).astype(BF16)
        return carry

    lax.fori_loop(0, NX, block, 0)

    h_t[...] = h_all[...].reshape(NX * ROWS, D).T

    def columns(j, carry):
        at = pl.ds(pl.multiple_of(j * 256, 256), 256)
        dw_o[:, at] = nn(h_t[...], ggu[:, at]).astype(BF16)
        return carry

    lax.fori_loop(0, 2 * FX // 256, columns, 0)
    hid_t[...] = hid[...].T
    for q in range(NX):
        cot_q = cot[:, :, q * 256 : (q + 1) * 256].reshape(NX * ROWS, 256)
        grad = nn(hid_t[...], cot_q).astype(BF16)
        for o in range(8):
            for rg in range(9):
                for l in range(2):
                    row, there = o * 144 + rg * 16, (q * 8 + o) * 32 + l * 16
                    dw_o[there : there + 16, 2 * FX + rg * 128 : 2 * FX + rg * 128 + 128] = grad[
                        row : row + 16, l * 128 : l * 128 + 128
                    ]

    grad_h = part[me].astype(F32)
    for k in (1, 3, 2):
        t = lax.rem(me + k, NX)
        send_grad(t, t).wait_recv()
        grad_h = grad_h + gparts[t].astype(F32)
    for k in (1, 3, 2):
        t = lax.rem(me + k, NX)
        send_h(t, me).wait_send()
        send_grad(t, me).wait_send()
    middle = mid_o[...]
    r = lax.rsqrt(jnp.mean(middle * middle, axis=-1, keepdims=True) + EPSILON)
    weighted = grad_h * g_ffn[...]
    inner = jnp.mean(weighted * middle, axis=-1, keepdims=True)
    gain_o[...] = jnp.sum(grad_h * middle * r, axis=0, keepdims=True)
    grad_middle = cot[me].astype(F32) + r * weighted - middle * (r * r * r) * inner
    gmid_o[...] = grad_middle
    branch_o[...] = grad_middle.astype(BF16)
    for q in range(NX):
        grad = nt(branch_o[...], w_o[q * QX : (q + 1) * QX, :]).astype(BF16).astype(F32)
        for p in range(2):
            top, bottom = grad[:BLK, p * 128 : p * 128 + 128], grad[BLK:, p * 128 : p * 128 + 128]
            back_o[4 * q + 2 * p, :, :] = jnp.where(m, top, swap(bottom)).astype(BF16)
            back_o[4 * q + 2 * p + 1, :, :] = jnp.where(m, swap(top), bottom).astype(BF16)


def middle_part(number, parts, tokens, cot, g_ffn, wide):
    vmem = pl.BlockSpec(memory_space=pltpu.VMEM)
    blocks = (NX, ROWS, D)
    return pl.pallas_call(
        middle_kernel,
        in_specs=[vmem] * 4 + [pl.BlockSpec(memory_space=pl.ANY)],
        out_specs=[vmem] * 8,
        out_shape=[
            jax.ShapeDtypeStruct((ROWS, D), F32),
            jax.ShapeDtypeStruct(blocks, BF16),
            jax.ShapeDtypeStruct((D, 3 * FX), BF16),
            jax.ShapeDtypeStruct((ROWS, D), F32),
            jax.ShapeDtypeStruct((ROWS, D), BF16),
            jax.ShapeDtypeStruct((NX, ROWS, QX), BF16),
            jax.ShapeDtypeStruct((16, BLK, 2 * HD), BF16),
            jax.ShapeDtypeStruct((1, D), F32),
        ],
        scratch_shapes=[
            pltpu.VMEM((D, D), BF16),
            pltpu.VMEM((D, 2 * FX), BF16),
            pltpu.VMEM((D, FX), BF16),
            pltpu.VMEM((4, FX, D // 4), BF16),
            pltpu.VMEM(blocks, BF16),
            pltpu.VMEM(blocks, BF16),
            pltpu.VMEM(blocks, BF16),
            pltpu.VMEM((ROWS, 2 * FX), F32),
            pltpu.VMEM((ROWS, FX), F32),
            pltpu.VMEM((NX * ROWS, 2 * FX), BF16),
            pltpu.VMEM((NX * ROWS, FX), BF16),
            pltpu.VMEM((D, NX * ROWS), BF16),
            pltpu.VMEM((FX, NX * ROWS), BF16),
            pltpu.SemaphoreType.DMA((3,)),
            pltpu.SemaphoreType.DMA((NX,)),
            pltpu.SemaphoreType.DMA((NX,)),
            pltpu.SemaphoreType.DMA((NX,)),
            pltpu.SemaphoreType.DMA((NX,)),
        ],
        compiler_params=pltpu.CompilerParams(
            collective_id=number, has_side_effects=True, vmem_limit_bytes=VMEM_BYTES
        ),
        name="middle_part",
    )(parts, tokens, cot, g_ffn, wide)


def project_back_kernel(
    recv,
    raw,
    h,
    w,
    cos_r,
    sin_r,
    g_q,
    g_k,
    g_attn,
    mixed_x,
    branch_x,
    result,
    gain_ffn,
    tokens,
    grad_middle,
    middle,
    out_o,
    tokens_o,
    qkv_o,
    wo_o,
    gains_o,
    low,
    attn,
    gh,
    gh_parts,
    result_parts,
    dw,
    sibling_dw,
    reduced,
    dw_parts,
    gains,
    sibling_gains,
    gains_all,
    ss_r,
    rs_r,
    ss_h,
    rs_h,
    ss_s,
    rs_s,
    ss_w,
    rs_w,
    ss_g,
    rs_g,
):
    x, z, y, c = coords()
    ctx = z * 4 + y
    barrier = pltpu.get_barrier_semaphore()
    for k in range(1, NX):
        pl.semaphore_signal(
            barrier, inc=1, device_id=(lax.rem(x + k, NX), z, y, c), device_id_type=MESH
        )
    pl.semaphore_signal(barrier, inc=1, device_id=(x, z, y, 1 - c), device_id_type=MESH)

    def greet(k, carry):
        t = lax.rem(ctx + k, 16)
        dev = (x, t // 4, lax.rem(t, 4), c)
        pl.semaphore_signal(barrier, inc=1, device_id=dev, device_id_type=MESH)
        return carry

    lax.fori_loop(1, 16, greet, 0)
    pl.semaphore_wait(barrier, NX + 15)

    def along_x(src, dst, ss, rs, t, place):
        return pltpu.make_async_remote_copy(
            src_ref=src.at[t],
            dst_ref=dst.at[place],
            send_sem=ss.at[t],
            recv_sem=rs.at[place],
            device_id=(t, z, y, c),
            device_id_type=MESH,
        )

    def to_sibling(i):
        src, dst = ((dw.at[1 - c], sibling_dw), (gains, sibling_gains))[i]
        return pltpu.make_async_remote_copy(
            src_ref=src,
            dst_ref=dst,
            send_sem=ss_s.at[i],
            recv_sem=rs_s.at[i],
            device_id=(x, z, y, 1 - c),
            device_id_type=MESH,
        )

    def over_ctx(i, t, place):
        src, dst, ss, rs = (
            (reduced.at[t], dw_parts, ss_w, rs_w),
            (gains, gains_all, ss_g, rs_g),
        )[i]
        return pltpu.make_async_remote_copy(
            src_ref=src,
            dst_ref=dst.at[place],
            send_sem=ss.at[t],
            recv_sem=rs.at[place],
            device_id=(x, t // 4, lax.rem(t, 4), c),
            device_id_type=MESH,
        )

    m = low_half((ROWS, 2 * HD))
    mh = low_half((BLK, 2 * HD))
    gq_sum = jnp.zeros((1, 2 * HD), F32)
    gk_sum = jnp.zeros((1, 2 * HD), F32)
    for n, k in enumerate((1, 3, 2, 0)):
        s = lax.rem(x + k, NX)
        at = pl.ds(pl.multiple_of(s * ROWS, ROWS), ROWS)
        place = place_of(x, s) * 4
        cos_s, sin_s = cos_r[at, :], sin_r[at, :]
        part = [recv[place + hh, :ROWS, :].astype(F32) for hh in range(4)]
        vals = [recv[place + hh, ROWS:, :].astype(F32) for hh in range(4)]
        grads = [
            jnp.where(m, part[0], swap(part[1])),
            jnp.where(m, part[2], swap(part[3])),
            jnp.where(m, swap(part[0] + part[1]), part[2] + part[3]),
        ]
        for p in range(3):
            turned = grads[p] * cos_s + swap_halves(grads[p] * sin_s)
            v = raw[at, p * 128 : (p + 1) * 128]
            gain = g_q[...] if p < 2 else g_k[...]
            r = lax.rsqrt(head_mean(v * v) + EPSILON)
            weighted = turned * gain
            grad = r * weighted - v * (r * r * r) * head_mean(weighted * v)
            low[at, p * 128 : (p + 1) * 128] = grad.astype(BF16)
            term = jnp.sum(turned * v * r, axis=0, keepdims=True)
            if p < 2:
                gq_sum = gq_sum + term
            else:
                gk_sum = gk_sum + term
        a, b = vals[0] + vals[1], vals[2] + vals[3]
        grad_v = jnp.concatenate([jnp.where(mh, a, swap(b)), jnp.where(mh, swap(a), b)], 0)
        low[at, 3 * 128 :] = grad_v.astype(BF16)
        grad_h = nt(low[at, :], w[...])
        gh[s] = grad_h.astype(BF16)
        if k:
            along_x(gh, gh_parts, ss_h, rs_h, s, x).start()
        term = jnp.sum(grad_h * h[at, :].astype(F32), axis=0, keepdims=True)
        attn[...] = term if n == 0 else attn[...] + term
    for i in range(8):
        cols = slice(i * 128, i * 128 + 128)
        gains[i : i + 1, :] = attn[:, cols] / g_attn[:, cols]
        gains[8 + i : 9 + i, :] = gain_ffn[:, cols]
    gains[16:, :] = jnp.concatenate([gq_sum, gk_sum, jnp.zeros((6, 2 * HD), F32)], 0)
    grad_w = tn(h[...], low[...]).astype(BF16)
    for i in range(32):
        dw[i % 2, i // 2, :, : QX + 2 * KX] = grad_w[i * 32 : (i + 1) * 32, :]
    grad_w = tn(
        mixed_x[...].reshape(NX * ROWS, QX), branch_x[...].reshape(NX * ROWS, D)
    ).astype(BF16)
    for q in range(4):
        for i in range(8):
            dw[i % 2, q * 4 + i // 2, :, QX + 2 * KX :] = grad_w[
                i * 32 : (i + 1) * 32, q * 256 : (q + 1) * 256
            ]
    to_sibling(0).start()
    to_sibling(1).start()
    for k in (1, 3, 2):
        along_x(result, result_parts, ss_r, rs_r, lax.rem(x + k, NX), x).start()
    to_sibling(1).wait()
    gains[...] = gains[...] + sibling_gains[...]
    to_sibling(0).wait()

    def send(k, carry):
        t = lax.rem(ctx + k, 16)
        reduced[t] = (dw[c, t].astype(F32) + sibling_dw[t].astype(F32)).astype(BF16)
        over_ctx(0, t, ctx).start()
        over_ctx(1, t, ctx).start()
        return carry

    lax.fori_loop(1, 16, send, 0)
    total = dw[c, ctx].astype(F32) + sibling_dw[ctx].astype(F32)
    all_gains = gains[...]

    grad_h = gh[x].astype(F32)
    for k in (1, 3, 2):
        t = lax.rem(x + k, NX)
        along_x(gh, gh_parts, ss_h, rs_h, t, t).wait_recv()
        grad_h = grad_h + gh_parts[t].astype(F32)
    inputs = tokens[...].astype(F32)
    r = lax.rsqrt(jnp.mean(inputs * inputs, axis=-1, keepdims=True) + EPSILON)
    weighted = grad_h * g_attn[...]
    inner = jnp.mean(weighted * inputs, axis=-1, keepdims=True)
    tokens_o[...] = (
        grad_middle[...] + r * weighted - inputs * (r * r * r) * inner
    ).astype(BF16)
    out = middle[...] + result[x].astype(F32)
    for k in (1, 3, 2):
        t = lax.rem(x + k, NX)
        along_x(result, result_parts, ss_r, rs_r, t, t).wait_recv()
        out = out + result_parts[t].astype(F32)
    out_o[...] = out.astype(BF16)

    def collect(k, carry):
        t = lax.rem(ctx + k, 16)
        over_ctx(0, t, t).wait_recv()
        over_ctx(1, t, t).wait_recv()
        return carry[0] + dw_parts[t].astype(F32), carry[1] + gains_all[t]

    total, all_gains = lax.fori_loop(1, 16, collect, (total, all_gains))
    qkv_o[...] = total[:, : QX + 2 * KX].astype(BF16)
    wo_o[...] = total[:, QX + 2 * KX :].astype(BF16)
    gains_o[...] = all_gains

    def drain(k, carry):
        t = lax.rem(ctx + k, 16)
        over_ctx(0, t, ctx).wait_send()
        over_ctx(1, t, ctx).wait_send()
        return carry

    lax.fori_loop(1, 16, drain, 0)
    for k in (1, 3, 2):
        t = lax.rem(x + k, NX)
        along_x(gh, gh_parts, ss_h, rs_h, t, x).wait_send()
        along_x(result, result_parts, ss_r, rs_r, t, x).wait_send()


def project_back(number, *operands):
    vmem = pl.BlockSpec(memory_space=pltpu.VMEM)
    tokens = (NX, ROWS, D)
    wide = QX + 2 * KX + QX
    return pl.pallas_call(
        project_back_kernel,
        in_specs=[vmem] * 16,
        out_specs=[vmem] * 5,
        out_shape=[
            jax.ShapeDtypeStruct((ROWS, D), BF16),
            jax.ShapeDtypeStruct((ROWS, D), BF16),
            jax.ShapeDtypeStruct((32, QX + 2 * KX), BF16),
            jax.ShapeDtypeStruct((32, QX), BF16),
            jax.ShapeDtypeStruct((24, 2 * HD), F32),
        ],
        scratch_shapes=[
            pltpu.VMEM((NX * ROWS, QX + 2 * KX), BF16),
            pltpu.VMEM((1, D), F32),
            pltpu.VMEM(tokens, BF16),
            pltpu.VMEM(tokens, BF16),
            pltpu.VMEM(tokens, BF16),
            pltpu.VMEM((2, 16, 32, wide), BF16),
            pltpu.VMEM((16, 32, wide), BF16),
            pltpu.VMEM((16, 32, wide), BF16),
            pltpu.VMEM((16, 32, wide), BF16),
            pltpu.VMEM((24, 2 * HD), F32),
            pltpu.VMEM((24, 2 * HD), F32),
            pltpu.VMEM((16, 24, 2 * HD), F32),
        ]
        + [pltpu.SemaphoreType.DMA((n,)) for n in (NX, NX, NX, NX, 2, 2, 16, 16, 16, 16)],
        compiler_params=pltpu.CompilerParams(
            collective_id=number, has_side_effects=True, vmem_limit_bytes=VMEM_BYTES
        ),
        name="project_back",
    )(*operands)


def hand_out_kernel(qkv, gu, wo, wd, gains, q_o, k_o, v_o, o_o, g_o, u_o, d_o, ga_o, gf_o, gh_o):
    for s in range(NX):
        q_o[:, s * QX : (s + 1) * QX] = qkv[s, :, :QX].astype(F32)
        k_o[:, s * KX : (s + 1) * KX] = qkv[s, :, QX : QX + KX].astype(F32)
        v_o[:, s * KX : (s + 1) * KX] = qkv[s, :, QX + KX :].astype(F32)
        g_o[:, s * FX : (s + 1) * FX] = gu[s, :, :FX].astype(F32)
        u_o[:, s * FX : (s + 1) * FX] = gu[s, :, FX:].astype(F32)
        o_o[:, s * 256 : (s + 1) * 256] = wo[s, :, :].astype(F32)
        for rg in range(9):
            for l in range(2):
                at = slice(s * 256 + l * 128, s * 256 + l * 128 + 128)
                d_o[rg * 16 : rg * 16 + 16, at] = wd[
                    s, l * 16 : l * 16 + 16, rg * 128 : rg * 128 + 128
                ].astype(F32)
    total = gains[0] + gains[1] + gains[2] + gains[3]
    for i in range(8):
        ga_o[:, i * 128 : i * 128 + 128] = total[i : i + 1, :]
        gf_o[:, i * 128 : i * 128 + 128] = total[8 + i : 9 + i, :]
    gh_o[...] = total[16:, :] + swap(total[16:, :])


def hand_out(*operands):
    vmem = pl.BlockSpec(memory_space=pltpu.VMEM)
    shapes = [(32, D), (32, KV * HD), (32, KV * HD), (32, D), (32, FF), (32, FF), (FF // 32, D)]
    shapes += [(1, D), (1, D), (8, 2 * HD)]
    return pl.pallas_call(
        hand_out_kernel,
        in_specs=[vmem] * 5,
        out_specs=[vmem] * 10,
        out_shape=[jax.ShapeDtypeStruct(s, F32) for s in shapes],
        compiler_params=pltpu.CompilerParams(vmem_limit_bytes=VMEM_BYTES),
        name="hand_out",
    )(*operands)


def angle_constants():
    frequencies = ROPE_BASE ** (-np.arange(0, HD // 2, dtype=np.float64) * 2.0 / HD)
    phases = np.arange(LEN, dtype=np.float64)[:, None] * frequencies[None, :]
    cos, sin = np.cos(phases).astype(np.float32), np.sin(phases).astype(np.float32)
    return np.concatenate([cos] * 4, 1), np.concatenate([-sin, sin, -sin, sin], 1)


def columns_of(w, x, width):
    return lax.dynamic_slice_in_dim(w, x * width, width, axis=1)


def by_tiles(blocks):
    return blocks.reshape(-1, 9, 16, 2, 128).transpose(0, 3, 2, 1, 4).reshape(-1, 32, FX)


def body(
    tokens,
    pairs,
    w_query,
    w_key,
    w_value,
    w_out,
    w_gate,
    w_up,
    w_down,
    g_attn,
    g_query,
    g_key,
    g_ffn,
    cotangent,
):
    x = lax.axis_index("seq")
    cos_np, sin_np = angle_constants()
    cos_t, sin_t = jnp.asarray(cos_np), jnp.asarray(sin_np)
    gq2 = jnp.concatenate([g_query, g_query])[None]
    gk2 = jnp.concatenate([g_key, g_key])[None]

    swap_xz = [(a * 4 + b, b * 4 + a) for a in range(4) for b in range(4)]
    down_part = lax.ppermute(columns_of(w_down, x, D // 4), ("seq", "ctx_0"), swap_xz)
    mine = jnp.concatenate(
        [w_out, columns_of(w_gate, x, FX), columns_of(w_up, x, FX), by_tiles(down_part[None])[0]],
        axis=1,
    )

    wide = lax.all_gather(mine, CTX_FSDP, axis=0, tiled=True)
    h_all, w_qkv, pair = gather_in(1, tokens[0], g_attn[None], w_query, w_key, w_value, pairs)
    h_all = h_all.reshape(NX * ROWS, D)
    w_qkv = w_qkv.reshape(D, QX + 2 * KX)
    pair = pair.reshape(NX * 8, 128)

    send, raw, cos_r, sin_r = project(pair, h_all, w_qkv, cos_t, sin_t, gq2, gk2)
    recv, cot_all = exchange(2, "to_heads", ("c", "a2a", send), ("x", "ag", cotangent[0]))
    heads_out, q_s, k_s, v_s, o_t, inv = attend(pair, recv)
    (mixed_parts,) = exchange(3, "to_tokens", ("t", "a2a", heads_out))
    middle, result4, grad_w_ffn, grad_middle, grad_branch, mixed, back_parts, gain_ffn = middle_part(
        4, mixed_parts, tokens[0], cot_all, g_ffn[None], wide
    )
    sums = lax.psum_scatter(grad_w_ffn, CTX_FSDP, scatter_dimension=0, tiled=True)
    (recv_g,) = exchange(6, "to_heads_back", ("r", "a2a", back_parts))
    sends_back = attend_back(pair, recv_g, q_s, k_s, v_s, o_t, inv)
    recv_back, branch_x, mixed_x = exchange(
        7,
        "to_tokens_back",
        ("c", "a2a", sends_back),
        ("x", "ag", grad_branch),
        ("x", "a2a", mixed),
    )
    output, grad_tokens, sum_qkv, sum_o, gains = project_back(
        8,
        recv_back,
        raw,
        h_all,
        w_qkv,
        cos_r,
        sin_r,
        gq2,
        gk2,
        g_attn[None],
        mixed_x,
        branch_x,
        result4,
        gain_ffn,
        tokens[0],
        grad_middle,
        middle,
    )
    qkv, gate_up, out_rows, down_rows, gains = exchange(
        9,
        "gather_out",
        ("x", "ag", sum_qkv),
        ("x", "ag", sums, (0, 2 * FX)),
        ("d", "ag", sum_o),
        ("d", "ag", sums, (2 * FX, FX)),
        ("x", "ag", gains),
    )
    *weights, gain_a, gain_f, gain_h = hand_out(qkv, gate_up, out_rows, down_rows, gains)
    return (
        output[None],
        grad_tokens[None],
        *weights,
        gain_a[0],
        gain_h[0, :HD],
        gain_h[1, :HD],
        gain_f[0],
    )


def solution(mesh):
    finer = Mesh(
        mesh.devices.reshape(mesh.shape["seq"], 4, 4, mesh.shape["fsdp"]),
        ("seq", "ctx_0", "ctx_1", "fsdp"),
    )
    tokens_spec = P(("seq", "fsdp"), CTX, None)
    rows_spec = P(CTX_FSDP, None)
    return jax.shard_map(
        body,
        mesh=finer,
        in_specs=(tokens_spec, P(("seq", "fsdp"), None))
        + (rows_spec,) * 7
        + (P(),) * 4
        + (tokens_spec,),
        out_specs=(tokens_spec, tokens_spec) + (rows_spec,) * 7 + (P(),) * 4,
        check_vma=False,
    )
```

```python
import functools

import jax
import jax.numpy as jnp
import numpy as np
from jax import lax
from jax.experimental import pallas as pl
from jax.experimental.pallas import tpu as pltpu
from jax.sharding import Mesh
from jax.sharding import PartitionSpec as P

D = 1024
H = 16
KV = 8
HD = 64
FF = 4608
LEN = 2560
BLK = 80
ROWS = 2 * BLK
NX = 4
FX = FF // NX
QX = H * HD // NX
KX = KV * HD // NX
TILE = 512
N_TILES = LEN // TILE
CTX = ("ctx_0", "ctx_1")
CTX_FSDP = ("ctx_0", "ctx_1", "fsdp")
SEQ_CTX_FSDP = ("seq", "ctx_0", "ctx_1", "fsdp")
EPSILON = 1e-05
ROPE_BASE = 1000000.0
MESH = pl.DeviceIdType.MESH
BF16 = jnp.bfloat16
F32 = jnp.float32
VMEM_BYTES = 56 * 1024 * 1024


SIZE = {"x": 4, "c": 16, "p": 32, "t": 16, "r": 16, "d": 4}


def coords():
    return tuple(lax.axis_index(a) for a in SEQ_CTX_FSDP)


def twisted(x, v):
    return lax.rem(v + 2 * (1 - lax.rem(x, 2)) * (1 - lax.rem(v, 2)), 4)


def sequence_at(x, z):
    return lax.rem(x + twisted(x, z), 4)


def place_of(x, s):
    return twisted(x, lax.rem(s - x + 4, 4))


def target(group, t):
    s, z, y, c = coords()
    if group == "x":
        return (t, z, y, c), s
    if group == "c":
        return (s, t // 4, lax.rem(t, 4), c), z * 4 + y
    if group == "p":
        return (s, t // 8, lax.rem(t // 2, 4), lax.rem(t, 2)), (z * 4 + y) * 2 + c
    if group == "t":
        return (sequence_at(s, z), t // 4, lax.rem(t, 4), c), s * 4 + y
    if group == "d":
        return (t, s, y, c), z
    return (t // 4, place_of(t // 4, s), lax.rem(t, 4), c), z * 4 + y


def source(group, t):
    s, z, y, c = coords()
    if group == "t":
        return (t // 4, place_of(t // 4, s), lax.rem(t, 4), c)
    if group == "r":
        return (sequence_at(s, z), t // 4, lax.rem(t, 4), c)
    if group == "d":
        return (z, t, y, c)
    return target(group, t)[0]


def own(group):
    s, z, y, c = coords()
    if group == "t":
        return sequence_at(s, z) == s, z * 4 + y, s * 4 + y
    if group == "r":
        return sequence_at(s, z) == s, s * 4 + y, z * 4 + y
    if group == "d":
        return s == z, s, z
    me = target(group, 0)[1]
    return None, me, me


def exchange_kernel(items, *refs):
    n = len(items)
    srcs, outs, sems = refs[:n], refs[n : 2 * n], refs[2 * n :]
    barrier = pltpu.get_barrier_semaphore()
    expected = 0
    starts = []
    for i, (g, _, _) in enumerate(items):
        has_own, sent, _ = own(g)
        size = SIZE[g]
        if has_own is None:
            starts.append((jnp.int32(1), sent))
            expected = expected + size - 1
        else:
            starts.append((has_own.astype(jnp.int32), sent))
            expected = expected + size - has_own.astype(jnp.int32)
        place = own(g)[2]
        first = starts[i][0]

        def greet(k, carry, g=g, size=size, place=place):
            dev = source(g, lax.rem(place + k, size))
            pl.semaphore_signal(barrier, inc=1, device_id=dev, device_id_type=MESH)
            return carry

        lax.fori_loop(first, size, greet, 0)

    def block_of(i, t):
        _, mode, cols = items[i]
        if cols is not None:
            return srcs[i].at[:, pl.ds(*cols)]
        return srcs[i] if mode == "ag" else srcs[i].at[t]

    def own_copy(i):
        g = items[i][0]
        _, sent, place = own(g)
        src = block_of(i, sent)
        return pltpu.make_async_copy(src, outs[i].at[place], sems[3 * i + 2])

    for i, (g, _, _) in enumerate(items):
        if own(g)[0] is None:
            own_copy(i).start()
        else:
            pl.when(own(g)[0])(lambda i=i: own_copy(i).start())
    pl.semaphore_wait(barrier, expected)

    def remote(i, t, place):
        g = items[i][0]
        dev, there = target(g, t)
        src = block_of(i, t)
        return pltpu.make_async_remote_copy(
            src_ref=src,
            dst_ref=outs[i].at[there if place is None else place],
            send_sem=sems[3 * i].at[t],
            recv_sem=sems[3 * i + 1].at[there if place is None else place],
            device_id=dev,
            device_id_type=MESH,
        )

    for i, (g, _, _) in enumerate(items):
        first, sent = starts[i]

        def send(k, carry, i=i, g=g, sent=sent):
            remote(i, lax.rem(sent + k, SIZE[g]), None).start()
            return carry

        lax.fori_loop(first, SIZE[g], send, 0)
    for i, (g, _, _) in enumerate(items):
        first, sent = starts[i]
        place = own(g)[2]

        def drain(k, carry, i=i, g=g, sent=sent, place=place):
            remote(i, lax.rem(sent + k, SIZE[g]), None).wait_send()
            remote(i, lax.rem(sent + k, SIZE[g]), lax.rem(place + k, SIZE[g])).wait_recv()
            return carry

        lax.fori_loop(first, SIZE[g], drain, 0)
        if own(g)[0] is None:
            own_copy(i).wait()
        else:
            pl.when(own(g)[0])(lambda i=i: own_copy(i).wait())


def exchange(number, name, *parts):
    items = tuple((part[0], part[1], part[3] if len(part) > 3 else None) for part in parts)
    arrays = [part[2] for part in parts]
    outs = []
    for (g, m, cols), a in zip(items, arrays):
        shape = a.shape if m == "ag" else a.shape[1:]
        shape = shape if cols is None else shape[:-1] + (cols[1],)
        outs.append(jax.ShapeDtypeStruct((SIZE[g],) + shape, a.dtype))
    scratch = []
    for g, _, _ in items:
        scratch += [
            pltpu.SemaphoreType.DMA((SIZE[g],)),
            pltpu.SemaphoreType.DMA((SIZE[g],)),
            pltpu.SemaphoreType.DMA,
        ]
    return pl.pallas_call(
        functools.partial(exchange_kernel, items),
        out_shape=outs,
        in_specs=[pl.BlockSpec(memory_space=pl.ANY)] * len(arrays),
        out_specs=[pl.BlockSpec(memory_space=pl.ANY)] * len(arrays),
        scratch_shapes=scratch,
        compiler_params=pltpu.CompilerParams(collective_id=number, has_side_effects=True),
        name=name,
    )(*arrays)


def lanes(shape):
    return lax.broadcasted_iota(jnp.int32, shape, len(shape) - 1)


def low_half(shape):
    return lanes(shape) < HD


def swap(v):
    return pltpu.roll(v, HD, 1)


def swap_halves(v):
    first = lax.rem(lanes(v.shape), HD) < HD // 2
    return jnp.where(first, pltpu.roll(v, 2 * HD - HD // 2, 1), pltpu.roll(v, HD // 2, 1))


def head_mean(v):
    m = low_half(v.shape)
    a = jnp.sum(jnp.where(m, v, 0.0), axis=-1, keepdims=True)
    b = jnp.sum(jnp.where(m, 0.0, v), axis=-1, keepdims=True)
    return jnp.where(m, a, b) * (1.0 / HD)


def nt(a, b):
    return lax.dot_general(a, b, (((1,), (1,)), ((), ())), preferred_element_type=F32)


def nn(a, b):
    return lax.dot_general(a, b, (((1,), (0,)), ((), ())), preferred_element_type=F32)


def tn(a, b):
    return lax.dot_general(a, b, (((0,), (0,)), ((), ())), preferred_element_type=F32)


def my_pairs(pairs):
    x, z, _, _ = coords()
    line = sequence_at(x, z) * 8
    return [pairs[line, j] for j in range(16)]


def rows_of(block):
    return pl.ds(pl.multiple_of(block * BLK, 16), BLK)


def rope_rows(block, table):
    return jnp.concatenate([table[rows_of(block), :], table[rows_of(31 - block), :]], 0)


def gather_in_kernel(
    tokens,
    g_attn,
    w_q,
    w_k,
    w_v,
    pairs,
    h_o,
    w_o,
    pairs_o,
    h,
    w,
    row,
    ss_h,
    rs_h,
    ss_p,
    rs_p,
    ss_w,
    rs_w,
    ss_f,
    rs_f,
    own_sem,
):
    x, z, y, c = coords()
    ctx = z * 4 + y
    barrier = pltpu.get_barrier_semaphore()
    for k in range(1, NX):
        pl.semaphore_signal(
            barrier, inc=1, device_id=(lax.rem(x + k, NX), z, y, c), device_id_type=MESH
        )
    pl.semaphore_signal(barrier, inc=1, device_id=(x, z, y, 1 - c), device_id_type=MESH)

    def greet(k, carry):
        t = lax.rem(ctx + k, 16)
        dev = (x, t // 4, lax.rem(t, 4), c)
        pl.semaphore_signal(barrier, inc=1, device_id=dev, device_id_type=MESH)
        return carry

    lax.fori_loop(1, 16, greet, 0)
    w[:, :QX] = w_q[:, pl.ds(pl.multiple_of(x * QX, QX), QX)]
    w[:, QX : QX + KX] = w_k[:, pl.ds(pl.multiple_of(x * KX, KX), KX)]
    w[:, QX + KX :] = w_v[:, pl.ds(pl.multiple_of(x * KX, KX), KX)]
    row[...] = jnp.zeros_like(row)
    row[0:1, :16] = pairs[...]
    inputs = tokens[...].astype(F32)
    inv_rms = lax.rsqrt(jnp.mean(inputs * inputs, axis=-1, keepdims=True) + EPSILON)
    h[...] = (inputs * inv_rms * g_attn[...]).astype(BF16)

    def along_x(src, dst, ss, rs, t, place):
        return pltpu.make_async_remote_copy(
            src_ref=src,
            dst_ref=dst.at[place],
            send_sem=ss.at[t],
            recv_sem=rs.at[place],
            device_id=(t, z, y, c),
            device_id_type=MESH,
        )

    def over_ctx(t, place):
        return pltpu.make_async_remote_copy(
            src_ref=w,
            dst_ref=w_o.at[place * 2 + c],
            send_sem=ss_w.at[t],
            recv_sem=rs_w.at[place],
            device_id=(x, t // 4, lax.rem(t, 4), c),
            device_id_type=MESH,
        )

    def to_sibling(t, core, src):
        return pltpu.make_async_remote_copy(
            src_ref=src,
            dst_ref=w_o.at[t * 2 + core],
            send_sem=ss_f.at[t],
            recv_sem=rs_f.at[t],
            device_id=(x, z, y, 1 - c),
            device_id_type=MESH,
        )

    mine = [
        pltpu.make_async_copy(h, h_o.at[x], own_sem.at[0]),
        pltpu.make_async_copy(row, pairs_o.at[x], own_sem.at[1]),
        pltpu.make_async_copy(w, w_o.at[ctx * 2 + c], own_sem.at[2]),
    ]
    for copy in mine:
        copy.start()
    pl.semaphore_wait(barrier, NX + 15)
    for k in (1, 3, 2):
        t = lax.rem(x + k, NX)
        along_x(h, h_o, ss_h, rs_h, t, x).start()
        along_x(row, pairs_o, ss_p, rs_p, t, x).start()

    def send(k, carry):
        over_ctx(lax.rem(ctx + k, 16), ctx).start()
        return carry

    lax.fori_loop(1, 16, send, 0)
    to_sibling(ctx, c, w).start()

    def forward(k, carry):
        t = lax.rem(ctx + k, 16)
        over_ctx(t, t).wait_recv()
        to_sibling(t, c, w_o.at[t * 2 + c]).start()
        return carry

    lax.fori_loop(1, 16, forward, 0)

    def drain(k, carry):
        t = lax.rem(ctx + k, 16)
        to_sibling(t, 1 - c, w).wait_recv()
        to_sibling(t, c, w).wait_send()
        return carry

    lax.fori_loop(0, 16, drain, 0)

    def drain_ctx(k, carry):
        over_ctx(lax.rem(ctx + k, 16), ctx).wait_send()
        return carry

    lax.fori_loop(1, 16, drain_ctx, 0)
    for k in (1, 3, 2):
        t = lax.rem(x + k, NX)
        along_x(h, h_o, ss_h, rs_h, t, x).wait_send()
        along_x(row, pairs_o, ss_p, rs_p, t, x).wait_send()
        along_x(h, h_o, ss_h, rs_h, t, t).wait_recv()
        along_x(row, pairs_o, ss_p, rs_p, t, t).wait_recv()
    for copy in mine:
        copy.wait()


def gather_in(number, *operands):
    wide = QX + 2 * KX
    return pl.pallas_call(
        gather_in_kernel,
        in_specs=[pl.BlockSpec(memory_space=pltpu.VMEM)] * 6,
        out_specs=[pl.BlockSpec(memory_space=pl.ANY)] * 3,
        out_shape=[
            jax.ShapeDtypeStruct((NX, ROWS, D), BF16),
            jax.ShapeDtypeStruct((32, 32, wide), BF16),
            jax.ShapeDtypeStruct((NX, 8, 128), jnp.int32),
        ],
        scratch_shapes=[
            pltpu.VMEM((ROWS, D), BF16),
            pltpu.VMEM((32, wide), BF16),
            pltpu.VMEM((8, 128), jnp.int32),
        ]
        + [pltpu.SemaphoreType.DMA((n,)) for n in (NX, NX, NX, NX, 16, 16, 16, 16, 3)],
        compiler_params=pltpu.CompilerParams(collective_id=number, has_side_effects=True),
        name="gather_in",
    )(*operands)


def project_kernel(pairs, h, w, cos_t, sin_t, g_q, g_k, send, raw, cos_o, sin_o, acc):
    x, z, y, _ = coords()
    acc[...] = nn(h[...], w[...])
    m = low_half((ROWS, 2 * HD))
    mh = low_half((BLK, 2 * HD))
    for s in range(NX):
        at = slice(s * ROWS, (s + 1) * ROWS)
        cos_r, sin_r = (rope_rows(pairs[s * 8, z * 4 + y], table) for table in (cos_t, sin_t))
        cos_o[at, :], sin_o[at, :] = cos_r, sin_r
        raw[at, :] = acc[at, : QX + KX]
        turned = []
        for p in range(3):
            v = acc[at, p * 128 : (p + 1) * 128]
            gain = g_q[...] if p < 2 else g_k[...]
            normed = v * lax.rsqrt(head_mean(v * v) + EPSILON) * gain
            turned.append(normed * cos_r + swap_halves(normed) * sin_r)
        keys = turned[2]
        swapped_keys = swap(keys)
        values = acc[at, 3 * 128 :]
        top, bottom = values[:BLK], values[BLK:]
        packed = (jnp.where(mh, top, swap(bottom)), jnp.where(mh, swap(top), bottom))
        for hh in range(4):
            q = turned[hh // 2]
            q = q if hh % 2 == 0 else swap(q)
            k = swapped_keys if hh < 2 else keys
            send[place_of(x, s) * 4 + hh, :ROWS, :] = jnp.where(m, q, k).astype(BF16)
            send[place_of(x, s) * 4 + hh, ROWS:, :] = packed[hh // 2].astype(BF16)


def project(pairs, h, w, cos_t, sin_t, g_q, g_k):
    return pl.pallas_call(
        project_kernel,
        grid_spec=pltpu.PrefetchScalarGridSpec(
            num_scalar_prefetch=1,
            in_specs=[pl.BlockSpec(memory_space=pltpu.VMEM)] * 6,
            out_specs=[pl.BlockSpec(memory_space=pltpu.VMEM)] * 4,
            scratch_shapes=[pltpu.VMEM((NX * ROWS, QX + 2 * KX), F32)],
        ),
        out_shape=[
            jax.ShapeDtypeStruct((16, ROWS + BLK, 2 * HD), BF16),
            jax.ShapeDtypeStruct((NX * ROWS, QX + KX), F32),
            jax.ShapeDtypeStruct((NX * ROWS, 2 * HD), F32),
            jax.ShapeDtypeStruct((NX * ROWS, 2 * HD), F32),
        ],
        compiler_params=pltpu.CompilerParams(vmem_limit_bytes=VMEM_BYTES),
        name="project",
    )(pairs, h, w, cos_t, sin_t, g_q, g_k)


def attend_kernel(pairs, recv, out, q_s, k_s, v_s, o_t, inv, o_s, v_t):
    m = low_half((BLK, 2 * HD))
    pair = my_pairs(pairs)
    for j in range(16):
        packed = recv[j, ROWS:, :].astype(F32)
        for half in range(2):
            block = pair[j] if half == 0 else 31 - pair[j]
            both = recv[j, half * BLK : (half + 1) * BLK, :].astype(F32)
            vals = packed if half == 0 else swap(packed)
            q_s[rows_of(block), :] = jnp.where(m, both * HD**-0.5, 0.0).astype(BF16)
            k_s[rows_of(block), :] = jnp.where(m, swap(both), 0.0).astype(BF16)
            v_s[rows_of(block), :] = jnp.where(m, vals, 0.0).astype(BF16)
    for t in range(N_TILES):
        at = slice(t * TILE, (t + 1) * TILE)
        v_t[:, at] = v_s[at, :].T[:HD]
    causal = lax.broadcasted_iota(jnp.int32, (TILE, TILE), 0) <= lanes((TILE, TILE))
    for i in range(N_TILES):
        at = slice(i * TILE, (i + 1) * TILE)
        q = q_s[at, :]

        e = jnp.where(causal, jnp.exp(nt(k_s[at, :], q)), 0.0)
        first = (jnp.sum(e, axis=0, keepdims=True), nn(v_t[:, at], e.astype(BF16)))

        def step(t, carry, q=q):
            total, acc = carry
            there = pl.ds(pl.multiple_of(t * TILE, TILE), TILE)
            e = jnp.exp(nt(k_s[there, :], q))
            total = total + jnp.sum(e, axis=0, keepdims=True)
            return total, acc + nn(v_t[:, there], e.astype(BF16))

        total, acc = lax.fori_loop(0, i, step, first) if i else first
        over = 1.0 / total
        attended = acc * over
        o_t[:, at] = attended
        inv[:, at] = jnp.broadcast_to(over, (8, TILE))
        o_s[at, :] = jnp.concatenate([attended, jnp.zeros_like(attended)], 0).T
    for j in range(16):
        low_rows = o_s[rows_of(pair[j]), :]
        high_rows = o_s[rows_of(31 - pair[j]), :]
        out[j, :, :] = (low_rows + swap(high_rows)).astype(BF16)


def attend(pairs, recv):
    wide = jax.ShapeDtypeStruct((LEN, 2 * HD), BF16)
    return pl.pallas_call(
        attend_kernel,
        grid_spec=pltpu.PrefetchScalarGridSpec(
            num_scalar_prefetch=1,
            in_specs=[pl.BlockSpec(memory_space=pltpu.VMEM)],
            out_specs=[pl.BlockSpec(memory_space=pltpu.VMEM)] * 6,
            scratch_shapes=[pltpu.VMEM((LEN, 2 * HD), F32), pltpu.VMEM((HD, LEN), BF16)],
        ),
        out_shape=[
            jax.ShapeDtypeStruct((16, BLK, 2 * HD), BF16),
            wide,
            wide,
            wide,
            jax.ShapeDtypeStruct((HD, LEN), F32),
            jax.ShapeDtypeStruct((8, LEN), F32),
        ],
        compiler_params=pltpu.CompilerParams(vmem_limit_bytes=VMEM_BYTES),
        name="attend",
    )(pairs, recv)


def attend_back_kernel(pairs, recv, q_s, k_s, v_s, o_t, inv, out, g_s, k_t, delta, dq_t, dk_s, dv_s):
    m = low_half((BLK, 2 * HD))
    pair = my_pairs(pairs)
    for j in range(16):
        packed = recv[j, :, :].astype(F32)
        g_s[rows_of(pair[j]), :] = jnp.where(m, packed, 0.0).astype(BF16)
        g_s[rows_of(31 - pair[j]), :] = jnp.where(m, swap(packed), 0.0).astype(BF16)
    for t in range(N_TILES):
        at = slice(t * TILE, (t + 1) * TILE)
        k_t[:, at] = k_s[at, :].T[:HD]
        g_t = g_s[at, :].astype(F32).T[:HD]
        row = jnp.sum(g_t * o_t[:, at], axis=0, keepdims=True)
        delta[:, at] = jnp.broadcast_to(row, (8, TILE))
    dq_t[...] = jnp.zeros_like(dq_t)
    causal = lax.broadcasted_iota(jnp.int32, (TILE, TILE), 0) <= lanes((TILE, TILE))
    for i in range(N_TILES):
        at = slice(i * TILE, (i + 1) * TILE)
        k, v, kt = k_s[at, :], v_s[at, :], k_t[:, at]

        def pair_of_tiles(there, masked, k=k, v=v, kt=kt):
            q, g = q_s[there, :], g_s[there, :]
            e = jnp.exp(nt(k, q))
            if masked:
                e = jnp.where(causal, e, 0.0)
            probs = e * inv[0:1, there]
            ds = (probs * (nt(v, g) - delta[0:1, there])).astype(BF16)
            dq_t[:, there] = dq_t[:, there] + nn(kt, ds)
            return nn(ds, q), nn(probs.astype(BF16), g)

        first = pair_of_tiles(at, True)

        def step(t, carry, pair_of_tiles=pair_of_tiles):
            dk, dv = pair_of_tiles(pl.ds(pl.multiple_of(t * TILE, TILE), TILE), False)
            return carry[0] + dk, carry[1] + dv

        dk, dv = lax.fori_loop(i + 1, N_TILES, step, first) if i + 1 < N_TILES else first
        dk_s[at, :] = dk
        dv_s[at, :] = dv
    for i in range(N_TILES):
        at = slice(i * TILE, (i + 1) * TILE)
        dq = dq_t[:, at] * HD**-0.5
        dk_s[at, :] = jnp.concatenate([dq, jnp.zeros_like(dq)], 0).T + swap(dk_s[at, :])
    for j in range(16):
        for half in range(2):
            block = pair[j] if half == 0 else 31 - pair[j]
            out[j, half * BLK : (half + 1) * BLK, :] = dk_s[rows_of(block), :].astype(BF16)
        out[j, ROWS:, :] = (dv_s[rows_of(pair[j]), :] + swap(dv_s[rows_of(31 - pair[j]), :])).astype(BF16)


def attend_back(pairs, recv, q_s, k_s, v_s, o_t, inv):
    return pl.pallas_call(
        attend_back_kernel,
        grid_spec=pltpu.PrefetchScalarGridSpec(
            num_scalar_prefetch=1,
            in_specs=[pl.BlockSpec(memory_space=pltpu.VMEM)] * 6,
            out_specs=pl.BlockSpec(memory_space=pltpu.VMEM),
            scratch_shapes=[
                pltpu.VMEM((LEN, 2 * HD), BF16),
                pltpu.VMEM((HD, LEN), BF16),
                pltpu.VMEM((8, LEN), F32),
                pltpu.VMEM((HD, LEN), F32),
                pltpu.VMEM((LEN, 2 * HD), F32),
                pltpu.VMEM((LEN, 2 * HD), F32),
            ],
        ),
        out_shape=jax.ShapeDtypeStruct((16, ROWS + BLK, 2 * HD), BF16),
        compiler_params=pltpu.CompilerParams(vmem_limit_bytes=VMEM_BYTES),
        name="attend_back",
    )(pairs, recv, q_s, k_s, v_s, o_t, inv)


def middle_kernel(
    parts,
    tokens,
    cot,
    g_ffn,
    wide,
    mid_o,
    result_o,
    dw_o,
    gmid_o,
    branch_o,
    mixed_o,
    back_o,
    gain_o,
    w_o,
    w_gu,
    dnp,
    w_dn,
    h_all,
    part,
    gparts,
    gu_s,
    dh_s,
    ggu,
    hid,
    h_t,
    hid_t,
    dw,
    sibling_dw,
    wsem,
    ss1,
    rs1,
    ss2,
    rs2,
    ss3,
    rs3,
):
    me, z, y, c = coords()
    barrier = pltpu.get_barrier_semaphore()
    for k in range(1, NX):
        pl.semaphore_signal(
            barrier, inc=1, device_id=(lax.rem(me + k, NX), z, y, c), device_id_type=MESH
        )
    pl.semaphore_signal(barrier, inc=1, device_id=(me, z, y, 1 - c), device_id_type=MESH)
    loads = [
        pltpu.make_async_copy(wide.at[:, pl.ds(at, width)], there, wsem.at[i])
        for i, (at, width, there) in enumerate(
            ((0, D, w_o), (D, 2 * FX, w_gu), (D + 2 * FX, FX, dnp))
        )
    ]
    for load in loads:
        load.start()
    m = low_half((BLK, 2 * HD))
    for p in range(8):
        a, b = parts[2 * p, :, :].astype(F32), parts[2 * p + 1, :, :].astype(F32)
        at = slice((p % 2) * 128, (p % 2) * 128 + 128)
        mixed_o[p // 2, :BLK, at] = jnp.where(m, a, swap(b)).astype(BF16)
        mixed_o[p // 2, BLK:, at] = jnp.where(m, swap(a), b).astype(BF16)
    loads[0].wait()
    middle = tokens[...].astype(F32)
    for q in range(NX):
        middle = middle + nn(mixed_o[q, :, :], w_o[q * QX : (q + 1) * QX, :])
    mid_o[...] = middle
    r = lax.rsqrt(jnp.mean(middle * middle, axis=-1, keepdims=True) + EPSILON)
    h_all[me] = (middle * r * g_ffn[...]).astype(BF16)
    pl.semaphore_wait(barrier, NX)

    def send_h(t, place):
        return pltpu.make_async_remote_copy(
            src_ref=h_all.at[me],
            dst_ref=h_all.at[place],
            send_sem=ss1.at[t],
            recv_sem=rs1.at[place],
            device_id=(t, z, y, c),
            device_id_type=MESH,
        )

    def send_grad(t, place):
        return pltpu.make_async_remote_copy(
            src_ref=part.at[t],
            dst_ref=gparts.at[place],
            send_sem=ss2.at[t],
            recv_sem=rs2.at[place],
            device_id=(t, z, y, c),
            device_id_type=MESH,
        )

    for k in (1, 3, 2):
        send_h(lax.rem(me + k, NX), me).start()
    loads[1].wait()
    loads[2].wait()
    for o in range(32):
        for rg in range(9):
            for l in range(2):
                row = (o % 8) * 144 + rg * 16
                w_dn[o // 8, row : row + 16, l * 128 : l * 128 + 128] = dnp[
                    o * 32 + l * 16 : o * 32 + l * 16 + 16, rg * 128 : rg * 128 + 128
                ]

    def block(k, carry):
        t = lax.rem(me + k + k // 2 - 2 * (k // 2) * lax.rem(k, 2), NX)

        @pl.when(k > 0)
        def _():
            send_h(t, t).wait_recv()

        rows = pl.ds(pl.multiple_of(t * ROWS, ROWS), ROWS)
        gu_s[...] = nn(h_all[t], w_gu[...])
        cot_t = cot[t]
        grad_hidden = nt(cot_t[:, :256], w_dn[0])
        for q in range(1, NX):
            grad_hidden = grad_hidden + nt(cot_t[:, q * 256 : (q + 1) * 256], w_dn[q])
        dh_s[...] = grad_hidden
        for j in range(FX // 128):
            at, above = slice(j * 128, j * 128 + 128), slice(FX + j * 128, FX + j * 128 + 128)
            gate, up, dh = gu_s[:, at], gu_s[:, above], dh_s[:, at]
            sig = jax.nn.sigmoid(gate)
            silu = gate * sig
            hid[rows, at] = (silu * up).astype(BF16)
            ggu[rows, at] = (dh * up * (sig * (1.0 + gate * (1.0 - sig)))).astype(BF16)
            ggu[rows, above] = (dh * silu).astype(BF16)
        part[t] = nt(ggu[rows, :], w_gu[...]).astype(BF16)

        @pl.when(k > 0)
        def _():
            send_grad(t, me).start()

        hidden = hid[rows, :]
        for q in range(NX):
            result_o[t, :, q * 256 : (q + 1) * 256] = nn(hidden, w_dn[q]).astype(BF16)
        return carry

    lax.fori_loop(0, NX, block, 0)

    def to_sibling(i, at):
        return pltpu.make_async_remote_copy(
            src_ref=dw.at[pl.ds(pl.multiple_of((1 - c) * 512, 512), 512), at],
            dst_ref=sibling_dw.at[:, at],
            send_sem=ss3.at[i],
            recv_sem=rs3.at[i],
            device_id=(me, z, y, 1 - c),
            device_id_type=MESH,
        )

    down = pl.ds(2 * FX, FX)
    hid_t[...] = hid[...].T
    for q in range(NX):
        cot_q = cot[:, :, q * 256 : (q + 1) * 256].reshape(NX * ROWS, 256)
        grad = nn(hid_t[...], cot_q).astype(BF16)
        for o in range(8):
            for rg in range(9):
                for l in range(2):
                    row = o * 144 + rg * 16
                    there = ((o % 2) * 16 + (o // 2) * 4 + q) * 32 + l * 16
                    dw[there : there + 16, 2 * FX + rg * 128 : 2 * FX + rg * 128 + 128] = grad[
                        row : row + 16, l * 128 : l * 128 + 128
                    ]
    to_sibling(9, down).start()
    h_rows = h_all[...].reshape(NX * ROWS, D).T
    for o in range(32):
        there = ((o % 2) * 16 + (o // 2 % 4) * 4 + o // 8) * 32
        h_t[there : there + 32, :] = h_rows[o * 32 : o * 32 + 32, :]

    def chunk(j):
        return pl.ds(pl.multiple_of(j * 256, 256), 256)

    def columns(j, carry):
        dw[:, chunk(j)] = nn(h_t[...], ggu[:, chunk(j)]).astype(BF16)
        to_sibling(j, chunk(j)).start()
        return carry

    lax.fori_loop(0, 2 * FX // 256, columns, 0)

    grad_h = part[me].astype(F32)
    for k in (1, 3, 2):
        t = lax.rem(me + k, NX)
        send_grad(t, t).wait_recv()
        grad_h = grad_h + gparts[t].astype(F32)
    for k in (1, 3, 2):
        t = lax.rem(me + k, NX)
        send_h(t, me).wait_send()
        send_grad(t, me).wait_send()
    middle = mid_o[...]
    r = lax.rsqrt(jnp.mean(middle * middle, axis=-1, keepdims=True) + EPSILON)
    weighted = grad_h * g_ffn[...]
    inner = jnp.mean(weighted * middle, axis=-1, keepdims=True)
    gain_o[...] = jnp.sum(grad_h * middle * r, axis=0, keepdims=True)
    grad_middle = cot[me].astype(F32) + r * weighted - middle * (r * r * r) * inner
    gmid_o[...] = grad_middle
    branch_o[...] = grad_middle.astype(BF16)
    for q in range(NX):
        grad = nt(branch_o[...], w_o[q * QX : (q + 1) * QX, :]).astype(BF16).astype(F32)
        for p in range(2):
            top, bottom = grad[:BLK, p * 128 : p * 128 + 128], grad[BLK:, p * 128 : p * 128 + 128]
            back_o[4 * q + 2 * p, :, :] = jnp.where(m, top, swap(bottom)).astype(BF16)
            back_o[4 * q + 2 * p + 1, :, :] = jnp.where(m, swap(top), bottom).astype(BF16)
    half = pl.ds(pl.multiple_of(c * 512, 512), 512)

    def both(at):
        dw_o[:, at] = (dw[half, at].astype(F32) + sibling_dw[:, at].astype(F32)).astype(BF16)

    to_sibling(9, down).wait()
    both(down)

    def add(j, carry):
        to_sibling(j, chunk(j)).wait()
        both(chunk(j))
        return carry

    lax.fori_loop(0, 2 * FX // 256, add, 0)


def middle_part(number, parts, tokens, cot, g_ffn, wide):
    vmem = pl.BlockSpec(memory_space=pltpu.VMEM)
    blocks = (NX, ROWS, D)
    return pl.pallas_call(
        middle_kernel,
        in_specs=[vmem] * 4 + [pl.BlockSpec(memory_space=pl.ANY)],
        out_specs=[vmem] * 8,
        out_shape=[
            jax.ShapeDtypeStruct((ROWS, D), F32),
            jax.ShapeDtypeStruct(blocks, BF16),
            jax.ShapeDtypeStruct((D // 2, 3 * FX), BF16),
            jax.ShapeDtypeStruct((ROWS, D), F32),
            jax.ShapeDtypeStruct((ROWS, D), BF16),
            jax.ShapeDtypeStruct((NX, ROWS, QX), BF16),
            jax.ShapeDtypeStruct((16, BLK, 2 * HD), BF16),
            jax.ShapeDtypeStruct((1, D), F32),
        ],
        scratch_shapes=[
            pltpu.VMEM((D, D), BF16),
            pltpu.VMEM((D, 2 * FX), BF16),
            pltpu.VMEM((D, FX), BF16),
            pltpu.VMEM((4, FX, D // 4), BF16),
            pltpu.VMEM(blocks, BF16),
            pltpu.VMEM(blocks, BF16),
            pltpu.VMEM(blocks, BF16),
            pltpu.VMEM((ROWS, 2 * FX), F32),
            pltpu.VMEM((ROWS, FX), F32),
            pltpu.VMEM((NX * ROWS, 2 * FX), BF16),
            pltpu.VMEM((NX * ROWS, FX), BF16),
            pltpu.VMEM((D, NX * ROWS), BF16),
            pltpu.VMEM((FX, NX * ROWS), BF16),
            pltpu.VMEM((D, 3 * FX), BF16),
            pltpu.VMEM((D // 2, 3 * FX), BF16),
            pltpu.SemaphoreType.DMA((3,)),
            pltpu.SemaphoreType.DMA((NX,)),
            pltpu.SemaphoreType.DMA((NX,)),
            pltpu.SemaphoreType.DMA((NX,)),
            pltpu.SemaphoreType.DMA((NX,)),
            pltpu.SemaphoreType.DMA((10,)),
            pltpu.SemaphoreType.DMA((10,)),
        ],
        compiler_params=pltpu.CompilerParams(
            collective_id=number, has_side_effects=True, vmem_limit_bytes=VMEM_BYTES
        ),
        name="middle_part",
    )(parts, tokens, cot, g_ffn, wide)


def project_back_kernel(
    recv,
    raw,
    h,
    w,
    cos_r,
    sin_r,
    g_q,
    g_k,
    g_attn,
    mixed_x,
    branch_x,
    result,
    gain_ffn,
    tokens,
    grad_middle,
    middle,
    out_o,
    tokens_o,
    qkv_o,
    wo_o,
    gains_o,
    low,
    attn,
    gh,
    gh_parts,
    result_parts,
    dw,
    sibling_dw,
    reduced,
    dw_parts,
    gains,
    sibling_gains,
    gains_all,
    ss_r,
    rs_r,
    ss_h,
    rs_h,
    ss_s,
    rs_s,
    ss_w,
    rs_w,
    ss_g,
    rs_g,
):
    x, z, y, c = coords()
    ctx = z * 4 + y
    barrier = pltpu.get_barrier_semaphore()
    for k in range(1, NX):
        pl.semaphore_signal(
            barrier, inc=1, device_id=(lax.rem(x + k, NX), z, y, c), device_id_type=MESH
        )
    pl.semaphore_signal(barrier, inc=1, device_id=(x, z, y, 1 - c), device_id_type=MESH)

    def greet(k, carry):
        t = lax.rem(ctx + k, 16)
        dev = (x, t // 4, lax.rem(t, 4), c)
        pl.semaphore_signal(barrier, inc=1, device_id=dev, device_id_type=MESH)
        return carry

    lax.fori_loop(1, 16, greet, 0)
    pl.semaphore_wait(barrier, NX + 15)

    def along_x(src, dst, ss, rs, t, place):
        return pltpu.make_async_remote_copy(
            src_ref=src.at[t],
            dst_ref=dst.at[place],
            send_sem=ss.at[t],
            recv_sem=rs.at[place],
            device_id=(t, z, y, c),
            device_id_type=MESH,
        )

    def to_sibling(i):
        src, dst = ((dw.at[1 - c], sibling_dw), (gains, sibling_gains))[i]
        return pltpu.make_async_remote_copy(
            src_ref=src,
            dst_ref=dst,
            send_sem=ss_s.at[i],
            recv_sem=rs_s.at[i],
            device_id=(x, z, y, 1 - c),
            device_id_type=MESH,
        )

    def over_ctx(i, t, place):
        src, dst, ss, rs = (
            (reduced.at[t], dw_parts, ss_w, rs_w),
            (gains, gains_all, ss_g, rs_g),
        )[i]
        return pltpu.make_async_remote_copy(
            src_ref=src,
            dst_ref=dst.at[place],
            send_sem=ss.at[t],
            recv_sem=rs.at[place],
            device_id=(x, t // 4, lax.rem(t, 4), c),
            device_id_type=MESH,
        )

    m = low_half((ROWS, 2 * HD))
    mh = low_half((BLK, 2 * HD))
    gq_sum = jnp.zeros((1, 2 * HD), F32)
    gk_sum = jnp.zeros((1, 2 * HD), F32)
    for n, k in enumerate((1, 3, 2, 0)):
        s = lax.rem(x + k, NX)
        at = pl.ds(pl.multiple_of(s * ROWS, ROWS), ROWS)
        place = place_of(x, s) * 4
        cos_s, sin_s = cos_r[at, :], sin_r[at, :]
        part = [recv[place + hh, :ROWS, :].astype(F32) for hh in range(4)]
        vals = [recv[place + hh, ROWS:, :].astype(F32) for hh in range(4)]
        grads = [
            jnp.where(m, part[0], swap(part[1])),
            jnp.where(m, part[2], swap(part[3])),
            jnp.where(m, swap(part[0] + part[1]), part[2] + part[3]),
        ]
        for p in range(3):
            turned = grads[p] * cos_s + swap_halves(grads[p] * sin_s)
            v = raw[at, p * 128 : (p + 1) * 128]
            gain = g_q[...] if p < 2 else g_k[...]
            r = lax.rsqrt(head_mean(v * v) + EPSILON)
            weighted = turned * gain
            grad = r * weighted - v * (r * r * r) * head_mean(weighted * v)
            low[at, p * 128 : (p + 1) * 128] = grad.astype(BF16)
            term = jnp.sum(turned * v * r, axis=0, keepdims=True)
            if p < 2:
                gq_sum = gq_sum + term
            else:
                gk_sum = gk_sum + term
        a, b = vals[0] + vals[1], vals[2] + vals[3]
        grad_v = jnp.concatenate([jnp.where(mh, a, swap(b)), jnp.where(mh, swap(a), b)], 0)
        low[at, 3 * 128 :] = grad_v.astype(BF16)
        grad_h = nt(low[at, :], w[...])
        gh[s] = grad_h.astype(BF16)
        if k:
            along_x(gh, gh_parts, ss_h, rs_h, s, x).start()
        term = jnp.sum(grad_h * h[at, :].astype(F32), axis=0, keepdims=True)
        attn[...] = term if n == 0 else attn[...] + term
    for i in range(8):
        cols = slice(i * 128, i * 128 + 128)
        gains[i : i + 1, :] = attn[:, cols] / g_attn[:, cols]
        gains[8 + i : 9 + i, :] = gain_ffn[:, cols]
    gains[16:, :] = jnp.concatenate([gq_sum, gk_sum, jnp.zeros((6, 2 * HD), F32)], 0)
    grad_w = tn(h[...], low[...]).astype(BF16)
    for i in range(32):
        dw[i % 2, i // 2, :, : QX + 2 * KX] = grad_w[i * 32 : (i + 1) * 32, :]
    grad_w = tn(
        mixed_x[...].reshape(NX * ROWS, QX), branch_x[...].reshape(NX * ROWS, D)
    ).astype(BF16)
    for q in range(4):
        for i in range(8):
            dw[i % 2, q * 4 + i // 2, :, QX + 2 * KX :] = grad_w[
                i * 32 : (i + 1) * 32, q * 256 : (q + 1) * 256
            ]
    to_sibling(0).start()
    to_sibling(1).start()
    for k in (1, 3, 2):
        along_x(result, result_parts, ss_r, rs_r, lax.rem(x + k, NX), x).start()
    to_sibling(1).wait()
    gains[...] = gains[...] + sibling_gains[...]
    to_sibling(0).wait()

    def send(k, carry):
        t = lax.rem(ctx + k, 16)
        reduced[t] = (dw[c, t].astype(F32) + sibling_dw[t].astype(F32)).astype(BF16)
        over_ctx(0, t, ctx).start()
        over_ctx(1, t, ctx).start()
        return carry

    lax.fori_loop(1, 16, send, 0)
    total = dw[c, ctx].astype(F32) + sibling_dw[ctx].astype(F32)
    all_gains = gains[...]

    grad_h = gh[x].astype(F32)
    for k in (1, 3, 2):
        t = lax.rem(x + k, NX)
        along_x(gh, gh_parts, ss_h, rs_h, t, t).wait_recv()
        grad_h = grad_h + gh_parts[t].astype(F32)
    inputs = tokens[...].astype(F32)
    r = lax.rsqrt(jnp.mean(inputs * inputs, axis=-1, keepdims=True) + EPSILON)
    weighted = grad_h * g_attn[...]
    inner = jnp.mean(weighted * inputs, axis=-1, keepdims=True)
    tokens_o[...] = (
        grad_middle[...] + r * weighted - inputs * (r * r * r) * inner
    ).astype(BF16)
    out = middle[...] + result[x].astype(F32)
    for k in (1, 3, 2):
        t = lax.rem(x + k, NX)
        along_x(result, result_parts, ss_r, rs_r, t, t).wait_recv()
        out = out + result_parts[t].astype(F32)
    out_o[...] = out.astype(BF16)

    def collect(k, carry):
        t = lax.rem(ctx + k, 16)
        over_ctx(0, t, t).wait_recv()
        over_ctx(1, t, t).wait_recv()
        return carry[0] + dw_parts[t].astype(F32), carry[1] + gains_all[t]

    total, all_gains = lax.fori_loop(1, 16, collect, (total, all_gains))
    qkv_o[...] = total[:, : QX + 2 * KX].astype(BF16)
    wo_o[...] = total[:, QX + 2 * KX :].astype(BF16)
    gains_o[...] = all_gains

    def drain(k, carry):
        t = lax.rem(ctx + k, 16)
        over_ctx(0, t, ctx).wait_send()
        over_ctx(1, t, ctx).wait_send()
        return carry

    lax.fori_loop(1, 16, drain, 0)
    for k in (1, 3, 2):
        t = lax.rem(x + k, NX)
        along_x(gh, gh_parts, ss_h, rs_h, t, x).wait_send()
        along_x(result, result_parts, ss_r, rs_r, t, x).wait_send()


def project_back(number, *operands):
    vmem = pl.BlockSpec(memory_space=pltpu.VMEM)
    tokens = (NX, ROWS, D)
    wide = QX + 2 * KX + QX
    return pl.pallas_call(
        project_back_kernel,
        in_specs=[vmem] * 16,
        out_specs=[vmem] * 5,
        out_shape=[
            jax.ShapeDtypeStruct((ROWS, D), BF16),
            jax.ShapeDtypeStruct((ROWS, D), BF16),
            jax.ShapeDtypeStruct((32, QX + 2 * KX), BF16),
            jax.ShapeDtypeStruct((32, QX), BF16),
            jax.ShapeDtypeStruct((24, 2 * HD), F32),
        ],
        scratch_shapes=[
            pltpu.VMEM((NX * ROWS, QX + 2 * KX), BF16),
            pltpu.VMEM((1, D), F32),
            pltpu.VMEM(tokens, BF16),
            pltpu.VMEM(tokens, BF16),
            pltpu.VMEM(tokens, BF16),
            pltpu.VMEM((2, 16, 32, wide), BF16),
            pltpu.VMEM((16, 32, wide), BF16),
            pltpu.VMEM((16, 32, wide), BF16),
            pltpu.VMEM((16, 32, wide), BF16),
            pltpu.VMEM((24, 2 * HD), F32),
            pltpu.VMEM((24, 2 * HD), F32),
            pltpu.VMEM((16, 24, 2 * HD), F32),
        ]
        + [pltpu.SemaphoreType.DMA((n,)) for n in (NX, NX, NX, NX, 2, 2, 16, 16, 16, 16)],
        compiler_params=pltpu.CompilerParams(
            collective_id=number, has_side_effects=True, vmem_limit_bytes=VMEM_BYTES
        ),
        name="project_back",
    )(*operands)


def hand_out_kernel(qkv, gu, wo, wd, gains, q_o, k_o, v_o, o_o, g_o, u_o, d_o, ga_o, gf_o, gh_o):
    for s in range(NX):
        q_o[:, s * QX : (s + 1) * QX] = qkv[s, :, :QX].astype(F32)
        k_o[:, s * KX : (s + 1) * KX] = qkv[s, :, QX : QX + KX].astype(F32)
        v_o[:, s * KX : (s + 1) * KX] = qkv[s, :, QX + KX :].astype(F32)
        g_o[:, s * FX : (s + 1) * FX] = gu[s, :, :FX].astype(F32)
        u_o[:, s * FX : (s + 1) * FX] = gu[s, :, FX:].astype(F32)
        o_o[:, s * 256 : (s + 1) * 256] = wo[s, :, :].astype(F32)
        for rg in range(9):
            for l in range(2):
                at = slice(s * 256 + l * 128, s * 256 + l * 128 + 128)
                d_o[rg * 16 : rg * 16 + 16, at] = wd[
                    s, l * 16 : l * 16 + 16, rg * 128 : rg * 128 + 128
                ].astype(F32)
    total = gains[0] + gains[1] + gains[2] + gains[3]
    for i in range(8):
        ga_o[:, i * 128 : i * 128 + 128] = total[i : i + 1, :]
        gf_o[:, i * 128 : i * 128 + 128] = total[8 + i : 9 + i, :]
    gh_o[...] = total[16:, :] + swap(total[16:, :])


def hand_out(*operands):
    vmem = pl.BlockSpec(memory_space=pltpu.VMEM)
    shapes = [(32, D), (32, KV * HD), (32, KV * HD), (32, D), (32, FF), (32, FF), (FF // 32, D)]
    shapes += [(1, D), (1, D), (8, 2 * HD)]
    return pl.pallas_call(
        hand_out_kernel,
        in_specs=[vmem] * 5,
        out_specs=[vmem] * 10,
        out_shape=[jax.ShapeDtypeStruct(s, F32) for s in shapes],
        compiler_params=pltpu.CompilerParams(vmem_limit_bytes=VMEM_BYTES),
        name="hand_out",
    )(*operands)


def angle_constants():
    frequencies = ROPE_BASE ** (-np.arange(0, HD // 2, dtype=np.float64) * 2.0 / HD)
    phases = np.arange(LEN, dtype=np.float64)[:, None] * frequencies[None, :]
    cos, sin = np.cos(phases).astype(np.float32), np.sin(phases).astype(np.float32)
    return np.concatenate([cos] * 4, 1), np.concatenate([-sin, sin, -sin, sin], 1)


def columns_of(w, x, width):
    return lax.dynamic_slice_in_dim(w, x * width, width, axis=1)


def by_tiles(blocks):
    return blocks.reshape(-1, 9, 16, 2, 128).transpose(0, 3, 2, 1, 4).reshape(-1, 32, FX)


def body(
    tokens,
    pairs,
    w_query,
    w_key,
    w_value,
    w_out,
    w_gate,
    w_up,
    w_down,
    g_attn,
    g_query,
    g_key,
    g_ffn,
    cotangent,
):
    x = lax.axis_index("seq")
    cos_np, sin_np = angle_constants()
    cos_t, sin_t = jnp.asarray(cos_np), jnp.asarray(sin_np)
    gq2 = jnp.concatenate([g_query, g_query])[None]
    gk2 = jnp.concatenate([g_key, g_key])[None]

    swap_xz = [(a * 4 + b, b * 4 + a) for a in range(4) for b in range(4)]
    down_part = lax.ppermute(columns_of(w_down, x, D // 4), ("seq", "ctx_0"), swap_xz)
    mine = jnp.concatenate(
        [w_out, columns_of(w_gate, x, FX), columns_of(w_up, x, FX), by_tiles(down_part[None])[0]],
        axis=1,
    )

    wide = lax.all_gather(mine, CTX_FSDP, axis=0, tiled=True)
    h_all, w_qkv, pair = gather_in(1, tokens[0], g_attn[None], w_query, w_key, w_value, pairs)
    h_all = h_all.reshape(NX * ROWS, D)
    w_qkv = w_qkv.reshape(D, QX + 2 * KX)
    pair = pair.reshape(NX * 8, 128)

    send, raw, cos_r, sin_r = project(pair, h_all, w_qkv, cos_t, sin_t, gq2, gk2)
    recv, cot_all = exchange(2, "to_heads", ("c", "a2a", send), ("x", "ag", cotangent[0]))
    heads_out, q_s, k_s, v_s, o_t, inv = attend(pair, recv)
    (mixed_parts,) = exchange(3, "to_tokens", ("t", "a2a", heads_out))
    middle, result4, grad_w_ffn, grad_middle, grad_branch, mixed, back_parts, gain_ffn = middle_part(
        4, mixed_parts, tokens[0], cot_all, g_ffn[None], wide
    )
    sums = lax.psum_scatter(grad_w_ffn, "ctx_1", scatter_dimension=0, tiled=True)
    sums = lax.psum_scatter(sums, "ctx_0", scatter_dimension=0, tiled=True)
    (recv_g,) = exchange(6, "to_heads_back", ("r", "a2a", back_parts))
    sends_back = attend_back(pair, recv_g, q_s, k_s, v_s, o_t, inv)
    recv_back, branch_x, mixed_x = exchange(
        7,
        "to_tokens_back",
        ("c", "a2a", sends_back),
        ("x", "ag", grad_branch),
        ("x", "a2a", mixed),
    )
    output, grad_tokens, sum_qkv, sum_o, gains = project_back(
        8,
        recv_back,
        raw,
        h_all,
        w_qkv,
        cos_r,
        sin_r,
        gq2,
        gk2,
        g_attn[None],
        mixed_x,
        branch_x,
        result4,
        gain_ffn,
        tokens[0],
        grad_middle,
        middle,
    )
    qkv, gate_up, out_rows, down_rows, gains = exchange(
        9,
        "gather_out",
        ("x", "ag", sum_qkv),
        ("x", "ag", sums, (0, 2 * FX)),
        ("d", "ag", sum_o),
        ("d", "ag", sums, (2 * FX, FX)),
        ("x", "ag", gains),
    )
    *weights, gain_a, gain_f, gain_h = hand_out(qkv, gate_up, out_rows, down_rows, gains)
    return (
        output[None],
        grad_tokens[None],
        *weights,
        gain_a[0],
        gain_h[0, :HD],
        gain_h[1, :HD],
        gain_f[0],
    )


def solution(mesh):
    finer = Mesh(
        mesh.devices.reshape(mesh.shape["seq"], 4, 4, mesh.shape["fsdp"]),
        ("seq", "ctx_0", "ctx_1", "fsdp"),
    )
    tokens_spec = P(("seq", "fsdp"), CTX, None)
    rows_spec = P(CTX_FSDP, None)
    return jax.shard_map(
        body,
        mesh=finer,
        in_specs=(tokens_spec, P(("seq", "fsdp"), None))
        + (rows_spec,) * 7
        + (P(),) * 4
        + (tokens_spec,),
        out_specs=(tokens_spec, tokens_spec) + (rows_spec,) * 7 + (P(),) * 4,
        check_vma=False,
    )
```

```python
import functools

import jax
import jax.numpy as jnp
import numpy as np
from jax import lax
from jax.experimental import pallas as pl
from jax.experimental.pallas import tpu as pltpu
from jax.sharding import Mesh
from jax.sharding import PartitionSpec as P

D = 1024
H = 16
KV = 8
HD = 64
FF = 4608
LEN = 2560
BLK = 80
ROWS = 2 * BLK
NX = 4
FX = FF // NX
QX = H * HD // NX
KX = KV * HD // NX
TILE = 512
N_TILES = LEN // TILE
CTX = ("ctx_0", "ctx_1")
CTX_FSDP = ("ctx_0", "ctx_1", "fsdp")
SEQ_CTX_FSDP = ("seq", "ctx_0", "ctx_1", "fsdp")
EPSILON = 1e-05
ROPE_BASE = 1000000.0
MESH = pl.DeviceIdType.MESH
BF16 = jnp.bfloat16
F32 = jnp.float32
VMEM_BYTES = 56 * 1024 * 1024


SIZE = {"x": 4, "c": 16, "p": 32, "t": 16, "r": 16, "d": 4}


def coords():
    return tuple(lax.axis_index(a) for a in SEQ_CTX_FSDP)


def twisted(x, v):
    return lax.rem(v + 2 * (1 - lax.rem(x, 2)) * (1 - lax.rem(v, 2)), 4)


def sequence_at(x, z):
    return lax.rem(x + twisted(x, z), 4)


def place_of(x, s):
    return twisted(x, lax.rem(s - x + 4, 4))


def target(group, t):
    s, z, y, c = coords()
    if group == "x":
        return (t, z, y, c), s
    if group == "c":
        return (s, t // 4, lax.rem(t, 4), c), z * 4 + y
    if group == "p":
        return (s, t // 8, lax.rem(t // 2, 4), lax.rem(t, 2)), (z * 4 + y) * 2 + c
    if group == "t":
        return (sequence_at(s, z), t // 4, lax.rem(t, 4), c), s * 4 + y
    if group == "d":
        return (t, s, y, c), z
    return (t // 4, place_of(t // 4, s), lax.rem(t, 4), c), z * 4 + y


def source(group, t):
    s, z, y, c = coords()
    if group == "t":
        return (t // 4, place_of(t // 4, s), lax.rem(t, 4), c)
    if group == "r":
        return (sequence_at(s, z), t // 4, lax.rem(t, 4), c)
    if group == "d":
        return (z, t, y, c)
    return target(group, t)[0]


def own(group):
    s, z, y, c = coords()
    if group == "t":
        return sequence_at(s, z) == s, z * 4 + y, s * 4 + y
    if group == "r":
        return sequence_at(s, z) == s, s * 4 + y, z * 4 + y
    if group == "d":
        return s == z, s, z
    me = target(group, 0)[1]
    return None, me, me


def exchange_kernel(items, *refs):
    n = len(items)
    srcs, outs, sems = refs[:n], refs[n : 2 * n], refs[2 * n :]
    barrier = pltpu.get_barrier_semaphore()
    expected = 0
    starts = []
    for i, (g, _, _) in enumerate(items):
        has_own, sent, _ = own(g)
        size = SIZE[g]
        if has_own is None:
            starts.append((jnp.int32(1), sent))
            expected = expected + size - 1
        else:
            starts.append((has_own.astype(jnp.int32), sent))
            expected = expected + size - has_own.astype(jnp.int32)
        place = own(g)[2]
        first = starts[i][0]

        def greet(k, carry, g=g, size=size, place=place):
            dev = source(g, lax.rem(place + k, size))
            pl.semaphore_signal(barrier, inc=1, device_id=dev, device_id_type=MESH)
            return carry

        lax.fori_loop(first, size, greet, 0)

    def block_of(i, t):
        _, mode, cols = items[i]
        if cols is not None:
            return srcs[i].at[:, pl.ds(*cols)]
        return srcs[i] if mode == "ag" else srcs[i].at[t]

    def own_copy(i):
        g = items[i][0]
        _, sent, place = own(g)
        src = block_of(i, sent)
        return pltpu.make_async_copy(src, outs[i].at[place], sems[3 * i + 2])

    for i, (g, _, _) in enumerate(items):
        if own(g)[0] is None:
            own_copy(i).start()
        else:
            pl.when(own(g)[0])(lambda i=i: own_copy(i).start())
    pl.semaphore_wait(barrier, expected)

    def remote(i, t, place):
        g = items[i][0]
        dev, there = target(g, t)
        src = block_of(i, t)
        return pltpu.make_async_remote_copy(
            src_ref=src,
            dst_ref=outs[i].at[there if place is None else place],
            send_sem=sems[3 * i].at[t],
            recv_sem=sems[3 * i + 1].at[there if place is None else place],
            device_id=dev,
            device_id_type=MESH,
        )

    for i, (g, _, _) in enumerate(items):
        first, sent = starts[i]

        def send(k, carry, i=i, g=g, sent=sent):
            remote(i, lax.rem(sent + k, SIZE[g]), None).start()
            return carry

        lax.fori_loop(first, SIZE[g], send, 0)
    for i, (g, _, _) in enumerate(items):
        first, sent = starts[i]
        place = own(g)[2]

        def drain(k, carry, i=i, g=g, sent=sent, place=place):
            remote(i, lax.rem(sent + k, SIZE[g]), None).wait_send()
            remote(i, lax.rem(sent + k, SIZE[g]), lax.rem(place + k, SIZE[g])).wait_recv()
            return carry

        lax.fori_loop(first, SIZE[g], drain, 0)
        if own(g)[0] is None:
            own_copy(i).wait()
        else:
            pl.when(own(g)[0])(lambda i=i: own_copy(i).wait())


def exchange(number, name, *parts):
    items = tuple((part[0], part[1], part[3] if len(part) > 3 else None) for part in parts)
    arrays = [part[2] for part in parts]
    outs = []
    for (g, m, cols), a in zip(items, arrays):
        shape = a.shape if m == "ag" else a.shape[1:]
        shape = shape if cols is None else shape[:-1] + (cols[1],)
        outs.append(jax.ShapeDtypeStruct((SIZE[g],) + shape, a.dtype))
    scratch = []
    for g, _, _ in items:
        scratch += [
            pltpu.SemaphoreType.DMA((SIZE[g],)),
            pltpu.SemaphoreType.DMA((SIZE[g],)),
            pltpu.SemaphoreType.DMA,
        ]
    return pl.pallas_call(
        functools.partial(exchange_kernel, items),
        out_shape=outs,
        in_specs=[pl.BlockSpec(memory_space=pl.ANY)] * len(arrays),
        out_specs=[pl.BlockSpec(memory_space=pl.ANY)] * len(arrays),
        scratch_shapes=scratch,
        compiler_params=pltpu.CompilerParams(collective_id=number, has_side_effects=True),
        name=name,
    )(*arrays)


def lanes(shape):
    return lax.broadcasted_iota(jnp.int32, shape, len(shape) - 1)


def low_half(shape):
    return lanes(shape) < HD


def swap(v):
    return pltpu.roll(v, HD, 1)


def swap_halves(v):
    first = lax.rem(lanes(v.shape), HD) < HD // 2
    return jnp.where(first, pltpu.roll(v, 2 * HD - HD // 2, 1), pltpu.roll(v, HD // 2, 1))


def head_mean(v):
    m = low_half(v.shape)
    a = jnp.sum(jnp.where(m, v, 0.0), axis=-1, keepdims=True)
    b = jnp.sum(jnp.where(m, 0.0, v), axis=-1, keepdims=True)
    return jnp.where(m, a, b) * (1.0 / HD)


def nt(a, b):
    return lax.dot_general(a, b, (((1,), (1,)), ((), ())), preferred_element_type=F32)


def nn(a, b):
    return lax.dot_general(a, b, (((1,), (0,)), ((), ())), preferred_element_type=F32)


def tn(a, b):
    return lax.dot_general(a, b, (((0,), (0,)), ((), ())), preferred_element_type=F32)


def my_pairs(pairs):
    x, z, _, _ = coords()
    line = sequence_at(x, z) * 8
    return [pairs[line, j] for j in range(16)]


def rows_of(block):
    return pl.ds(pl.multiple_of(block * BLK, 16), BLK)


def rope_rows(block, table):
    return jnp.concatenate([table[rows_of(block), :], table[rows_of(31 - block), :]], 0)


def gather_in_kernel(
    tokens,
    g_attn,
    w_q,
    w_k,
    w_v,
    pairs,
    h_o,
    w_o,
    pairs_o,
    h,
    w,
    row,
    ss_h,
    rs_h,
    ss_p,
    rs_p,
    ss_w,
    rs_w,
    ss_f,
    rs_f,
    own_sem,
):
    x, z, y, c = coords()
    ctx = z * 4 + y
    barrier = pltpu.get_barrier_semaphore()
    for k in range(1, NX):
        pl.semaphore_signal(
            barrier, inc=1, device_id=(lax.rem(x + k, NX), z, y, c), device_id_type=MESH
        )
    pl.semaphore_signal(barrier, inc=1, device_id=(x, z, y, 1 - c), device_id_type=MESH)

    def greet(k, carry):
        t = lax.rem(ctx + k, 16)
        dev = (x, t // 4, lax.rem(t, 4), c)
        pl.semaphore_signal(barrier, inc=1, device_id=dev, device_id_type=MESH)
        return carry

    lax.fori_loop(1, 16, greet, 0)
    w[:, :QX] = w_q[:, pl.ds(pl.multiple_of(x * QX, QX), QX)]
    w[:, QX : QX + KX] = w_k[:, pl.ds(pl.multiple_of(x * KX, KX), KX)]
    w[:, QX + KX :] = w_v[:, pl.ds(pl.multiple_of(x * KX, KX), KX)]
    row[...] = jnp.zeros_like(row)
    row[0:1, :16] = pairs[...]
    inputs = tokens[...].astype(F32)
    inv_rms = lax.rsqrt(jnp.mean(inputs * inputs, axis=-1, keepdims=True) + EPSILON)
    h[...] = (inputs * inv_rms * g_attn[...]).astype(BF16)

    def along_x(src, dst, ss, rs, t, place):
        return pltpu.make_async_remote_copy(
            src_ref=src,
            dst_ref=dst.at[place],
            send_sem=ss.at[t],
            recv_sem=rs.at[place],
            device_id=(t, z, y, c),
            device_id_type=MESH,
        )

    def over_ctx(t, place):
        return pltpu.make_async_remote_copy(
            src_ref=w,
            dst_ref=w_o.at[place * 2 + c],
            send_sem=ss_w.at[t],
            recv_sem=rs_w.at[place],
            device_id=(x, t // 4, lax.rem(t, 4), c),
            device_id_type=MESH,
        )

    def to_sibling(t, core, src):
        return pltpu.make_async_remote_copy(
            src_ref=src,
            dst_ref=w_o.at[t * 2 + core],
            send_sem=ss_f.at[t],
            recv_sem=rs_f.at[t],
            device_id=(x, z, y, 1 - c),
            device_id_type=MESH,
        )

    mine = [
        pltpu.make_async_copy(h, h_o.at[x], own_sem.at[0]),
        pltpu.make_async_copy(row, pairs_o.at[x], own_sem.at[1]),
        pltpu.make_async_copy(w, w_o.at[ctx * 2 + c], own_sem.at[2]),
    ]
    for copy in mine:
        copy.start()
    pl.semaphore_wait(barrier, NX + 15)
    for k in (1, 3, 2):
        t = lax.rem(x + k, NX)
        along_x(h, h_o, ss_h, rs_h, t, x).start()
        along_x(row, pairs_o, ss_p, rs_p, t, x).start()

    def send(k, carry):
        over_ctx(lax.rem(ctx + k, 16), ctx).start()
        return carry

    lax.fori_loop(1, 16, send, 0)
    to_sibling(ctx, c, w).start()

    def forward(k, carry):
        t = lax.rem(ctx + k, 16)
        over_ctx(t, t).wait_recv()
        to_sibling(t, c, w_o.at[t * 2 + c]).start()
        return carry

    lax.fori_loop(1, 16, forward, 0)

    def drain(k, carry):
        t = lax.rem(ctx + k, 16)
        to_sibling(t, 1 - c, w).wait_recv()
        to_sibling(t, c, w).wait_send()
        return carry

    lax.fori_loop(0, 16, drain, 0)

    def drain_ctx(k, carry):
        over_ctx(lax.rem(ctx + k, 16), ctx).wait_send()
        return carry

    lax.fori_loop(1, 16, drain_ctx, 0)
    for k in (1, 3, 2):
        t = lax.rem(x + k, NX)
        along_x(h, h_o, ss_h, rs_h, t, x).wait_send()
        along_x(row, pairs_o, ss_p, rs_p, t, x).wait_send()
        along_x(h, h_o, ss_h, rs_h, t, t).wait_recv()
        along_x(row, pairs_o, ss_p, rs_p, t, t).wait_recv()
    for copy in mine:
        copy.wait()


def gather_in(number, *operands):
    wide = QX + 2 * KX
    return pl.pallas_call(
        gather_in_kernel,
        in_specs=[pl.BlockSpec(memory_space=pltpu.VMEM)] * 6,
        out_specs=[pl.BlockSpec(memory_space=pl.ANY)] * 3,
        out_shape=[
            jax.ShapeDtypeStruct((NX, ROWS, D), BF16),
            jax.ShapeDtypeStruct((32, 32, wide), BF16),
            jax.ShapeDtypeStruct((NX, 8, 128), jnp.int32),
        ],
        scratch_shapes=[
            pltpu.VMEM((ROWS, D), BF16),
            pltpu.VMEM((32, wide), BF16),
            pltpu.VMEM((8, 128), jnp.int32),
        ]
        + [pltpu.SemaphoreType.DMA((n,)) for n in (NX, NX, NX, NX, 16, 16, 16, 16, 3)],
        compiler_params=pltpu.CompilerParams(collective_id=number, has_side_effects=True),
        name="gather_in",
    )(*operands)


def project_kernel(pairs, h, w, cos_t, sin_t, g_q, g_k, send, raw, cos_o, sin_o, acc):
    x, z, y, _ = coords()
    acc[...] = nn(h[...], w[...])
    m = low_half((ROWS, 2 * HD))
    mh = low_half((BLK, 2 * HD))
    for s in range(NX):
        at = slice(s * ROWS, (s + 1) * ROWS)
        cos_r, sin_r = (rope_rows(pairs[s * 8, z * 4 + y], table) for table in (cos_t, sin_t))
        cos_o[at, :], sin_o[at, :] = cos_r, sin_r
        raw[at, :] = acc[at, : QX + KX]
        turned = []
        for p in range(3):
            v = acc[at, p * 128 : (p + 1) * 128]
            gain = g_q[...] if p < 2 else g_k[...]
            normed = v * lax.rsqrt(head_mean(v * v) + EPSILON) * gain
            turned.append(normed * cos_r + swap_halves(normed) * sin_r)
        keys = turned[2]
        swapped_keys = swap(keys)
        values = acc[at, 3 * 128 :]
        top, bottom = values[:BLK], values[BLK:]
        packed = (jnp.where(mh, top, swap(bottom)), jnp.where(mh, swap(top), bottom))
        for hh in range(4):
            q = turned[hh // 2]
            q = q if hh % 2 == 0 else swap(q)
            k = swapped_keys if hh < 2 else keys
            send[place_of(x, s) * 4 + hh, :ROWS, :] = jnp.where(m, q, k).astype(BF16)
            send[place_of(x, s) * 4 + hh, ROWS:, :] = packed[hh // 2].astype(BF16)


def project(pairs, h, w, cos_t, sin_t, g_q, g_k):
    return pl.pallas_call(
        project_kernel,
        grid_spec=pltpu.PrefetchScalarGridSpec(
            num_scalar_prefetch=1,
            in_specs=[pl.BlockSpec(memory_space=pltpu.VMEM)] * 6,
            out_specs=[pl.BlockSpec(memory_space=pltpu.VMEM)] * 4,
            scratch_shapes=[pltpu.VMEM((NX * ROWS, QX + 2 * KX), F32)],
        ),
        out_shape=[
            jax.ShapeDtypeStruct((16, ROWS + BLK, 2 * HD), BF16),
            jax.ShapeDtypeStruct((NX * ROWS, QX + KX), F32),
            jax.ShapeDtypeStruct((NX * ROWS, 2 * HD), F32),
            jax.ShapeDtypeStruct((NX * ROWS, 2 * HD), F32),
        ],
        compiler_params=pltpu.CompilerParams(vmem_limit_bytes=VMEM_BYTES),
        name="project",
    )(pairs, h, w, cos_t, sin_t, g_q, g_k)


def attend_kernel(pairs, recv, out, q_s, k_s, v_s, o_t, inv, o_s, v_t):
    m = low_half((BLK, 2 * HD))
    pair = my_pairs(pairs)
    for j in range(16):
        packed = recv[j, ROWS:, :].astype(F32)
        for half in range(2):
            block = pair[j] if half == 0 else 31 - pair[j]
            both = recv[j, half * BLK : (half + 1) * BLK, :].astype(F32)
            vals = packed if half == 0 else swap(packed)
            q_s[rows_of(block), :] = jnp.where(m, both * HD**-0.5, 0.0).astype(BF16)
            k_s[rows_of(block), :] = jnp.where(m, swap(both), 0.0).astype(BF16)
            v_s[rows_of(block), :] = jnp.where(m, vals, 0.0).astype(BF16)
    for t in range(N_TILES):
        at = slice(t * TILE, (t + 1) * TILE)
        v_t[:, at] = v_s[at, :].T[:HD]
    causal = lax.broadcasted_iota(jnp.int32, (TILE, TILE), 0) <= lanes((TILE, TILE))
    for i in range(N_TILES):
        at = slice(i * TILE, (i + 1) * TILE)
        q = q_s[at, :]

        e = jnp.where(causal, jnp.exp(nt(k_s[at, :], q)), 0.0)
        first = (jnp.sum(e, axis=0, keepdims=True), nn(v_t[:, at], e.astype(BF16)))

        def step(t, carry, q=q):
            total, acc = carry
            there = pl.ds(pl.multiple_of(t * TILE, TILE), TILE)
            e = jnp.exp(nt(k_s[there, :], q))
            total = total + jnp.sum(e, axis=0, keepdims=True)
            return total, acc + nn(v_t[:, there], e.astype(BF16))

        total, acc = lax.fori_loop(0, i, step, first) if i else first
        over = 1.0 / total
        attended = acc * over
        o_t[:, at] = attended
        inv[:, at] = jnp.broadcast_to(over, (8, TILE))
        o_s[at, :] = jnp.concatenate([attended, jnp.zeros_like(attended)], 0).T
    for j in range(16):
        low_rows = o_s[rows_of(pair[j]), :]
        high_rows = o_s[rows_of(31 - pair[j]), :]
        out[j, :, :] = (low_rows + swap(high_rows)).astype(BF16)


def attend(pairs, recv):
    wide = jax.ShapeDtypeStruct((LEN, 2 * HD), BF16)
    return pl.pallas_call(
        attend_kernel,
        grid_spec=pltpu.PrefetchScalarGridSpec(
            num_scalar_prefetch=1,
            in_specs=[pl.BlockSpec(memory_space=pltpu.VMEM)],
            out_specs=[pl.BlockSpec(memory_space=pltpu.VMEM)] * 6,
            scratch_shapes=[pltpu.VMEM((LEN, 2 * HD), F32), pltpu.VMEM((HD, LEN), BF16)],
        ),
        out_shape=[
            jax.ShapeDtypeStruct((16, BLK, 2 * HD), BF16),
            wide,
            wide,
            wide,
            jax.ShapeDtypeStruct((HD, LEN), F32),
            jax.ShapeDtypeStruct((8, LEN), F32),
        ],
        compiler_params=pltpu.CompilerParams(vmem_limit_bytes=VMEM_BYTES),
        name="attend",
    )(pairs, recv)


def attend_back_kernel(pairs, recv, q_s, k_s, v_s, o_t, inv, out, g_s, k_t, delta, dq_t, dk_s, dv_s):
    m = low_half((BLK, 2 * HD))
    pair = my_pairs(pairs)
    for j in range(16):
        packed = recv[j, :, :].astype(F32)
        g_s[rows_of(pair[j]), :] = jnp.where(m, packed, 0.0).astype(BF16)
        g_s[rows_of(31 - pair[j]), :] = jnp.where(m, swap(packed), 0.0).astype(BF16)
    for t in range(N_TILES):
        at = slice(t * TILE, (t + 1) * TILE)
        k_t[:, at] = k_s[at, :].T[:HD]
        g_t = g_s[at, :].astype(F32).T[:HD]
        row = jnp.sum(g_t * o_t[:, at], axis=0, keepdims=True)
        delta[:, at] = jnp.broadcast_to(row, (8, TILE))
    dq_t[...] = jnp.zeros_like(dq_t)
    causal = lax.broadcasted_iota(jnp.int32, (TILE, TILE), 0) <= lanes((TILE, TILE))
    for i in range(N_TILES):
        at = slice(i * TILE, (i + 1) * TILE)
        k, v, kt = k_s[at, :], v_s[at, :], k_t[:, at]

        def pair_of_tiles(there, masked, k=k, v=v, kt=kt):
            q, g = q_s[there, :], g_s[there, :]
            e = jnp.exp(nt(k, q))
            if masked:
                e = jnp.where(causal, e, 0.0)
            probs = e * inv[0:1, there]
            ds = (probs * (nt(v, g) - delta[0:1, there])).astype(BF16)
            dq_t[:, there] = dq_t[:, there] + nn(kt, ds)
            return nn(ds, q), nn(probs.astype(BF16), g)

        first = pair_of_tiles(at, True)

        def step(t, carry, pair_of_tiles=pair_of_tiles):
            dk, dv = pair_of_tiles(pl.ds(pl.multiple_of(t * TILE, TILE), TILE), False)
            return carry[0] + dk, carry[1] + dv

        dk, dv = lax.fori_loop(i + 1, N_TILES, step, first) if i + 1 < N_TILES else first
        dk_s[at, :] = dk
        dv_s[at, :] = dv
    for i in range(N_TILES):
        at = slice(i * TILE, (i + 1) * TILE)
        dq = dq_t[:, at] * HD**-0.5
        dk_s[at, :] = jnp.concatenate([dq, jnp.zeros_like(dq)], 0).T + swap(dk_s[at, :])
    for j in range(16):
        for half in range(2):
            block = pair[j] if half == 0 else 31 - pair[j]
            out[j, half * BLK : (half + 1) * BLK, :] = dk_s[rows_of(block), :].astype(BF16)
        out[j, ROWS:, :] = (dv_s[rows_of(pair[j]), :] + swap(dv_s[rows_of(31 - pair[j]), :])).astype(BF16)


def attend_back(pairs, recv, q_s, k_s, v_s, o_t, inv):
    return pl.pallas_call(
        attend_back_kernel,
        grid_spec=pltpu.PrefetchScalarGridSpec(
            num_scalar_prefetch=1,
            in_specs=[pl.BlockSpec(memory_space=pltpu.VMEM)] * 6,
            out_specs=pl.BlockSpec(memory_space=pltpu.VMEM),
            scratch_shapes=[
                pltpu.VMEM((LEN, 2 * HD), BF16),
                pltpu.VMEM((HD, LEN), BF16),
                pltpu.VMEM((8, LEN), F32),
                pltpu.VMEM((HD, LEN), F32),
                pltpu.VMEM((LEN, 2 * HD), F32),
                pltpu.VMEM((LEN, 2 * HD), F32),
            ],
        ),
        out_shape=jax.ShapeDtypeStruct((16, ROWS + BLK, 2 * HD), BF16),
        compiler_params=pltpu.CompilerParams(vmem_limit_bytes=VMEM_BYTES),
        name="attend_back",
    )(pairs, recv, q_s, k_s, v_s, o_t, inv)


def middle_kernel(
    parts,
    tokens,
    cot,
    g_ffn,
    wide,
    mid_o,
    result_o,
    dw_o,
    gmid_o,
    branch_o,
    mixed_o,
    back_o,
    gain_o,
    w_o,
    w_gu,
    dnp,
    w_dn,
    h_all,
    part,
    gparts,
    gu_s,
    dh_s,
    ggu,
    hid,
    h_t,
    hid_t,
    dw,
    sibling_dw,
    wsem,
    ss1,
    rs1,
    ss2,
    rs2,
    ss3,
    rs3,
):
    me, z, y, c = coords()
    barrier = pltpu.get_barrier_semaphore()
    for k in range(1, NX):
        pl.semaphore_signal(
            barrier, inc=1, device_id=(lax.rem(me + k, NX), z, y, c), device_id_type=MESH
        )
    pl.semaphore_signal(barrier, inc=1, device_id=(me, z, y, 1 - c), device_id_type=MESH)
    loads = [
        pltpu.make_async_copy(wide.at[:, pl.ds(at, width)], there, wsem.at[i])
        for i, (at, width, there) in enumerate(
            ((0, D, w_o), (D, 2 * FX, w_gu), (D + 2 * FX, FX, dnp))
        )
    ]
    for load in loads:
        load.start()
    m = low_half((BLK, 2 * HD))
    for p in range(8):
        a, b = parts[2 * p, :, :].astype(F32), parts[2 * p + 1, :, :].astype(F32)
        at = slice((p % 2) * 128, (p % 2) * 128 + 128)
        mixed_o[p // 2, :BLK, at] = jnp.where(m, a, swap(b)).astype(BF16)
        mixed_o[p // 2, BLK:, at] = jnp.where(m, swap(a), b).astype(BF16)
    loads[0].wait()
    middle = tokens[...].astype(F32)
    for q in range(NX):
        middle = middle + nn(mixed_o[q, :, :], w_o[q * QX : (q + 1) * QX, :])
    mid_o[...] = middle
    r = lax.rsqrt(jnp.mean(middle * middle, axis=-1, keepdims=True) + EPSILON)
    h_all[me] = (middle * r * g_ffn[...]).astype(BF16)
    pl.semaphore_wait(barrier, NX)

    def send_h(t, place):
        return pltpu.make_async_remote_copy(
            src_ref=h_all.at[me],
            dst_ref=h_all.at[place],
            send_sem=ss1.at[t],
            recv_sem=rs1.at[place],
            device_id=(t, z, y, c),
            device_id_type=MESH,
        )

    def send_grad(t, place):
        return pltpu.make_async_remote_copy(
            src_ref=part.at[t],
            dst_ref=gparts.at[place],
            send_sem=ss2.at[t],
            recv_sem=rs2.at[place],
            device_id=(t, z, y, c),
            device_id_type=MESH,
        )

    for k in (1, 3, 2):
        send_h(lax.rem(me + k, NX), me).start()
    loads[1].wait()
    loads[2].wait()
    for o in range(32):
        for rg in range(9):
            for l in range(2):
                row = (o % 8) * 144 + rg * 16
                w_dn[o // 8, row : row + 16, l * 128 : l * 128 + 128] = dnp[
                    o * 32 + l * 16 : o * 32 + l * 16 + 16, rg * 128 : rg * 128 + 128
                ]

    def block(k, carry):
        t = lax.rem(me + k + k // 2 - 2 * (k // 2) * lax.rem(k, 2), NX)

        @pl.when(k > 0)
        def _():
            send_h(t, t).wait_recv()

        rows = pl.ds(pl.multiple_of(t * ROWS, ROWS), ROWS)
        gu_s[...] = nn(h_all[t], w_gu[...])
        cot_t = cot[t]
        grad_hidden = nt(cot_t[:, :256], w_dn[0])
        for q in range(1, NX):
            grad_hidden = grad_hidden + nt(cot_t[:, q * 256 : (q + 1) * 256], w_dn[q])
        dh_s[...] = grad_hidden
        for j in range(FX // 128):
            at, above = slice(j * 128, j * 128 + 128), slice(FX + j * 128, FX + j * 128 + 128)
            gate, up, dh = gu_s[:, at], gu_s[:, above], dh_s[:, at]
            sig = jax.nn.sigmoid(gate)
            silu = gate * sig
            hid[rows, at] = (silu * up).astype(BF16)
            ggu[rows, at] = (dh * up * (sig * (1.0 + gate * (1.0 - sig)))).astype(BF16)
            ggu[rows, above] = (dh * silu).astype(BF16)
        part[t] = nt(ggu[rows, :], w_gu[...]).astype(BF16)

        @pl.when(k > 0)
        def _():
            send_grad(t, me).start()

        hidden = hid[rows, :]
        for q in range(NX):
            result_o[t, :, q * 256 : (q + 1) * 256] = nn(hidden, w_dn[q]).astype(BF16)
        return carry

    lax.fori_loop(0, NX, block, 0)

    def to_sibling(i, at):
        return pltpu.make_async_remote_copy(
            src_ref=dw.at[pl.ds(pl.multiple_of((1 - c) * 512, 512), 512), at],
            dst_ref=sibling_dw.at[:, at],
            send_sem=ss3.at[i],
            recv_sem=rs3.at[i],
            device_id=(me, z, y, 1 - c),
            device_id_type=MESH,
        )

    down = pl.ds(2 * FX, FX)
    hid_t[...] = hid[...].T
    for q in range(NX):
        cot_q = cot[:, :, q * 256 : (q + 1) * 256].reshape(NX * ROWS, 256)
        grad = nn(hid_t[...], cot_q).astype(BF16)
        for o in range(8):
            for rg in range(9):
                for l in range(2):
                    row = o * 144 + rg * 16
                    there = ((o % 2) * 16 + (o // 2) * 4 + q) * 32 + l * 16
                    dw[there : there + 16, 2 * FX + rg * 128 : 2 * FX + rg * 128 + 128] = grad[
                        row : row + 16, l * 128 : l * 128 + 128
                    ]
    to_sibling(9, down).start()
    h_rows = h_all[...].reshape(NX * ROWS, D).T
    for o in range(32):
        there = ((o % 2) * 16 + (o // 2 % 4) * 4 + o // 8) * 32
        h_t[there : there + 32, :] = h_rows[o * 32 : o * 32 + 32, :]

    def chunk(j):
        return pl.ds(pl.multiple_of(j * 256, 256), 256)

    def columns(j, carry):
        dw[:, chunk(j)] = nn(h_t[...], ggu[:, chunk(j)]).astype(BF16)
        to_sibling(j, chunk(j)).start()
        return carry

    lax.fori_loop(0, 2 * FX // 256, columns, 0)

    grad_h = part[me].astype(F32)
    for k in (1, 3, 2):
        t = lax.rem(me + k, NX)
        send_grad(t, t).wait_recv()
        grad_h = grad_h + gparts[t].astype(F32)
    for k in (1, 3, 2):
        t = lax.rem(me + k, NX)
        send_h(t, me).wait_send()
        send_grad(t, me).wait_send()
    middle = mid_o[...]
    r = lax.rsqrt(jnp.mean(middle * middle, axis=-1, keepdims=True) + EPSILON)
    weighted = grad_h * g_ffn[...]
    inner = jnp.mean(weighted * middle, axis=-1, keepdims=True)
    gain_o[...] = jnp.sum(grad_h * middle * r, axis=0, keepdims=True)
    grad_middle = cot[me].astype(F32) + r * weighted - middle * (r * r * r) * inner
    gmid_o[...] = grad_middle
    branch_o[...] = grad_middle.astype(BF16)
    for q in range(NX):
        grad = nt(branch_o[...], w_o[q * QX : (q + 1) * QX, :]).astype(BF16).astype(F32)
        for p in range(2):
            top, bottom = grad[:BLK, p * 128 : p * 128 + 128], grad[BLK:, p * 128 : p * 128 + 128]
            back_o[4 * q + 2 * p, :, :] = jnp.where(m, top, swap(bottom)).astype(BF16)
            back_o[4 * q + 2 * p + 1, :, :] = jnp.where(m, swap(top), bottom).astype(BF16)
    half = pl.ds(pl.multiple_of(c * 512, 512), 512)

    def both(at):
        dw_o[:, at] = (dw[half, at].astype(F32) + sibling_dw[:, at].astype(F32)).astype(BF16)

    to_sibling(9, down).wait()
    both(down)

    def add(j, carry):
        to_sibling(j, chunk(j)).wait()
        both(chunk(j))
        return carry

    lax.fori_loop(0, 2 * FX // 256, add, 0)


def middle_part(number, parts, tokens, cot, g_ffn, wide):
    vmem = pl.BlockSpec(memory_space=pltpu.VMEM)
    blocks = (NX, ROWS, D)
    return pl.pallas_call(
        middle_kernel,
        in_specs=[vmem] * 4 + [pl.BlockSpec(memory_space=pl.ANY)],
        out_specs=[vmem] * 8,
        out_shape=[
            jax.ShapeDtypeStruct((ROWS, D), F32),
            jax.ShapeDtypeStruct(blocks, BF16),
            jax.ShapeDtypeStruct((D // 2, 3 * FX), BF16),
            jax.ShapeDtypeStruct((ROWS, D), F32),
            jax.ShapeDtypeStruct((ROWS, D), BF16),
            jax.ShapeDtypeStruct((NX, ROWS, QX), BF16),
            jax.ShapeDtypeStruct((16, BLK, 2 * HD), BF16),
            jax.ShapeDtypeStruct((1, D), F32),
        ],
        scratch_shapes=[
            pltpu.VMEM((D, D), BF16),
            pltpu.VMEM((D, 2 * FX), BF16),
            pltpu.VMEM((D, FX), BF16),
            pltpu.VMEM((4, FX, D // 4), BF16),
            pltpu.VMEM(blocks, BF16),
            pltpu.VMEM(blocks, BF16),
            pltpu.VMEM(blocks, BF16),
            pltpu.VMEM((ROWS, 2 * FX), F32),
            pltpu.VMEM((ROWS, FX), F32),
            pltpu.VMEM((NX * ROWS, 2 * FX), BF16),
            pltpu.VMEM((NX * ROWS, FX), BF16),
            pltpu.VMEM((D, NX * ROWS), BF16),
            pltpu.VMEM((FX, NX * ROWS), BF16),
            pltpu.VMEM((D, 3 * FX), BF16),
            pltpu.VMEM((D // 2, 3 * FX), BF16),
            pltpu.SemaphoreType.DMA((3,)),
            pltpu.SemaphoreType.DMA((NX,)),
            pltpu.SemaphoreType.DMA((NX,)),
            pltpu.SemaphoreType.DMA((NX,)),
            pltpu.SemaphoreType.DMA((NX,)),
            pltpu.SemaphoreType.DMA((10,)),
            pltpu.SemaphoreType.DMA((10,)),
        ],
        compiler_params=pltpu.CompilerParams(
            collective_id=number, has_side_effects=True, vmem_limit_bytes=VMEM_BYTES
        ),
        name="middle_part",
    )(parts, tokens, cot, g_ffn, wide)


def project_back_kernel(
    recv,
    raw,
    h,
    w,
    cos_r,
    sin_r,
    g_q,
    g_k,
    g_attn,
    mixed_x,
    branch_x,
    result,
    gain_ffn,
    tokens,
    grad_middle,
    middle,
    out_o,
    tokens_o,
    qkv_o,
    wo_o,
    gains_o,
    low,
    attn,
    gh,
    gh_parts,
    result_parts,
    dw,
    sibling_dw,
    reduced,
    dw_parts,
    gains,
    sibling_gains,
    gains_all,
    ss_r,
    rs_r,
    ss_h,
    rs_h,
    ss_s,
    rs_s,
    ss_w,
    rs_w,
    ss_g,
    rs_g,
):
    x, z, y, c = coords()
    ctx = z * 4 + y
    barrier = pltpu.get_barrier_semaphore()
    for k in range(1, NX):
        pl.semaphore_signal(
            barrier, inc=1, device_id=(lax.rem(x + k, NX), z, y, c), device_id_type=MESH
        )
    pl.semaphore_signal(barrier, inc=1, device_id=(x, z, y, 1 - c), device_id_type=MESH)

    def greet(k, carry):
        t = lax.rem(ctx + k, 16)
        dev = (x, t // 4, lax.rem(t, 4), c)
        pl.semaphore_signal(barrier, inc=1, device_id=dev, device_id_type=MESH)
        return carry

    lax.fori_loop(1, 16, greet, 0)
    pl.semaphore_wait(barrier, NX + 15)

    def along_x(src, dst, ss, rs, t, place):
        return pltpu.make_async_remote_copy(
            src_ref=src.at[t],
            dst_ref=dst.at[place],
            send_sem=ss.at[t],
            recv_sem=rs.at[place],
            device_id=(t, z, y, c),
            device_id_type=MESH,
        )

    def to_sibling(i):
        src, dst = ((dw.at[1 - c], sibling_dw), (gains, sibling_gains))[i]
        return pltpu.make_async_remote_copy(
            src_ref=src,
            dst_ref=dst,
            send_sem=ss_s.at[i],
            recv_sem=rs_s.at[i],
            device_id=(x, z, y, 1 - c),
            device_id_type=MESH,
        )

    def over_ctx(i, t, place):
        src, dst, ss, rs = (
            (reduced.at[t], dw_parts, ss_w, rs_w),
            (gains, gains_all, ss_g, rs_g),
        )[i]
        return pltpu.make_async_remote_copy(
            src_ref=src,
            dst_ref=dst.at[place],
            send_sem=ss.at[t],
            recv_sem=rs.at[place],
            device_id=(x, t // 4, lax.rem(t, 4), c),
            device_id_type=MESH,
        )

    m = low_half((ROWS, 2 * HD))
    mh = low_half((BLK, 2 * HD))
    gq_sum = jnp.zeros((1, 2 * HD), F32)
    gk_sum = jnp.zeros((1, 2 * HD), F32)
    for n, k in enumerate((1, 3, 2, 0)):
        s = lax.rem(x + k, NX)
        at = pl.ds(pl.multiple_of(s * ROWS, ROWS), ROWS)
        place = place_of(x, s) * 4
        cos_s, sin_s = cos_r[at, :], sin_r[at, :]
        part = [recv[place + hh, :ROWS, :].astype(F32) for hh in range(4)]
        vals = [recv[place + hh, ROWS:, :].astype(F32) for hh in range(4)]
        grads = [
            jnp.where(m, part[0], swap(part[1])),
            jnp.where(m, part[2], swap(part[3])),
            jnp.where(m, swap(part[0] + part[1]), part[2] + part[3]),
        ]
        for p in range(3):
            turned = grads[p] * cos_s + swap_halves(grads[p] * sin_s)
            v = raw[at, p * 128 : (p + 1) * 128]
            gain = g_q[...] if p < 2 else g_k[...]
            r = lax.rsqrt(head_mean(v * v) + EPSILON)
            weighted = turned * gain
            grad = r * weighted - v * (r * r * r) * head_mean(weighted * v)
            low[at, p * 128 : (p + 1) * 128] = grad.astype(BF16)
            term = jnp.sum(turned * v * r, axis=0, keepdims=True)
            if p < 2:
                gq_sum = gq_sum + term
            else:
                gk_sum = gk_sum + term
        a, b = vals[0] + vals[1], vals[2] + vals[3]
        grad_v = jnp.concatenate([jnp.where(mh, a, swap(b)), jnp.where(mh, swap(a), b)], 0)
        low[at, 3 * 128 :] = grad_v.astype(BF16)
        grad_h = nt(low[at, :], w[...])
        gh[s] = grad_h.astype(BF16)
        if k:
            along_x(gh, gh_parts, ss_h, rs_h, s, x).start()
        term = jnp.sum(grad_h * h[at, :].astype(F32), axis=0, keepdims=True)
        attn[...] = term if n == 0 else attn[...] + term
    for i in range(8):
        cols = slice(i * 128, i * 128 + 128)
        gains[i : i + 1, :] = attn[:, cols] / g_attn[:, cols]
        gains[8 + i : 9 + i, :] = gain_ffn[:, cols]
    gains[16:, :] = jnp.concatenate([gq_sum, gk_sum, jnp.zeros((6, 2 * HD), F32)], 0)
    grad_w = tn(h[...], low[...]).astype(BF16)
    for i in range(32):
        dw[i % 2, i // 2, :, : QX + 2 * KX] = grad_w[i * 32 : (i + 1) * 32, :]
    grad_w = tn(
        mixed_x[...].reshape(NX * ROWS, QX), branch_x[...].reshape(NX * ROWS, D)
    ).astype(BF16)
    for q in range(4):
        for i in range(8):
            dw[i % 2, q * 4 + i // 2, :, QX + 2 * KX :] = grad_w[
                i * 32 : (i + 1) * 32, q * 256 : (q + 1) * 256
            ]
    to_sibling(0).start()
    to_sibling(1).start()
    for k in (1, 3, 2):
        along_x(result, result_parts, ss_r, rs_r, lax.rem(x + k, NX), x).start()
    to_sibling(1).wait()
    gains[...] = gains[...] + sibling_gains[...]
    to_sibling(0).wait()

    def send(k, carry):
        t = lax.rem(ctx + k, 16)
        reduced[t] = (dw[c, t].astype(F32) + sibling_dw[t].astype(F32)).astype(BF16)
        over_ctx(0, t, ctx).start()
        over_ctx(1, t, ctx).start()
        return carry

    lax.fori_loop(1, 16, send, 0)
    total = dw[c, ctx].astype(F32) + sibling_dw[ctx].astype(F32)
    all_gains = gains[...]

    grad_h = gh[x].astype(F32)
    for k in (1, 3, 2):
        t = lax.rem(x + k, NX)
        along_x(gh, gh_parts, ss_h, rs_h, t, t).wait_recv()
        grad_h = grad_h + gh_parts[t].astype(F32)
    inputs = tokens[...].astype(F32)
    r = lax.rsqrt(jnp.mean(inputs * inputs, axis=-1, keepdims=True) + EPSILON)
    weighted = grad_h * g_attn[...]
    inner = jnp.mean(weighted * inputs, axis=-1, keepdims=True)
    tokens_o[...] = (
        grad_middle[...] + r * weighted - inputs * (r * r * r) * inner
    ).astype(BF16)
    out = middle[...] + result[x].astype(F32)
    for k in (1, 3, 2):
        t = lax.rem(x + k, NX)
        along_x(result, result_parts, ss_r, rs_r, t, t).wait_recv()
        out = out + result_parts[t].astype(F32)
    out_o[...] = out.astype(BF16)

    def collect(k, carry):
        t = lax.rem(ctx + k, 16)
        over_ctx(0, t, t).wait_recv()
        over_ctx(1, t, t).wait_recv()
        return carry[0] + dw_parts[t].astype(F32), carry[1] + gains_all[t]

    total, all_gains = lax.fori_loop(1, 16, collect, (total, all_gains))
    qkv_o[...] = total[:, : QX + 2 * KX].astype(BF16)
    wo_o[...] = total[:, QX + 2 * KX :].astype(BF16)
    gains_o[...] = all_gains

    def drain(k, carry):
        t = lax.rem(ctx + k, 16)
        over_ctx(0, t, ctx).wait_send()
        over_ctx(1, t, ctx).wait_send()
        return carry

    lax.fori_loop(1, 16, drain, 0)
    for k in (1, 3, 2):
        t = lax.rem(x + k, NX)
        along_x(gh, gh_parts, ss_h, rs_h, t, x).wait_send()
        along_x(result, result_parts, ss_r, rs_r, t, x).wait_send()


def project_back(number, *operands):
    vmem = pl.BlockSpec(memory_space=pltpu.VMEM)
    tokens = (NX, ROWS, D)
    wide = QX + 2 * KX + QX
    return pl.pallas_call(
        project_back_kernel,
        in_specs=[vmem] * 16,
        out_specs=[vmem] * 5,
        out_shape=[
            jax.ShapeDtypeStruct((ROWS, D), BF16),
            jax.ShapeDtypeStruct((ROWS, D), BF16),
            jax.ShapeDtypeStruct((32, QX + 2 * KX), BF16),
            jax.ShapeDtypeStruct((32, QX), BF16),
            jax.ShapeDtypeStruct((24, 2 * HD), F32),
        ],
        scratch_shapes=[
            pltpu.VMEM((NX * ROWS, QX + 2 * KX), BF16),
            pltpu.VMEM((1, D), F32),
            pltpu.VMEM(tokens, BF16),
            pltpu.VMEM(tokens, BF16),
            pltpu.VMEM(tokens, BF16),
            pltpu.VMEM((2, 16, 32, wide), BF16),
            pltpu.VMEM((16, 32, wide), BF16),
            pltpu.VMEM((16, 32, wide), BF16),
            pltpu.VMEM((16, 32, wide), BF16),
            pltpu.VMEM((24, 2 * HD), F32),
            pltpu.VMEM((24, 2 * HD), F32),
            pltpu.VMEM((16, 24, 2 * HD), F32),
        ]
        + [pltpu.SemaphoreType.DMA((n,)) for n in (NX, NX, NX, NX, 2, 2, 16, 16, 16, 16)],
        compiler_params=pltpu.CompilerParams(
            collective_id=number, has_side_effects=True, vmem_limit_bytes=VMEM_BYTES
        ),
        name="project_back",
    )(*operands)


def hand_out_kernel(qkv, gu, wo, wd, gains, q_o, k_o, v_o, o_o, g_o, u_o, d_o, ga_o, gf_o, gh_o):
    for s in range(NX):
        q_o[:, s * QX : (s + 1) * QX] = qkv[s, :, :QX].astype(F32)
        k_o[:, s * KX : (s + 1) * KX] = qkv[s, :, QX : QX + KX].astype(F32)
        v_o[:, s * KX : (s + 1) * KX] = qkv[s, :, QX + KX :].astype(F32)
        g_o[:, s * FX : (s + 1) * FX] = gu[s, :, :FX].astype(F32)
        u_o[:, s * FX : (s + 1) * FX] = gu[s, :, FX:].astype(F32)
        o_o[:, s * 256 : (s + 1) * 256] = wo[s, :, :].astype(F32)
        for rg in range(9):
            for l in range(2):
                at = slice(s * 256 + l * 128, s * 256 + l * 128 + 128)
                d_o[rg * 16 : rg * 16 + 16, at] = wd[
                    s, l * 16 : l * 16 + 16, rg * 128 : rg * 128 + 128
                ].astype(F32)
    total = gains[0] + gains[1] + gains[2] + gains[3]
    for i in range(8):
        ga_o[:, i * 128 : i * 128 + 128] = total[i : i + 1, :]
        gf_o[:, i * 128 : i * 128 + 128] = total[8 + i : 9 + i, :]
    gh_o[...] = total[16:, :] + swap(total[16:, :])


def hand_out(*operands):
    vmem = pl.BlockSpec(memory_space=pltpu.VMEM)
    shapes = [(32, D), (32, KV * HD), (32, KV * HD), (32, D), (32, FF), (32, FF), (FF // 32, D)]
    shapes += [(1, D), (1, D), (8, 2 * HD)]
    return pl.pallas_call(
        hand_out_kernel,
        in_specs=[vmem] * 5,
        out_specs=[vmem] * 10,
        out_shape=[jax.ShapeDtypeStruct(s, F32) for s in shapes],
        compiler_params=pltpu.CompilerParams(vmem_limit_bytes=VMEM_BYTES),
        name="hand_out",
    )(*operands)


def angle_constants():
    frequencies = ROPE_BASE ** (-np.arange(0, HD // 2, dtype=np.float64) * 2.0 / HD)
    phases = np.arange(LEN, dtype=np.float64)[:, None] * frequencies[None, :]
    cos, sin = np.cos(phases).astype(np.float32), np.sin(phases).astype(np.float32)
    return np.concatenate([cos] * 4, 1), np.concatenate([-sin, sin, -sin, sin], 1)


def columns_of(w, x, width):
    return lax.dynamic_slice_in_dim(w, x * width, width, axis=1)


def by_tiles(blocks):
    return blocks.reshape(-1, 9, 16, 2, 128).transpose(0, 3, 2, 1, 4).reshape(-1, 32, FX)


def body(
    tokens,
    pairs,
    w_query,
    w_key,
    w_value,
    w_out,
    w_gate,
    w_up,
    w_down,
    g_attn,
    g_query,
    g_key,
    g_ffn,
    cotangent,
):
    x = lax.axis_index("seq")
    cos_np, sin_np = angle_constants()
    cos_t, sin_t = jnp.asarray(cos_np), jnp.asarray(sin_np)
    gq2 = jnp.concatenate([g_query, g_query])[None]
    gk2 = jnp.concatenate([g_key, g_key])[None]

    swap_xz = [(a * 4 + b, b * 4 + a) for a in range(4) for b in range(4)]
    down_part = lax.ppermute(columns_of(w_down, x, D // 4), ("seq", "ctx_0"), swap_xz)
    mine = jnp.concatenate(
        [w_out, columns_of(w_gate, x, FX), columns_of(w_up, x, FX), by_tiles(down_part[None])[0]],
        axis=1,
    )

    wide = lax.all_gather(mine, CTX_FSDP, axis=0, tiled=True)
    h_all, w_qkv, pair = gather_in(1, tokens[0], g_attn[None], w_query, w_key, w_value, pairs)
    h_all = h_all.reshape(NX * ROWS, D)
    w_qkv = w_qkv.reshape(D, QX + 2 * KX)
    pair = pair.reshape(NX * 8, 128)

    send, raw, cos_r, sin_r = project(pair, h_all, w_qkv, cos_t, sin_t, gq2, gk2)
    recv, cot_all = exchange(2, "to_heads", ("c", "a2a", send), ("x", "ag", cotangent[0]))
    heads_out, q_s, k_s, v_s, o_t, inv = attend(pair, recv)
    (mixed_parts,) = exchange(3, "to_tokens", ("t", "a2a", heads_out))
    middle, result4, grad_w_ffn, grad_middle, grad_branch, mixed, back_parts, gain_ffn = middle_part(
        4, mixed_parts, tokens[0], cot_all, g_ffn[None], wide
    )
    sums = lax.psum_scatter(grad_w_ffn, "ctx_1", scatter_dimension=0, tiled=True)
    (recv_g,) = exchange(6, "to_heads_back", ("r", "a2a", back_parts))
    sends_back = attend_back(pair, recv_g, q_s, k_s, v_s, o_t, inv)
    recv_back, branch_x, mixed_x = exchange(
        7,
        "to_tokens_back",
        ("c", "a2a", sends_back),
        ("x", "ag", grad_branch),
        ("x", "a2a", mixed),
    )
    sums, recv_back = lax.optimization_barrier((sums, recv_back))
    sums = lax.psum_scatter(sums, "ctx_0", scatter_dimension=0, tiled=True)
    output, grad_tokens, sum_qkv, sum_o, gains = project_back(
        8,
        recv_back,
        raw,
        h_all,
        w_qkv,
        cos_r,
        sin_r,
        gq2,
        gk2,
        g_attn[None],
        mixed_x,
        branch_x,
        result4,
        gain_ffn,
        tokens[0],
        grad_middle,
        middle,
    )
    qkv, gate_up, out_rows, down_rows, gains = exchange(
        9,
        "gather_out",
        ("x", "ag", sum_qkv),
        ("x", "ag", sums, (0, 2 * FX)),
        ("d", "ag", sum_o),
        ("d", "ag", sums, (2 * FX, FX)),
        ("x", "ag", gains),
    )
    *weights, gain_a, gain_f, gain_h = hand_out(qkv, gate_up, out_rows, down_rows, gains)
    return (
        output[None],
        grad_tokens[None],
        *weights,
        gain_a[0],
        gain_h[0, :HD],
        gain_h[1, :HD],
        gain_f[0],
    )


def solution(mesh):
    finer = Mesh(
        mesh.devices.reshape(mesh.shape["seq"], 4, 4, mesh.shape["fsdp"]),
        ("seq", "ctx_0", "ctx_1", "fsdp"),
    )
    tokens_spec = P(("seq", "fsdp"), CTX, None)
    rows_spec = P(CTX_FSDP, None)
    return jax.shard_map(
        body,
        mesh=finer,
        in_specs=(tokens_spec, P(("seq", "fsdp"), None))
        + (rows_spec,) * 7
        + (P(),) * 4
        + (tokens_spec,),
        out_specs=(tokens_spec, tokens_spec) + (rows_spec,) * 7 + (P(),) * 4,
        check_vma=False,
    )
```

```python
import functools

import jax
import jax.numpy as jnp
import numpy as np
from jax import lax
from jax.experimental import pallas as pl
from jax.experimental.pallas import tpu as pltpu
from jax.sharding import Mesh
from jax.sharding import PartitionSpec as P

D = 1024
H = 16
KV = 8
HD = 64
FF = 4608
LEN = 2560
BLK = 80
ROWS = 2 * BLK
NX = 4
FX = FF // NX
QX = H * HD // NX
KX = KV * HD // NX
TILE = 512
N_TILES = LEN // TILE
CTX = ("ctx_0", "ctx_1")
CTX_FSDP = ("ctx_0", "ctx_1", "fsdp")
SEQ_CTX_FSDP = ("seq", "ctx_0", "ctx_1", "fsdp")
EPSILON = 1e-05
ROPE_BASE = 1000000.0
MESH = pl.DeviceIdType.MESH
BF16 = jnp.bfloat16
F32 = jnp.float32
VMEM_BYTES = 56 * 1024 * 1024


SIZE = {"x": 4, "c": 16, "p": 32, "t": 16, "r": 16, "d": 4}


def coords():
    return tuple(lax.axis_index(a) for a in SEQ_CTX_FSDP)


def twisted(x, v):
    return lax.rem(v + 2 * (1 - lax.rem(x, 2)) * (1 - lax.rem(v, 2)), 4)


def sequence_at(x, z):
    return lax.rem(x + twisted(x, z), 4)


def place_of(x, s):
    return twisted(x, lax.rem(s - x + 4, 4))


def target(group, t):
    s, z, y, c = coords()
    if group == "x":
        return (t, z, y, c), s
    if group == "c":
        return (s, t // 4, lax.rem(t, 4), c), z * 4 + y
    if group == "p":
        return (s, t // 8, lax.rem(t // 2, 4), lax.rem(t, 2)), (z * 4 + y) * 2 + c
    if group == "t":
        return (sequence_at(s, z), t // 4, lax.rem(t, 4), c), s * 4 + y
    if group == "d":
        return (t, s, y, c), z
    return (t // 4, place_of(t // 4, s), lax.rem(t, 4), c), z * 4 + y


def source(group, t):
    s, z, y, c = coords()
    if group == "t":
        return (t // 4, place_of(t // 4, s), lax.rem(t, 4), c)
    if group == "r":
        return (sequence_at(s, z), t // 4, lax.rem(t, 4), c)
    if group == "d":
        return (z, t, y, c)
    return target(group, t)[0]


def own(group):
    s, z, y, c = coords()
    if group == "t":
        return sequence_at(s, z) == s, z * 4 + y, s * 4 + y
    if group == "r":
        return sequence_at(s, z) == s, s * 4 + y, z * 4 + y
    if group == "d":
        return s == z, s, z
    me = target(group, 0)[1]
    return None, me, me


def exchange_kernel(items, *refs):
    n = len(items)
    srcs, outs, sems = refs[:n], refs[n : 2 * n], refs[2 * n :]
    barrier = pltpu.get_barrier_semaphore()
    expected = 0
    starts = []
    for i, (g, _, _) in enumerate(items):
        has_own, sent, _ = own(g)
        size = SIZE[g]
        if has_own is None:
            starts.append((jnp.int32(1), sent))
            expected = expected + size - 1
        else:
            starts.append((has_own.astype(jnp.int32), sent))
            expected = expected + size - has_own.astype(jnp.int32)
        place = own(g)[2]
        first = starts[i][0]

        def greet(k, carry, g=g, size=size, place=place):
            dev = source(g, lax.rem(place + k, size))
            pl.semaphore_signal(barrier, inc=1, device_id=dev, device_id_type=MESH)
            return carry

        lax.fori_loop(first, size, greet, 0)

    def block_of(i, t):
        _, mode, cols = items[i]
        if cols is not None:
            return srcs[i].at[:, pl.ds(*cols)]
        return srcs[i] if mode == "ag" else srcs[i].at[t]

    def own_copy(i):
        g = items[i][0]
        _, sent, place = own(g)
        src = block_of(i, sent)
        return pltpu.make_async_copy(src, outs[i].at[place], sems[3 * i + 2])

    for i, (g, _, _) in enumerate(items):
        if own(g)[0] is None:
            own_copy(i).start()
        else:
            pl.when(own(g)[0])(lambda i=i: own_copy(i).start())
    pl.semaphore_wait(barrier, expected)

    def remote(i, t, place):
        g = items[i][0]
        dev, there = target(g, t)
        src = block_of(i, t)
        return pltpu.make_async_remote_copy(
            src_ref=src,
            dst_ref=outs[i].at[there if place is None else place],
            send_sem=sems[3 * i].at[t],
            recv_sem=sems[3 * i + 1].at[there if place is None else place],
            device_id=dev,
            device_id_type=MESH,
        )

    for i, (g, _, _) in enumerate(items):
        first, sent = starts[i]

        def send(k, carry, i=i, g=g, sent=sent):
            remote(i, lax.rem(sent + k, SIZE[g]), None).start()
            return carry

        lax.fori_loop(first, SIZE[g], send, 0)
    for i, (g, _, _) in enumerate(items):
        first, sent = starts[i]
        place = own(g)[2]

        def drain(k, carry, i=i, g=g, sent=sent, place=place):
            remote(i, lax.rem(sent + k, SIZE[g]), None).wait_send()
            remote(i, lax.rem(sent + k, SIZE[g]), lax.rem(place + k, SIZE[g])).wait_recv()
            return carry

        lax.fori_loop(first, SIZE[g], drain, 0)
        if own(g)[0] is None:
            own_copy(i).wait()
        else:
            pl.when(own(g)[0])(lambda i=i: own_copy(i).wait())


def exchange(number, name, *parts):
    items = tuple((part[0], part[1], part[3] if len(part) > 3 else None) for part in parts)
    arrays = [part[2] for part in parts]
    outs = []
    for (g, m, cols), a in zip(items, arrays):
        shape = a.shape if m == "ag" else a.shape[1:]
        shape = shape if cols is None else shape[:-1] + (cols[1],)
        outs.append(jax.ShapeDtypeStruct((SIZE[g],) + shape, a.dtype))
    scratch = []
    for g, _, _ in items:
        scratch += [
            pltpu.SemaphoreType.DMA((SIZE[g],)),
            pltpu.SemaphoreType.DMA((SIZE[g],)),
            pltpu.SemaphoreType.DMA,
        ]
    return pl.pallas_call(
        functools.partial(exchange_kernel, items),
        out_shape=outs,
        in_specs=[pl.BlockSpec(memory_space=pl.ANY)] * len(arrays),
        out_specs=[pl.BlockSpec(memory_space=pl.ANY)] * len(arrays),
        scratch_shapes=scratch,
        compiler_params=pltpu.CompilerParams(collective_id=number, has_side_effects=True),
        name=name,
    )(*arrays)


def lanes(shape):
    return lax.broadcasted_iota(jnp.int32, shape, len(shape) - 1)


def low_half(shape):
    return lanes(shape) < HD


def swap(v):
    return pltpu.roll(v, HD, 1)


def swap_halves(v):
    first = lax.rem(lanes(v.shape), HD) < HD // 2
    return jnp.where(first, pltpu.roll(v, 2 * HD - HD // 2, 1), pltpu.roll(v, HD // 2, 1))


def head_mean(v):
    m = low_half(v.shape)
    a = jnp.sum(jnp.where(m, v, 0.0), axis=-1, keepdims=True)
    b = jnp.sum(jnp.where(m, 0.0, v), axis=-1, keepdims=True)
    return jnp.where(m, a, b) * (1.0 / HD)


def nt(a, b):
    return lax.dot_general(a, b, (((1,), (1,)), ((), ())), preferred_element_type=F32)


def nn(a, b):
    return lax.dot_general(a, b, (((1,), (0,)), ((), ())), preferred_element_type=F32)


def tn(a, b):
    return lax.dot_general(a, b, (((0,), (0,)), ((), ())), preferred_element_type=F32)


def my_pairs(pairs):
    x, z, _, _ = coords()
    line = sequence_at(x, z) * 8
    return [pairs[line, j] for j in range(16)]


def rows_of(block):
    return pl.ds(pl.multiple_of(block * BLK, 16), BLK)


def rope_rows(block, table):
    return jnp.concatenate([table[rows_of(block), :], table[rows_of(31 - block), :]], 0)


def gather_in_kernel(
    tokens,
    g_attn,
    w_q,
    w_k,
    w_v,
    pairs,
    h_o,
    w_o,
    pairs_o,
    h,
    w,
    row,
    ss_h,
    rs_h,
    ss_p,
    rs_p,
    ss_w,
    rs_w,
    ss_f,
    rs_f,
    own_sem,
):
    x, z, y, c = coords()
    ctx = z * 4 + y
    barrier = pltpu.get_barrier_semaphore()
    for k in range(1, NX):
        pl.semaphore_signal(
            barrier, inc=1, device_id=(lax.rem(x + k, NX), z, y, c), device_id_type=MESH
        )
    pl.semaphore_signal(barrier, inc=1, device_id=(x, z, y, 1 - c), device_id_type=MESH)

    def greet(k, carry):
        t = lax.rem(ctx + k, 16)
        dev = (x, t // 4, lax.rem(t, 4), c)
        pl.semaphore_signal(barrier, inc=1, device_id=dev, device_id_type=MESH)
        return carry

    lax.fori_loop(1, 16, greet, 0)
    w[:, :QX] = w_q[:, pl.ds(pl.multiple_of(x * QX, QX), QX)]
    w[:, QX : QX + KX] = w_k[:, pl.ds(pl.multiple_of(x * KX, KX), KX)]
    w[:, QX + KX :] = w_v[:, pl.ds(pl.multiple_of(x * KX, KX), KX)]
    row[...] = jnp.zeros_like(row)
    row[0:1, :16] = pairs[...]
    inputs = tokens[...].astype(F32)
    inv_rms = lax.rsqrt(jnp.mean(inputs * inputs, axis=-1, keepdims=True) + EPSILON)
    h[...] = (inputs * inv_rms * g_attn[...]).astype(BF16)

    def along_x(src, dst, ss, rs, t, place):
        return pltpu.make_async_remote_copy(
            src_ref=src,
            dst_ref=dst.at[place],
            send_sem=ss.at[t],
            recv_sem=rs.at[place],
            device_id=(t, z, y, c),
            device_id_type=MESH,
        )

    def over_ctx(t, place):
        return pltpu.make_async_remote_copy(
            src_ref=w,
            dst_ref=w_o.at[place * 2 + c],
            send_sem=ss_w.at[t],
            recv_sem=rs_w.at[place],
            device_id=(x, t // 4, lax.rem(t, 4), c),
            device_id_type=MESH,
        )

    def to_sibling(t, core, src):
        return pltpu.make_async_remote_copy(
            src_ref=src,
            dst_ref=w_o.at[t * 2 + core],
            send_sem=ss_f.at[t],
            recv_sem=rs_f.at[t],
            device_id=(x, z, y, 1 - c),
            device_id_type=MESH,
        )

    mine = [
        pltpu.make_async_copy(h, h_o.at[x], own_sem.at[0]),
        pltpu.make_async_copy(row, pairs_o.at[x], own_sem.at[1]),
        pltpu.make_async_copy(w, w_o.at[ctx * 2 + c], own_sem.at[2]),
    ]
    for copy in mine:
        copy.start()
    pl.semaphore_wait(barrier, NX + 15)
    for k in (1, 3, 2):
        t = lax.rem(x + k, NX)
        along_x(h, h_o, ss_h, rs_h, t, x).start()
        along_x(row, pairs_o, ss_p, rs_p, t, x).start()

    def send(k, carry):
        over_ctx(lax.rem(ctx + k, 16), ctx).start()
        return carry

    lax.fori_loop(1, 16, send, 0)
    to_sibling(ctx, c, w).start()

    def forward(k, carry):
        t = lax.rem(ctx + k, 16)
        over_ctx(t, t).wait_recv()
        to_sibling(t, c, w_o.at[t * 2 + c]).start()
        return carry

    lax.fori_loop(1, 16, forward, 0)

    def drain(k, carry):
        t = lax.rem(ctx + k, 16)
        to_sibling(t, 1 - c, w).wait_recv()
        to_sibling(t, c, w).wait_send()
        return carry

    lax.fori_loop(0, 16, drain, 0)

    def drain_ctx(k, carry):
        over_ctx(lax.rem(ctx + k, 16), ctx).wait_send()
        return carry

    lax.fori_loop(1, 16, drain_ctx, 0)
    for k in (1, 3, 2):
        t = lax.rem(x + k, NX)
        along_x(h, h_o, ss_h, rs_h, t, x).wait_send()
        along_x(row, pairs_o, ss_p, rs_p, t, x).wait_send()
        along_x(h, h_o, ss_h, rs_h, t, t).wait_recv()
        along_x(row, pairs_o, ss_p, rs_p, t, t).wait_recv()
    for copy in mine:
        copy.wait()


def gather_in(number, *operands):
    wide = QX + 2 * KX
    return pl.pallas_call(
        gather_in_kernel,
        in_specs=[pl.BlockSpec(memory_space=pltpu.VMEM)] * 6,
        out_specs=[pl.BlockSpec(memory_space=pl.ANY)] * 3,
        out_shape=[
            jax.ShapeDtypeStruct((NX, ROWS, D), BF16),
            jax.ShapeDtypeStruct((32, 32, wide), BF16),
            jax.ShapeDtypeStruct((NX, 8, 128), jnp.int32),
        ],
        scratch_shapes=[
            pltpu.VMEM((ROWS, D), BF16),
            pltpu.VMEM((32, wide), BF16),
            pltpu.VMEM((8, 128), jnp.int32),
        ]
        + [pltpu.SemaphoreType.DMA((n,)) for n in (NX, NX, NX, NX, 16, 16, 16, 16, 3)],
        compiler_params=pltpu.CompilerParams(collective_id=number, has_side_effects=True),
        name="gather_in",
    )(*operands)


def project_kernel(pairs, h, w, cos_t, sin_t, g_q, g_k, send, raw, cos_o, sin_o, acc):
    x, z, y, _ = coords()
    acc[...] = nn(h[...], w[...])
    m = low_half((ROWS, 2 * HD))
    mh = low_half((BLK, 2 * HD))
    for s in range(NX):
        at = slice(s * ROWS, (s + 1) * ROWS)
        cos_r, sin_r = (rope_rows(pairs[s * 8, z * 4 + y], table) for table in (cos_t, sin_t))
        cos_o[at, :], sin_o[at, :] = cos_r, sin_r
        raw[at, :] = acc[at, : QX + KX]
        turned = []
        for p in range(3):
            v = acc[at, p * 128 : (p + 1) * 128]
            gain = g_q[...] if p < 2 else g_k[...]
            normed = v * lax.rsqrt(head_mean(v * v) + EPSILON) * gain
            turned.append(normed * cos_r + swap_halves(normed) * sin_r)
        keys = turned[2]
        swapped_keys = swap(keys)
        values = acc[at, 3 * 128 :]
        top, bottom = values[:BLK], values[BLK:]
        packed = (jnp.where(mh, top, swap(bottom)), jnp.where(mh, swap(top), bottom))
        for hh in range(4):
            q = turned[hh // 2]
            q = q if hh % 2 == 0 else swap(q)
            k = swapped_keys if hh < 2 else keys
            send[place_of(x, s) * 4 + hh, :ROWS, :] = jnp.where(m, q, k).astype(BF16)
            send[place_of(x, s) * 4 + hh, ROWS:, :] = packed[hh // 2].astype(BF16)


def project(pairs, h, w, cos_t, sin_t, g_q, g_k):
    return pl.pallas_call(
        project_kernel,
        grid_spec=pltpu.PrefetchScalarGridSpec(
            num_scalar_prefetch=1,
            in_specs=[pl.BlockSpec(memory_space=pltpu.VMEM)] * 6,
            out_specs=[pl.BlockSpec(memory_space=pltpu.VMEM)] * 4,
            scratch_shapes=[pltpu.VMEM((NX * ROWS, QX + 2 * KX), F32)],
        ),
        out_shape=[
            jax.ShapeDtypeStruct((16, ROWS + BLK, 2 * HD), BF16),
            jax.ShapeDtypeStruct((NX * ROWS, QX + KX), F32),
            jax.ShapeDtypeStruct((NX * ROWS, 2 * HD), F32),
            jax.ShapeDtypeStruct((NX * ROWS, 2 * HD), F32),
        ],
        compiler_params=pltpu.CompilerParams(vmem_limit_bytes=VMEM_BYTES),
        name="project",
    )(pairs, h, w, cos_t, sin_t, g_q, g_k)


def attend_kernel(pairs, recv, out, q_s, k_s, v_s, o_t, inv, o_s, v_t):
    m = low_half((BLK, 2 * HD))
    pair = my_pairs(pairs)
    for j in range(16):
        packed = recv[j, ROWS:, :].astype(F32)
        for half in range(2):
            block = pair[j] if half == 0 else 31 - pair[j]
            both = recv[j, half * BLK : (half + 1) * BLK, :].astype(F32)
            vals = packed if half == 0 else swap(packed)
            q_s[rows_of(block), :] = jnp.where(m, both * HD**-0.5, 0.0).astype(BF16)
            k_s[rows_of(block), :] = jnp.where(m, swap(both), 0.0).astype(BF16)
            v_s[rows_of(block), :] = jnp.where(m, vals, 0.0).astype(BF16)
    for t in range(N_TILES):
        at = slice(t * TILE, (t + 1) * TILE)
        v_t[:, at] = v_s[at, :].T[:HD]
    causal = lax.broadcasted_iota(jnp.int32, (TILE, TILE), 0) <= lanes((TILE, TILE))
    for i in range(N_TILES):
        at = slice(i * TILE, (i + 1) * TILE)
        q = q_s[at, :]

        e = jnp.where(causal, jnp.exp(nt(k_s[at, :], q)), 0.0)
        first = (jnp.sum(e, axis=0, keepdims=True), nn(v_t[:, at], e.astype(BF16)))

        def step(t, carry, q=q):
            total, acc = carry
            there = pl.ds(pl.multiple_of(t * TILE, TILE), TILE)
            e = jnp.exp(nt(k_s[there, :], q))
            total = total + jnp.sum(e, axis=0, keepdims=True)
            return total, acc + nn(v_t[:, there], e.astype(BF16))

        total, acc = lax.fori_loop(0, i, step, first) if i else first
        over = 1.0 / total
        attended = acc * over
        o_t[:, at] = attended
        inv[:, at] = jnp.broadcast_to(over, (8, TILE))
        o_s[at, :] = jnp.concatenate([attended, jnp.zeros_like(attended)], 0).T
    for j in range(16):
        low_rows = o_s[rows_of(pair[j]), :]
        high_rows = o_s[rows_of(31 - pair[j]), :]
        out[j, :, :] = (low_rows + swap(high_rows)).astype(BF16)


def attend(pairs, recv):
    wide = jax.ShapeDtypeStruct((LEN, 2 * HD), BF16)
    return pl.pallas_call(
        attend_kernel,
        grid_spec=pltpu.PrefetchScalarGridSpec(
            num_scalar_prefetch=1,
            in_specs=[pl.BlockSpec(memory_space=pltpu.VMEM)],
            out_specs=[pl.BlockSpec(memory_space=pltpu.VMEM)] * 6,
            scratch_shapes=[pltpu.VMEM((LEN, 2 * HD), F32), pltpu.VMEM((HD, LEN), BF16)],
        ),
        out_shape=[
            jax.ShapeDtypeStruct((16, BLK, 2 * HD), BF16),
            wide,
            wide,
            wide,
            jax.ShapeDtypeStruct((HD, LEN), F32),
            jax.ShapeDtypeStruct((8, LEN), F32),
        ],
        compiler_params=pltpu.CompilerParams(vmem_limit_bytes=VMEM_BYTES),
        name="attend",
    )(pairs, recv)


def attend_back_kernel(pairs, recv, q_s, k_s, v_s, o_t, inv, out, g_s, k_t, delta, dq_t, dk_s, dv_s):
    m = low_half((BLK, 2 * HD))
    pair = my_pairs(pairs)
    for j in range(16):
        packed = recv[j, :, :].astype(F32)
        g_s[rows_of(pair[j]), :] = jnp.where(m, packed, 0.0).astype(BF16)
        g_s[rows_of(31 - pair[j]), :] = jnp.where(m, swap(packed), 0.0).astype(BF16)
    for t in range(N_TILES):
        at = slice(t * TILE, (t + 1) * TILE)
        k_t[:, at] = k_s[at, :].T[:HD]
        g_t = g_s[at, :].astype(F32).T[:HD]
        row = jnp.sum(g_t * o_t[:, at], axis=0, keepdims=True)
        delta[:, at] = jnp.broadcast_to(row, (8, TILE))
    dq_t[...] = jnp.zeros_like(dq_t)
    causal = lax.broadcasted_iota(jnp.int32, (TILE, TILE), 0) <= lanes((TILE, TILE))
    for i in range(N_TILES):
        at = slice(i * TILE, (i + 1) * TILE)
        k, v, kt = k_s[at, :], v_s[at, :], k_t[:, at]

        def pair_of_tiles(there, masked, k=k, v=v, kt=kt):
            q, g = q_s[there, :], g_s[there, :]
            e = jnp.exp(nt(k, q))
            if masked:
                e = jnp.where(causal, e, 0.0)
            probs = e * inv[0:1, there]
            ds = (probs * (nt(v, g) - delta[0:1, there])).astype(BF16)
            dq_t[:, there] = dq_t[:, there] + nn(kt, ds)
            return nn(ds, q), nn(probs.astype(BF16), g)

        first = pair_of_tiles(at, True)

        def step(t, carry, pair_of_tiles=pair_of_tiles):
            dk, dv = pair_of_tiles(pl.ds(pl.multiple_of(t * TILE, TILE), TILE), False)
            return carry[0] + dk, carry[1] + dv

        dk, dv = lax.fori_loop(i + 1, N_TILES, step, first) if i + 1 < N_TILES else first
        dk_s[at, :] = dk
        dv_s[at, :] = dv
    for i in range(N_TILES):
        at = slice(i * TILE, (i + 1) * TILE)
        dq = dq_t[:, at] * HD**-0.5
        dk_s[at, :] = jnp.concatenate([dq, jnp.zeros_like(dq)], 0).T + swap(dk_s[at, :])
    for j in range(16):
        for half in range(2):
            block = pair[j] if half == 0 else 31 - pair[j]
            out[j, half * BLK : (half + 1) * BLK, :] = dk_s[rows_of(block), :].astype(BF16)
        out[j, ROWS:, :] = (dv_s[rows_of(pair[j]), :] + swap(dv_s[rows_of(31 - pair[j]), :])).astype(BF16)


def attend_back(pairs, recv, q_s, k_s, v_s, o_t, inv):
    return pl.pallas_call(
        attend_back_kernel,
        grid_spec=pltpu.PrefetchScalarGridSpec(
            num_scalar_prefetch=1,
            in_specs=[pl.BlockSpec(memory_space=pltpu.VMEM)] * 6,
            out_specs=pl.BlockSpec(memory_space=pltpu.VMEM),
            scratch_shapes=[
                pltpu.VMEM((LEN, 2 * HD), BF16),
                pltpu.VMEM((HD, LEN), BF16),
                pltpu.VMEM((8, LEN), F32),
                pltpu.VMEM((HD, LEN), F32),
                pltpu.VMEM((LEN, 2 * HD), F32),
                pltpu.VMEM((LEN, 2 * HD), F32),
            ],
        ),
        out_shape=jax.ShapeDtypeStruct((16, ROWS + BLK, 2 * HD), BF16),
        compiler_params=pltpu.CompilerParams(vmem_limit_bytes=VMEM_BYTES),
        name="attend_back",
    )(pairs, recv, q_s, k_s, v_s, o_t, inv)


def middle_kernel(
    parts,
    tokens,
    cot,
    g_ffn,
    wide,
    mid_o,
    result_o,
    dw_o,
    gmid_o,
    branch_o,
    mixed_o,
    back_o,
    gain_o,
    w_o,
    w_gu,
    dnp,
    w_dn,
    h_all,
    part,
    gparts,
    gu_s,
    dh_s,
    ggu,
    hid,
    h_t,
    hid_t,
    dw,
    sibling_dw,
    wsem,
    ss1,
    rs1,
    ss2,
    rs2,
    ss3,
    rs3,
):
    me, z, y, c = coords()
    barrier = pltpu.get_barrier_semaphore()
    for k in range(1, NX):
        pl.semaphore_signal(
            barrier, inc=1, device_id=(lax.rem(me + k, NX), z, y, c), device_id_type=MESH
        )
    pl.semaphore_signal(barrier, inc=1, device_id=(me, z, y, 1 - c), device_id_type=MESH)
    loads = [
        pltpu.make_async_copy(wide.at[:, pl.ds(at, width)], there, wsem.at[i])
        for i, (at, width, there) in enumerate(
            ((0, D, w_o), (D, 2 * FX, w_gu), (D + 2 * FX, FX, dnp))
        )
    ]
    for load in loads:
        load.start()
    m = low_half((BLK, 2 * HD))
    for p in range(8):
        a, b = parts[2 * p, :, :].astype(F32), parts[2 * p + 1, :, :].astype(F32)
        at = slice((p % 2) * 128, (p % 2) * 128 + 128)
        mixed_o[p // 2, :BLK, at] = jnp.where(m, a, swap(b)).astype(BF16)
        mixed_o[p // 2, BLK:, at] = jnp.where(m, swap(a), b).astype(BF16)
    loads[0].wait()
    middle = tokens[...].astype(F32)
    for q in range(NX):
        middle = middle + nn(mixed_o[q, :, :], w_o[q * QX : (q + 1) * QX, :])
    mid_o[...] = middle
    r = lax.rsqrt(jnp.mean(middle * middle, axis=-1, keepdims=True) + EPSILON)
    h_all[me] = (middle * r * g_ffn[...]).astype(BF16)
    pl.semaphore_wait(barrier, NX)

    def send_h(t, place):
        return pltpu.make_async_remote_copy(
            src_ref=h_all.at[me],
            dst_ref=h_all.at[place],
            send_sem=ss1.at[t],
            recv_sem=rs1.at[place],
            device_id=(t, z, y, c),
            device_id_type=MESH,
        )

    def send_grad(t, place):
        return pltpu.make_async_remote_copy(
            src_ref=part.at[t],
            dst_ref=gparts.at[place],
            send_sem=ss2.at[t],
            recv_sem=rs2.at[place],
            device_id=(t, z, y, c),
            device_id_type=MESH,
        )

    for k in (1, 3, 2):
        send_h(lax.rem(me + k, NX), me).start()
    loads[1].wait()
    loads[2].wait()
    for o in range(32):
        for rg in range(9):
            for l in range(2):
                row = (o % 8) * 144 + rg * 16
                w_dn[o // 8, row : row + 16, l * 128 : l * 128 + 128] = dnp[
                    o * 32 + l * 16 : o * 32 + l * 16 + 16, rg * 128 : rg * 128 + 128
                ]

    def block(k, carry):
        t = lax.rem(me + k + k // 2 - 2 * (k // 2) * lax.rem(k, 2), NX)

        @pl.when(k > 0)
        def _():
            send_h(t, t).wait_recv()

        rows = pl.ds(pl.multiple_of(t * ROWS, ROWS), ROWS)
        gu_s[...] = nn(h_all[t], w_gu[...])
        cot_t = cot[t]
        grad_hidden = nt(cot_t[:, :256], w_dn[0])
        for q in range(1, NX):
            grad_hidden = grad_hidden + nt(cot_t[:, q * 256 : (q + 1) * 256], w_dn[q])
        dh_s[...] = grad_hidden
        for j in range(FX // 128):
            at, above = slice(j * 128, j * 128 + 128), slice(FX + j * 128, FX + j * 128 + 128)
            gate, up, dh = gu_s[:, at], gu_s[:, above], dh_s[:, at]
            sig = jax.nn.sigmoid(gate)
            silu = gate * sig
            hid[rows, at] = (silu * up).astype(BF16)
            ggu[rows, at] = (dh * up * (sig * (1.0 + gate * (1.0 - sig)))).astype(BF16)
            ggu[rows, above] = (dh * silu).astype(BF16)
        part[t] = nt(ggu[rows, :], w_gu[...]).astype(BF16)

        @pl.when(k > 0)
        def _():
            send_grad(t, me).start()

        hidden = hid[rows, :]
        for q in range(NX):
            result_o[t, :, q * 256 : (q + 1) * 256] = nn(hidden, w_dn[q]).astype(BF16)
        return carry

    lax.fori_loop(0, NX, block, 0)

    def to_sibling(i, at):
        return pltpu.make_async_remote_copy(
            src_ref=dw.at[pl.ds(pl.multiple_of((1 - c) * 512, 512), 512), at],
            dst_ref=sibling_dw.at[:, at],
            send_sem=ss3.at[i],
            recv_sem=rs3.at[i],
            device_id=(me, z, y, 1 - c),
            device_id_type=MESH,
        )

    down = pl.ds(2 * FX, FX)
    hid_t[...] = hid[...].T
    for q in range(NX):
        cot_q = cot[:, :, q * 256 : (q + 1) * 256].reshape(NX * ROWS, 256)
        grad = nn(hid_t[...], cot_q).astype(BF16)
        for o in range(8):
            for rg in range(9):
                for l in range(2):
                    row = o * 144 + rg * 16
                    there = ((o % 2) * 16 + q * 4 + o // 2) * 32 + l * 16
                    dw[there : there + 16, 2 * FX + rg * 128 : 2 * FX + rg * 128 + 128] = grad[
                        row : row + 16, l * 128 : l * 128 + 128
                    ]
    to_sibling(9, down).start()
    h_rows = h_all[...].reshape(NX * ROWS, D).T
    for o in range(32):
        there = ((o % 2) * 16 + o // 2) * 32
        h_t[there : there + 32, :] = h_rows[o * 32 : o * 32 + 32, :]

    def chunk(j):
        return pl.ds(pl.multiple_of(j * 256, 256), 256)

    def columns(j, carry):
        dw[:, chunk(j)] = nn(h_t[...], ggu[:, chunk(j)]).astype(BF16)
        to_sibling(j, chunk(j)).start()
        return carry

    lax.fori_loop(0, 2 * FX // 256, columns, 0)

    grad_h = part[me].astype(F32)
    for k in (1, 3, 2):
        t = lax.rem(me + k, NX)
        send_grad(t, t).wait_recv()
        grad_h = grad_h + gparts[t].astype(F32)
    for k in (1, 3, 2):
        t = lax.rem(me + k, NX)
        send_h(t, me).wait_send()
        send_grad(t, me).wait_send()
    middle = mid_o[...]
    r = lax.rsqrt(jnp.mean(middle * middle, axis=-1, keepdims=True) + EPSILON)
    weighted = grad_h * g_ffn[...]
    inner = jnp.mean(weighted * middle, axis=-1, keepdims=True)
    gain_o[...] = jnp.sum(grad_h * middle * r, axis=0, keepdims=True)
    grad_middle = cot[me].astype(F32) + r * weighted - middle * (r * r * r) * inner
    gmid_o[...] = grad_middle
    branch_o[...] = grad_middle.astype(BF16)
    for q in range(NX):
        grad = nt(branch_o[...], w_o[q * QX : (q + 1) * QX, :]).astype(BF16).astype(F32)
        for p in range(2):
            top, bottom = grad[:BLK, p * 128 : p * 128 + 128], grad[BLK:, p * 128 : p * 128 + 128]
            back_o[4 * q + 2 * p, :, :] = jnp.where(m, top, swap(bottom)).astype(BF16)
            back_o[4 * q + 2 * p + 1, :, :] = jnp.where(m, swap(top), bottom).astype(BF16)
    half = pl.ds(pl.multiple_of(c * 512, 512), 512)

    def both(at):
        dw_o[:, at] = (dw[half, at].astype(F32) + sibling_dw[:, at].astype(F32)).astype(BF16)

    to_sibling(9, down).wait()
    both(down)

    def add(j, carry):
        to_sibling(j, chunk(j)).wait()
        both(chunk(j))
        return carry

    lax.fori_loop(0, 2 * FX // 256, add, 0)


def middle_part(number, parts, tokens, cot, g_ffn, wide):
    vmem = pl.BlockSpec(memory_space=pltpu.VMEM)
    blocks = (NX, ROWS, D)
    return pl.pallas_call(
        middle_kernel,
        in_specs=[vmem] * 4 + [pl.BlockSpec(memory_space=pl.ANY)],
        out_specs=[vmem] * 8,
        out_shape=[
            jax.ShapeDtypeStruct((ROWS, D), F32),
            jax.ShapeDtypeStruct(blocks, BF16),
            jax.ShapeDtypeStruct((D // 2, 3 * FX), BF16),
            jax.ShapeDtypeStruct((ROWS, D), F32),
            jax.ShapeDtypeStruct((ROWS, D), BF16),
            jax.ShapeDtypeStruct((NX, ROWS, QX), BF16),
            jax.ShapeDtypeStruct((16, BLK, 2 * HD), BF16),
            jax.ShapeDtypeStruct((1, D), F32),
        ],
        scratch_shapes=[
            pltpu.VMEM((D, D), BF16),
            pltpu.VMEM((D, 2 * FX), BF16),
            pltpu.VMEM((D, FX), BF16),
            pltpu.VMEM((4, FX, D // 4), BF16),
            pltpu.VMEM(blocks, BF16),
            pltpu.VMEM(blocks, BF16),
            pltpu.VMEM(blocks, BF16),
            pltpu.VMEM((ROWS, 2 * FX), F32),
            pltpu.VMEM((ROWS, FX), F32),
            pltpu.VMEM((NX * ROWS, 2 * FX), BF16),
            pltpu.VMEM((NX * ROWS, FX), BF16),
            pltpu.VMEM((D, NX * ROWS), BF16),
            pltpu.VMEM((FX, NX * ROWS), BF16),
            pltpu.VMEM((D, 3 * FX), BF16),
            pltpu.VMEM((D // 2, 3 * FX), BF16),
            pltpu.SemaphoreType.DMA((3,)),
            pltpu.SemaphoreType.DMA((NX,)),
            pltpu.SemaphoreType.DMA((NX,)),
            pltpu.SemaphoreType.DMA((NX,)),
            pltpu.SemaphoreType.DMA((NX,)),
            pltpu.SemaphoreType.DMA((10,)),
            pltpu.SemaphoreType.DMA((10,)),
        ],
        compiler_params=pltpu.CompilerParams(
            collective_id=number, has_side_effects=True, vmem_limit_bytes=VMEM_BYTES
        ),
        name="middle_part",
    )(parts, tokens, cot, g_ffn, wide)


def project_back_kernel(
    recv,
    raw,
    h,
    w,
    cos_r,
    sin_r,
    g_q,
    g_k,
    g_attn,
    mixed_x,
    branch_x,
    result,
    gain_ffn,
    tokens,
    grad_middle,
    middle,
    out_o,
    tokens_o,
    qkv_o,
    wo_o,
    gains_o,
    low,
    attn,
    gh,
    gh_parts,
    result_parts,
    dw,
    sibling_dw,
    reduced,
    dw_parts,
    gains,
    sibling_gains,
    gains_all,
    dwo,
    sibling_dwo,
    reduced_o,
    dwo_parts,
    ss_r,
    rs_r,
    ss_h,
    rs_h,
    ss_s,
    rs_s,
    ss_w,
    rs_w,
    ss_g,
    rs_g,
    ss_o,
    rs_o,
):
    x, z, y, c = coords()
    ctx = z * 4 + y
    barrier = pltpu.get_barrier_semaphore()
    for k in range(1, NX):
        pl.semaphore_signal(
            barrier, inc=1, device_id=(lax.rem(x + k, NX), z, y, c), device_id_type=MESH
        )
    pl.semaphore_signal(barrier, inc=1, device_id=(x, z, y, 1 - c), device_id_type=MESH)

    def greet(k, carry):
        t = lax.rem(ctx + k, 16)
        dev = (x, t // 4, lax.rem(t, 4), c)
        pl.semaphore_signal(barrier, inc=1, device_id=dev, device_id_type=MESH)
        return carry

    lax.fori_loop(1, 16, greet, 0)
    pl.semaphore_wait(barrier, NX + 15)

    def along_x(src, dst, ss, rs, t, place):
        return pltpu.make_async_remote_copy(
            src_ref=src.at[t],
            dst_ref=dst.at[place],
            send_sem=ss.at[t],
            recv_sem=rs.at[place],
            device_id=(t, z, y, c),
            device_id_type=MESH,
        )

    def to_sibling(i):
        src, dst = (
            (dw.at[1 - c], sibling_dw),
            (gains, sibling_gains),
            (dwo.at[1 - c], sibling_dwo),
        )[i]
        return pltpu.make_async_remote_copy(
            src_ref=src,
            dst_ref=dst,
            send_sem=ss_s.at[i],
            recv_sem=rs_s.at[i],
            device_id=(x, z, y, 1 - c),
            device_id_type=MESH,
        )

    def over_ctx(i, t, place):
        src, dst, ss, rs = (
            (reduced.at[t], dw_parts, ss_w, rs_w),
            (gains, gains_all, ss_g, rs_g),
            (reduced_o.at[t], dwo_parts, ss_o, rs_o),
        )[i]
        return pltpu.make_async_remote_copy(
            src_ref=src,
            dst_ref=dst.at[place],
            send_sem=ss.at[t],
            recv_sem=rs.at[place],
            device_id=(x, t // 4, lax.rem(t, 4), c),
            device_id_type=MESH,
        )

    for k in (1, 3, 2):
        along_x(result, result_parts, ss_r, rs_r, lax.rem(x + k, NX), x).start()
    grad_w = tn(
        mixed_x[...].reshape(NX * ROWS, QX), branch_x[...].reshape(NX * ROWS, D)
    ).astype(BF16)
    for q in range(4):
        for i in range(8):
            dwo[i % 2, q * 4 + i // 2, :, :] = grad_w[
                i * 32 : (i + 1) * 32, q * 256 : (q + 1) * 256
            ]
    to_sibling(2).start()
    m = low_half((ROWS, 2 * HD))
    mh = low_half((BLK, 2 * HD))
    gq_sum = jnp.zeros((1, 2 * HD), F32)
    gk_sum = jnp.zeros((1, 2 * HD), F32)
    for n, k in enumerate((1, 3, 2, 0)):
        s = lax.rem(x + k, NX)
        at = pl.ds(pl.multiple_of(s * ROWS, ROWS), ROWS)
        place = place_of(x, s) * 4
        cos_s, sin_s = cos_r[at, :], sin_r[at, :]
        part = [recv[place + hh, :ROWS, :].astype(F32) for hh in range(4)]
        vals = [recv[place + hh, ROWS:, :].astype(F32) for hh in range(4)]
        grads = [
            jnp.where(m, part[0], swap(part[1])),
            jnp.where(m, part[2], swap(part[3])),
            jnp.where(m, swap(part[0] + part[1]), part[2] + part[3]),
        ]
        for p in range(3):
            turned = grads[p] * cos_s + swap_halves(grads[p] * sin_s)
            v = raw[at, p * 128 : (p + 1) * 128]
            gain = g_q[...] if p < 2 else g_k[...]
            r = lax.rsqrt(head_mean(v * v) + EPSILON)
            weighted = turned * gain
            grad = r * weighted - v * (r * r * r) * head_mean(weighted * v)
            low[at, p * 128 : (p + 1) * 128] = grad.astype(BF16)
            term = jnp.sum(turned * v * r, axis=0, keepdims=True)
            if p < 2:
                gq_sum = gq_sum + term
            else:
                gk_sum = gk_sum + term
        a, b = vals[0] + vals[1], vals[2] + vals[3]
        grad_v = jnp.concatenate([jnp.where(mh, a, swap(b)), jnp.where(mh, swap(a), b)], 0)
        low[at, 3 * 128 :] = grad_v.astype(BF16)
        grad_h = nt(low[at, :], w[...])
        gh[s] = grad_h.astype(BF16)
        if k:
            along_x(gh, gh_parts, ss_h, rs_h, s, x).start()
        term = jnp.sum(grad_h * h[at, :].astype(F32), axis=0, keepdims=True)
        attn[...] = term if n == 0 else attn[...] + term
        if n == 0:
            to_sibling(2).wait()

            def send_o(k, carry):
                t = lax.rem(ctx + k, 16)
                both = dwo[c, t].astype(F32) + sibling_dwo[t].astype(F32)
                reduced_o[t] = both.astype(BF16)
                over_ctx(2, t, ctx).start()
                return carry

            lax.fori_loop(1, 16, send_o, 0)
    for i in range(8):
        cols = slice(i * 128, i * 128 + 128)
        gains[i : i + 1, :] = attn[:, cols] / g_attn[:, cols]
        gains[8 + i : 9 + i, :] = gain_ffn[:, cols]
    gains[16:, :] = jnp.concatenate([gq_sum, gk_sum, jnp.zeros((6, 2 * HD), F32)], 0)
    grad_w = tn(h[...], low[...]).astype(BF16)
    for i in range(32):
        dw[i % 2, i // 2, :, :] = grad_w[i * 32 : (i + 1) * 32, :]
    to_sibling(0).start()
    to_sibling(1).start()
    to_sibling(1).wait()
    gains[...] = gains[...] + sibling_gains[...]
    to_sibling(0).wait()

    def send(k, carry):
        t = lax.rem(ctx + k, 16)
        reduced[t] = (dw[c, t].astype(F32) + sibling_dw[t].astype(F32)).astype(BF16)
        over_ctx(0, t, ctx).start()
        over_ctx(1, t, ctx).start()
        return carry

    lax.fori_loop(1, 16, send, 0)
    total = dw[c, ctx].astype(F32) + sibling_dw[ctx].astype(F32)
    total_o = dwo[c, ctx].astype(F32) + sibling_dwo[ctx].astype(F32)
    all_gains = gains[...]

    grad_h = gh[x].astype(F32)
    for k in (1, 3, 2):
        t = lax.rem(x + k, NX)
        along_x(gh, gh_parts, ss_h, rs_h, t, t).wait_recv()
        grad_h = grad_h + gh_parts[t].astype(F32)
    inputs = tokens[...].astype(F32)
    r = lax.rsqrt(jnp.mean(inputs * inputs, axis=-1, keepdims=True) + EPSILON)
    weighted = grad_h * g_attn[...]
    inner = jnp.mean(weighted * inputs, axis=-1, keepdims=True)
    tokens_o[...] = (
        grad_middle[...] + r * weighted - inputs * (r * r * r) * inner
    ).astype(BF16)
    out = middle[...] + result[x].astype(F32)
    for k in (1, 3, 2):
        t = lax.rem(x + k, NX)
        along_x(result, result_parts, ss_r, rs_r, t, t).wait_recv()
        out = out + result_parts[t].astype(F32)
    out_o[...] = out.astype(BF16)

    def collect(k, carry):
        t = lax.rem(ctx + k, 16)
        over_ctx(0, t, t).wait_recv()
        over_ctx(1, t, t).wait_recv()
        over_ctx(2, t, t).wait_recv()
        return (
            carry[0] + dw_parts[t].astype(F32),
            carry[1] + gains_all[t],
            carry[2] + dwo_parts[t].astype(F32),
        )

    total, all_gains, total_o = lax.fori_loop(1, 16, collect, (total, all_gains, total_o))
    qkv_o[...] = total.astype(BF16)
    wo_o[...] = total_o.astype(BF16)
    gains_o[...] = all_gains

    def drain(k, carry):
        t = lax.rem(ctx + k, 16)
        over_ctx(0, t, ctx).wait_send()
        over_ctx(1, t, ctx).wait_send()
        over_ctx(2, t, ctx).wait_send()
        return carry

    lax.fori_loop(1, 16, drain, 0)
    for k in (1, 3, 2):
        t = lax.rem(x + k, NX)
        along_x(gh, gh_parts, ss_h, rs_h, t, x).wait_send()
        along_x(result, result_parts, ss_r, rs_r, t, x).wait_send()


def project_back(number, *operands):
    vmem = pl.BlockSpec(memory_space=pltpu.VMEM)
    tokens = (NX, ROWS, D)
    wide = QX + 2 * KX
    return pl.pallas_call(
        project_back_kernel,
        in_specs=[vmem] * 16,
        out_specs=[vmem] * 5,
        out_shape=[
            jax.ShapeDtypeStruct((ROWS, D), BF16),
            jax.ShapeDtypeStruct((ROWS, D), BF16),
            jax.ShapeDtypeStruct((32, QX + 2 * KX), BF16),
            jax.ShapeDtypeStruct((32, QX), BF16),
            jax.ShapeDtypeStruct((24, 2 * HD), F32),
        ],
        scratch_shapes=[
            pltpu.VMEM((NX * ROWS, QX + 2 * KX), BF16),
            pltpu.VMEM((1, D), F32),
            pltpu.VMEM(tokens, BF16),
            pltpu.VMEM(tokens, BF16),
            pltpu.VMEM(tokens, BF16),
            pltpu.VMEM((2, 16, 32, wide), BF16),
            pltpu.VMEM((16, 32, wide), BF16),
            pltpu.VMEM((16, 32, wide), BF16),
            pltpu.VMEM((16, 32, wide), BF16),
            pltpu.VMEM((24, 2 * HD), F32),
            pltpu.VMEM((24, 2 * HD), F32),
            pltpu.VMEM((16, 24, 2 * HD), F32),
            pltpu.VMEM((2, 16, 32, QX), BF16),
            pltpu.VMEM((16, 32, QX), BF16),
            pltpu.VMEM((16, 32, QX), BF16),
            pltpu.VMEM((16, 32, QX), BF16),
        ]
        + [pltpu.SemaphoreType.DMA((n,)) for n in (NX, NX, NX, NX, 3, 3) + (16,) * 6],
        compiler_params=pltpu.CompilerParams(
            collective_id=number, has_side_effects=True, vmem_limit_bytes=VMEM_BYTES
        ),
        name="project_back",
    )(*operands)


def hand_out_kernel(qkv, gu, wo, wd, gains, q_o, k_o, v_o, o_o, g_o, u_o, d_o, ga_o, gf_o, gh_o):
    for s in range(NX):
        q_o[:, s * QX : (s + 1) * QX] = qkv[s, :, :QX].astype(F32)
        k_o[:, s * KX : (s + 1) * KX] = qkv[s, :, QX : QX + KX].astype(F32)
        v_o[:, s * KX : (s + 1) * KX] = qkv[s, :, QX + KX :].astype(F32)
        g_o[:, s * FX : (s + 1) * FX] = gu[s, :, :FX].astype(F32)
        u_o[:, s * FX : (s + 1) * FX] = gu[s, :, FX:].astype(F32)
        o_o[:, s * 256 : (s + 1) * 256] = wo[s, :, :].astype(F32)
        for rg in range(9):
            for l in range(2):
                at = slice(s * 256 + l * 128, s * 256 + l * 128 + 128)
                d_o[rg * 16 : rg * 16 + 16, at] = wd[
                    s, l * 16 : l * 16 + 16, rg * 128 : rg * 128 + 128
                ].astype(F32)
    total = gains[0] + gains[1] + gains[2] + gains[3]
    for i in range(8):
        ga_o[:, i * 128 : i * 128 + 128] = total[i : i + 1, :]
        gf_o[:, i * 128 : i * 128 + 128] = total[8 + i : 9 + i, :]
    gh_o[...] = total[16:, :] + swap(total[16:, :])


def hand_out(*operands):
    vmem = pl.BlockSpec(memory_space=pltpu.VMEM)
    shapes = [(32, D), (32, KV * HD), (32, KV * HD), (32, D), (32, FF), (32, FF), (FF // 32, D)]
    shapes += [(1, D), (1, D), (8, 2 * HD)]
    return pl.pallas_call(
        hand_out_kernel,
        in_specs=[vmem] * 5,
        out_specs=[vmem] * 10,
        out_shape=[jax.ShapeDtypeStruct(s, F32) for s in shapes],
        compiler_params=pltpu.CompilerParams(vmem_limit_bytes=VMEM_BYTES),
        name="hand_out",
    )(*operands)


def angle_constants():
    frequencies = ROPE_BASE ** (-np.arange(0, HD // 2, dtype=np.float64) * 2.0 / HD)
    phases = np.arange(LEN, dtype=np.float64)[:, None] * frequencies[None, :]
    cos, sin = np.cos(phases).astype(np.float32), np.sin(phases).astype(np.float32)
    return np.concatenate([cos] * 4, 1), np.concatenate([-sin, sin, -sin, sin], 1)


def columns_of(w, x, width):
    return lax.dynamic_slice_in_dim(w, x * width, width, axis=1)


def by_tiles(blocks):
    return blocks.reshape(-1, 9, 16, 2, 128).transpose(0, 3, 2, 1, 4).reshape(-1, 32, FX)


def body(
    tokens,
    pairs,
    w_query,
    w_key,
    w_value,
    w_out,
    w_gate,
    w_up,
    w_down,
    g_attn,
    g_query,
    g_key,
    g_ffn,
    cotangent,
):
    x = lax.axis_index("seq")
    cos_np, sin_np = angle_constants()
    cos_t, sin_t = jnp.asarray(cos_np), jnp.asarray(sin_np)
    gq2 = jnp.concatenate([g_query, g_query])[None]
    gk2 = jnp.concatenate([g_key, g_key])[None]

    swap_xz = [(a * 4 + b, b * 4 + a) for a in range(4) for b in range(4)]
    down_part = lax.ppermute(columns_of(w_down, x, D // 4), ("seq", "ctx_0"), swap_xz)
    mine = jnp.concatenate(
        [w_out, columns_of(w_gate, x, FX), columns_of(w_up, x, FX), by_tiles(down_part[None])[0]],
        axis=1,
    )

    wide = lax.all_gather(mine, CTX_FSDP, axis=0, tiled=True)
    h_all, w_qkv, pair = gather_in(1, tokens[0], g_attn[None], w_query, w_key, w_value, pairs)
    h_all = h_all.reshape(NX * ROWS, D)
    w_qkv = w_qkv.reshape(D, QX + 2 * KX)
    pair = pair.reshape(NX * 8, 128)

    send, raw, cos_r, sin_r = project(pair, h_all, w_qkv, cos_t, sin_t, gq2, gk2)
    recv, cot_all = exchange(2, "to_heads", ("c", "a2a", send), ("x", "ag", cotangent[0]))
    heads_out, q_s, k_s, v_s, o_t, inv = attend(pair, recv)
    (mixed_parts,) = exchange(3, "to_tokens", ("t", "a2a", heads_out))
    middle, result4, grad_w_ffn, grad_middle, grad_branch, mixed, back_parts, gain_ffn = middle_part(
        4, mixed_parts, tokens[0], cot_all, g_ffn[None], wide
    )
    sums = lax.psum_scatter(grad_w_ffn, CTX, scatter_dimension=0, tiled=True)
    (recv_g,) = exchange(6, "to_heads_back", ("r", "a2a", back_parts))
    sends_back = attend_back(pair, recv_g, q_s, k_s, v_s, o_t, inv)
    recv_back, branch_x, mixed_x = exchange(
        7,
        "to_tokens_back",
        ("c", "a2a", sends_back),
        ("x", "ag", grad_branch),
        ("x", "a2a", mixed),
    )
    output, grad_tokens, sum_qkv, sum_o, gains = project_back(
        8,
        recv_back,
        raw,
        h_all,
        w_qkv,
        cos_r,
        sin_r,
        gq2,
        gk2,
        g_attn[None],
        mixed_x,
        branch_x,
        result4,
        gain_ffn,
        tokens[0],
        grad_middle,
        middle,
    )
    qkv, gate_up, out_rows, down_rows, gains = exchange(
        9,
        "gather_out",
        ("x", "ag", sum_qkv),
        ("x", "ag", sums, (0, 2 * FX)),
        ("d", "ag", sum_o),
        ("d", "ag", sums, (2 * FX, FX)),
        ("x", "ag", gains),
    )
    *weights, gain_a, gain_f, gain_h = hand_out(qkv, gate_up, out_rows, down_rows, gains)
    return (
        output[None],
        grad_tokens[None],
        *weights,
        gain_a[0],
        gain_h[0, :HD],
        gain_h[1, :HD],
        gain_f[0],
    )


def solution(mesh):
    finer = Mesh(
        mesh.devices.reshape(mesh.shape["seq"], 4, 4, mesh.shape["fsdp"]),
        ("seq", "ctx_0", "ctx_1", "fsdp"),
    )
    tokens_spec = P(("seq", "fsdp"), CTX, None)
    rows_spec = P(CTX_FSDP, None)
    return jax.shard_map(
        body,
        mesh=finer,
        in_specs=(tokens_spec, P(("seq", "fsdp"), None))
        + (rows_spec,) * 7
        + (P(),) * 4
        + (tokens_spec,),
        out_specs=(tokens_spec, tokens_spec) + (rows_spec,) * 7 + (P(),) * 4,
        check_vma=False,
    )
```

```python
import functools

import jax
import jax.numpy as jnp
import numpy as np
from jax import lax
from jax.experimental import pallas as pl
from jax.experimental.pallas import tpu as pltpu
from jax.sharding import Mesh
from jax.sharding import PartitionSpec as P

D = 1024
H = 16
KV = 8
HD = 64
FF = 4608
LEN = 2560
BLK = 80
ROWS = 2 * BLK
NX = 4
FX = FF // NX
QX = H * HD // NX
KX = KV * HD // NX
TILE = 512
N_TILES = LEN // TILE
CTX = ("ctx_0", "ctx_1")
CTX_FSDP = ("ctx_0", "ctx_1", "fsdp")
SEQ_CTX_FSDP = ("seq", "ctx_0", "ctx_1", "fsdp")
EPSILON = 1e-05
ROPE_BASE = 1000000.0
MESH = pl.DeviceIdType.MESH
BF16 = jnp.bfloat16
F32 = jnp.float32
VMEM_BYTES = 56 * 1024 * 1024


SIZE = {"x": 4, "c": 16, "p": 32, "t": 16, "r": 16, "d": 4}


def coords():
    return tuple(lax.axis_index(a) for a in SEQ_CTX_FSDP)


def twisted(x, v):
    return lax.rem(v + 2 * (1 - lax.rem(x, 2)) * (1 - lax.rem(v, 2)), 4)


def sequence_at(x, z):
    return lax.rem(x + twisted(x, z), 4)


def place_of(x, s):
    return twisted(x, lax.rem(s - x + 4, 4))


def target(group, t):
    s, z, y, c = coords()
    if group == "x":
        return (t, z, y, c), s
    if group == "c":
        return (s, t // 4, lax.rem(t, 4), c), z * 4 + y
    if group == "p":
        return (s, t // 8, lax.rem(t // 2, 4), lax.rem(t, 2)), (z * 4 + y) * 2 + c
    if group == "t":
        return (sequence_at(s, z), t // 4, lax.rem(t, 4), c), s * 4 + y
    if group == "d":
        return (t, s, y, c), z
    return (t // 4, place_of(t // 4, s), lax.rem(t, 4), c), z * 4 + y


def source(group, t):
    s, z, y, c = coords()
    if group == "t":
        return (t // 4, place_of(t // 4, s), lax.rem(t, 4), c)
    if group == "r":
        return (sequence_at(s, z), t // 4, lax.rem(t, 4), c)
    if group == "d":
        return (z, t, y, c)
    return target(group, t)[0]


def own(group):
    s, z, y, c = coords()
    if group == "t":
        return sequence_at(s, z) == s, z * 4 + y, s * 4 + y
    if group == "r":
        return sequence_at(s, z) == s, s * 4 + y, z * 4 + y
    if group == "d":
        return s == z, s, z
    me = target(group, 0)[1]
    return None, me, me


def exchange_kernel(items, *refs):
    n = len(items)
    srcs, outs, sems = refs[:n], refs[n : 2 * n], refs[2 * n :]
    barrier = pltpu.get_barrier_semaphore()
    expected = 0
    starts = []
    for i, (g, _, _) in enumerate(items):
        has_own, sent, _ = own(g)
        size = SIZE[g]
        if has_own is None:
            starts.append((jnp.int32(1), sent))
            expected = expected + size - 1
        else:
            starts.append((has_own.astype(jnp.int32), sent))
            expected = expected + size - has_own.astype(jnp.int32)
        place = own(g)[2]
        first = starts[i][0]

        def greet(k, carry, g=g, size=size, place=place):
            dev = source(g, lax.rem(place + k, size))
            pl.semaphore_signal(barrier, inc=1, device_id=dev, device_id_type=MESH)
            return carry

        lax.fori_loop(first, size, greet, 0)

    def block_of(i, t):
        _, mode, cols = items[i]
        if cols is not None:
            return srcs[i].at[:, pl.ds(*cols)]
        return srcs[i] if mode == "ag" else srcs[i].at[t]

    def own_copy(i):
        g = items[i][0]
        _, sent, place = own(g)
        src = block_of(i, sent)
        return pltpu.make_async_copy(src, outs[i].at[place], sems[3 * i + 2])

    for i, (g, _, _) in enumerate(items):
        if own(g)[0] is None:
            own_copy(i).start()
        else:
            pl.when(own(g)[0])(lambda i=i: own_copy(i).start())
    pl.semaphore_wait(barrier, expected)

    def remote(i, t, place):
        g = items[i][0]
        dev, there = target(g, t)
        src = block_of(i, t)
        return pltpu.make_async_remote_copy(
            src_ref=src,
            dst_ref=outs[i].at[there if place is None else place],
            send_sem=sems[3 * i].at[t],
            recv_sem=sems[3 * i + 1].at[there if place is None else place],
            device_id=dev,
            device_id_type=MESH,
        )

    for i, (g, _, _) in enumerate(items):
        first, sent = starts[i]

        def send(k, carry, i=i, g=g, sent=sent):
            remote(i, lax.rem(sent + k, SIZE[g]), None).start()
            return carry

        lax.fori_loop(first, SIZE[g], send, 0)
    for i, (g, _, _) in enumerate(items):
        first, sent = starts[i]
        place = own(g)[2]

        def drain(k, carry, i=i, g=g, sent=sent, place=place):
            remote(i, lax.rem(sent + k, SIZE[g]), None).wait_send()
            remote(i, lax.rem(sent + k, SIZE[g]), lax.rem(place + k, SIZE[g])).wait_recv()
            return carry

        lax.fori_loop(first, SIZE[g], drain, 0)
        if own(g)[0] is None:
            own_copy(i).wait()
        else:
            pl.when(own(g)[0])(lambda i=i: own_copy(i).wait())


def exchange(number, name, *parts):
    items = tuple((part[0], part[1], part[3] if len(part) > 3 else None) for part in parts)
    arrays = [part[2] for part in parts]
    outs = []
    for (g, m, cols), a in zip(items, arrays):
        shape = a.shape if m == "ag" else a.shape[1:]
        shape = shape if cols is None else shape[:-1] + (cols[1],)
        outs.append(jax.ShapeDtypeStruct((SIZE[g],) + shape, a.dtype))
    scratch = []
    for g, _, _ in items:
        scratch += [
            pltpu.SemaphoreType.DMA((SIZE[g],)),
            pltpu.SemaphoreType.DMA((SIZE[g],)),
            pltpu.SemaphoreType.DMA,
        ]
    return pl.pallas_call(
        functools.partial(exchange_kernel, items),
        out_shape=outs,
        in_specs=[pl.BlockSpec(memory_space=pl.ANY)] * len(arrays),
        out_specs=[pl.BlockSpec(memory_space=pl.ANY)] * len(arrays),
        scratch_shapes=scratch,
        compiler_params=pltpu.CompilerParams(collective_id=number, has_side_effects=True),
        name=name,
    )(*arrays)


def lanes(shape):
    return lax.broadcasted_iota(jnp.int32, shape, len(shape) - 1)


def low_half(shape):
    return lanes(shape) < HD


def swap(v):
    return pltpu.roll(v, HD, 1)


def swap_halves(v):
    first = lax.rem(lanes(v.shape), HD) < HD // 2
    return jnp.where(first, pltpu.roll(v, 2 * HD - HD // 2, 1), pltpu.roll(v, HD // 2, 1))


def head_mean(v):
    m = low_half(v.shape)
    a = jnp.sum(jnp.where(m, v, 0.0), axis=-1, keepdims=True)
    b = jnp.sum(jnp.where(m, 0.0, v), axis=-1, keepdims=True)
    return jnp.where(m, a, b) * (1.0 / HD)


def nt(a, b):
    return lax.dot_general(a, b, (((1,), (1,)), ((), ())), preferred_element_type=F32)


def nn(a, b):
    return lax.dot_general(a, b, (((1,), (0,)), ((), ())), preferred_element_type=F32)


def tn(a, b):
    return lax.dot_general(a, b, (((0,), (0,)), ((), ())), preferred_element_type=F32)


def my_pairs(pairs):
    x, z, _, _ = coords()
    line = sequence_at(x, z) * 8
    return [pairs[line, j] for j in range(16)]


def rows_of(block):
    return pl.ds(pl.multiple_of(block * BLK, 16), BLK)


def rope_rows(block, table):
    return jnp.concatenate([table[rows_of(block), :], table[rows_of(31 - block), :]], 0)


def gather_in_kernel(
    tokens,
    g_attn,
    w_q,
    w_k,
    w_v,
    pairs,
    h_o,
    w_o,
    pairs_o,
    h,
    w,
    row,
    ss_h,
    rs_h,
    ss_p,
    rs_p,
    ss_w,
    rs_w,
    ss_f,
    rs_f,
    own_sem,
):
    x, z, y, c = coords()
    ctx = z * 4 + y
    barrier = pltpu.get_barrier_semaphore()
    for k in range(1, NX):
        pl.semaphore_signal(
            barrier, inc=1, device_id=(lax.rem(x + k, NX), z, y, c), device_id_type=MESH
        )
    pl.semaphore_signal(barrier, inc=1, device_id=(x, z, y, 1 - c), device_id_type=MESH)

    def greet(k, carry):
        t = lax.rem(ctx + k, 16)
        dev = (x, t // 4, lax.rem(t, 4), c)
        pl.semaphore_signal(barrier, inc=1, device_id=dev, device_id_type=MESH)
        return carry

    lax.fori_loop(1, 16, greet, 0)
    w[:, :QX] = w_q[:, pl.ds(pl.multiple_of(x * QX, QX), QX)]
    w[:, QX : QX + KX] = w_k[:, pl.ds(pl.multiple_of(x * KX, KX), KX)]
    w[:, QX + KX :] = w_v[:, pl.ds(pl.multiple_of(x * KX, KX), KX)]
    row[...] = jnp.zeros_like(row)
    row[0:1, :16] = pairs[...]
    inputs = tokens[...].astype(F32)
    inv_rms = lax.rsqrt(jnp.mean(inputs * inputs, axis=-1, keepdims=True) + EPSILON)
    h[...] = (inputs * inv_rms * g_attn[...]).astype(BF16)

    def along_x(src, dst, ss, rs, t, place):
        return pltpu.make_async_remote_copy(
            src_ref=src,
            dst_ref=dst.at[place],
            send_sem=ss.at[t],
            recv_sem=rs.at[place],
            device_id=(t, z, y, c),
            device_id_type=MESH,
        )

    def over_ctx(t, place):
        return pltpu.make_async_remote_copy(
            src_ref=w,
            dst_ref=w_o.at[place * 2 + c],
            send_sem=ss_w.at[t],
            recv_sem=rs_w.at[place],
            device_id=(x, t // 4, lax.rem(t, 4), c),
            device_id_type=MESH,
        )

    def to_sibling(t, core, src):
        return pltpu.make_async_remote_copy(
            src_ref=src,
            dst_ref=w_o.at[t * 2 + core],
            send_sem=ss_f.at[t],
            recv_sem=rs_f.at[t],
            device_id=(x, z, y, 1 - c),
            device_id_type=MESH,
        )

    mine = [
        pltpu.make_async_copy(h, h_o.at[x], own_sem.at[0]),
        pltpu.make_async_copy(row, pairs_o.at[x], own_sem.at[1]),
        pltpu.make_async_copy(w, w_o.at[ctx * 2 + c], own_sem.at[2]),
    ]
    for copy in mine:
        copy.start()
    pl.semaphore_wait(barrier, NX + 15)
    for k in (1, 3, 2):
        t = lax.rem(x + k, NX)
        along_x(h, h_o, ss_h, rs_h, t, x).start()
        along_x(row, pairs_o, ss_p, rs_p, t, x).start()

    def send(k, carry):
        over_ctx(lax.rem(ctx + k, 16), ctx).start()
        return carry

    lax.fori_loop(1, 16, send, 0)
    to_sibling(ctx, c, w).start()

    def forward(k, carry):
        t = lax.rem(ctx + k, 16)
        over_ctx(t, t).wait_recv()
        to_sibling(t, c, w_o.at[t * 2 + c]).start()
        return carry

    lax.fori_loop(1, 16, forward, 0)

    def drain(k, carry):
        t = lax.rem(ctx + k, 16)
        to_sibling(t, 1 - c, w).wait_recv()
        to_sibling(t, c, w).wait_send()
        return carry

    lax.fori_loop(0, 16, drain, 0)

    def drain_ctx(k, carry):
        over_ctx(lax.rem(ctx + k, 16), ctx).wait_send()
        return carry

    lax.fori_loop(1, 16, drain_ctx, 0)
    for k in (1, 3, 2):
        t = lax.rem(x + k, NX)
        along_x(h, h_o, ss_h, rs_h, t, x).wait_send()
        along_x(row, pairs_o, ss_p, rs_p, t, x).wait_send()
        along_x(h, h_o, ss_h, rs_h, t, t).wait_recv()
        along_x(row, pairs_o, ss_p, rs_p, t, t).wait_recv()
    for copy in mine:
        copy.wait()


def gather_in(number, *operands):
    wide = QX + 2 * KX
    return pl.pallas_call(
        gather_in_kernel,
        in_specs=[pl.BlockSpec(memory_space=pltpu.VMEM)] * 6,
        out_specs=[pl.BlockSpec(memory_space=pl.ANY)] * 3,
        out_shape=[
            jax.ShapeDtypeStruct((NX, ROWS, D), BF16),
            jax.ShapeDtypeStruct((32, 32, wide), BF16),
            jax.ShapeDtypeStruct((NX, 8, 128), jnp.int32),
        ],
        scratch_shapes=[
            pltpu.VMEM((ROWS, D), BF16),
            pltpu.VMEM((32, wide), BF16),
            pltpu.VMEM((8, 128), jnp.int32),
        ]
        + [pltpu.SemaphoreType.DMA((n,)) for n in (NX, NX, NX, NX, 16, 16, 16, 16, 3)],
        compiler_params=pltpu.CompilerParams(collective_id=number, has_side_effects=True),
        name="gather_in",
    )(*operands)


def project_kernel(pairs, h, w, cos_t, sin_t, g_q, g_k, send, raw, cos_o, sin_o, acc):
    x, z, y, _ = coords()
    acc[...] = nn(h[...], w[...])
    m = low_half((ROWS, 2 * HD))
    mh = low_half((BLK, 2 * HD))
    for s in range(NX):
        at = slice(s * ROWS, (s + 1) * ROWS)
        cos_r, sin_r = (rope_rows(pairs[s * 8, z * 4 + y], table) for table in (cos_t, sin_t))
        cos_o[at, :], sin_o[at, :] = cos_r, sin_r
        raw[at, :] = acc[at, : QX + KX]
        turned = []
        for p in range(3):
            v = acc[at, p * 128 : (p + 1) * 128]
            gain = g_q[...] if p < 2 else g_k[...]
            normed = v * lax.rsqrt(head_mean(v * v) + EPSILON) * gain
            turned.append(normed * cos_r + swap_halves(normed) * sin_r)
        keys = turned[2]
        swapped_keys = swap(keys)
        values = acc[at, 3 * 128 :]
        top, bottom = values[:BLK], values[BLK:]
        packed = (jnp.where(mh, top, swap(bottom)), jnp.where(mh, swap(top), bottom))
        for hh in range(4):
            q = turned[hh // 2]
            q = q if hh % 2 == 0 else swap(q)
            k = swapped_keys if hh < 2 else keys
            send[place_of(x, s) * 4 + hh, :ROWS, :] = jnp.where(m, q, k).astype(BF16)
            send[place_of(x, s) * 4 + hh, ROWS:, :] = packed[hh // 2].astype(BF16)


def project(pairs, h, w, cos_t, sin_t, g_q, g_k):
    return pl.pallas_call(
        project_kernel,
        grid_spec=pltpu.PrefetchScalarGridSpec(
            num_scalar_prefetch=1,
            in_specs=[pl.BlockSpec(memory_space=pltpu.VMEM)] * 6,
            out_specs=[pl.BlockSpec(memory_space=pltpu.VMEM)] * 4,
            scratch_shapes=[pltpu.VMEM((NX * ROWS, QX + 2 * KX), F32)],
        ),
        out_shape=[
            jax.ShapeDtypeStruct((16, ROWS + BLK, 2 * HD), BF16),
            jax.ShapeDtypeStruct((NX * ROWS, QX + KX), F32),
            jax.ShapeDtypeStruct((NX * ROWS, 2 * HD), F32),
            jax.ShapeDtypeStruct((NX * ROWS, 2 * HD), F32),
        ],
        compiler_params=pltpu.CompilerParams(vmem_limit_bytes=VMEM_BYTES),
        name="project",
    )(pairs, h, w, cos_t, sin_t, g_q, g_k)


def attend_kernel(pairs, recv, out, q_s, k_s, v_s, o_t, inv, o_s, v_t):
    m = low_half((BLK, 2 * HD))
    pair = my_pairs(pairs)
    for j in range(16):
        packed = recv[j, ROWS:, :].astype(F32)
        for half in range(2):
            block = pair[j] if half == 0 else 31 - pair[j]
            both = recv[j, half * BLK : (half + 1) * BLK, :].astype(F32)
            vals = packed if half == 0 else swap(packed)
            q_s[rows_of(block), :] = jnp.where(m, both * HD**-0.5, 0.0).astype(BF16)
            k_s[rows_of(block), :] = jnp.where(m, swap(both), 0.0).astype(BF16)
            v_s[rows_of(block), :] = jnp.where(m, vals, 0.0).astype(BF16)
    for t in range(N_TILES):
        at = slice(t * TILE, (t + 1) * TILE)
        v_t[:, at] = v_s[at, :].T[:HD]
    causal = lax.broadcasted_iota(jnp.int32, (TILE, TILE), 0) <= lanes((TILE, TILE))
    for i in range(N_TILES):
        at = slice(i * TILE, (i + 1) * TILE)
        q = q_s[at, :]

        e = jnp.where(causal, jnp.exp(nt(k_s[at, :], q)), 0.0)
        first = (jnp.sum(e, axis=0, keepdims=True), nn(v_t[:, at], e.astype(BF16)))

        def step(t, carry, q=q):
            total, acc = carry
            there = pl.ds(pl.multiple_of(t * TILE, TILE), TILE)
            e = jnp.exp(nt(k_s[there, :], q))
            total = total + jnp.sum(e, axis=0, keepdims=True)
            return total, acc + nn(v_t[:, there], e.astype(BF16))

        total, acc = lax.fori_loop(0, i, step, first) if i else first
        over = 1.0 / total
        attended = acc * over
        o_t[:, at] = attended
        inv[:, at] = jnp.broadcast_to(over, (8, TILE))
        o_s[at, :] = jnp.concatenate([attended, jnp.zeros_like(attended)], 0).T
    for j in range(16):
        low_rows = o_s[rows_of(pair[j]), :]
        high_rows = o_s[rows_of(31 - pair[j]), :]
        out[j, :, :] = (low_rows + swap(high_rows)).astype(BF16)


def attend(pairs, recv):
    wide = jax.ShapeDtypeStruct((LEN, 2 * HD), BF16)
    return pl.pallas_call(
        attend_kernel,
        grid_spec=pltpu.PrefetchScalarGridSpec(
            num_scalar_prefetch=1,
            in_specs=[pl.BlockSpec(memory_space=pltpu.VMEM)],
            out_specs=[pl.BlockSpec(memory_space=pltpu.VMEM)] * 6,
            scratch_shapes=[pltpu.VMEM((LEN, 2 * HD), F32), pltpu.VMEM((HD, LEN), BF16)],
        ),
        out_shape=[
            jax.ShapeDtypeStruct((16, BLK, 2 * HD), BF16),
            wide,
            wide,
            wide,
            jax.ShapeDtypeStruct((HD, LEN), F32),
            jax.ShapeDtypeStruct((8, LEN), F32),
        ],
        compiler_params=pltpu.CompilerParams(vmem_limit_bytes=VMEM_BYTES),
        name="attend",
    )(pairs, recv)


def attend_back_kernel(pairs, recv, q_s, k_s, v_s, o_t, inv, out, g_s, k_t, delta, dq_t, dk_s, dv_s):
    m = low_half((BLK, 2 * HD))
    pair = my_pairs(pairs)
    for j in range(16):
        packed = recv[j, :, :].astype(F32)
        g_s[rows_of(pair[j]), :] = jnp.where(m, packed, 0.0).astype(BF16)
        g_s[rows_of(31 - pair[j]), :] = jnp.where(m, swap(packed), 0.0).astype(BF16)
    for t in range(N_TILES):
        at = slice(t * TILE, (t + 1) * TILE)
        k_t[:, at] = k_s[at, :].T[:HD]
        g_t = g_s[at, :].astype(F32).T[:HD]
        row = jnp.sum(g_t * o_t[:, at], axis=0, keepdims=True)
        delta[:, at] = jnp.broadcast_to(row, (8, TILE))
    dq_t[...] = jnp.zeros_like(dq_t)
    causal = lax.broadcasted_iota(jnp.int32, (TILE, TILE), 0) <= lanes((TILE, TILE))
    for i in range(N_TILES):
        at = slice(i * TILE, (i + 1) * TILE)
        k, v, kt = k_s[at, :], v_s[at, :], k_t[:, at]

        def pair_of_tiles(there, masked, k=k, v=v, kt=kt):
            q, g = q_s[there, :], g_s[there, :]
            e = jnp.exp(nt(k, q))
            if masked:
                e = jnp.where(causal, e, 0.0)
            probs = e * inv[0:1, there]
            ds = (probs * (nt(v, g) - delta[0:1, there])).astype(BF16)
            dq_t[:, there] = dq_t[:, there] + nn(kt, ds)
            return nn(ds, q), nn(probs.astype(BF16), g)

        first = pair_of_tiles(at, True)

        def step(t, carry, pair_of_tiles=pair_of_tiles):
            dk, dv = pair_of_tiles(pl.ds(pl.multiple_of(t * TILE, TILE), TILE), False)
            return carry[0] + dk, carry[1] + dv

        dk, dv = lax.fori_loop(i + 1, N_TILES, step, first) if i + 1 < N_TILES else first
        dk_s[at, :] = dk
        dv_s[at, :] = dv
    for i in range(N_TILES):
        at = slice(i * TILE, (i + 1) * TILE)
        dq = dq_t[:, at] * HD**-0.5
        dk_s[at, :] = jnp.concatenate([dq, jnp.zeros_like(dq)], 0).T + swap(dk_s[at, :])
    for j in range(16):
        for half in range(2):
            block = pair[j] if half == 0 else 31 - pair[j]
            out[j, half * BLK : (half + 1) * BLK, :] = dk_s[rows_of(block), :].astype(BF16)
        out[j, ROWS:, :] = (dv_s[rows_of(pair[j]), :] + swap(dv_s[rows_of(31 - pair[j]), :])).astype(BF16)


def attend_back(pairs, recv, q_s, k_s, v_s, o_t, inv):
    return pl.pallas_call(
        attend_back_kernel,
        grid_spec=pltpu.PrefetchScalarGridSpec(
            num_scalar_prefetch=1,
            in_specs=[pl.BlockSpec(memory_space=pltpu.VMEM)] * 6,
            out_specs=pl.BlockSpec(memory_space=pltpu.VMEM),
            scratch_shapes=[
                pltpu.VMEM((LEN, 2 * HD), BF16),
                pltpu.VMEM((HD, LEN), BF16),
                pltpu.VMEM((8, LEN), F32),
                pltpu.VMEM((HD, LEN), F32),
                pltpu.VMEM((LEN, 2 * HD), F32),
                pltpu.VMEM((LEN, 2 * HD), F32),
            ],
        ),
        out_shape=jax.ShapeDtypeStruct((16, ROWS + BLK, 2 * HD), BF16),
        compiler_params=pltpu.CompilerParams(vmem_limit_bytes=VMEM_BYTES),
        name="attend_back",
    )(pairs, recv, q_s, k_s, v_s, o_t, inv)


def middle_kernel(
    parts,
    tokens,
    cot,
    g_ffn,
    wide,
    mid_o,
    result_o,
    dw_o,
    gmid_o,
    branch_o,
    mixed_o,
    back_o,
    gain_o,
    w_o,
    w_gu,
    dnp,
    w_dn,
    h_all,
    part,
    gparts,
    gu_s,
    dh_s,
    ggu,
    hid,
    h_t,
    hid_t,
    wsem,
    ss1,
    rs1,
    ss2,
    rs2,
):
    me, z, y, c = coords()
    barrier = pltpu.get_barrier_semaphore()
    for k in range(1, NX):
        pl.semaphore_signal(
            barrier, inc=1, device_id=(lax.rem(me + k, NX), z, y, c), device_id_type=MESH
        )
    loads = [
        pltpu.make_async_copy(wide.at[:, pl.ds(at, width)], there, wsem.at[i])
        for i, (at, width, there) in enumerate(
            ((0, D, w_o), (D, 2 * FX, w_gu), (D + 2 * FX, FX, dnp))
        )
    ]
    for load in loads:
        load.start()
    m = low_half((BLK, 2 * HD))
    for p in range(8):
        a, b = parts[2 * p, :, :].astype(F32), parts[2 * p + 1, :, :].astype(F32)
        at = slice((p % 2) * 128, (p % 2) * 128 + 128)
        mixed_o[p // 2, :BLK, at] = jnp.where(m, a, swap(b)).astype(BF16)
        mixed_o[p // 2, BLK:, at] = jnp.where(m, swap(a), b).astype(BF16)
    loads[0].wait()
    middle = tokens[...].astype(F32)
    for q in range(NX):
        middle = middle + nn(mixed_o[q, :, :], w_o[q * QX : (q + 1) * QX, :])
    mid_o[...] = middle
    r = lax.rsqrt(jnp.mean(middle * middle, axis=-1, keepdims=True) + EPSILON)
    h_all[me] = (middle * r * g_ffn[...]).astype(BF16)
    pl.semaphore_wait(barrier, NX - 1)

    def send_h(t, place):
        return pltpu.make_async_remote_copy(
            src_ref=h_all.at[me],
            dst_ref=h_all.at[place],
            send_sem=ss1.at[t],
            recv_sem=rs1.at[place],
            device_id=(t, z, y, c),
            device_id_type=MESH,
        )

    def send_grad(t, place):
        return pltpu.make_async_remote_copy(
            src_ref=part.at[t],
            dst_ref=gparts.at[place],
            send_sem=ss2.at[t],
            recv_sem=rs2.at[place],
            device_id=(t, z, y, c),
            device_id_type=MESH,
        )

    for k in (1, 3, 2):
        send_h(lax.rem(me + k, NX), me).start()
    loads[1].wait()
    loads[2].wait()
    for o in range(32):
        for rg in range(9):
            for l in range(2):
                row = (o % 8) * 144 + rg * 16
                w_dn[o // 8, row : row + 16, l * 128 : l * 128 + 128] = dnp[
                    o * 32 + l * 16 : o * 32 + l * 16 + 16, rg * 128 : rg * 128 + 128
                ]

    def block(k, carry):
        t = lax.rem(me + k + k // 2 - 2 * (k // 2) * lax.rem(k, 2), NX)

        @pl.when(k > 0)
        def _():
            send_h(t, t).wait_recv()

        rows = pl.ds(pl.multiple_of(t * ROWS, ROWS), ROWS)
        gu_s[...] = nn(h_all[t], w_gu[...])
        cot_t = cot[t]
        grad_hidden = nt(cot_t[:, :256], w_dn[0])
        for q in range(1, NX):
            grad_hidden = grad_hidden + nt(cot_t[:, q * 256 : (q + 1) * 256], w_dn[q])
        dh_s[...] = grad_hidden
        for j in range(FX // 128):
            at, above = slice(j * 128, j * 128 + 128), slice(FX + j * 128, FX + j * 128 + 128)
            gate, up, dh = gu_s[:, at], gu_s[:, above], dh_s[:, at]
            sig = jax.nn.sigmoid(gate)
            silu = gate * sig
            hid[rows, at] = (silu * up).astype(BF16)
            ggu[rows, at] = (dh * up * (sig * (1.0 + gate * (1.0 - sig)))).astype(BF16)
            ggu[rows, above] = (dh * silu).astype(BF16)
        part[t] = nt(ggu[rows, :], w_gu[...]).astype(BF16)

        @pl.when(k > 0)
        def _():
            send_grad(t, me).start()

        hidden = hid[rows, :]
        for q in range(NX):
            result_o[t, :, q * 256 : (q + 1) * 256] = nn(hidden, w_dn[q]).astype(BF16)
        return carry

    lax.fori_loop(0, NX, block, 0)

    h_t[...] = h_all[...].reshape(NX * ROWS, D).T

    def columns(j, carry):
        at = pl.ds(pl.multiple_of(j * 256, 256), 256)
        dw_o[:, at] = nn(h_t[...], ggu[:, at]).astype(BF16)
        return carry

    lax.fori_loop(0, 2 * FX // 256, columns, 0)
    hid_t[...] = hid[...].T
    for q in range(NX):
        cot_q = cot[:, :, q * 256 : (q + 1) * 256].reshape(NX * ROWS, 256)
        grad = nn(hid_t[...], cot_q).astype(BF16)
        for o in range(8):
            for rg in range(9):
                for l in range(2):
                    row, there = o * 144 + rg * 16, (q * 8 + o) * 32 + l * 16
                    dw_o[there : there + 16, 2 * FX + rg * 128 : 2 * FX + rg * 128 + 128] = grad[
                        row : row + 16, l * 128 : l * 128 + 128
                    ]

    grad_h = part[me].astype(F32)
    for k in (1, 3, 2):
        t = lax.rem(me + k, NX)
        send_grad(t, t).wait_recv()
        grad_h = grad_h + gparts[t].astype(F32)
    for k in (1, 3, 2):
        t = lax.rem(me + k, NX)
        send_h(t, me).wait_send()
        send_grad(t, me).wait_send()
    middle = mid_o[...]
    r = lax.rsqrt(jnp.mean(middle * middle, axis=-1, keepdims=True) + EPSILON)
    weighted = grad_h * g_ffn[...]
    inner = jnp.mean(weighted * middle, axis=-1, keepdims=True)
    gain_o[...] = jnp.sum(grad_h * middle * r, axis=0, keepdims=True)
    grad_middle = cot[me].astype(F32) + r * weighted - middle * (r * r * r) * inner
    gmid_o[...] = grad_middle
    branch_o[...] = grad_middle.astype(BF16)
    for q in range(NX):
        grad = nt(branch_o[...], w_o[q * QX : (q + 1) * QX, :]).astype(BF16).astype(F32)
        for p in range(2):
            top, bottom = grad[:BLK, p * 128 : p * 128 + 128], grad[BLK:, p * 128 : p * 128 + 128]
            back_o[4 * q + 2 * p, :, :] = jnp.where(m, top, swap(bottom)).astype(BF16)
            back_o[4 * q + 2 * p + 1, :, :] = jnp.where(m, swap(top), bottom).astype(BF16)


def middle_part(number, parts, tokens, cot, g_ffn, wide):
    vmem = pl.BlockSpec(memory_space=pltpu.VMEM)
    blocks = (NX, ROWS, D)
    return pl.pallas_call(
        middle_kernel,
        in_specs=[vmem] * 4 + [pl.BlockSpec(memory_space=pl.ANY)],
        out_specs=[vmem] * 8,
        out_shape=[
            jax.ShapeDtypeStruct((ROWS, D), F32),
            jax.ShapeDtypeStruct(blocks, BF16),
            jax.ShapeDtypeStruct((D, 3 * FX), BF16),
            jax.ShapeDtypeStruct((ROWS, D), F32),
            jax.ShapeDtypeStruct((ROWS, D), BF16),
            jax.ShapeDtypeStruct((NX, ROWS, QX), BF16),
            jax.ShapeDtypeStruct((16, BLK, 2 * HD), BF16),
            jax.ShapeDtypeStruct((1, D), F32),
        ],
        scratch_shapes=[
            pltpu.VMEM((D, D), BF16),
            pltpu.VMEM((D, 2 * FX), BF16),
            pltpu.VMEM((D, FX), BF16),
            pltpu.VMEM((4, FX, D // 4), BF16),
            pltpu.VMEM(blocks, BF16),
            pltpu.VMEM(blocks, BF16),
            pltpu.VMEM(blocks, BF16),
            pltpu.VMEM((ROWS, 2 * FX), F32),
            pltpu.VMEM((ROWS, FX), F32),
            pltpu.VMEM((NX * ROWS, 2 * FX), BF16),
            pltpu.VMEM((NX * ROWS, FX), BF16),
            pltpu.VMEM((D, NX * ROWS), BF16),
            pltpu.VMEM((FX, NX * ROWS), BF16),
            pltpu.SemaphoreType.DMA((3,)),
            pltpu.SemaphoreType.DMA((NX,)),
            pltpu.SemaphoreType.DMA((NX,)),
            pltpu.SemaphoreType.DMA((NX,)),
            pltpu.SemaphoreType.DMA((NX,)),
        ],
        compiler_params=pltpu.CompilerParams(
            collective_id=number, has_side_effects=True, vmem_limit_bytes=VMEM_BYTES
        ),
        name="middle_part",
    )(parts, tokens, cot, g_ffn, wide)


def project_back_kernel(
    recv,
    raw,
    h,
    w,
    cos_r,
    sin_r,
    g_q,
    g_k,
    g_attn,
    mixed_x,
    branch_x,
    result,
    gain_ffn,
    tokens,
    grad_middle,
    middle,
    out_o,
    tokens_o,
    qkv_o,
    wo_o,
    gains_o,
    low,
    attn,
    gh,
    gh_parts,
    result_parts,
    dw,
    sibling_dw,
    reduced,
    dw_parts,
    gains,
    sibling_gains,
    gains_all,
    dwo,
    sibling_dwo,
    reduced_o,
    dwo_parts,
    ss_r,
    rs_r,
    ss_h,
    rs_h,
    ss_s,
    rs_s,
    ss_w,
    rs_w,
    ss_g,
    rs_g,
    ss_o,
    rs_o,
):
    x, z, y, c = coords()
    ctx = z * 4 + y
    barrier = pltpu.get_barrier_semaphore()
    for k in range(1, NX):
        pl.semaphore_signal(
            barrier, inc=1, device_id=(lax.rem(x + k, NX), z, y, c), device_id_type=MESH
        )
    pl.semaphore_signal(barrier, inc=1, device_id=(x, z, y, 1 - c), device_id_type=MESH)

    def greet(k, carry):
        t = lax.rem(ctx + k, 16)
        dev = (x, t // 4, lax.rem(t, 4), c)
        pl.semaphore_signal(barrier, inc=1, device_id=dev, device_id_type=MESH)
        return carry

    lax.fori_loop(1, 16, greet, 0)
    pl.semaphore_wait(barrier, NX + 15)

    def along_x(src, dst, ss, rs, t, place):
        return pltpu.make_async_remote_copy(
            src_ref=src.at[t],
            dst_ref=dst.at[place],
            send_sem=ss.at[t],
            recv_sem=rs.at[place],
            device_id=(t, z, y, c),
            device_id_type=MESH,
        )

    def to_sibling(i):
        src, dst = (
            (dw.at[1 - c], sibling_dw),
            (gains, sibling_gains),
            (dwo.at[1 - c], sibling_dwo),
        )[i]
        return pltpu.make_async_remote_copy(
            src_ref=src,
            dst_ref=dst,
            send_sem=ss_s.at[i],
            recv_sem=rs_s.at[i],
            device_id=(x, z, y, 1 - c),
            device_id_type=MESH,
        )

    def over_ctx(i, t, place):
        src, dst, ss, rs = (
            (reduced.at[t], dw_parts, ss_w, rs_w),
            (gains, gains_all, ss_g, rs_g),
            (reduced_o.at[t], dwo_parts, ss_o, rs_o),
        )[i]
        return pltpu.make_async_remote_copy(
            src_ref=src,
            dst_ref=dst.at[place],
            send_sem=ss.at[t],
            recv_sem=rs.at[place],
            device_id=(x, t // 4, lax.rem(t, 4), c),
            device_id_type=MESH,
        )

    for k in (1, 3, 2):
        along_x(result, result_parts, ss_r, rs_r, lax.rem(x + k, NX), x).start()
    grad_w = tn(
        mixed_x[...].reshape(NX * ROWS, QX), branch_x[...].reshape(NX * ROWS, D)
    ).astype(BF16)
    for q in range(4):
        for i in range(8):
            dwo[i % 2, q * 4 + i // 2, :, :] = grad_w[
                i * 32 : (i + 1) * 32, q * 256 : (q + 1) * 256
            ]
    to_sibling(2).start()
    m = low_half((ROWS, 2 * HD))
    mh = low_half((BLK, 2 * HD))
    gq_sum = jnp.zeros((1, 2 * HD), F32)
    gk_sum = jnp.zeros((1, 2 * HD), F32)
    for n, k in enumerate((1, 3, 2, 0)):
        s = lax.rem(x + k, NX)
        at = pl.ds(pl.multiple_of(s * ROWS, ROWS), ROWS)
        place = place_of(x, s) * 4
        cos_s, sin_s = cos_r[at, :], sin_r[at, :]
        part = [recv[place + hh, :ROWS, :].astype(F32) for hh in range(4)]
        vals = [recv[place + hh, ROWS:, :].astype(F32) for hh in range(4)]
        grads = [
            jnp.where(m, part[0], swap(part[1])),
            jnp.where(m, part[2], swap(part[3])),
            jnp.where(m, swap(part[0] + part[1]), part[2] + part[3]),
        ]
        for p in range(3):
            turned = grads[p] * cos_s + swap_halves(grads[p] * sin_s)
            v = raw[at, p * 128 : (p + 1) * 128]
            gain = g_q[...] if p < 2 else g_k[...]
            r = lax.rsqrt(head_mean(v * v) + EPSILON)
            weighted = turned * gain
            grad = r * weighted - v * (r * r * r) * head_mean(weighted * v)
            low[at, p * 128 : (p + 1) * 128] = grad.astype(BF16)
            term = jnp.sum(turned * v * r, axis=0, keepdims=True)
            if p < 2:
                gq_sum = gq_sum + term
            else:
                gk_sum = gk_sum + term
        a, b = vals[0] + vals[1], vals[2] + vals[3]
        grad_v = jnp.concatenate([jnp.where(mh, a, swap(b)), jnp.where(mh, swap(a), b)], 0)
        low[at, 3 * 128 :] = grad_v.astype(BF16)
        grad_h = nt(low[at, :], w[...])
        gh[s] = grad_h.astype(BF16)
        if k:
            along_x(gh, gh_parts, ss_h, rs_h, s, x).start()
        term = jnp.sum(grad_h * h[at, :].astype(F32), axis=0, keepdims=True)
        attn[...] = term if n == 0 else attn[...] + term
        if n == 0:
            to_sibling(2).wait()

            def send_o(k, carry):
                t = lax.rem(ctx + k, 16)
                both = dwo[c, t].astype(F32) + sibling_dwo[t].astype(F32)
                reduced_o[t] = both.astype(BF16)
                over_ctx(2, t, ctx).start()
                return carry

            lax.fori_loop(1, 16, send_o, 0)
    for i in range(8):
        cols = slice(i * 128, i * 128 + 128)
        gains[i : i + 1, :] = attn[:, cols] / g_attn[:, cols]
        gains[8 + i : 9 + i, :] = gain_ffn[:, cols]
    gains[16:, :] = jnp.concatenate([gq_sum, gk_sum, jnp.zeros((6, 2 * HD), F32)], 0)
    grad_w = tn(h[...], low[...]).astype(BF16)
    for i in range(32):
        dw[i % 2, i // 2, :, :] = grad_w[i * 32 : (i + 1) * 32, :]
    to_sibling(0).start()
    to_sibling(1).start()
    to_sibling(1).wait()
    gains[...] = gains[...] + sibling_gains[...]
    to_sibling(0).wait()

    def send(k, carry):
        t = lax.rem(ctx + k, 16)
        reduced[t] = (dw[c, t].astype(F32) + sibling_dw[t].astype(F32)).astype(BF16)
        over_ctx(0, t, ctx).start()
        over_ctx(1, t, ctx).start()
        return carry

    lax.fori_loop(1, 16, send, 0)
    total = dw[c, ctx].astype(F32) + sibling_dw[ctx].astype(F32)
    total_o = dwo[c, ctx].astype(F32) + sibling_dwo[ctx].astype(F32)
    all_gains = gains[...]

    grad_h = gh[x].astype(F32)
    for k in (1, 3, 2):
        t = lax.rem(x + k, NX)
        along_x(gh, gh_parts, ss_h, rs_h, t, t).wait_recv()
        grad_h = grad_h + gh_parts[t].astype(F32)
    inputs = tokens[...].astype(F32)
    r = lax.rsqrt(jnp.mean(inputs * inputs, axis=-1, keepdims=True) + EPSILON)
    weighted = grad_h * g_attn[...]
    inner = jnp.mean(weighted * inputs, axis=-1, keepdims=True)
    tokens_o[...] = (
        grad_middle[...] + r * weighted - inputs * (r * r * r) * inner
    ).astype(BF16)
    out = middle[...] + result[x].astype(F32)
    for k in (1, 3, 2):
        t = lax.rem(x + k, NX)
        along_x(result, result_parts, ss_r, rs_r, t, t).wait_recv()
        out = out + result_parts[t].astype(F32)
    out_o[...] = out.astype(BF16)

    def collect(k, carry):
        t = lax.rem(ctx + k, 16)
        over_ctx(0, t, t).wait_recv()
        over_ctx(1, t, t).wait_recv()
        over_ctx(2, t, t).wait_recv()
        return (
            carry[0] + dw_parts[t].astype(F32),
            carry[1] + gains_all[t],
            carry[2] + dwo_parts[t].astype(F32),
        )

    total, all_gains, total_o = lax.fori_loop(1, 16, collect, (total, all_gains, total_o))
    qkv_o[...] = total.astype(BF16)
    wo_o[...] = total_o.astype(BF16)
    gains_o[...] = all_gains

    def drain(k, carry):
        t = lax.rem(ctx + k, 16)
        over_ctx(0, t, ctx).wait_send()
        over_ctx(1, t, ctx).wait_send()
        over_ctx(2, t, ctx).wait_send()
        return carry

    lax.fori_loop(1, 16, drain, 0)
    for k in (1, 3, 2):
        t = lax.rem(x + k, NX)
        along_x(gh, gh_parts, ss_h, rs_h, t, x).wait_send()
        along_x(result, result_parts, ss_r, rs_r, t, x).wait_send()


def project_back(number, *operands):
    vmem = pl.BlockSpec(memory_space=pltpu.VMEM)
    tokens = (NX, ROWS, D)
    wide = QX + 2 * KX
    return pl.pallas_call(
        project_back_kernel,
        in_specs=[vmem] * 16,
        out_specs=[vmem] * 5,
        out_shape=[
            jax.ShapeDtypeStruct((ROWS, D), BF16),
            jax.ShapeDtypeStruct((ROWS, D), BF16),
            jax.ShapeDtypeStruct((32, QX + 2 * KX), BF16),
            jax.ShapeDtypeStruct((32, QX), BF16),
            jax.ShapeDtypeStruct((24, 2 * HD), F32),
        ],
        scratch_shapes=[
            pltpu.VMEM((NX * ROWS, QX + 2 * KX), BF16),
            pltpu.VMEM((1, D), F32),
            pltpu.VMEM(tokens, BF16),
            pltpu.VMEM(tokens, BF16),
            pltpu.VMEM(tokens, BF16),
            pltpu.VMEM((2, 16, 32, wide), BF16),
            pltpu.VMEM((16, 32, wide), BF16),
            pltpu.VMEM((16, 32, wide), BF16),
            pltpu.VMEM((16, 32, wide), BF16),
            pltpu.VMEM((24, 2 * HD), F32),
            pltpu.VMEM((24, 2 * HD), F32),
            pltpu.VMEM((16, 24, 2 * HD), F32),
            pltpu.VMEM((2, 16, 32, QX), BF16),
            pltpu.VMEM((16, 32, QX), BF16),
            pltpu.VMEM((16, 32, QX), BF16),
            pltpu.VMEM((16, 32, QX), BF16),
        ]
        + [pltpu.SemaphoreType.DMA((n,)) for n in (NX, NX, NX, NX, 3, 3) + (16,) * 6],
        compiler_params=pltpu.CompilerParams(
            collective_id=number, has_side_effects=True, vmem_limit_bytes=VMEM_BYTES
        ),
        name="project_back",
    )(*operands)


def hand_out_kernel(qkv, gu, wo, wd, gains, q_o, k_o, v_o, o_o, g_o, u_o, d_o, ga_o, gf_o, gh_o):
    for s in range(NX):
        q_o[:, s * QX : (s + 1) * QX] = qkv[s, :, :QX].astype(F32)
        k_o[:, s * KX : (s + 1) * KX] = qkv[s, :, QX : QX + KX].astype(F32)
        v_o[:, s * KX : (s + 1) * KX] = qkv[s, :, QX + KX :].astype(F32)
        g_o[:, s * FX : (s + 1) * FX] = gu[s, :, :FX].astype(F32)
        u_o[:, s * FX : (s + 1) * FX] = gu[s, :, FX:].astype(F32)
        o_o[:, s * 256 : (s + 1) * 256] = wo[s, :, :].astype(F32)
        for rg in range(9):
            for l in range(2):
                at = slice(s * 256 + l * 128, s * 256 + l * 128 + 128)
                d_o[rg * 16 : rg * 16 + 16, at] = wd[
                    s, l * 16 : l * 16 + 16, rg * 128 : rg * 128 + 128
                ].astype(F32)
    total = gains[0] + gains[1] + gains[2] + gains[3]
    for i in range(8):
        ga_o[:, i * 128 : i * 128 + 128] = total[i : i + 1, :]
        gf_o[:, i * 128 : i * 128 + 128] = total[8 + i : 9 + i, :]
    gh_o[...] = total[16:, :] + swap(total[16:, :])


def hand_out(*operands):
    vmem = pl.BlockSpec(memory_space=pltpu.VMEM)
    shapes = [(32, D), (32, KV * HD), (32, KV * HD), (32, D), (32, FF), (32, FF), (FF // 32, D)]
    shapes += [(1, D), (1, D), (8, 2 * HD)]
    return pl.pallas_call(
        hand_out_kernel,
        in_specs=[vmem] * 5,
        out_specs=[vmem] * 10,
        out_shape=[jax.ShapeDtypeStruct(s, F32) for s in shapes],
        compiler_params=pltpu.CompilerParams(vmem_limit_bytes=VMEM_BYTES),
        name="hand_out",
    )(*operands)


def angle_constants():
    frequencies = ROPE_BASE ** (-np.arange(0, HD // 2, dtype=np.float64) * 2.0 / HD)
    phases = np.arange(LEN, dtype=np.float64)[:, None] * frequencies[None, :]
    cos, sin = np.cos(phases).astype(np.float32), np.sin(phases).astype(np.float32)
    return np.concatenate([cos] * 4, 1), np.concatenate([-sin, sin, -sin, sin], 1)


def columns_of(w, x, width):
    return lax.dynamic_slice_in_dim(w, x * width, width, axis=1)


def by_tiles(blocks):
    return blocks.reshape(-1, 9, 16, 2, 128).transpose(0, 3, 2, 1, 4).reshape(-1, 32, FX)


def body(
    tokens,
    pairs,
    w_query,
    w_key,
    w_value,
    w_out,
    w_gate,
    w_up,
    w_down,
    g_attn,
    g_query,
    g_key,
    g_ffn,
    cotangent,
):
    x = lax.axis_index("seq")
    cos_np, sin_np = angle_constants()
    cos_t, sin_t = jnp.asarray(cos_np), jnp.asarray(sin_np)
    gq2 = jnp.concatenate([g_query, g_query])[None]
    gk2 = jnp.concatenate([g_key, g_key])[None]

    swap_xz = [(a * 4 + b, b * 4 + a) for a in range(4) for b in range(4)]
    down_part = lax.ppermute(columns_of(w_down, x, D // 4), ("seq", "ctx_0"), swap_xz)
    mine = jnp.concatenate(
        [w_out, columns_of(w_gate, x, FX), columns_of(w_up, x, FX), by_tiles(down_part[None])[0]],
        axis=1,
    )

    wide = lax.all_gather(mine, CTX_FSDP, axis=0, tiled=True)
    h_all, w_qkv, pair = gather_in(1, tokens[0], g_attn[None], w_query, w_key, w_value, pairs)
    h_all = h_all.reshape(NX * ROWS, D)
    w_qkv = w_qkv.reshape(D, QX + 2 * KX)
    pair = pair.reshape(NX * 8, 128)

    send, raw, cos_r, sin_r = project(pair, h_all, w_qkv, cos_t, sin_t, gq2, gk2)
    recv, cot_all = exchange(2, "to_heads", ("c", "a2a", send), ("x", "ag", cotangent[0]))
    heads_out, q_s, k_s, v_s, o_t, inv = attend(pair, recv)
    (mixed_parts,) = exchange(3, "to_tokens", ("t", "a2a", heads_out))
    middle, result4, grad_w_ffn, grad_middle, grad_branch, mixed, back_parts, gain_ffn = middle_part(
        4, mixed_parts, tokens[0], cot_all, g_ffn[None], wide
    )
    sums = lax.psum_scatter(grad_w_ffn, CTX_FSDP, scatter_dimension=0, tiled=True)
    (recv_g,) = exchange(6, "to_heads_back", ("r", "a2a", back_parts))
    sends_back = attend_back(pair, recv_g, q_s, k_s, v_s, o_t, inv)
    recv_back, branch_x, mixed_x = exchange(
        7,
        "to_tokens_back",
        ("c", "a2a", sends_back),
        ("x", "ag", grad_branch),
        ("x", "a2a", mixed),
    )
    output, grad_tokens, sum_qkv, sum_o, gains = project_back(
        8,
        recv_back,
        raw,
        h_all,
        w_qkv,
        cos_r,
        sin_r,
        gq2,
        gk2,
        g_attn[None],
        mixed_x,
        branch_x,
        result4,
        gain_ffn,
        tokens[0],
        grad_middle,
        middle,
    )
    qkv, gate_up, out_rows, down_rows, gains = exchange(
        9,
        "gather_out",
        ("x", "ag", sum_qkv),
        ("x", "ag", sums, (0, 2 * FX)),
        ("d", "ag", sum_o),
        ("d", "ag", sums, (2 * FX, FX)),
        ("x", "ag", gains),
    )
    *weights, gain_a, gain_f, gain_h = hand_out(qkv, gate_up, out_rows, down_rows, gains)
    return (
        output[None],
        grad_tokens[None],
        *weights,
        gain_a[0],
        gain_h[0, :HD],
        gain_h[1, :HD],
        gain_f[0],
    )


def solution(mesh):
    finer = Mesh(
        mesh.devices.reshape(mesh.shape["seq"], 4, 4, mesh.shape["fsdp"]),
        ("seq", "ctx_0", "ctx_1", "fsdp"),
    )
    tokens_spec = P(("seq", "fsdp"), CTX, None)
    rows_spec = P(CTX_FSDP, None)
    return jax.shard_map(
        body,
        mesh=finer,
        in_specs=(tokens_spec, P(("seq", "fsdp"), None))
        + (rows_spec,) * 7
        + (P(),) * 4
        + (tokens_spec,),
        out_specs=(tokens_spec, tokens_spec) + (rows_spec,) * 7 + (P(),) * 4,
        check_vma=False,
    )
```
